32 devices in a mesh: dp: 8 (over z, y), tensor: 4 (over x, core).
Axes of the slice: x: 2, y: 2, z: 4, core: 2. Of those that a mesh axis runs over, the one named last changes fastest.
Arguments:
- tokens: bfloat16 [16384, 768], P(('dp', 'tensor')), may hold values from -6 to 6
- doc_lengths: int32 [32, 8], P('dp'), may hold values from 0 to 512, as said below
- qkv_weight: bfloat16 [768, 2304], P(None, 'tensor'), may hold values from -0.21875 to 0.21875
- attn_out_weight: bfloat16 [768, 768], P('tensor'), may hold values from -1.25 to 1.25
- norm1_gain: float32 [768], replicated, may hold values from 0.5 to 1.5
- norm1_bias: float32 [768], replicated, may hold values from -0.8 to 0.8
- ffn_in_weight: bfloat16 [768, 3072], P(None, 'tensor'), may hold values from -0.21875 to 0.21875
- ffn_out_weight: bfloat16 [3072, 768], P('tensor'), may hold values from -0.109375 to 0.109375
- norm2_gain: float32 [768], replicated, may hold values from 0.5 to 1.5
- norm2_bias: float32 [768], replicated, may hold values from -0.8 to 0.8
- adapter_down: bfloat16 [16, 768, 48], P(None, ('dp', 'tensor')), may hold values from -0.21875 to 0.21875
- adapter_up: bfloat16 [16, 48, 768], P(None, None, ('dp', 'tensor')), may hold values from -1.75 to 1.75
- merging_query: bfloat16 [768, 768], P(('dp', 'tensor')), may hold values from -0.4375 to 0.4375
- merging_key: bfloat16 [768, 768], P(('dp', 'tensor')), may hold values from -0.21875 to 0.21875
- merging_value: bfloat16 [768, 768], P(('dp', 'tensor')), may hold values from -0.21875 to 0.21875
- merging_gain: float32 [768], replicated, may hold values from 0.5 to 1.5
- merging_bias: float32 [768], replicated, may hold values from -0.8 to 0.8
- out_grad: bfloat16 [16384, 768], P(('dp', 'tensor')), may hold values from -6 to 6
Outputs:
- layer_out: float32 [16384, 768], P(('dp', 'tensor'))
- input_grad: float32 [16384, 768], P(('dp', 'tensor'))
- grad_query: float32 [768, 768], P(('dp', 'tensor'))
- grad_key: float32 [768, 768], P(('dp', 'tensor'))
- grad_value: float32 [768, 768], P(('dp', 'tensor'))
- grad_gain: float32 [768], replicated
- grad_bias: float32 [768], replicated
- adapter_mass: float32 [16], replicated
The draws below stay inside these ranges and needn't reach their ends.
Inputs may be any that keep to these rules, and one draw needn't show every extreme that they name: `doc_lengths`: A row's 8 lengths, some of which may be 0, sum to at most 512; the slots past the sum are padding. Some row holds one document of 512 tokens.
All inputs are finite; a program needn't handle non-finite values.
Results may differ from the reference program's by a relative error of at most 0.04.
Values may be sent and summed in bfloat16 or wider, within the bound.
No kernel may reach another device: no remote copies, remote signals or barrier semaphores. Data moves between devices by JAX's collectives and lax.ppermute only.
A program may use at most 192 MiB of HBM per device.

```python
import math
import jax
import jax.numpy as jnp
from jax import lax

D = 768
HEADS = 12
HEAD_DIM = 64
FF = 3072
ADAPTERS = 16
ADAPTER_DIM = 48
SEQ = 512
DOCS = 8
ROWS_DEVICE = 1
ROWS = 32
TOKENS = 16384


def draw_doc_lengths(key, part):
    row_ids = jnp.arange(ROWS, dtype=jnp.int32)
    owner = row_ids // ROWS_DEVICE
    final_owner = max(ROWS // ROWS_DEVICE - 1, 1)
    shortfall = (final_owner - owner) * (SEQ * 2 // 3) // final_owner
    filled = SEQ - shortfall
    cut_key, shape_key = jax.random.split(key)
    raw_cuts = jax.random.randint(cut_key, (ROWS, DOCS - 1), 0, SEQ + 1)
    skew_cuts = jax.random.randint(shape_key, (ROWS, DOCS - 1), 0, SEQ + 1)
    tailed = raw_cuts * skew_cuts // SEQ
    cuts = tailed * filled[:, None] // SEQ
    ordered = jnp.sort(cuts, axis=1)
    edges = jnp.concatenate([jnp.zeros((ROWS, 1), jnp.int32), ordered.astype(jnp.int32), filled[:, None].astype(jnp.int32)], axis=1)
    lengths = edges[:, 1:] - edges[:, :-1]
    single = jnp.zeros((DOCS,), jnp.int32).at[0].set(SEQ)
    lengths = jnp.where((row_ids == ROWS - 1)[:, None], single[None, :], lengths)
    return lengths.astype(jnp.int32)


def level_of(rng, dims, cuts, low, top_value):
    loudness = 1.0
    for dim, shards_of in cuts:
        steps = jax.random.uniform(jax.random.fold_in(jax.random.fold_in(rng, 6), dim), (shards_of,), jnp.float32, low / len(cuts), top_value / len(cuts))
        loudness = loudness * jnp.repeat(jnp.exp(steps), dims[dim] // shards_of).reshape((-1,) + (1,) * (len(dims) - 1 - dim))
    return loudness


def normal_values(rng, extent, width, reach, cuts=(), kind=jnp.bfloat16):
    result = width * jax.random.normal(rng, extent, jnp.float32)
    if cuts:
        result = result * level_of(rng, extent, cuts, -0.22, 0.18)
    return jnp.clip(result, -reach, reach).astype(kind)


def setup_inputs(seed: int = 0) -> dict:
    splits = jax.random.split(jax.random.key(seed), 19)
    tokens = normal_values(splits[0], (TOKENS, D), 1.0, 6.0, ((0, 32),))
    doc_lengths = draw_doc_lengths(jax.random.fold_in(splits[18], 71), 0)
    qkv_weight = normal_values(splits[2], (D, 3 * D), D ** -0.5, 0.21875, ((1, 4),))
    attn_out_weight = normal_values(splits[3], (D, D), (D // 32) ** -0.5, 1.25, ((0, 4),))
    norm1_gain = jnp.clip(1.0 + 0.1 * jax.random.normal(splits[4], (D,), jnp.float32), 0.5, 1.5)
    norm1_bias = normal_values(splits[5], (D,), 0.2, 0.8, (), jnp.float32)
    ffn_in_weight = normal_values(splits[6], (D, FF), D ** -0.5, 0.21875, ((1, 4),))
    ffn_out_weight = normal_values(splits[7], (FF, D), FF ** -0.5, 0.109375, ((0, 4),))
    norm2_gain = jnp.clip(1.0 + 0.1 * jax.random.normal(splits[8], (D,), jnp.float32), 0.5, 1.5)
    norm2_bias = normal_values(splits[9], (D,), 0.2, 0.8, (), jnp.float32)
    adapter_down = normal_values(splits[10], (ADAPTERS, D, ADAPTER_DIM), D ** -0.5, 0.21875, ((1, 32),))
    adapter_up = normal_values(splits[11], (ADAPTERS, ADAPTER_DIM, D), (ADAPTER_DIM // 4) ** -0.5, 1.75, ((2, 32),))
    merging_query = normal_values(splits[12], (D, D), (D // 4) ** -0.5, 0.4375, ((0, 32),))
    merging_key = normal_values(splits[13], (D, D), D ** -0.5, 0.21875, ((0, 32),))
    merging_value = normal_values(splits[14], (D, D), D ** -0.5, 0.21875, ((0, 32),))
    merging_gain = jnp.clip(1.0 + 0.1 * jax.random.normal(splits[15], (D,), jnp.float32), 0.5, 1.5)
    merging_bias = normal_values(splits[16], (D,), 0.2, 0.8, (), jnp.float32)
    out_grad = normal_values(splits[17], (TOKENS, D), 1.0, 6.0, ((0, 32),))
    return dict(tokens=tokens, doc_lengths=doc_lengths, qkv_weight=qkv_weight, attn_out_weight=attn_out_weight, norm1_gain=norm1_gain, norm1_bias=norm1_bias, ffn_in_weight=ffn_in_weight, ffn_out_weight=ffn_out_weight, norm2_gain=norm2_gain, norm2_bias=norm2_bias, adapter_down=adapter_down, adapter_up=adapter_up, merging_query=merging_query, merging_key=merging_key, merging_value=merging_value, merging_gain=merging_gain, merging_bias=merging_bias, out_grad=out_grad)


@jax.custom_vjp
def low(v):
    return lax.optimization_barrier(v.astype(jnp.bfloat16)).astype(jnp.float32)

@jax.custom_vjp
def low_back(v):
    return v

def low_keep(v):
    return (low(v), None)

def low_pass(kept, grad):
    return (grad,)

def back_keep(v):
    return (v, None)

def back_low(kept, grad):
    return (low(grad),)
low.defvjp(low_keep, low_pass)
low_back.defvjp(back_keep, back_low)
highest = lax.Precision.HIGHEST

def product(left_side, right_side):
    return jnp.dot(left_side, right_side, precision=highest)

def normalize(argument, gain, shift):
    centre = lax.optimization_barrier(jnp.mean(argument, axis=-1, keepdims=True))
    centered = argument - centre
    scaled = centered * lax.rsqrt(lax.optimization_barrier(jnp.mean(centered * centered, axis=-1, keepdims=True)) + 1e-12)
    return scaled * gain + shift

def gelu(argument):
    return 0.5 * argument * (1.0 + lax.erf(argument * 0.7071067811865476))

def segment_info(lengths):
    doc_ends = jnp.cumsum(lengths, axis=1)
    position = jnp.arange(SEQ, dtype=jnp.int32)
    segment = lax.optimization_barrier(jnp.sum((position[None, :, None] >= doc_ends[:, None, :]).astype(jnp.int32), axis=2))
    valid = position[None, :] < doc_ends[:, -1:]
    return (segment, valid)

def attend(pieces):
    row_block, segment = pieces
    queries = row_block[:, :, 0]
    key_rows = row_block[:, :, 1]
    value_rows = row_block[:, :, 2]
    scores = low_back(jnp.einsum('qhd,khd->hqk', queries, key_rows, precision=highest) * HEAD_DIM ** (-0.5))
    same_doc = segment[:, None] == segment[None, :]
    scores = jnp.where(same_doc[None], scores, -1e+30)
    attn_prob = low(jax.nn.softmax(scores, axis=-1))
    attended = jnp.einsum('hqk,khd->qhd', attn_prob, value_rows, precision=highest)
    return low(low_back(attended)).reshape(SEQ, HEADS * HEAD_DIM)

def layer(inputs, segment, frozen, merging_query, merging_key, merging_value, merging_gain, merging_bias):
    qkv_weight, attn_out_weight, norm1_gain, norm1_bias, ffn_in_weight, ffn_out_weight, norm2_gain, norm2_bias, adapter_down, adapter_up = frozen
    row_count = segment.shape[0]
    qkv = low(low_back(product(inputs, qkv_weight))).reshape(row_count, SEQ, HEADS, 3, HEAD_DIM)
    attended = lax.map(jax.checkpoint(attend), (qkv, segment)).reshape(row_count * SEQ, D)
    first = normalize(inputs + low_back(product(attended, attn_out_weight)), norm1_gain, norm1_bias)
    pre_act = low_back(product(low(first), ffn_in_weight))
    second = normalize(first + low_back(product(low(gelu(pre_act)), ffn_out_weight)), norm2_gain, norm2_bias)
    second_low = low(second)
    middle = low_back(jnp.einsum('td,adr->tar', second_low, adapter_down, precision=highest))
    adapted = low(low_back(second[:, None, :] + jnp.einsum('tar,ard->tad', low(gelu(middle)), adapter_up, precision=highest)))
    fquery = low(low_back(product(second_low, merging_query)))
    probe = low(low_back(product(fquery, merging_key.T)))
    logits = low_back(jnp.einsum('td,tad->ta', probe, adapted, precision=highest) * D ** (-0.5))
    mix = jax.nn.softmax(logits, axis=-1)
    blended = low(low_back(jnp.einsum('ta,tad->td', low(mix), adapted, precision=highest)))
    joined = normalize(second + low_back(product(blended, merging_value)), merging_gain, merging_bias)
    return (joined, mix)

def reference(tokens, doc_lengths, qkv_weight, attn_out_weight, norm1_gain, norm1_bias, ffn_in_weight, ffn_out_weight, norm2_gain, norm2_bias, adapter_down, adapter_up, merging_query, merging_key, merging_value, merging_gain, merging_bias, out_grad):
    frozen = tuple((arr.astype(jnp.float32) for arr in (qkv_weight, attn_out_weight, norm1_gain, norm1_bias, ffn_in_weight, ffn_out_weight, norm2_gain, norm2_bias, adapter_down, adapter_up)))
    trained = tuple((arr.astype(jnp.float32) for arr in (merging_query, merging_key, merging_value, merging_gain, merging_bias)))
    group = math.gcd(ROWS, max(1, 4096 // SEQ))
    turns = ROWS // group
    token_groups = tokens.reshape(turns, group * SEQ, D)
    length_groups = doc_lengths.reshape(turns, group, DOCS)
    grad_groups = out_grad.reshape(turns, group * SEQ, D)

    def step(running, pieces):
        sums, mass_sum, count = running
        token_group, length_group, grad_group = pieces
        segment, valid = segment_info(length_group)
        keep_mask = valid.reshape(-1).astype(jnp.float32)

        def forward(inputs, query_w, key_w, value_w, gain_w, bias_w):
            return layer(inputs, segment, frozen, query_w, key_w, value_w, gain_w, bias_w)
        (joined, mix), pull = jax.vjp(forward, token_group.astype(jnp.float32), trained[0], trained[1], trained[2], trained[3], trained[4])
        grads = pull((grad_group.astype(jnp.float32) * keep_mask[:, None], jnp.zeros_like(mix)))
        sums = tuple((total + grad for total, grad in zip(sums, grads[1:])))
        mass_sum = mass_sum + lax.optimization_barrier(jnp.sum(mix * keep_mask[:, None], axis=0))
        count = count + jnp.sum(keep_mask)
        return ((sums, mass_sum, count), (joined, grads[0]))
    start_state = (tuple((jnp.zeros_like(arr) for arr in trained)), jnp.zeros((ADAPTERS,), jnp.float32), jnp.zeros((), jnp.float32))
    (sums, mass_sum, count), (outputs, input_grads) = lax.scan(step, start_state, (token_groups, length_groups, grad_groups))
    return (outputs.reshape(TOKENS, D), input_grads.reshape(TOKENS, D), sums[0], sums[1], sums[2], sums[3], sums[4], mass_sum / count)
```

```python
import functools

import jax
import jax.numpy as jnp
from jax import lax
from jax.experimental import pallas as pl
from jax.experimental.pallas import tpu as pltpu
from jax.sharding import PartitionSpec as P

HEAD_DIM = 64
AXES = ("dp", "tensor")
VMEM_BYTES = 58 * 1024 * 1024
LANES = 128
EPS = 1e-12
BIG_NEGATIVE = -1e30
ROOT_HALF = 0.7071067811865476
ROOT_TAU = 0.3989422804014327
F32, BF16 = jnp.float32, jnp.bfloat16

SMEM = pl.BlockSpec(memory_space=pltpu.SMEM)
VMEM = pl.BlockSpec(memory_space=pltpu.VMEM)
ANY = pl.BlockSpec(memory_space=pl.ANY)


def dot(a, b):
    return lax.dot_general(a, b, (((1,), (0,)), ((), ())), preferred_element_type=F32)


def dot_last(a, b):
    return lax.dot_general(a, b, (((1,), (1,)), ((), ())), preferred_element_type=F32)


def dot_first(a, b):
    return lax.dot_general(a, b, (((0,), (0,)), ((), ())), preferred_element_type=F32)


def normalize(u):
    centered = u - jnp.mean(u, axis=-1, keepdims=True)
    inv_std = lax.rsqrt(jnp.mean(centered * centered, axis=-1, keepdims=True) + EPS)
    return centered * inv_std, inv_std


def norm_back(grad, normed, inv_std):
    return inv_std * (
        grad
        - jnp.mean(grad, axis=-1, keepdims=True)
        - normed * jnp.mean(grad * normed, axis=-1, keepdims=True)
    )


def gelu_both(u):
    half = 0.5 * (1.0 + lax.erf(u * ROOT_HALF))
    return u * half, half + u * jnp.exp(-0.5 * u * u) * ROOT_TAU


def piece_copies(pieces, place, parity, scratch, sems):
    out = {}
    for i, (piece, (quarter, side)) in enumerate(zip(pieces, place)):
        rows = piece.shape[0]
        if side is None:
            target = scratch.at[quarter]
        else:
            first = parity if side == 0 else 1 - parity
            target = scratch.at[quarter, pl.ds(pl.multiple_of(first * rows, 16), rows)]
        out.setdefault(quarter, []).append(pltpu.make_async_copy(piece, target, sems.at[i]))
    return out


def bring_quarters(step, groups):
    @pl.when(step == 0)
    def _():
        for copies in groups:
            for quarter in sorted(copies):
                for copy in copies[quarter]:
                    copy.start()

    for quarter in range(4):

        @pl.when(step == quarter)
        def _(quarter=quarter):
            for copies in groups:
                for copy in copies[quarter]:
                    copy.wait()


PLACE = ((0, None), (1, None), (2, 0), (2, 1), (3, 0), (3, 1))
N_PIECES = len(PLACE)


def segment_bias(meta_ref, lengths_ref, bias_ref):
    seq = bias_ref.shape[0]
    row = meta_ref[1]
    by_row = lax.broadcasted_iota(jnp.int32, (seq, 1), 0)
    by_lane = lax.broadcasted_iota(jnp.int32, (1, seq), 1)
    seg_row = jnp.zeros((seq, 1), jnp.int32)
    seg_lane = jnp.zeros((1, seq), jnp.int32)
    end = jnp.int32(0)
    for i in range(lengths_ref.shape[1]):
        end = end + lengths_ref[row, i]
        seg_row = seg_row + jnp.where(by_row >= end, 1, 0)
        seg_lane = seg_lane + jnp.where(by_lane >= end, 1, 0)
    bias_ref[...] = jnp.where(seg_row == seg_lane, 0.0, BIG_NEGATIVE).astype(F32)


def attend_forward(*refs):
    meta, lengths, tokens, gain, shift = refs[:5]
    qkv_pieces, out_pieces = refs[5 : 5 + N_PIECES], refs[5 + N_PIECES : 5 + 2 * N_PIECES]
    rest = refs[5 + 2 * N_PIECES :]
    flat_out, turned_out, att_out, prob_out, first_out, normed_out, inv_out = rest[:7]
    qkv_w, out_w, bias, total, sems, out_sems = rest[7:]
    step = pl.program_id(0)
    parity = meta[0]
    bring_quarters(
        step,
        (
            piece_copies(qkv_pieces, PLACE, parity, qkv_w, sems),
            piece_copies(out_pieces, PLACE, parity, out_w, out_sems),
        ),
    )

    @pl.when(step == 0)
    def _():
        segment_bias(meta, lengths, bias)
        total[...] = tokens[...].astype(F32)

    flat = dot(tokens[...], qkv_w[step]).astype(BF16)
    flat_out[0] = flat
    turned = flat.T
    turned_out[0] = turned
    width = 3 * HEAD_DIM
    for head in range(flat.shape[1] // width):
        base = head * width
        keys = flat[:, base + HEAD_DIM : base + 2 * HEAD_DIM]
        queries = turned[base : base + HEAD_DIM] * BF16(HEAD_DIM**-0.5)
        values = turned[base + 2 * HEAD_DIM : base + width]
        scores = dot(keys, queries) + bias[...]
        exponent = jnp.exp(scores - jnp.max(scores, axis=0, keepdims=True))
        prob = (exponent * (1.0 / jnp.sum(exponent, axis=0, keepdims=True))).astype(BF16)
        prob_out[0, head] = prob
        att_out[0, head * HEAD_DIM : (head + 1) * HEAD_DIM] = dot(values, prob).astype(BF16)
    total[...] += dot(att_out[0].T, out_w[step])

    @pl.when(step == 3)
    def _():
        normed, inv_std = normalize(total[...])
        normed_out[...] = normed
        inv_out[...] = inv_std
        first_out[...] = normed * gain[...] + shift[...]


def whole(shape):
    return pl.BlockSpec(shape, lambda i: (0,) * len(shape))


def by_quarter(shape):
    return pl.BlockSpec((1, *shape), lambda i: (i,) + (0,) * len(shape))


def sds(shape, dtype):
    return jax.ShapeDtypeStruct(shape, dtype)


def params(**kw):
    return pltpu.CompilerParams(vmem_limit_bytes=VMEM_BYTES, **kw)


def call_attend_forward(meta, lengths, tokens, gain, shift, qkv_pieces, out_pieces):
    seq, width = tokens.shape
    columns = qkv_pieces[0].shape[1]
    heads = columns // (3 * HEAD_DIM)
    inner = heads * HEAD_DIM
    return pl.pallas_call(
        attend_forward,
        grid=(4,),
        in_specs=[SMEM, SMEM, whole((seq, width)), whole((1, width)), whole((1, width))]
        + [ANY] * (2 * N_PIECES),
        out_specs=[
            by_quarter((seq, columns)),
            by_quarter((columns, seq)),
            by_quarter((inner, seq)),
            by_quarter((heads, seq, seq)),
            whole((seq, width)),
            whole((seq, width)),
            whole((seq, 1)),
        ],
        out_shape=[
            sds((4, seq, columns), BF16),
            sds((4, columns, seq), BF16),
            sds((4, inner, seq), BF16),
            sds((4, heads, seq, seq), BF16),
            sds((seq, width), F32),
            sds((seq, width), F32),
            sds((seq, 1), F32),
        ],
        scratch_shapes=[
            pltpu.VMEM((4, width, columns), BF16),
            pltpu.VMEM((4, inner, width), BF16),
            pltpu.VMEM((seq, seq), F32),
            pltpu.VMEM((seq, width), F32),
            pltpu.SemaphoreType.DMA((N_PIECES,)),
            pltpu.SemaphoreType.DMA((N_PIECES,)),
        ],
        compiler_params=params(),
        name="attend_forward",
    )(meta, lengths, tokens, gain, shift, *qkv_pieces, *out_pieces)


def ffn_forward(*refs):
    meta, first = refs[:2]
    in_pieces, out_pieces = refs[2 : 2 + N_PIECES], refs[2 + N_PIECES : 2 + 2 * N_PIECES]
    slope_out, sum_out, in_w, out_w, low, sems, out_sems = refs[2 + 2 * N_PIECES :]
    step = pl.program_id(0)
    bring_quarters(
        step,
        (
            piece_copies(in_pieces, PLACE, meta[0], in_w, sems),
            piece_copies(out_pieces, PLACE, meta[0], out_w, out_sems),
        ),
    )

    @pl.when(step == 0)
    def _():
        low[...] = first[...].astype(BF16)
        sum_out[...] = first[...]

    value, slope = gelu_both(dot(low[...], in_w[step]))
    slope_out[0] = slope.astype(BF16)
    sum_out[...] += dot(value.astype(BF16), out_w[step])


def call_ffn_forward(meta, first, in_pieces, out_pieces):
    seq, width = first.shape
    hidden = in_pieces[0].shape[1]
    return pl.pallas_call(
        ffn_forward,
        grid=(4,),
        in_specs=[SMEM, whole((seq, width))] + [ANY] * (2 * N_PIECES),
        out_specs=[by_quarter((seq, hidden)), whole((seq, width))],
        out_shape=[sds((4, seq, hidden), BF16), sds((seq, width), F32)],
        scratch_shapes=[
            pltpu.VMEM((4, width, hidden), BF16),
            pltpu.VMEM((4, hidden, width), BF16),
            pltpu.VMEM((seq, width), BF16),
            pltpu.SemaphoreType.DMA((N_PIECES,)),
            pltpu.SemaphoreType.DMA((N_PIECES,)),
        ],
        compiler_params=params(),
        name="ffn_forward",
    )(meta, first, *in_pieces, *out_pieces)


def merging(
    n_adapters,
    meta,
    lengths,
    sums,
    gain2,
    shift2,
    gain3,
    shift3,
    out_grad,
    weights,
    layer_out,
    grad_sum2_out,
    grad_low_out,
    grad_out,
    lines_out,
):
    seq, width = sums.shape
    scale = width**-0.5
    down, up, query, key, value = (weights.at[i] for i in range(5))
    spread = jnp.where(
        lax.broadcasted_iota(jnp.int32, (LANES, width), 0)
        == lax.broadcasted_iota(jnp.int32, (LANES, width), 1) // (width // n_adapters),
        1.0,
        0.0,
    ).astype(BF16)
    real_lane = lax.broadcasted_iota(jnp.int32, (1, LANES), 1) < n_adapters

    def by_adapter(terms):
        high = terms.astype(BF16)
        rest = (terms - high.astype(F32)).astype(BF16)
        return dot_last(high, spread) + dot_last(rest, spread)

    normed2, inv_std2 = normalize(sums[...])
    second = normed2 * gain2[...] + shift2[...]
    second_low = second.astype(BF16)
    middle = dot(second_low, down[...])
    act, slope = gelu_both(middle)
    act = act.astype(BF16).astype(F32)
    fquery = dot(second_low, query[...]).astype(BF16)
    probe = dot_last(fquery, key[...]).astype(BF16)
    probe_up = dot(probe, up[...])
    logits = scale * (
        jnp.sum(probe.astype(F32) * second, axis=1, keepdims=True) + by_adapter(act * probe_up)
    )
    logits = jnp.where(real_lane, logits, BIG_NEGATIVE)
    exponent = jnp.exp(logits - jnp.max(logits, axis=1, keepdims=True))
    mix = exponent / jnp.sum(exponent, axis=1, keepdims=True)
    mix_low = mix.astype(BF16)
    mix_sum = jnp.sum(mix_low.astype(F32), axis=1, keepdims=True)
    mix_wide = dot(mix_low, spread)
    blended = (second * mix_sum + dot_last((mix_wide * act).astype(BF16), up[...])).astype(BF16)
    normed3, inv_std3 = normalize(second + dot(blended, value[...]))
    layer_out[...] = normed3 * gain3[...] + shift3[...]

    count = jnp.int32(0)
    for i in range(lengths.shape[1]):
        count = count + lengths[meta[1], i]
    keep = jnp.where(lax.broadcasted_iota(jnp.int32, (seq, 1), 0) < count, 1.0, 0.0)
    cot = out_grad[...].astype(F32) * keep
    lines_out[...] = jnp.zeros_like(lines_out)
    lines_out[0:1] = jnp.sum(cot * normed3, axis=0, keepdims=True)
    lines_out[1:2] = jnp.sum(cot, axis=0, keepdims=True)
    mass = jnp.sum(mix * keep, axis=0, keepdims=True)
    lane = lax.broadcasted_iota(jnp.int32, (1, LANES), 1)
    lines_out[2:3, :LANES] = jnp.where(lane == n_adapters, jnp.sum(keep), mass)

    grad_pre = norm_back(cot * gain3[...], normed3, inv_std3)
    grad_proj = grad_pre.astype(BF16)
    grad_out[2] = dot_first(blended, grad_proj).astype(grad_out.dtype)
    grad_blend = dot_last(grad_proj, value[...]).astype(BF16)
    blend_up = dot(grad_blend, up[...])
    grad_mix = jnp.sum(grad_blend.astype(F32) * second, axis=1, keepdims=True) + by_adapter(
        act * blend_up
    )
    grad_logits = (mix * (grad_mix - jnp.sum(grad_mix * mix, axis=1, keepdims=True))).astype(BF16)
    logit_sum = jnp.sum(grad_logits.astype(F32), axis=1, keepdims=True)
    logit_wide = dot(grad_logits, spread)
    grad_probe = (
        scale * (second * logit_sum + dot_last((logit_wide * act).astype(BF16), up[...]))
    ).astype(BF16)
    grad_out[1] = dot_first(grad_probe, fquery).astype(grad_out.dtype)
    grad_fquery = dot(grad_probe, key[...]).astype(BF16)
    grad_out[0] = dot_first(second_low, grad_fquery).astype(grad_out.dtype)
    grad_middle = ((mix_wide * blend_up + (scale * logit_wide) * probe_up) * slope).astype(BF16)
    grad_second = (
        grad_pre
        + dot_last(grad_fquery, query[...])
        + grad_blend.astype(F32) * mix_sum
        + probe.astype(F32) * (scale * logit_sum)
        + dot_last(grad_middle, down[...])
    )
    grad_sum2 = norm_back(grad_second * gain2[...], normed2, inv_std2)
    grad_sum2_out[...] = grad_sum2
    grad_low_out[...] = grad_sum2.astype(BF16)


def call_merging(
    n_adapters, meta, lengths, sums, gain2, shift2, gain3, shift3, out_grad, weights, grad_type
):
    seq, width = sums.shape
    return pl.pallas_call(
        functools.partial(merging, n_adapters),
        in_specs=[SMEM, SMEM] + [VMEM] * 7,
        out_specs=[VMEM] * 5,
        out_shape=[
            sds((seq, width), F32),
            sds((seq, width), F32),
            sds((seq, width), BF16),
            sds((3, width, width), grad_type),
            sds((8, width), F32),
        ],
        compiler_params=params(),
        name="merging",
    )(meta, lengths, sums, gain2, shift2, gain3, shift3, out_grad, weights)


def ffn_backward(*refs):
    meta, grad_sum2, grad_low, normed1, inv_std1, gain1, slope = refs[:7]
    in_pieces, out_pieces = refs[7 : 7 + N_PIECES], refs[7 + N_PIECES : 7 + 2 * N_PIECES]
    grad_out, grad_low_out, in_w, out_w, total, sems, out_sems = refs[7 + 2 * N_PIECES :]
    step = pl.program_id(0)
    bring_quarters(
        step,
        (
            piece_copies(out_pieces, PLACE, meta[0], out_w, out_sems),
            piece_copies(in_pieces, PLACE, meta[0], in_w, sems),
        ),
    )

    @pl.when(step == 0)
    def _():
        total[...] = grad_sum2[...]

    grad_pre = (dot_last(grad_low[...], out_w[step]) * slope[0].astype(F32)).astype(BF16)
    total[...] += dot_last(grad_pre, in_w[step])

    @pl.when(step == 3)
    def _():
        grad = norm_back(total[...] * gain1[...], normed1[...], inv_std1[...])
        grad_out[...] = grad
        grad_low_out[...] = grad.astype(BF16)


def call_ffn_backward(
    meta, grad_sum2, grad_low, normed1, inv_std1, gain1, slope, in_pieces, out_pieces
):
    seq, width = grad_sum2.shape
    hidden = in_pieces[0].shape[1]
    return pl.pallas_call(
        ffn_backward,
        grid=(4,),
        in_specs=[
            SMEM,
            whole((seq, width)),
            whole((seq, width)),
            whole((seq, width)),
            whole((seq, 1)),
            whole((1, width)),
            by_quarter((seq, hidden)),
        ]
        + [ANY] * (2 * N_PIECES),
        out_specs=[whole((seq, width)), whole((seq, width))],
        out_shape=[sds((seq, width), F32), sds((seq, width), BF16)],
        scratch_shapes=[
            pltpu.VMEM((4, width, hidden), BF16),
            pltpu.VMEM((4, hidden, width), BF16),
            pltpu.VMEM((seq, width), F32),
            pltpu.SemaphoreType.DMA((N_PIECES,)),
            pltpu.SemaphoreType.DMA((N_PIECES,)),
        ],
        compiler_params=params(),
        name="ffn_backward",
    )(meta, grad_sum2, grad_low, normed1, inv_std1, gain1, slope, *in_pieces, *out_pieces)


def attend_backward(*refs):
    meta, grad_sum1, grad_low, flat_ref, turned_ref, att_ref, prob_ref = refs[:7]
    qkv_pieces, out_pieces = refs[7 : 7 + N_PIECES], refs[7 + N_PIECES : 7 + 2 * N_PIECES]
    input_grad, qkv_w, out_w, grad_turned, sems, out_sems = refs[7 + 2 * N_PIECES :]
    step = pl.program_id(0)
    bring_quarters(
        step,
        (
            piece_copies(out_pieces, PLACE, meta[0], out_w, out_sems),
            piece_copies(qkv_pieces, PLACE, meta[0], qkv_w, sems),
        ),
    )

    @pl.when(step == 0)
    def _():
        input_grad[...] = grad_sum1[...]

    grad_att = dot_last(out_w[step], grad_low[...]).astype(BF16)
    width = 3 * HEAD_DIM
    root = HEAD_DIM**-0.5
    for head in range(att_ref.shape[1] // HEAD_DIM):
        base = head * width
        queries = turned_ref[0, base : base + HEAD_DIM]
        keys = turned_ref[0, base + HEAD_DIM : base + 2 * HEAD_DIM]
        values = flat_ref[0, :, base + 2 * HEAD_DIM : base + width]
        part = slice(head * HEAD_DIM, (head + 1) * HEAD_DIM)
        grad = grad_att[part]
        prob = prob_ref[0, head]
        row_dot = jnp.sum(grad.astype(F32) * att_ref[0, part].astype(F32), axis=0, keepdims=True)
        grad_scores = (prob.astype(F32) * (dot(values, grad) - row_dot)).astype(BF16)
        grad_turned[base : base + HEAD_DIM] = (dot(keys, grad_scores) * root).astype(BF16)
        grad_turned[base + HEAD_DIM : base + 2 * HEAD_DIM] = (
            dot_last(queries, grad_scores) * root
        ).astype(BF16)
        grad_turned[base + 2 * HEAD_DIM : base + width] = dot_last(grad, prob).astype(BF16)
    input_grad[...] += dot_last(grad_turned[...].T, qkv_w[step])


def call_attend_backward(
    meta, grad_sum1, grad_low, flat, turned, att, prob, qkv_pieces, out_pieces
):
    seq, width = grad_sum1.shape
    columns = qkv_pieces[0].shape[1]
    heads = columns // (3 * HEAD_DIM)
    inner = heads * HEAD_DIM
    return pl.pallas_call(
        attend_backward,
        grid=(4,),
        in_specs=[
            SMEM,
            whole((seq, width)),
            whole((seq, width)),
            by_quarter((seq, columns)),
            by_quarter((columns, seq)),
            by_quarter((inner, seq)),
            by_quarter((heads, seq, seq)),
        ]
        + [ANY] * (2 * N_PIECES),
        out_specs=whole((seq, width)),
        out_shape=sds((seq, width), F32),
        scratch_shapes=[
            pltpu.VMEM((4, width, columns), BF16),
            pltpu.VMEM((4, inner, width), BF16),
            pltpu.VMEM((columns, seq), BF16),
            pltpu.SemaphoreType.DMA((N_PIECES,)),
            pltpu.SemaphoreType.DMA((N_PIECES,)),
        ],
        compiler_params=params(),
        name="attend_backward",
    )(meta, grad_sum1, grad_low, flat, turned, att, prob, *qkv_pieces, *out_pieces)


class Hops:
    def __init__(self, mesh):
        self.count = mesh.size
        self.tensor = mesh.shape["tensor"]
        self.dp = mesh.shape["dp"]

    def flip(self, array, bits):
        return lax.ppermute(array, AXES, [(i, i ^ bits) for i in range(self.count)])


def frozen_pieces(hops, weight, parity):
    half = weight.shape[0] // 2
    mine = lax.dynamic_slice_in_dim(weight, parity * half, half, 0)
    across = hops.flip(mine, 2)
    around = hops.flip(across, hops.tensor)
    other = hops.flip(weight, 1)
    return (weight, other, across, around, hops.flip(across, 1), hops.flip(around, 1))


def per_device(
    hops,
    tokens,
    doc_lengths,
    qkv_weight,
    attn_out_weight,
    norm1_gain,
    norm1_bias,
    ffn_in_weight,
    ffn_out_weight,
    norm2_gain,
    norm2_bias,
    adapter_down,
    adapter_up,
    merging_query,
    merging_key,
    merging_value,
    merging_gain,
    merging_bias,
    out_grad,
):
    n_adapters, rows, rank = adapter_down.shape
    parity = lax.axis_index("dp") % 2
    meta = jnp.stack([parity, lax.axis_index("tensor")]).astype(jnp.int32)
    line = lambda v: v[None, :]

    qkv_pieces = frozen_pieces(hops, qkv_weight, parity)
    out_pieces = frozen_pieces(hops, attn_out_weight, parity)
    in_pieces = frozen_pieces(hops, ffn_in_weight, parity)
    up_pieces = frozen_pieces(hops, ffn_out_weight, parity)
    shard = jnp.stack(
        [
            jnp.transpose(adapter_down, (1, 0, 2)).reshape(rows, n_adapters * rank),
            adapter_up.reshape(n_adapters * rank, rows).T,
            merging_query,
            merging_key,
            merging_value,
        ]
    )
    weights = lax.all_gather(shard, AXES, axis=1, tiled=True)

    flat, turned, att, prob, first, normed1, inv_std1 = call_attend_forward(
        meta, doc_lengths, tokens, line(norm1_gain), line(norm1_bias), qkv_pieces, out_pieces
    )
    slope, sums = call_ffn_forward(meta, first, in_pieces, up_pieces)
    layer_out, grad_sum2, grad_sum2_low, grads, lines = call_merging(
        n_adapters,
        meta,
        doc_lengths,
        sums,
        line(norm2_gain),
        line(norm2_bias),
        line(merging_gain),
        line(merging_bias),
        out_grad,
        weights,
        F32,
    )
    grad_sum1, grad_sum1_low = call_ffn_backward(
        meta, grad_sum2, grad_sum2_low, normed1, inv_std1, line(norm1_gain), slope, in_pieces, up_pieces
    )
    input_grad = call_attend_backward(
        meta, grad_sum1, grad_sum1_low, flat, turned, att, prob, qkv_pieces, out_pieces
    )
    grads = lax.psum_scatter(grads, AXES, scatter_dimension=1, tiled=True)
    lines = lax.psum(lines, AXES)
    return (
        layer_out,
        input_grad,
        grads[0],
        grads[1],
        grads[2],
        lines[0],
        lines[1],
        lines[2, :n_adapters] / lines[2, n_adapters],
    )


def solution(mesh):
    split = P(AXES, None)
    in_specs = (
        split,
        P("dp", None),
        P(None, "tensor"),
        P("tensor", None),
        P(),
        P(),
        P(None, "tensor"),
        P("tensor", None),
        P(),
        P(),
        P(None, AXES, None),
        P(None, None, AXES),
        split,
        split,
        split,
        P(),
        P(),
        split,
    )
    out_specs = (split, split, split, split, split, P(), P(), P())
    return jax.shard_map(
        functools.partial(per_device, Hops(mesh)),
        mesh=mesh,
        in_specs=in_specs,
        out_specs=out_specs,
        check_vma=False,
    )
```

```python
import functools

import jax
import jax.numpy as jnp
from jax import lax
from jax.experimental import pallas as pl
from jax.experimental.pallas import tpu as pltpu
from jax.sharding import PartitionSpec as P

HEAD_DIM = 64
AXES = ("dp", "tensor")
VMEM_BYTES = 58 * 1024 * 1024
LANES = 128
EPS = 1e-12
BIG_NEGATIVE = -1e30
ROOT_HALF = 0.7071067811865476
ROOT_TAU = 0.3989422804014327
F32, BF16 = jnp.float32, jnp.bfloat16

CORE, ACROSS, PAIR_Y, PAIR_Z, DEPTH, ROW = range(6)
GAIN1, SHIFT1, GAIN2, SHIFT2, GAIN3, SHIFT3 = range(6)

SMEM = pl.BlockSpec(memory_space=pltpu.SMEM)
VMEM = pl.BlockSpec(memory_space=pltpu.VMEM)
ANY = pl.BlockSpec(memory_space=pl.ANY)


def line_of(lines, i):
    return lines[i : i + 1]


def dot(a, b):
    return lax.dot_general(a, b, (((1,), (0,)), ((), ())), preferred_element_type=F32)


def dot_last(a, b):
    return lax.dot_general(a, b, (((1,), (1,)), ((), ())), preferred_element_type=F32)


def dot_first(a, b):
    return lax.dot_general(a, b, (((0,), (0,)), ((), ())), preferred_element_type=F32)


def normalize(u):
    centered = u - jnp.mean(u, axis=-1, keepdims=True)
    inv_std = lax.rsqrt(jnp.mean(centered * centered, axis=-1, keepdims=True) + EPS)
    return centered * inv_std, inv_std


def norm_back(grad, normed, inv_std):
    return inv_std * (
        grad
        - jnp.mean(grad, axis=-1, keepdims=True)
        - normed * jnp.mean(grad * normed, axis=-1, keepdims=True)
    )


def gelu_both(u):
    half = 0.5 * (1.0 + lax.erf(u * ROOT_HALF))
    return u * half, half + u * jnp.exp(-0.5 * u * u) * ROOT_TAU


def piece_copies(pieces, place, parity, scratch, sems):
    out = {}
    for i, (piece, (quarter, side)) in enumerate(zip(pieces, place)):
        rows = piece.shape[0]
        if side is None:
            target = scratch.at[quarter]
        else:
            first = parity if side == 0 else 1 - parity
            target = scratch.at[quarter, pl.ds(pl.multiple_of(first * rows, 16), rows)]
        out.setdefault(quarter, []).append(pltpu.make_async_copy(piece, target, sems.at[i]))
    return out


def bring_quarters(step, groups):
    @pl.when(step == 0)
    def _():
        for copies in groups:
            for quarter in sorted(copies):
                for copy in copies[quarter]:
                    copy.start()

    for quarter in range(4):

        @pl.when(step == quarter)
        def _(quarter=quarter):
            for copies in groups:
                for copy in copies[quarter]:
                    copy.wait()


PLACE = ((0, None), (1, None), (2, 0), (2, 1), (3, 0), (3, 1))
N_PIECES = len(PLACE)


def segment_bias(meta_ref, lengths_ref, bias_ref):
    seq = bias_ref.shape[0]
    row = meta_ref[ROW]
    by_row = lax.broadcasted_iota(jnp.int32, (seq, 1), 0)
    by_lane = lax.broadcasted_iota(jnp.int32, (1, seq), 1)
    seg_row = jnp.zeros((seq, 1), jnp.int32)
    seg_lane = jnp.zeros((1, seq), jnp.int32)
    end = jnp.int32(0)
    for i in range(lengths_ref.shape[1]):
        end = end + lengths_ref[row, i]
        seg_row = seg_row + jnp.where(by_row >= end, 1, 0)
        seg_lane = seg_lane + jnp.where(by_lane >= end, 1, 0)
    bias_ref[...] = jnp.where(seg_row == seg_lane, 0.0, BIG_NEGATIVE).astype(F32)


def attend_forward(columns, *refs):
    meta, lengths, tokens, lines = refs[:4]
    pieces, rest = refs[4 : 4 + N_PIECES], refs[4 + N_PIECES :]
    flat_out, turned_out, att_out, prob_out, first_out, normed_out, inv_out = rest[:7]
    weight, bias, total, sems = rest[7:]
    step = pl.program_id(0)
    bring_quarters(step, (piece_copies(pieces, PLACE, meta[PAIR_Y], weight, sems),))

    @pl.when(step == 0)
    def _():
        segment_bias(meta, lengths, bias)
        total[...] = tokens[...].astype(F32)

    turned = dot_last(weight[step, :columns], tokens[...]).astype(BF16)
    turned_out[0] = turned
    flat = turned.T
    flat_out[0] = flat
    width = 3 * HEAD_DIM
    for head in range(columns // width):
        base = head * width
        keys = flat[:, base + HEAD_DIM : base + 2 * HEAD_DIM]
        queries = turned[base : base + HEAD_DIM] * BF16(HEAD_DIM**-0.5)
        values = turned[base + 2 * HEAD_DIM : base + width]
        scores = dot(keys, queries) + bias[...]
        exponent = jnp.exp(scores - jnp.max(scores, axis=0, keepdims=True))
        prob = (exponent * (1.0 / jnp.sum(exponent, axis=0, keepdims=True))).astype(BF16)
        prob_out[0, head] = prob
        att_out[0, head * HEAD_DIM : (head + 1) * HEAD_DIM] = dot(values, prob).astype(BF16)
    total[...] += dot(att_out[0].T, weight[step, columns:])

    @pl.when(step == 3)
    def _():
        normed, inv_std = normalize(total[...])
        normed_out[...] = normed
        inv_out[...] = inv_std
        first_out[...] = normed * line_of(lines, GAIN1) + line_of(lines, SHIFT1)


def whole(shape):
    return pl.BlockSpec(shape, lambda i: (0,) * len(shape))


def by_quarter(shape):
    return pl.BlockSpec((1, *shape), lambda i: (i,) + (0,) * len(shape))


def sds(shape, dtype):
    return jax.ShapeDtypeStruct(shape, dtype)


def params(**kw):
    return pltpu.CompilerParams(vmem_limit_bytes=VMEM_BYTES, **kw)


def cost(us):
    return pl.CostEstimate(flops=int(us * 1.1e9), bytes_accessed=1 << 20, transcendentals=0)


def call_attend_forward(columns, meta, lengths, tokens, lines, pieces):
    seq, width = tokens.shape
    rows = pieces[0].shape[0]
    heads = columns // (3 * HEAD_DIM)
    inner = heads * HEAD_DIM
    return pl.pallas_call(
        functools.partial(attend_forward, columns),
        grid=(4,),
        in_specs=[SMEM, SMEM, whole((seq, width)), whole(lines.shape)] + [ANY] * N_PIECES,
        out_specs=[
            by_quarter((seq, columns)),
            by_quarter((columns, seq)),
            by_quarter((inner, seq)),
            by_quarter((heads, seq, seq)),
            whole((seq, width)),
            whole((seq, width)),
            whole((seq, 1)),
        ],
        out_shape=[
            sds((4, seq, columns), BF16),
            sds((4, columns, seq), BF16),
            sds((4, inner, seq), BF16),
            sds((4, heads, seq, seq), BF16),
            sds((seq, width), F32),
            sds((seq, width), F32),
            sds((seq, 1), F32),
        ],
        scratch_shapes=[
            pltpu.VMEM((4, rows, width), BF16),
            pltpu.VMEM((seq, seq), F32),
            pltpu.VMEM((seq, width), F32),
            pltpu.SemaphoreType.DMA((N_PIECES,)),
        ],
        compiler_params=params(),
        cost_estimate=cost(16),
        name="attend_forward",
    )(meta, lengths, tokens, lines, *pieces)


def ffn_forward(*refs):
    meta, first = refs[:2]
    in_pieces, out_pieces = refs[2 : 2 + N_PIECES], refs[2 + N_PIECES : 2 + 2 * N_PIECES]
    slope_out, sum_out, in_w, out_w, low, sems, out_sems = refs[2 + 2 * N_PIECES :]
    step = pl.program_id(0)
    bring_quarters(
        step,
        (
            piece_copies(in_pieces, PLACE, meta[PAIR_Z], in_w, sems),
            piece_copies(out_pieces, PLACE, meta[PAIR_Z], out_w, out_sems),
        ),
    )

    @pl.when(step == 0)
    def _():
        low[...] = first[...].astype(BF16)
        sum_out[...] = first[...]

    value, slope = gelu_both(dot(low[...], in_w[step]))
    slope_out[0] = slope.astype(BF16)
    sum_out[...] += dot(value.astype(BF16), out_w[step])


def call_ffn_forward(meta, first, in_pieces, out_pieces):
    seq, width = first.shape
    hidden = in_pieces[0].shape[1]
    return pl.pallas_call(
        ffn_forward,
        grid=(4,),
        in_specs=[SMEM, whole((seq, width))] + [ANY] * (2 * N_PIECES),
        out_specs=[by_quarter((seq, hidden)), whole((seq, width))],
        out_shape=[sds((4, seq, hidden), BF16), sds((seq, width), F32)],
        scratch_shapes=[
            pltpu.VMEM((4, width, hidden), BF16),
            pltpu.VMEM((4, hidden, width), BF16),
            pltpu.VMEM((seq, width), BF16),
            pltpu.SemaphoreType.DMA((N_PIECES,)),
            pltpu.SemaphoreType.DMA((N_PIECES,)),
        ],
        compiler_params=params(),
        cost_estimate=cost(11),
        name="ffn_forward",
    )(meta, first, *in_pieces, *out_pieces)


def tile_copies(meta, tiles, weights, sems):
    n_mats, width, _ = weights.shape
    half = width // 2
    copies = []
    for y_rel in range(2):
        for z_rel in range(4):
            for core_rel in range(2):
                tile = tiles[(y_rel * 4 + z_rel) * 2 + core_rel]
                rows = tile.shape[1]
                side = pl.multiple_of((meta[CORE] ^ core_rel) * half, LANES)
                for x_rel in range(2):
                    chip = ((meta[DEPTH] ^ z_rel) * 2 + (meta[PAIR_Y] ^ y_rel)) * 2
                    chip = chip + (meta[ACROSS] ^ x_rel)
                    target = weights.at[
                        :, pl.ds(pl.multiple_of(chip * rows, 16), rows), pl.ds(side, half)
                    ]
                    source = tile.at[pl.ds(x_rel * n_mats, n_mats)]
                    copies.append(pltpu.make_async_copy(source, target, sems.at[len(copies)]))
    return copies


def split_lines(total):
    high = total.astype(BF16).astype(F32)
    return jnp.concatenate([high, total - high], axis=0)


def merging(n_adapters, tiled, meta, lengths, sums, lines, out_grad, *refs):
    n_tiles = 16 if tiled else 1
    tiles, refs = refs[:n_tiles], refs[n_tiles:]
    layer_out, grad_sum2_out, grad_low_out = refs[:3]
    if tiled:
        keep_out, send_out, weights, grads, sems = refs[3:]
        copies = tile_copies(meta, tiles, weights, sems)
        for copy in copies:
            copy.start()
    else:
        grads, lines_out = refs[3:]
        weights = tiles[0]
    seq, width = sums.shape
    scale = width**-0.5
    down, up, query, key, value = (weights.at[i] for i in range(5))
    gain2, shift2 = line_of(lines, GAIN2), line_of(lines, SHIFT2)
    gain3, shift3 = line_of(lines, GAIN3), line_of(lines, SHIFT3)
    spread = jnp.where(
        lax.broadcasted_iota(jnp.int32, (LANES, width), 0)
        == lax.broadcasted_iota(jnp.int32, (LANES, width), 1) // (width // n_adapters),
        1.0,
        0.0,
    ).astype(BF16)
    real_lane = lax.broadcasted_iota(jnp.int32, (1, LANES), 1) < n_adapters

    def by_adapter(terms):
        high = terms.astype(BF16)
        rest = (terms - high.astype(F32)).astype(BF16)
        return dot_last(high, spread) + dot_last(rest, spread)

    normed2, inv_std2 = normalize(sums[...])
    second = normed2 * gain2 + shift2
    second_low = second.astype(BF16)
    if tiled:
        for copy in copies:
            copy.wait()
    middle = dot(second_low, down[...])
    act, slope = gelu_both(middle)
    act = act.astype(BF16).astype(F32)
    fquery = dot(second_low, query[...]).astype(BF16)
    probe = dot_last(fquery, key[...]).astype(BF16)
    probe_up = dot(probe, up[...])
    logits = scale * (
        jnp.sum(probe.astype(F32) * second, axis=1, keepdims=True) + by_adapter(act * probe_up)
    )
    logits = jnp.where(real_lane, logits, BIG_NEGATIVE)
    exponent = jnp.exp(logits - jnp.max(logits, axis=1, keepdims=True))
    mix = exponent / jnp.sum(exponent, axis=1, keepdims=True)
    mix_low = mix.astype(BF16)
    mix_sum = jnp.sum(mix_low.astype(F32), axis=1, keepdims=True)
    mix_wide = dot(mix_low, spread)
    blended = (second * mix_sum + dot_last((mix_wide * act).astype(BF16), up[...])).astype(BF16)
    normed3, inv_std3 = normalize(second + dot(blended, value[...]))
    layer_out[...] = normed3 * gain3 + shift3

    count = jnp.int32(0)
    for i in range(lengths.shape[1]):
        count = count + lengths[meta[ROW], i]
    keep = jnp.where(lax.broadcasted_iota(jnp.int32, (seq, 1), 0) < count, 1.0, 0.0)
    cot = out_grad[...].astype(F32) * keep
    mass = jnp.sum(mix * keep, axis=0, keepdims=True)
    lane = lax.broadcasted_iota(jnp.int32, (1, LANES), 1)
    mass = jnp.where(lane == n_adapters, jnp.sum(keep), mass)
    sum_lines = jnp.concatenate(
        [
            jnp.sum(cot * normed3, axis=0, keepdims=True),
            jnp.sum(cot, axis=0, keepdims=True),
            jnp.concatenate([mass, jnp.zeros((1, width - LANES), F32)], axis=1),
            jnp.zeros((1, width), F32),
        ],
        axis=0,
    )

    grad_pre = norm_back(cot * gain3, normed3, inv_std3)
    grad_proj = grad_pre.astype(BF16)
    grads[2] = dot_first(blended, grad_proj)
    grad_blend = dot_last(grad_proj, value[...]).astype(BF16)
    blend_up = dot(grad_blend, up[...])
    grad_mix = jnp.sum(grad_blend.astype(F32) * second, axis=1, keepdims=True) + by_adapter(
        act * blend_up
    )
    grad_logits = (mix * (grad_mix - jnp.sum(grad_mix * mix, axis=1, keepdims=True))).astype(BF16)
    logit_sum = jnp.sum(grad_logits.astype(F32), axis=1, keepdims=True)
    logit_wide = dot(grad_logits, spread)
    grad_probe = (
        scale * (second * logit_sum + dot_last((logit_wide * act).astype(BF16), up[...]))
    ).astype(BF16)
    grads[1] = dot_first(grad_probe, fquery)
    grad_fquery = dot(grad_probe, key[...]).astype(BF16)
    grads[0] = dot_first(second_low, grad_fquery)
    grad_middle = ((mix_wide * blend_up + (scale * logit_wide) * probe_up) * slope).astype(BF16)
    grad_second = (
        grad_pre
        + dot_last(grad_fquery, query[...])
        + grad_blend.astype(F32) * mix_sum
        + probe.astype(F32) * (scale * logit_sum)
        + dot_last(grad_middle, down[...])
    )
    grad_sum2 = norm_back(grad_second * gain2, normed2, inv_std2)
    grad_sum2_out[...] = grad_sum2
    grad_low_out[...] = grad_sum2.astype(BF16)

    if not tiled:
        lines_out[...] = jnp.concatenate([sum_lines, jnp.zeros_like(sum_lines)], axis=0)
        return
    tail = split_lines(sum_lines)
    rows = width // 32

    @pl.loop(0, 16)
    def _(chip):
        z_rel = (chip // 4) ^ meta[DEPTH]
        y_rel = (chip // 2 % 2) ^ meta[PAIR_Y]
        x_rel = (chip % 2) ^ meta[ACROSS]
        for core_rel, out in ((0, keep_out), (1, send_out)):
            first = pl.multiple_of((chip * 2 + (meta[CORE] ^ core_rel)) * rows, 8)
            block = [grads[i, pl.ds(first, rows)] for i in range(3)] + [tail]
            out[x_rel, y_rel, z_rel] = jnp.concatenate(block, axis=0).astype(BF16)


def call_merging(n_adapters, tiled, meta, lengths, sums, lines, out_grad, tiles):
    seq, width = sums.shape
    block = 3 * width // 32 + 8
    if tiled:
        out_shape = [sds((2, 2, 4, block, width), BF16)] * 2
        scratch = [
            pltpu.VMEM((5, width, width), BF16),
            pltpu.VMEM((3, width, width), F32),
            pltpu.SemaphoreType.DMA((32,)),
        ]
    else:
        out_shape = [sds((3, width, width), F32), sds((8, width), F32)]
        scratch = []
    return pl.pallas_call(
        functools.partial(merging, n_adapters, tiled),
        in_specs=[SMEM, SMEM] + [VMEM] * 3 + [ANY if tiled else VMEM] * len(tiles),
        out_specs=[VMEM] * 5,
        out_shape=[sds((seq, width), F32), sds((seq, width), F32), sds((seq, width), BF16)]
        + out_shape,
        scratch_shapes=scratch,
        compiler_params=params(),
        cost_estimate=cost(18),
        name="merging",
    )(meta, lengths, sums, lines, out_grad, *tiles)


def ffn_backward(*refs):
    meta, grad_sum2, grad_low, normed1, inv_std1, lines, slope = refs[:7]
    in_pieces, out_pieces = refs[7 : 7 + N_PIECES], refs[7 + N_PIECES : 7 + 2 * N_PIECES]
    grad_out, grad_low_out, in_w, out_w, total, sems, out_sems = refs[7 + 2 * N_PIECES :]
    step = pl.program_id(0)
    bring_quarters(
        step,
        (
            piece_copies(out_pieces, PLACE, meta[PAIR_Z], out_w, out_sems),
            piece_copies(in_pieces, PLACE, meta[PAIR_Z], in_w, sems),
        ),
    )

    @pl.when(step == 0)
    def _():
        total[...] = grad_sum2[...]

    grad_pre = (dot_last(grad_low[...], out_w[step]) * slope[0].astype(F32)).astype(BF16)
    total[...] += dot_last(grad_pre, in_w[step])

    @pl.when(step == 3)
    def _():
        grad = norm_back(total[...] * line_of(lines, GAIN1), normed1[...], inv_std1[...])
        grad_out[...] = grad
        grad_low_out[...] = grad.astype(BF16)


def call_ffn_backward(
    meta, grad_sum2, grad_low, normed1, inv_std1, lines, slope, in_pieces, out_pieces
):
    seq, width = grad_sum2.shape
    hidden = in_pieces[0].shape[1]
    return pl.pallas_call(
        ffn_backward,
        grid=(4,),
        in_specs=[
            SMEM,
            whole((seq, width)),
            whole((seq, width)),
            whole((seq, width)),
            whole((seq, 1)),
            whole(lines.shape),
            by_quarter((seq, hidden)),
        ]
        + [ANY] * (2 * N_PIECES),
        out_specs=[whole((seq, width)), whole((seq, width))],
        out_shape=[sds((seq, width), F32), sds((seq, width), BF16)],
        scratch_shapes=[
            pltpu.VMEM((4, width, hidden), BF16),
            pltpu.VMEM((4, hidden, width), BF16),
            pltpu.VMEM((seq, width), F32),
            pltpu.SemaphoreType.DMA((N_PIECES,)),
            pltpu.SemaphoreType.DMA((N_PIECES,)),
        ],
        compiler_params=params(),
        cost_estimate=cost(12),
        name="ffn_backward",
    )(meta, grad_sum2, grad_low, normed1, inv_std1, lines, slope, *in_pieces, *out_pieces)


def attend_backward(columns, *refs):
    meta, grad_sum1, grad_low, flat_ref, turned_ref, att_ref, prob_ref = refs[:7]
    pieces = refs[7 : 7 + N_PIECES]
    input_grad, weight, grad_turned, sems = refs[7 + N_PIECES :]
    step = pl.program_id(0)
    bring_quarters(step, (piece_copies(pieces, PLACE, meta[PAIR_Y], weight, sems),))

    @pl.when(step == 0)
    def _():
        input_grad[...] = grad_sum1[...]

    grad_att = dot_last(weight[step, columns:], grad_low[...]).astype(BF16)
    width = 3 * HEAD_DIM
    root = HEAD_DIM**-0.5
    for head in range(att_ref.shape[1] // HEAD_DIM):
        base = head * width
        queries = turned_ref[0, base : base + HEAD_DIM]
        keys = turned_ref[0, base + HEAD_DIM : base + 2 * HEAD_DIM]
        values = flat_ref[0, :, base + 2 * HEAD_DIM : base + width]
        part = slice(head * HEAD_DIM, (head + 1) * HEAD_DIM)
        grad = grad_att[part]
        prob = prob_ref[0, head]
        row_dot = jnp.sum(grad.astype(F32) * att_ref[0, part].astype(F32), axis=0, keepdims=True)
        grad_scores = (prob.astype(F32) * (dot(values, grad) - row_dot)).astype(BF16)
        grad_turned[base : base + HEAD_DIM] = (dot(keys, grad_scores) * root).astype(BF16)
        grad_turned[base + HEAD_DIM : base + 2 * HEAD_DIM] = (
            dot_last(queries, grad_scores) * root
        ).astype(BF16)
        grad_turned[base + 2 * HEAD_DIM : base + width] = dot_last(grad, prob).astype(BF16)
    input_grad[...] += dot(grad_turned[...].T, weight[step, :columns])


def call_attend_backward(columns, meta, grad_sum1, grad_low, flat, turned, att, prob, pieces):
    seq, width = grad_sum1.shape
    rows = pieces[0].shape[0]
    heads = columns // (3 * HEAD_DIM)
    inner = heads * HEAD_DIM
    return pl.pallas_call(
        functools.partial(attend_backward, columns),
        grid=(4,),
        in_specs=[
            SMEM,
            whole((seq, width)),
            whole((seq, width)),
            by_quarter((seq, columns)),
            by_quarter((columns, seq)),
            by_quarter((inner, seq)),
            by_quarter((heads, seq, seq)),
        ]
        + [ANY] * N_PIECES,
        out_specs=whole((seq, width)),
        out_shape=sds((seq, width), F32),
        scratch_shapes=[
            pltpu.VMEM((4, rows, width), BF16),
            pltpu.VMEM((columns, seq), BF16),
            pltpu.SemaphoreType.DMA((N_PIECES,)),
        ],
        compiler_params=params(),
        cost_estimate=cost(16),
        name="attend_backward",
    )(meta, grad_sum1, grad_low, flat, turned, att, prob, *pieces)


def prepare(meta, down, up, query, key, value, g1, s1, g2, s2, g3, s3, keep, send, lines, shard):
    n_adapters, _, rank = down.shape
    for i in range(n_adapters):
        shard[0, :, i * rank : (i + 1) * rank] = down[i].astype(F32)
        shard[1, :, i * rank : (i + 1) * rank] = up[i].astype(F32)
    for i, ref in enumerate((query, key, value)):
        shard[2 + i] = ref[...].astype(F32)
    half = keep.shape[2]
    mine = pl.multiple_of(meta[CORE] * half, LANES)
    other = pl.multiple_of((1 - meta[CORE]) * half, LANES)
    keep[...] = shard[:, :, pl.ds(mine, half)].astype(BF16)
    send[...] = shard[:, :, pl.ds(other, half)].astype(BF16)
    for i, ref in enumerate((g1, s1, g2, s2, g3, s3)):
        lines[i : i + 1] = ref[...].reshape(1, -1)
    lines[6:8] = jnp.zeros((2, lines.shape[1]), F32)


def call_prepare(meta, down, up, query, key, value, *vectors):
    rows, width = query.shape
    half = sds((5, rows, width // 2), BF16)
    return pl.pallas_call(
        prepare,
        in_specs=[SMEM] + [VMEM] * 11,
        out_specs=[VMEM] * 3,
        out_shape=[half, half, sds((8, width), F32)],
        scratch_shapes=[pltpu.VMEM((5, rows, width), F32)],
        compiler_params=params(),
        cost_estimate=cost(1),
        name="prepare",
    )(meta, down, up, query, key, value, *vectors)


def add_blocks(*blocks):
    total = functools.reduce(jnp.add, (b.astype(F32) for b in blocks))
    tail = total[-8:-4] + total[-4:]
    return jnp.concatenate([total[:-8], split_lines(tail)], axis=0)


def sum_cores(keep, got, p_keep, p_send, q_keep, q_send):
    half = p_keep.shape[-1]
    for x in range(2):
        for y in range(2):

            @pl.loop(0, 4)
            def _(z, x=x, y=y):
                total = add_blocks(keep[x, y, z], got[x, y, z]).astype(BF16)
                (p_send if x else p_keep)[y, z] = total[:, :half]
                (q_send if y else q_keep)[x, z] = total[:, half:]


def sum_first(p_keep, p_got, q_keep, q_got, p2_keep, p2_send, q2_keep, q2_send):
    @pl.loop(0, 4)
    def _(z):
        for out, index in ((p2_keep, 0), (p2_send, 1)):
            out[z] = add_blocks(p_keep[index, z], p_got[index, z]).astype(BF16)
        for out, index in ((q2_keep, 0), (q2_send, 1)):
            out[z] = add_blocks(q_keep[index, z], q_got[index, z]).astype(BF16)


def sum_second(p_keep, p_got, q_keep, q_got, *outs):
    half = p_keep.shape[-1]
    for z in range(4):
        outs[z][:, :half] = add_blocks(p_keep[z], p_got[z]).astype(BF16)
        outs[z][:, half:] = add_blocks(q_keep[z], q_got[z]).astype(BF16)


def sum_last(n_adapters, keep, got1, got2, got3, query, key, value, gain, bias, mass):
    total = add_blocks(keep[...], got1[...], got2[...], got3[...])
    rows = query.shape[0]
    for i, out in enumerate((query, key, value)):
        out[...] = total[i * rows : (i + 1) * rows]
    lines = total[-8:-4] + total[-4:]
    gain[...] = lines[0]
    bias[...] = lines[1]
    mass[...] = lines[2, :n_adapters] / lines[2:3, n_adapters : n_adapters + 1].reshape(1)


def small_call(body, name, out_shape, *operands):
    return pl.pallas_call(
        body,
        in_specs=[VMEM] * len(operands),
        out_specs=[VMEM] * len(out_shape),
        out_shape=out_shape,
        compiler_params=params(),
        cost_estimate=cost(2),
        name=name,
    )(*operands)


def sum_gradients(hops, keep, send, n_adapters):
    block, width = keep.shape[3:]
    half = width // 2
    pair = [sds((2, 4, block, half), BF16)] * 4
    single = [sds((4, block, half), BF16)] * 4
    got = hops.flip(send, 1)
    pk, ps, qk, qs = small_call(sum_cores, "sum_cores", pair, keep, got)
    pg, qg = hops.flip(ps, ALONG_X), hops.flip(qs, ALONG_Y)
    pk, ps, qk, qs = small_call(sum_first, "sum_first", single, pk, pg, qk, qg)
    pg, qg = hops.flip(ps, ALONG_Y), hops.flip(qs, ALONG_X)
    parts = small_call(sum_second, "sum_second", [sds((block, width), BF16)] * 4, pk, pg, qk, qg)
    got = [hops.flip(part, z * ALONG_Z) for z, part in enumerate(parts) if z]
    rows = (block - 8) // 3
    outs = [sds((rows, width), F32)] * 3 + [sds((width,), F32)] * 2 + [sds((n_adapters,), F32)]
    return small_call(
        functools.partial(sum_last, n_adapters), "sum_last", outs, parts[0], *got
    )


ALONG_X, ALONG_Y, ALONG_Z = 2, 4, 8


class Hops:
    def __init__(self, mesh):
        self.count = mesh.size
        self.tiled = mesh.shape["dp"] == 8 and mesh.shape["tensor"] == 4

    def flip(self, array, bits):
        return lax.ppermute(array, AXES, [(i, i ^ bits) for i in range(self.count)])


def after(array, *others):
    return lax.optimization_barrier((array, *others))[0]


def half_of(block, parity):
    half = block.shape[0] // 2
    return lax.dynamic_slice_in_dim(block, parity * half, half, 0)


def per_device(
    hops,
    tokens,
    doc_lengths,
    qkv_weight,
    attn_out_weight,
    norm1_gain,
    norm1_bias,
    ffn_in_weight,
    ffn_out_weight,
    norm2_gain,
    norm2_bias,
    adapter_down,
    adapter_up,
    merging_query,
    merging_key,
    merging_value,
    merging_gain,
    merging_bias,
    out_grad,
):
    n_adapters, rows, rank = adapter_down.shape
    columns = qkv_weight.shape[1]
    tensor, dp = lax.axis_index("tensor"), lax.axis_index("dp")
    pair_y, pair_z = dp % 2, dp // 2 % 2
    meta = jnp.stack([tensor % 2, tensor // 2, pair_y, pair_z, dp // 2, tensor]).astype(jnp.int32)
    flip = hops.flip

    attn = jnp.concatenate([qkv_weight.T, attn_out_weight], axis=0)
    attn_x = flip(half_of(attn, pair_y), ALONG_X)
    keep, send, lines = call_prepare(
        meta,
        adapter_down,
        jnp.transpose(adapter_up, (0, 2, 1)),
        merging_query,
        merging_key,
        merging_value,
        norm1_gain,
        norm1_bias,
        norm2_gain,
        norm2_bias,
        merging_gain,
        merging_bias,
    )
    if hops.tiled:
        got = flip(send, 1)
        tile = jnp.where(
            tensor % 2 == 0,
            jnp.concatenate([keep, got], axis=1),
            jnp.concatenate([got, keep], axis=1),
        )
        tile_x = flip(tile, ALONG_X)
        both = jnp.concatenate([tile, tile_x], axis=0)
    attn_core = flip(attn, 1)
    in_x = flip(half_of(after(ffn_in_weight, attn_core), pair_z), ALONG_X)
    attn_y = flip(attn_x, ALONG_Y)
    out_x = flip(half_of(after(ffn_out_weight, attn_x), pair_z), ALONG_X)
    attn_pieces = (attn, attn_core, attn_x, attn_y, flip(attn_x, 1), flip(attn_y, 1))
    in_z, out_z = flip(in_x, ALONG_Z), flip(out_x, ALONG_Z)
    in_pieces = (ffn_in_weight, flip(ffn_in_weight, 1), in_x, in_z, flip(in_x, 1), flip(in_z, 1))
    up_pieces = (
        ffn_out_weight,
        flip(ffn_out_weight, 1),
        out_x,
        out_z,
        flip(out_x, 1),
        flip(out_z, 1),
    )
    if hops.tiled:
        by_z = [both] + [flip(both, z * ALONG_Z) for z in range(1, 4)]
        mine = by_z + [flip(t, ALONG_Y) for t in by_z]
        tiles = [t for own in mine for t in (own, flip(own, 1))]
    else:
        shard = [
            jnp.transpose(adapter_down, (1, 0, 2)).reshape(rows, n_adapters * rank),
            adapter_up.reshape(n_adapters * rank, rows).T,
            merging_query,
            merging_key,
            merging_value,
        ]
        tiles = [lax.all_gather(jnp.stack(shard), AXES, axis=1, tiled=True)]

    flat, turned, att, prob, first, normed1, inv_std1 = call_attend_forward(
        columns, meta, doc_lengths, tokens, lines, attn_pieces
    )
    slope, sums = call_ffn_forward(meta, first, in_pieces, up_pieces)
    layer_out, grad_sum2, grad_sum2_low, *grads = call_merging(
        n_adapters, hops.tiled, meta, doc_lengths, sums, lines, out_grad, tiles
    )
    grad_sum1, grad_sum1_low = call_ffn_backward(
        meta, grad_sum2, grad_sum2_low, normed1, inv_std1, lines, slope, in_pieces, up_pieces
    )
    input_grad = call_attend_backward(
        columns, meta, grad_sum1, grad_sum1_low, flat, turned, att, prob, attn_pieces
    )
    if hops.tiled:
        return (layer_out, input_grad, *sum_gradients(hops, *grads, n_adapters))
    squares = lax.psum_scatter(grads[0], AXES, scatter_dimension=1, tiled=True)
    sums = lax.psum(grads[1], AXES)
    mass = sums[2, :n_adapters] / sums[2, n_adapters]
    return (layer_out, input_grad, squares[0], squares[1], squares[2], sums[0], sums[1], mass)


def solution(mesh):
    split = P(AXES, None)
    in_specs = (
        split,
        P("dp", None),
        P(None, "tensor"),
        P("tensor", None),
        P(),
        P(),
        P(None, "tensor"),
        P("tensor", None),
        P(),
        P(),
        P(None, AXES, None),
        P(None, None, AXES),
        split,
        split,
        split,
        P(),
        P(),
        split,
    )
    out_specs = (split, split, split, split, split, P(), P(), P())
    return jax.shard_map(
        functools.partial(per_device, Hops(mesh)),
        mesh=mesh,
        in_specs=in_specs,
        out_specs=out_specs,
        check_vma=False,
    )
```

```python
import functools

import jax
import jax.numpy as jnp
from jax import lax
from jax.experimental import pallas as pl
from jax.experimental.pallas import tpu as pltpu
from jax.sharding import PartitionSpec as P

HEAD_DIM = 64
AXES = ("dp", "tensor")
ATTEND_MIB, FFN_MIB, MERGE_MIB = 24, 24, 30
LANES = 128
COST = 0.0
EPS = 1e-12
BIG_NEGATIVE = -1e30
ROOT_HALF = 0.7071067811865476
ROOT_TAU = 0.3989422804014327
F32, BF16 = jnp.float32, jnp.bfloat16

CORE, ACROSS, PAIR_Y, PAIR_Z, DEPTH, ROW = range(6)
GAIN1, SHIFT1, GAIN2, SHIFT2, GAIN3, SHIFT3 = range(6)

SMEM = pl.BlockSpec(memory_space=pltpu.SMEM)
VMEM = pl.BlockSpec(memory_space=pltpu.VMEM)
ANY = pl.BlockSpec(memory_space=pl.ANY)
HBM = pl.BlockSpec(memory_space=pltpu.HBM)


def line_of(lines, i):
    return lines[i : i + 1]


def dot(a, b):
    return lax.dot_general(a, b, (((1,), (0,)), ((), ())), preferred_element_type=F32)


def dot_last(a, b):
    return lax.dot_general(a, b, (((1,), (1,)), ((), ())), preferred_element_type=F32)


def dot_first(a, b):
    return lax.dot_general(a, b, (((0,), (0,)), ((), ())), preferred_element_type=F32)


def normalize(u):
    centered = u - jnp.mean(u, axis=-1, keepdims=True)
    inv_std = lax.rsqrt(jnp.mean(centered * centered, axis=-1, keepdims=True) + EPS)
    return centered * inv_std, inv_std


def norm_back(grad, normed, inv_std):
    return inv_std * (
        grad
        - jnp.mean(grad, axis=-1, keepdims=True)
        - normed * jnp.mean(grad * normed, axis=-1, keepdims=True)
    )


def gelu_both(u):
    half = 0.5 * (1.0 + lax.erf(u * ROOT_HALF))
    return u * half, half + u * jnp.exp(-0.5 * u * u) * ROOT_TAU


def segment_bias(meta_ref, lengths_ref, bias_ref):
    seq = bias_ref.shape[0]
    row = meta_ref[ROW]
    by_row = lax.broadcasted_iota(jnp.int32, (seq, 1), 0)
    by_lane = lax.broadcasted_iota(jnp.int32, (1, seq), 1)
    seg_row = jnp.zeros((seq, 1), jnp.int32)
    seg_lane = jnp.zeros((1, seq), jnp.int32)
    end = jnp.int32(0)
    for i in range(lengths_ref.shape[1]):
        end = end + lengths_ref[row, i]
        seg_row = seg_row + jnp.where(by_row >= end, 1, 0)
        seg_lane = seg_lane + jnp.where(by_lane >= end, 1, 0)
    bias_ref[...] = jnp.where(seg_row == seg_lane, 0.0, BIG_NEGATIVE).astype(F32)


def attend_forward(columns, last, meta, lengths, tokens, before, lines, weight0, weight1, *refs):
    turned_out, att_out, prob_out, first_out = refs[:4]
    bias = refs[-1]
    segment_bias(meta, lengths, bias)
    total = before[...].astype(F32)
    width = 3 * HEAD_DIM
    for quarter, weight in enumerate((weight0, weight1)):
        turned = dot_last(weight[:columns], tokens[...]).astype(BF16)
        turned_out[quarter] = turned
        flat = turned.T
        for head in range(columns // width):
            base = head * width
            keys = flat[:, base + HEAD_DIM : base + 2 * HEAD_DIM]
            queries = turned[base : base + HEAD_DIM] * BF16(HEAD_DIM**-0.5)
            values = turned[base + 2 * HEAD_DIM : base + width]
            scores = dot(keys, queries) + bias[...]
            exponent = jnp.exp(scores - jnp.max(scores, axis=0, keepdims=True))
            prob = (exponent * (1.0 / jnp.sum(exponent, axis=0, keepdims=True))).astype(BF16)
            prob_out[quarter, head] = prob
            part = slice(head * HEAD_DIM, (head + 1) * HEAD_DIM)
            att_out[quarter, part] = dot(values, prob).astype(BF16)
        total = total + dot(att_out[quarter].T, weight[columns:])
    if not last:
        first_out[...] = total
        return
    normed_out, inv_out = refs[4:6]
    normed, inv_std = normalize(total)
    normed_out[...] = normed
    inv_out[...] = inv_std
    first_out[...] = normed * line_of(lines, GAIN1) + line_of(lines, SHIFT1)


def sds(shape, dtype):
    return jax.ShapeDtypeStruct(shape, dtype)


def params(mib):
    return pltpu.CompilerParams(vmem_limit_bytes=mib << 20)


def kernel(body, deps, mib, *, in_specs, **kw):
    n = len(deps)
    call = pl.pallas_call(
        lambda *refs: body(*refs[n:]),
        in_specs=[ANY] * n + in_specs,
        compiler_params=params(mib),
        **kw,
    )
    return functools.partial(call, *deps)


def sync(name, meta, joins, carries, deps):
    sides = [j[0] if isinstance(j[0], int) else None for j in joins]
    parts = [j[1:] if isinstance(j[0], int) else j for j in joins]
    flat = [p for j in parts for p in j]

    def body(meta_ref, *refs):
        refs = refs[len(carries) :]
        sources, outs = list(refs[: len(flat)]), refs[len(flat) : len(flat) + len(parts)]
        for side, join, out in zip(sides, parts, outs):
            row = 0
            for i, part in enumerate(join):
                size = part.shape[0]
                if side is not None:
                    n = len(join) // 2
                    row = pl.multiple_of(((meta_ref[side] ^ (i // n)) * n + i % n) * size, 16)
                out[pl.ds(row, size)] = sources.pop(0)[...]
                row = row + size

    joined = [sds((sum(p.shape[0] for p in j), *j[0].shape[1:]), j[0].dtype) for j in parts]
    n_deps = len(deps)
    out = kernel(
        body,
        deps,
        16,
        in_specs=[SMEM] + [ANY] * len(carries) + [VMEM] * len(flat),
        out_specs=[VMEM] * len(joined) + [ANY] * len(carries),
        out_shape=joined + [sds(c.shape, c.dtype) for c in carries],
        input_output_aliases={n_deps + 1 + i: len(joined) + i for i in range(len(carries))},
        cost_estimate=cost(0),
        name=name,
    )(meta, *carries, *flat)
    return out


def in_hbm(array):
    return pltpu.with_memory_space_constraint(array, pltpu.HBM)


def cost(us):
    return pl.CostEstimate(flops=int(us * 1.1e9 * COST), bytes_accessed=1024, transcendentals=0)


def call_attend_forward(deps, columns, last, meta, lengths, tokens, before, lines, quarters):
    seq, width = tokens.shape
    heads = columns // (3 * HEAD_DIM)
    inner = heads * HEAD_DIM
    square, narrow = sds((seq, width), F32), sds((seq, 1), F32)
    out_shape = [
        pltpu.HBM((2, columns, seq), BF16),
        pltpu.HBM((2, inner, seq), BF16),
        pltpu.HBM((2, heads, seq, seq), BF16),
        square,
    ] + [square, narrow] * last
    return kernel(
        functools.partial(attend_forward, columns, last),
        deps,
        ATTEND_MIB,
        in_specs=[SMEM, SMEM] + [VMEM] * 5,
        out_specs=[VMEM] * len(out_shape),
        out_shape=out_shape,
        scratch_shapes=[pltpu.VMEM((seq, seq), F32)],
        cost_estimate=cost(8),
        name="attend_forward",
    )(meta, lengths, tokens, before, lines, *quarters)


def ffn_forward(blocks, first, before, *refs):
    slope_out, sum_out = refs[-2:]
    low = first[...].astype(BF16)
    total = before[...]
    outs = list(refs[2:-2])
    for quarter in range(2):
        value, slope = gelu_both(dot(low, refs[quarter][...]))
        slope_out[quarter] = slope.astype(BF16)
        value = value.astype(BF16)
        row = 0
        for _ in range(blocks):
            out = outs.pop(0)
            total = total + dot(value[:, row : row + out.shape[0]], out[...])
            row += out.shape[0]
    sum_out[...] = total


def call_ffn_forward(deps, first, before, in_quarters, out_quarters):
    seq, width = first.shape
    hidden = in_quarters[0].shape[1]
    return kernel(
        functools.partial(ffn_forward, len(out_quarters) // 2),
        deps,
        FFN_MIB,
        in_specs=[VMEM] * (4 + len(out_quarters)),
        out_specs=[VMEM] * 2,
        out_shape=[sds((2, seq, hidden), BF16), sds((seq, width), F32)],
        cost_estimate=cost(5),
        name="ffn_forward",
    )(first, before, *in_quarters, *out_quarters)


def assemble(name, meta, weights, tiles):
    n_mats = tiles[0][0].shape[0] // (2 * len(tiles[0][1]))
    rows, half = tiles[0][0].shape[1:]
    count = sum(2 * len(parts) for _, parts, _ in tiles)
    before = [] if weights is None else [weights]

    def body(meta_ref, *refs):
        refs = refs[len(before) :]
        out, sems = refs[-2:]
        copies = []
        for ref, (_, parts, core_rel) in zip(refs, tiles):
            side = pl.multiple_of((meta_ref[CORE] ^ core_rel) * half, LANES)
            for j, (y_rel, z_rel) in enumerate(parts):
                for x_rel in range(2):
                    chip = ((meta_ref[DEPTH] ^ z_rel) * 2 + (meta_ref[PAIR_Y] ^ y_rel)) * 2
                    chip = chip + (meta_ref[ACROSS] ^ x_rel)
                    first = pl.multiple_of(chip * rows, 16)
                    target = out.at[:, pl.ds(first, rows), pl.ds(side, half)]
                    source = ref.at[pl.ds((2 * j + x_rel) * n_mats, n_mats)]
                    copies.append(pltpu.make_async_copy(source, target, sems.at[len(copies)]))
        for copy in copies:
            copy.start()
        for copy in copies:
            copy.wait()

    return kernel(
        body,
        [],
        16,
        in_specs=[SMEM] + [ANY] * len(before) + [VMEM] * len(tiles),
        out_specs=ANY,
        out_shape=sds((n_mats, 2 * half, 2 * half), BF16),
        input_output_aliases={1: 0} if before else {},
        scratch_shapes=[pltpu.SemaphoreType.DMA((count,))],
        cost_estimate=cost(0),
        name=name,
    )(meta, *before, *(tile for tile, _, _ in tiles))


def split_lines(total):
    high = total.astype(BF16).astype(F32)
    return jnp.concatenate([high, total - high], axis=0)


def merging(n_adapters, meta, lengths, sums, lines, out_grad, matrices, *refs):
    layer_out, grad_sum2_out, grad_low_out, keep_out, send_out, grads = refs
    seq, width = sums.shape
    scale = width**-0.5
    down, up, query, key, value = (matrices.at[i] for i in range(5))
    gain2, shift2 = line_of(lines, GAIN2), line_of(lines, SHIFT2)
    gain3, shift3 = line_of(lines, GAIN3), line_of(lines, SHIFT3)
    spread = jnp.where(
        lax.broadcasted_iota(jnp.int32, (LANES, width), 0)
        == lax.broadcasted_iota(jnp.int32, (LANES, width), 1) // (width // n_adapters),
        1.0,
        0.0,
    ).astype(BF16)
    real_lane = lax.broadcasted_iota(jnp.int32, (1, LANES), 1) < n_adapters

    def by_adapter(terms):
        high = terms.astype(BF16)
        rest = (terms - high.astype(F32)).astype(BF16)
        return dot_last(high, spread) + dot_last(rest, spread)

    mean2 = jnp.mean(sums[...], axis=-1, keepdims=True)
    centered = sums[...] - mean2
    inv_std2 = lax.rsqrt(jnp.mean(centered * centered, axis=-1, keepdims=True) + EPS)
    second = centered * inv_std2 * gain2 + shift2
    second_low = second.astype(BF16)
    act, slope = (v.astype(BF16) for v in gelu_both(dot(second_low, down[...])))
    fquery = dot(second_low, query[...]).astype(BF16)
    probe = dot_last(fquery, key[...]).astype(BF16)
    probe_up = dot(probe, up[...])
    logits = scale * (
        jnp.sum(probe.astype(F32) * second, axis=1, keepdims=True) + by_adapter(act * probe_up)
    )
    logits = jnp.where(real_lane, logits, BIG_NEGATIVE)
    exponent = jnp.exp(logits - jnp.max(logits, axis=1, keepdims=True))
    mix = exponent / jnp.sum(exponent, axis=1, keepdims=True)
    mix_low = mix.astype(BF16)
    mix_sum = jnp.sum(mix_low.astype(F32), axis=1, keepdims=True)
    mix_wide = dot(mix_low, spread).astype(BF16)
    blended = (second * mix_sum + dot_last((mix_wide * act).astype(BF16), up[...])).astype(BF16)
    normed3, inv_std3 = normalize(second + dot(blended, value[...]))
    layer_out[...] = normed3 * gain3 + shift3

    count = jnp.int32(0)
    for i in range(lengths.shape[1]):
        count = count + lengths[meta[ROW], i]
    keep = jnp.where(lax.broadcasted_iota(jnp.int32, (seq, 1), 0) < count, 1.0, 0.0)
    cot = out_grad[...].astype(F32) * keep
    mass = jnp.sum(mix * keep, axis=0, keepdims=True)
    lane = lax.broadcasted_iota(jnp.int32, (1, LANES), 1)
    mass = jnp.where(lane == n_adapters, jnp.sum(keep), mass)
    sum_lines = jnp.concatenate(
        [
            jnp.sum(cot * normed3, axis=0, keepdims=True),
            jnp.sum(cot, axis=0, keepdims=True),
            jnp.concatenate([mass, jnp.zeros((1, width - LANES), F32)], axis=1),
            jnp.zeros((1, width), F32),
        ],
        axis=0,
    )

    grad_pre = norm_back(cot * gain3, normed3, inv_std3)
    grad_proj = grad_pre.astype(BF16)
    grads[2] = dot_first(blended, grad_proj)
    grad_blend = dot_last(grad_proj, value[...]).astype(BF16)
    blend_up = dot(grad_blend, up[...])
    grad_mix = jnp.sum(grad_blend.astype(F32) * second, axis=1, keepdims=True) + by_adapter(
        act * blend_up
    )
    grad_logits = (mix * (grad_mix - jnp.sum(grad_mix * mix, axis=1, keepdims=True))).astype(BF16)
    logit_sum = jnp.sum(grad_logits.astype(F32), axis=1, keepdims=True)
    logit_wide = dot(grad_logits, spread).astype(BF16)
    grad_probe = (
        scale * (second * logit_sum + dot_last((logit_wide * act).astype(BF16), up[...]))
    ).astype(BF16)
    grads[1] = dot_first(grad_probe, fquery)
    grad_fquery = dot(grad_probe, key[...]).astype(BF16)
    grads[0] = dot_first(second_low, grad_fquery)
    grad_act = mix_wide.astype(F32) * blend_up + (scale * logit_wide.astype(F32)) * probe_up
    grad_middle = (grad_act * slope.astype(F32)).astype(BF16)
    grad_second = (
        grad_pre
        + dot_last(grad_fquery, query[...])
        + grad_blend.astype(F32) * mix_sum
        + probe.astype(F32) * (scale * logit_sum)
        + dot_last(grad_middle, down[...])
    )
    grad_sum2 = norm_back(grad_second * gain2, (sums[...] - mean2) * inv_std2, inv_std2)
    grad_sum2_out[...] = grad_sum2
    grad_low_out[...] = grad_sum2.astype(BF16)

    tail = split_lines(sum_lines)
    rows = width // 32

    @pl.loop(0, 16)
    def _(chip):
        z_rel = (chip // 4) ^ meta[DEPTH]
        y_rel = (chip // 2 % 2) ^ meta[PAIR_Y]
        x_rel = (chip % 2) ^ meta[ACROSS]
        for core_rel, out in ((0, keep_out), (1, send_out)):
            first = pl.multiple_of((chip * 2 + (meta[CORE] ^ core_rel)) * rows, 8)
            block = [grads[i, pl.ds(first, rows)] for i in range(3)] + [tail]
            out[x_rel, y_rel, z_rel] = jnp.concatenate(block, axis=0).astype(BF16)


def call_merging(n_adapters, meta, lengths, sums, lines, out_grad, matrices):
    seq, width = sums.shape
    block = 3 * width // 32 + 8
    return pl.pallas_call(
        functools.partial(merging, n_adapters),
        in_specs=[SMEM, SMEM] + [VMEM] * 4,
        out_specs=[VMEM] * 5,
        out_shape=[sds((seq, width), F32), sds((seq, width), F32), sds((seq, width), BF16)]
        + [sds((2, 2, 4, block, width), BF16)] * 2,
        scratch_shapes=[
            pltpu.VMEM((3, width, width), F32),
        ],
        compiler_params=params(MERGE_MIB),
        cost_estimate=cost(18),
        name="merging",
    )(meta, lengths, sums, lines, out_grad, matrices)


def ffn_backward(last, blocks, grad_low, before, slope, in0, in1, *refs):
    low = grad_low[...]
    total = before[...]
    outs, refs = list(refs[: 2 * blocks]), refs[2 * blocks :]
    for quarter, into in enumerate((in0, in1)):
        grad_act = [dot_last(low, outs.pop(0)[...]) for _ in range(blocks)]
        grad_act = grad_act[0] if blocks == 1 else jnp.concatenate(grad_act, axis=1)
        grad_pre = (grad_act * slope[quarter].astype(F32)).astype(BF16)
        total = total + dot_last(grad_pre, into[...])
    if not last:
        refs[0][...] = total
        return
    normed1, inv_std1, lines, grad_out, grad_low_out = refs
    grad = norm_back(total * line_of(lines, GAIN1), normed1[...], inv_std1[...])
    grad_out[...] = grad
    grad_low_out[...] = grad.astype(BF16)


def call_ffn_backward(deps, grad_low, before, slope, in_quarters, out_quarters, *for_norm):
    seq, width = before.shape
    last = bool(for_norm)
    return kernel(
        functools.partial(ffn_backward, last, len(out_quarters) // 2),
        deps,
        FFN_MIB,
        in_specs=[VMEM] * (5 + len(out_quarters) + len(for_norm)),
        out_specs=[VMEM] * (1 + last),
        out_shape=[sds((seq, width), F32)] + [sds((seq, width), BF16)] * last,
        cost_estimate=cost(5),
        name="ffn_backward",
    )(grad_low, before, slope, *in_quarters, *out_quarters, *for_norm)


def attend_backward(
    columns, grad_low, before, turned_ref, att_ref, prob_ref, weight0, weight1, input_grad, grad_turned
):
    total = before[...]
    width = 3 * HEAD_DIM
    root = HEAD_DIM**-0.5
    for quarter, weight in enumerate((weight0, weight1)):
        grad_att = dot_last(weight[columns:], grad_low[...]).astype(BF16)
        for head in range(columns // width):
            base = head * width
            queries = turned_ref[quarter, base : base + HEAD_DIM]
            keys = turned_ref[quarter, base + HEAD_DIM : base + 2 * HEAD_DIM]
            values = turned_ref[quarter, base + 2 * HEAD_DIM : base + width].T
            part = slice(head * HEAD_DIM, (head + 1) * HEAD_DIM)
            grad = grad_att[part]
            prob = prob_ref[quarter, head]
            row_dot = jnp.sum(
                grad.astype(F32) * att_ref[quarter, part].astype(F32), axis=0, keepdims=True
            )
            grad_scores = (prob.astype(F32) * (dot(values, grad) - row_dot)).astype(BF16)
            grad_turned[base : base + HEAD_DIM] = (dot(keys, grad_scores) * root).astype(BF16)
            grad_turned[base + HEAD_DIM : base + 2 * HEAD_DIM] = (
                dot_last(queries, grad_scores) * root
            ).astype(BF16)
            grad_turned[base + 2 * HEAD_DIM : base + width] = dot_last(grad, prob).astype(BF16)
        total = total + dot(grad_turned[...].T, weight[:columns])
    input_grad[...] = total


def call_attend_backward(deps, columns, grad_low, before, turned, att, prob, quarters):
    seq, width = before.shape
    return kernel(
        functools.partial(attend_backward, columns),
        deps,
        ATTEND_MIB,
        in_specs=[VMEM] * 7,
        out_specs=VMEM,
        out_shape=sds((seq, width), F32),
        scratch_shapes=[pltpu.VMEM((columns, seq), BF16)],
        cost_estimate=cost(8),
        name="attend_backward",
    )(grad_low, before, turned, att, prob, *quarters)


def prepare(meta, down, up, query, key, value, g1, s1, g2, s2, g3, s3, keep, send, lines, shard):
    n_adapters, _, rank = down.shape
    for i in range(n_adapters):
        shard[0, :, i * rank : (i + 1) * rank] = down[i].astype(F32)
        shard[1, :, i * rank : (i + 1) * rank] = up[i].astype(F32)
    for i, ref in enumerate((query, key, value)):
        shard[2 + i] = ref[...].astype(F32)
    half = keep.shape[2]
    mine = pl.multiple_of(meta[CORE] * half, LANES)
    other = pl.multiple_of((1 - meta[CORE]) * half, LANES)
    keep[...] = shard[:, :, pl.ds(mine, half)].astype(BF16)
    send[...] = shard[:, :, pl.ds(other, half)].astype(BF16)
    for i, ref in enumerate((g1, s1, g2, s2, g3, s3)):
        lines[i : i + 1] = ref[...].reshape(1, -1)
    lines[6:8] = jnp.zeros((2, lines.shape[1]), F32)


def call_prepare(meta, down, up, query, key, value, *vectors):
    rows, width = query.shape
    half = sds((5, rows, width // 2), BF16)
    return pl.pallas_call(
        prepare,
        in_specs=[SMEM] + [VMEM] * 11,
        out_specs=[VMEM] * 3,
        out_shape=[half, half, sds((8, width), F32)],
        scratch_shapes=[pltpu.VMEM((5, rows, width), F32)],
        compiler_params=params(16),
        cost_estimate=cost(1),
        name="prepare",
    )(meta, *(in_hbm(a) for a in (down, up, query, key, value, *vectors)))


def add_blocks(*blocks):
    total = functools.reduce(jnp.add, (b.astype(F32) for b in blocks))
    tail = total[-8:-4] + total[-4:]
    return jnp.concatenate([total[:-8], split_lines(tail)], axis=0)


def sum_cores(keep, got, p_keep, p_send, q_keep, q_send):
    half = p_keep.shape[-1]
    for x in range(2):
        for y in range(2):

            @pl.loop(0, 4)
            def _(z, x=x, y=y):
                total = add_blocks(keep[x, y, z], got[x, y, z]).astype(BF16)
                (p_send if x else p_keep)[y, z] = total[:, :half]
                (q_send if y else q_keep)[x, z] = total[:, half:]


def sum_first(p_keep, p_got, q_keep, q_got, p2_keep, p2_send, q2_keep, q2_send):
    @pl.loop(0, 4)
    def _(z):
        for out, index in ((p2_keep, 0), (p2_send, 1)):
            out[z] = add_blocks(p_keep[index, z], p_got[index, z]).astype(BF16)
        for out, index in ((q2_keep, 0), (q2_send, 1)):
            out[z] = add_blocks(q_keep[index, z], q_got[index, z]).astype(BF16)


def sum_second(p_keep, p_got, q_keep, q_got, *outs):
    half = p_keep.shape[-1]
    for z in range(4):
        outs[z][:, :half] = add_blocks(p_keep[z], p_got[z]).astype(BF16)
        outs[z][:, half:] = add_blocks(q_keep[z], q_got[z]).astype(BF16)


def sum_last(n_adapters, keep, got1, got2, got3, query, key, value, gain, bias, mass):
    total = add_blocks(keep[...], got1[...], got2[...], got3[...])
    rows = query.shape[0]
    for i, out in enumerate((query, key, value)):
        out[...] = total[i * rows : (i + 1) * rows]
    lines = total[-8:-4] + total[-4:]
    gain[...] = lines[0]
    bias[...] = lines[1]
    mass[...] = lines[2, :n_adapters] / lines[2:3, n_adapters : n_adapters + 1].reshape(1)


def small_call(body, name, out_shape, dep, *operands):
    return kernel(
        body,
        (dep,),
        16,
        in_specs=[VMEM] * len(operands),
        out_specs=[VMEM] * len(out_shape),
        out_shape=out_shape,
        cost_estimate=cost(1),
        name=name,
    )(*operands)


def sum_gradients(hops, keep, send, n_adapters, works):
    block, width = keep.shape[3:]
    half = width // 2
    pair = [sds((2, 4, block, half), BF16)] * 4
    single = [sds((4, block, half), BF16)] * 4
    got = hops.flip(send, 1)
    dep = works[0](keep)
    pk, ps, qk, qs = small_call(sum_cores, "sum_cores", pair, dep, keep, got)
    pg, qg = hops.flip(ps, ALONG_X), hops.flip(qs, ALONG_Y)
    dep = works[1](pk)
    pk, ps, qk, qs = small_call(sum_first, "sum_first", single, dep, pk, pg, qk, qg)
    pg, qg = hops.flip(ps, ALONG_Y), hops.flip(qs, ALONG_X)
    dep = works[2](pk)
    parts = small_call(
        sum_second, "sum_second", [sds((block, width), BF16)] * 4, dep, pk, pg, qk, qg
    )
    got = [hops.flip(part, z * ALONG_Z) for z, part in enumerate(parts) if z]
    rows = (block - 8) // 3
    outs = [sds((rows, width), F32)] * 3 + [sds((width,), F32)] * 2 + [sds((n_adapters,), F32)]
    last = functools.partial(sum_last, n_adapters)
    return small_call(last, "sum_last", outs, dep, parts[0], *got)


ALONG_X, ALONG_Y, ALONG_Z = 2, 4, 8


class Hops:
    def __init__(self, mesh):
        self.count = mesh.size
        self.tiled = mesh.shape["dp"] == 8 and mesh.shape["tensor"] == 4

    def flip(self, array, bits):
        return lax.ppermute(array, AXES, [(i, i ^ bits) for i in range(self.count)])


def half_of(block, parity):
    half = block.shape[0] // 2
    return lax.dynamic_slice_in_dim(block, parity * half, half, 0)


def plain_schedule(
    meta, doc_lengths, tokens, out_grad, lines, columns, n_adapters, attn, into, out, shard
):
    attn, into, out = (lax.all_gather(w, "tensor", axis=0) for w in (attn, into, out))
    weights = lax.all_gather(shard, AXES, axis=1, tiled=True)
    pairs = [slice(i, i + 2) for i in range(0, attn.shape[0], 2)]
    before, saved, slopes = tokens, [], []
    for pair in pairs:
        last = pair is pairs[-1]
        results = call_attend_forward(
            [], columns, last, meta, doc_lengths, tokens, before, lines, tuple(attn[pair])
        )
        saved.append(results[:3])
        before = results[3]
    first, normed1, inv_std1 = results[3:]
    sums = first
    for pair in pairs:
        slope, sums = call_ffn_forward([], first, sums, tuple(into[pair]), tuple(out[pair]))
        slopes.append(slope)
    layer_out, total, low, keep, send = call_merging(
        n_adapters, meta, doc_lengths, sums, lines, out_grad, weights
    )
    width = tokens.shape[1]
    blocks = jnp.transpose(jnp.stack([keep, send]), (3, 2, 1, 0, 4, 5)).reshape(32, -1, width)
    squares = blocks[:, :-8].reshape(32, 3, width // 32, width)
    squares = jnp.transpose(squares, (1, 0, 2, 3)).reshape(3, width, width).astype(F32)
    squares = lax.psum_scatter(squares, AXES, scatter_dimension=1, tiled=True)
    tail = blocks[0, -8:].astype(F32)
    totals = lax.psum(tail[:4] + tail[4:], AXES)
    for pair, slope in zip(pairs, slopes):
        for_norm = (normed1, inv_std1, lines) if pair is pairs[-1] else ()
        total, *rest = call_ffn_backward(
            [], low, total, slope, tuple(into[pair]), tuple(out[pair]), *for_norm
        )
    (low,) = rest
    for pair, kept in zip(pairs, saved):
        total = call_attend_backward([], columns, low, total, *kept, tuple(attn[pair]))
    mass = totals[2, :n_adapters] / totals[2, n_adapters]
    return (layer_out, total, squares[0], squares[1], squares[2], totals[0], totals[1], mass)


def per_device(
    hops,
    tokens,
    doc_lengths,
    qkv_weight,
    attn_out_weight,
    norm1_gain,
    norm1_bias,
    ffn_in_weight,
    ffn_out_weight,
    norm2_gain,
    norm2_bias,
    adapter_down,
    adapter_up,
    merging_query,
    merging_key,
    merging_value,
    merging_gain,
    merging_bias,
    out_grad,
):
    n_adapters, rows, rank = adapter_down.shape
    columns = qkv_weight.shape[1]
    tensor, dp = lax.axis_index("tensor"), lax.axis_index("dp")
    pair_y, pair_z = dp % 2, dp // 2 % 2
    meta = jnp.stack([tensor % 2, tensor // 2, pair_y, pair_z, dp // 2, tensor]).astype(jnp.int32)
    flip = hops.flip
    if not hops.tiled:
        meta = meta * (jnp.arange(meta.shape[0]) == ROW)

    keep, send, lines = call_prepare(
        meta,
        adapter_down,
        jnp.transpose(adapter_up, (0, 2, 1)),
        merging_query,
        merging_key,
        merging_value,
        norm1_gain,
        norm1_bias,
        norm2_gain,
        norm2_bias,
        merging_gain,
        merging_bias,
    )
    attn = jnp.concatenate([qkv_weight.T, attn_out_weight], axis=0)
    if not hops.tiled:
        shard = jnp.concatenate([keep, send], axis=2)
        return plain_schedule(
            meta, doc_lengths, tokens, out_grad, lines, columns, n_adapters, attn, ffn_in_weight, ffn_out_weight, shard
        )
    attn_x = flip(half_of(attn, pair_y), ALONG_X)
    in_half = half_of(ffn_in_weight, pair_z)
    cut = ffn_out_weight.shape[0] * 2 // 3
    out_a, out_b = ffn_out_weight[:cut], ffn_out_weight[cut:]
    attn_core = flip(attn, 1)
    in_core, out_core = flip(ffn_in_weight, 1), flip(ffn_out_weight, 1)
    got = flip(send, 1)
    tile = jnp.where(
        tensor % 2 == 0,
        jnp.concatenate([keep, got], axis=1),
        jnp.concatenate([got, keep], axis=1),
    )
    tile_x = flip(tile, ALONG_X)
    both, attn_x, in_half = sync("phase1", meta, [[tile, tile_x]], [attn_x, in_half], [attn_core])
    in_x, attn_y, z2 = flip(in_half, ALONG_X), flip(attn_x, ALONG_Y), flip(both, 2 * ALONG_Z)
    saved_near = call_attend_forward(
        [both], columns, False, meta, doc_lengths, tokens, tokens, lines, (attn, attn_core)
    )
    attn_far, joined, out_a, in_x, both, z2 = sync(
        "phase2",
        meta,
        [[PAIR_Y, attn_x, attn_y], [both, z2]],
        [out_a, in_x, both, z2],
        [saved_near[3]],
    )
    attn_far_c, out_ax, z1 = flip(attn_far, 1), flip(out_a, ALONG_X), flip(joined, ALONG_Z)
    y0, y2 = flip(both, ALONG_Y), flip(z2, ALONG_Y)
    *saved_far, first, normed1, inv_std1 = call_attend_forward(
        [], columns, True, meta, doc_lengths, tokens, saved_near[3], lines, (attn_far, attn_far_c)
    )
    in_x, out_ax, out_b, z1, joined, y2, y0, first = sync(
        "phase3",
        meta,
        [],
        [in_x, out_ax, out_b, z1, joined, y2, y0, first],
        [in_core, out_core],
    )
    out_bx, in_z, y1 = flip(out_b, ALONG_X), flip(in_x, ALONG_Z), flip(z1, ALONG_Y)
    joined_c, z1_c, y0_c, y2_c = flip(joined, 1), flip(z1, 1), flip(y0, 1), flip(y2, 1)
    out_ax_c = flip(out_ax, 1)
    slope_near, sums = call_ffn_forward(
        [], first, first, (ffn_in_weight, in_core), (ffn_out_weight, out_core)
    )
    own, other = 0, 1
    weights = assemble(
        "assemble",
        meta,
        None,
        [
            (joined, ((0, 0), (0, 2)), own),
            (joined_c, ((0, 0), (0, 2)), other),
            (z1, ((0, 1), (0, 3)), own),
            (z1_c, ((0, 1), (0, 3)), other),
            (y0, ((1, 0),), own),
            (y0_c, ((1, 0),), other),
            (y2, ((1, 2),), own),
            (y2_c, ((1, 2),), other),
        ],
    )
    in_far, out_bx, y1 = sync(
        "phase4", meta, [[PAIR_Z, in_x, in_z]], [out_bx, y1], [sums, weights, out_ax_c]
    )
    in_far_c, out_bx_c, y1_c = flip(in_far, 1), flip(out_bx, 1), flip(y1, 1)
    out_far = (out_ax, out_bx, out_ax_c, out_bx_c)
    slope_far, sums = call_ffn_forward([], first, sums, (in_far, in_far_c), out_far)
    last_parts = ((1, 1), (1, 3))
    weights = assemble(
        "assemble_last", meta, weights, [(y1, last_parts, own), (y1_c, last_parts, other)]
    )
    layer_out, grad_sum2, grad_sum2_low, *grads = call_merging(
        n_adapters, meta, doc_lengths, sums, lines, out_grad, weights
    )
    done = {}

    def first_work(dep):
        (done["near"],) = call_ffn_backward(
            [dep],
            grad_sum2_low,
            grad_sum2,
            slope_near,
            (ffn_in_weight, in_core),
            (ffn_out_weight, out_core),
        )
        return done["near"]

    def second_work(dep):
        done["sum1"], done["low1"] = call_ffn_backward(
            [dep],
            grad_sum2_low,
            done["near"],
            slope_far,
            (in_far, in_far_c),
            out_far,
            normed1,
            inv_std1,
            lines,
        )
        done["near"] = call_attend_backward(
            [], columns, done["low1"], done["sum1"], *saved_near[:3], (attn, attn_core)
        )
        return done["near"]

    def third_work(dep):
        done["far"] = call_attend_backward(
            [dep], columns, done["low1"], done["near"], *saved_far[:3], (attn_far, attn_far_c)
        )
        return done["far"]

    works = (first_work, second_work, third_work)
    summed = sum_gradients(hops, *grads, n_adapters, works)
    return (layer_out, done["far"], *summed)


def solution(mesh):
    split = P(AXES, None)
    in_specs = (
        split,
        P("dp", None),
        P(None, "tensor"),
        P("tensor", None),
        P(),
        P(),
        P(None, "tensor"),
        P("tensor", None),
        P(),
        P(),
        P(None, AXES, None),
        P(None, None, AXES),
        split,
        split,
        split,
        P(),
        P(),
        split,
    )
    out_specs = (split, split, split, split, split, P(), P(), P())
    return jax.shard_map(
        functools.partial(per_device, Hops(mesh)),
        mesh=mesh,
        in_specs=in_specs,
        out_specs=out_specs,
        check_vma=False,
    )
```

```python
import functools

import jax
import jax.numpy as jnp
from jax import lax
from jax.experimental import pallas as pl
from jax.experimental.pallas import tpu as pltpu
from jax.sharding import PartitionSpec as P

HEAD_DIM = 64
AXES = ("dp", "tensor")
ATTEND_MIB, FFN_MIB, MERGE_MIB = 24, 24, 30
LANES = 128
COST = 0.0
EPS = 1e-12
BIG_NEGATIVE = -1e30
ROOT_HALF = 0.7071067811865476
ROOT_TAU = 0.3989422804014327
F32, BF16 = jnp.float32, jnp.bfloat16

CORE, ACROSS, PAIR_Y, PAIR_Z, DEPTH, ROW = range(6)
GAIN1, SHIFT1, GAIN2, SHIFT2, GAIN3, SHIFT3 = range(6)

SMEM = pl.BlockSpec(memory_space=pltpu.SMEM)
VMEM = pl.BlockSpec(memory_space=pltpu.VMEM)
ANY = pl.BlockSpec(memory_space=pl.ANY)
HBM = pl.BlockSpec(memory_space=pltpu.HBM)


def line_of(lines, i):
    return lines[i : i + 1]


def dot(a, b):
    return lax.dot_general(a, b, (((1,), (0,)), ((), ())), preferred_element_type=F32)


def dot_last(a, b):
    return lax.dot_general(a, b, (((1,), (1,)), ((), ())), preferred_element_type=F32)


def dot_first(a, b):
    return lax.dot_general(a, b, (((0,), (0,)), ((), ())), preferred_element_type=F32)


def normalize(u):
    centered = u - jnp.mean(u, axis=-1, keepdims=True)
    inv_std = lax.rsqrt(jnp.mean(centered * centered, axis=-1, keepdims=True) + EPS)
    return centered * inv_std, inv_std


def norm_back(grad, normed, inv_std):
    return inv_std * (
        grad
        - jnp.mean(grad, axis=-1, keepdims=True)
        - normed * jnp.mean(grad * normed, axis=-1, keepdims=True)
    )


def gelu_both(u):
    half = 0.5 * (1.0 + lax.erf(u * ROOT_HALF))
    return u * half, half + u * jnp.exp(-0.5 * u * u) * ROOT_TAU


def segment_bias(meta_ref, lengths_ref, bias_ref):
    seq = bias_ref.shape[0]
    row = meta_ref[ROW]
    by_row = lax.broadcasted_iota(jnp.int32, (seq, 1), 0)
    by_lane = lax.broadcasted_iota(jnp.int32, (1, seq), 1)
    seg_row = jnp.zeros((seq, 1), jnp.int32)
    seg_lane = jnp.zeros((1, seq), jnp.int32)
    end = jnp.int32(0)
    for i in range(lengths_ref.shape[1]):
        end = end + lengths_ref[row, i]
        seg_row = seg_row + jnp.where(by_row >= end, 1, 0)
        seg_lane = seg_lane + jnp.where(by_lane >= end, 1, 0)
    bias_ref[...] = jnp.where(seg_row == seg_lane, 0.0, BIG_NEGATIVE).astype(F32)


def attend_forward(columns, last, meta, lengths, tokens, before, lines, weight0, weight1, *refs):
    saved, first_out, bias = refs[:6], refs[6], refs[-1]
    segment_bias(meta, lengths, bias)
    total = before[...].astype(F32)
    width = 3 * HEAD_DIM
    for quarter, weight in enumerate((weight0, weight1)):
        turned = dot_last(weight[:columns], tokens[...]).astype(BF16)
        turned_out, att_out, prob_out = saved[3 * quarter : 3 * quarter + 3]
        turned_out[...] = turned

        @pl.loop(0, columns // width)
        def _(head, turned_out=turned_out, att_out=att_out, prob_out=prob_out):
            base = pl.multiple_of(head * width, width)
            queries, keys, values = (
                turned_out[pl.ds(base + i * HEAD_DIM, HEAD_DIM)] for i in range(3)
            )
            scores = dot(keys.T, queries * BF16(HEAD_DIM**-0.5)) + bias[...]
            exponent = jnp.exp(scores - jnp.max(scores, axis=0, keepdims=True))
            prob = (exponent * (1.0 / jnp.sum(exponent, axis=0, keepdims=True))).astype(BF16)
            prob_out[head] = prob
            part = pl.ds(pl.multiple_of(head * HEAD_DIM, HEAD_DIM), HEAD_DIM)
            att_out[part] = dot(values, prob).astype(BF16)

        total = total + dot(att_out[...].T, weight[columns:])
    if not last:
        first_out[...] = total
        return
    normed_out, inv_out = refs[7:9]
    normed, inv_std = normalize(total)
    normed_out[...] = normed
    inv_out[...] = inv_std
    first_out[...] = normed * line_of(lines, GAIN1) + line_of(lines, SHIFT1)


def sds(shape, dtype):
    return jax.ShapeDtypeStruct(shape, dtype)


def params(mib):
    return pltpu.CompilerParams(vmem_limit_bytes=mib << 20)


def kernel(body, deps, mib, *, in_specs, **kw):
    n = len(deps)
    call = pl.pallas_call(
        lambda *refs: body(*refs[n:]),
        in_specs=[ANY] * n + in_specs,
        compiler_params=params(mib),
        **kw,
    )
    return functools.partial(call, *deps)


def sync(name, meta, joins, carries, deps):
    sides = [j[0] if isinstance(j[0], int) else None for j in joins]
    parts = [j[1:] if isinstance(j[0], int) else j for j in joins]
    flat = [p for j in parts for p in j]

    def body(meta_ref, *refs):
        refs = refs[len(carries) :]
        sources, outs = list(refs[: len(flat)]), refs[len(flat) : len(flat) + len(parts)]
        for side, join, out in zip(sides, parts, outs):
            row = 0
            for i, part in enumerate(join):
                size = part.shape[0]
                if side is not None:
                    n = len(join) // 2
                    row = pl.multiple_of(((meta_ref[side] ^ (i // n)) * n + i % n) * size, 16)
                out[pl.ds(row, size)] = sources.pop(0)[...]
                row = row + size

    joined = [sds((sum(p.shape[0] for p in j), *j[0].shape[1:]), j[0].dtype) for j in parts]
    n_deps = len(deps)
    out = kernel(
        body,
        deps,
        16,
        in_specs=[SMEM] + [ANY] * len(carries) + [VMEM] * len(flat),
        out_specs=[VMEM] * len(joined) + [ANY] * len(carries),
        out_shape=joined + [sds(c.shape, c.dtype) for c in carries],
        input_output_aliases={n_deps + 1 + i: len(joined) + i for i in range(len(carries))},
        cost_estimate=cost(0),
        name=name,
    )(meta, *carries, *flat)
    return out


def in_hbm(array):
    return pltpu.with_memory_space_constraint(array, pltpu.HBM)


def cost(us):
    return pl.CostEstimate(flops=int(us * 1.1e9 * COST), bytes_accessed=1024, transcendentals=0)


def call_attend_forward(deps, columns, last, meta, lengths, tokens, before, lines, quarters):
    seq, width = tokens.shape
    heads = columns // (3 * HEAD_DIM)
    inner = heads * HEAD_DIM
    square, narrow = sds((seq, width), F32), sds((seq, 1), F32)
    out_shape = [
        pltpu.HBM((columns, seq), BF16),
        pltpu.HBM((inner, seq), BF16),
        pltpu.HBM((heads, seq, seq), BF16),
    ] * 2 + [square] + [square, narrow] * last
    return kernel(
        functools.partial(attend_forward, columns, last),
        deps,
        ATTEND_MIB,
        in_specs=[SMEM, SMEM] + [VMEM] * 5,
        out_specs=[VMEM] * len(out_shape),
        out_shape=out_shape,
        scratch_shapes=[pltpu.VMEM((seq, seq), F32)],
        cost_estimate=cost(8),
        name="attend_forward",
    )(meta, lengths, tokens, before, lines, *quarters)


def ffn_forward(blocks, first, before, *refs):
    slope_out, sum_out = refs[-2:]
    low = first[...].astype(BF16)
    total = before[...]
    outs = list(refs[2:-2])
    for quarter in range(2):
        value, slope = gelu_both(dot(low, refs[quarter][...]))
        slope_out[quarter] = slope.astype(BF16)
        value = value.astype(BF16)
        row = 0
        for _ in range(blocks):
            out = outs.pop(0)
            total = total + dot(value[:, row : row + out.shape[0]], out[...])
            row += out.shape[0]
    sum_out[...] = total


def call_ffn_forward(deps, first, before, in_quarters, out_quarters):
    seq, width = first.shape
    hidden = in_quarters[0].shape[1]
    return kernel(
        functools.partial(ffn_forward, len(out_quarters) // 2),
        deps,
        FFN_MIB,
        in_specs=[VMEM] * (4 + len(out_quarters)),
        out_specs=[VMEM] * 2,
        out_shape=[sds((2, seq, hidden), BF16), sds((seq, width), F32)],
        cost_estimate=cost(5),
        name="ffn_forward",
    )(first, before, *in_quarters, *out_quarters)


def assemble(name, meta, weights, tiles):
    n_mats = tiles[0][0].shape[0] // (2 * len(tiles[0][1]))
    rows, half = tiles[0][0].shape[1:]
    count = sum(2 * len(parts) for _, parts, _ in tiles)
    before = [] if weights is None else [weights]

    def body(meta_ref, *refs):
        refs = refs[len(before) :]
        out, sems = refs[-2:]
        copies = []
        for ref, (_, parts, core_rel) in zip(refs, tiles):
            side = pl.multiple_of((meta_ref[CORE] ^ core_rel) * half, LANES)
            for j, (y_rel, z_rel) in enumerate(parts):
                for x_rel in range(2):
                    chip = ((meta_ref[DEPTH] ^ z_rel) * 2 + (meta_ref[PAIR_Y] ^ y_rel)) * 2
                    chip = chip + (meta_ref[ACROSS] ^ x_rel)
                    first = pl.multiple_of(chip * rows, 16)
                    target = out.at[:, pl.ds(first, rows), pl.ds(side, half)]
                    source = ref.at[pl.ds((2 * j + x_rel) * n_mats, n_mats)]
                    copies.append(pltpu.make_async_copy(source, target, sems.at[len(copies)]))
        for copy in copies:
            copy.start()
        for copy in copies:
            copy.wait()

    return kernel(
        body,
        [],
        16,
        in_specs=[SMEM] + [ANY] * len(before) + [VMEM] * len(tiles),
        out_specs=ANY,
        out_shape=sds((n_mats, 2 * half, 2 * half), BF16),
        input_output_aliases={1: 0} if before else {},
        scratch_shapes=[pltpu.SemaphoreType.DMA((count,))],
        cost_estimate=cost(0),
        name=name,
    )(meta, *before, *(tile for tile, _, _ in tiles))


def split_lines(total):
    high = total.astype(BF16).astype(F32)
    return jnp.concatenate([high, total - high], axis=0)


def merging(n_adapters, meta, lengths, sums, lines, out_grad, matrices, *refs):
    layer_out, part_out, fquery_out, middle_out, keep_out, send_out, grads = refs
    seq, width = sums.shape
    scale = width**-0.5
    down, up, query, key, value = (matrices.at[i] for i in range(5))
    gain2, shift2 = line_of(lines, GAIN2), line_of(lines, SHIFT2)
    gain3, shift3 = line_of(lines, GAIN3), line_of(lines, SHIFT3)
    spread = jnp.where(
        lax.broadcasted_iota(jnp.int32, (LANES, width), 0)
        == lax.broadcasted_iota(jnp.int32, (LANES, width), 1) // (width // n_adapters),
        1.0,
        0.0,
    ).astype(BF16)
    real_lane = lax.broadcasted_iota(jnp.int32, (1, LANES), 1) < n_adapters

    def by_adapter(terms):
        high = terms.astype(BF16)
        rest = (terms - high.astype(F32)).astype(BF16)
        return dot_last(high, spread) + dot_last(rest, spread)

    mean2 = jnp.mean(sums[...], axis=-1, keepdims=True)
    centered = sums[...] - mean2
    inv_std2 = lax.rsqrt(jnp.mean(centered * centered, axis=-1, keepdims=True) + EPS)
    second = centered * inv_std2 * gain2 + shift2
    second_low = second.astype(BF16)
    act, slope = (v.astype(BF16) for v in gelu_both(dot(second_low, down[...])))
    fquery = dot(second_low, query[...]).astype(BF16)
    probe = dot_last(fquery, key[...]).astype(BF16)
    probe_up = dot(probe, up[...])
    logits = scale * (
        jnp.sum(probe.astype(F32) * second, axis=1, keepdims=True) + by_adapter(act * probe_up)
    )
    logits = jnp.where(real_lane, logits, BIG_NEGATIVE)
    exponent = jnp.exp(logits - jnp.max(logits, axis=1, keepdims=True))
    mix = exponent / jnp.sum(exponent, axis=1, keepdims=True)
    mix_low = mix.astype(BF16)
    mix_sum = jnp.sum(mix_low.astype(F32), axis=1, keepdims=True)
    mix_wide = dot(mix_low, spread).astype(BF16)
    blended = (second * mix_sum + dot_last((mix_wide * act).astype(BF16), up[...])).astype(BF16)
    normed3, inv_std3 = normalize(second + dot(blended, value[...]))
    layer_out[...] = normed3 * gain3 + shift3

    count = jnp.int32(0)
    for i in range(lengths.shape[1]):
        count = count + lengths[meta[ROW], i]
    keep = jnp.where(lax.broadcasted_iota(jnp.int32, (seq, 1), 0) < count, 1.0, 0.0)
    cot = out_grad[...].astype(F32) * keep
    mass = jnp.sum(mix * keep, axis=0, keepdims=True)
    lane = lax.broadcasted_iota(jnp.int32, (1, LANES), 1)
    mass = jnp.where(lane == n_adapters, jnp.sum(keep), mass)
    sum_lines = jnp.concatenate(
        [
            jnp.sum(cot * normed3, axis=0, keepdims=True),
            jnp.sum(cot, axis=0, keepdims=True),
            jnp.concatenate([mass, jnp.zeros((1, width - LANES), F32)], axis=1),
            jnp.zeros((1, width), F32),
        ],
        axis=0,
    )

    grad_pre = norm_back(cot * gain3, normed3, inv_std3)
    grad_proj = grad_pre.astype(BF16)
    grads[2] = dot_first(blended, grad_proj)
    grad_blend = dot_last(grad_proj, value[...]).astype(BF16)
    blend_up = dot(grad_blend, up[...])
    grad_mix = jnp.sum(grad_blend.astype(F32) * second, axis=1, keepdims=True) + by_adapter(
        act * blend_up
    )
    grad_logits = (mix * (grad_mix - jnp.sum(grad_mix * mix, axis=1, keepdims=True))).astype(BF16)
    logit_sum = jnp.sum(grad_logits.astype(F32), axis=1, keepdims=True)
    logit_wide = dot(grad_logits, spread).astype(BF16)
    grad_probe = (
        scale * (second * logit_sum + dot_last((logit_wide * act).astype(BF16), up[...]))
    ).astype(BF16)
    grads[1] = dot_first(grad_probe, fquery)
    grad_fquery = dot(grad_probe, key[...]).astype(BF16)
    grads[0] = dot_first(second_low, grad_fquery)
    grad_act = mix_wide.astype(F32) * blend_up + (scale * logit_wide.astype(F32)) * probe_up
    middle_out[...] = (grad_act * slope.astype(F32)).astype(BF16)
    fquery_out[...] = grad_fquery
    part_out[...] = (
        grad_pre + grad_blend.astype(F32) * mix_sum + probe.astype(F32) * (scale * logit_sum)
    )

    tail = split_lines(sum_lines)
    rows = width // 32

    @pl.loop(0, 16)
    def _(chip):
        z_rel = (chip // 4) ^ meta[DEPTH]
        y_rel = (chip // 2 % 2) ^ meta[PAIR_Y]
        x_rel = (chip % 2) ^ meta[ACROSS]
        for core_rel, out in ((0, keep_out), (1, send_out)):
            first = pl.multiple_of((chip * 2 + (meta[CORE] ^ core_rel)) * rows, 8)
            block = [grads[i, pl.ds(first, rows)] for i in range(3)] + [tail]
            out[x_rel, y_rel, z_rel] = jnp.concatenate(block, axis=0).astype(BF16)


def call_merging(n_adapters, meta, lengths, sums, lines, out_grad, matrices):
    seq, width = sums.shape
    block = 3 * width // 32 + 8
    return pl.pallas_call(
        functools.partial(merging, n_adapters),
        in_specs=[SMEM, SMEM] + [VMEM] * 4,
        out_specs=[VMEM] * 6,
        out_shape=[sds((seq, width), F32)] * 2
        + [sds((seq, width), BF16)] * 2
        + [sds((2, 2, 4, block, width), BF16)] * 2,
        scratch_shapes=[pltpu.VMEM((3, width, width), F32)],
        compiler_params=params(MERGE_MIB),
        cost_estimate=cost(18),
        name="merging",
    )(meta, lengths, sums, lines, out_grad, matrices)


def merging_input(sums, lines, part, grad_fquery, grad_middle, matrices, grad_out, grad_low_out):
    normed, inv_std = normalize(sums[...])
    grad = part[...] + dot_last(grad_fquery[...], matrices[2])
    grad = grad + dot_last(grad_middle[...], matrices[0])
    grad = norm_back(grad * line_of(lines, GAIN2), normed, inv_std)
    grad_out[...] = grad
    grad_low_out[...] = grad.astype(BF16)


def call_merging_input(deps, sums, lines, part, grad_fquery, grad_middle, matrices):
    return kernel(
        merging_input,
        deps,
        MERGE_MIB,
        in_specs=[VMEM] * 6,
        out_specs=[VMEM] * 2,
        out_shape=[sds(part.shape, F32), sds(part.shape, BF16)],
        cost_estimate=cost(3),
        name="merging_input",
    )(sums, lines, part, grad_fquery, grad_middle, matrices)


def ffn_backward(last, blocks, grad_low, before, slope, in0, in1, *refs):
    low = grad_low[...]
    total = before[...]
    outs, refs = list(refs[: 2 * blocks]), refs[2 * blocks :]
    for quarter, into in enumerate((in0, in1)):
        grad_act = [dot_last(low, outs.pop(0)[...]) for _ in range(blocks)]
        grad_act = grad_act[0] if blocks == 1 else jnp.concatenate(grad_act, axis=1)
        grad_pre = (grad_act * slope[quarter].astype(F32)).astype(BF16)
        total = total + dot_last(grad_pre, into[...])
    if not last:
        refs[0][...] = total
        return
    normed1, inv_std1, lines, grad_out, grad_low_out = refs
    grad = norm_back(total * line_of(lines, GAIN1), normed1[...], inv_std1[...])
    grad_out[...] = grad
    grad_low_out[...] = grad.astype(BF16)


def call_ffn_backward(deps, grad_low, before, slope, in_quarters, out_quarters, *for_norm):
    seq, width = before.shape
    last = bool(for_norm)
    return kernel(
        functools.partial(ffn_backward, last, len(out_quarters) // 2),
        deps,
        FFN_MIB,
        in_specs=[VMEM] * (5 + len(out_quarters) + len(for_norm)),
        out_specs=[VMEM] * (1 + last),
        out_shape=[sds((seq, width), F32)] + [sds((seq, width), BF16)] * last,
        cost_estimate=cost(5),
        name="ffn_backward",
    )(grad_low, before, slope, *in_quarters, *out_quarters, *for_norm)


def attend_backward(
    columns, grad_low, before, turned_ref, att_ref, prob_ref, weight, input_grad, token, grad_turned, grad_att
):
    width = 3 * HEAD_DIM
    root = HEAD_DIM**-0.5
    grad_att[...] = dot_last(weight[columns:], grad_low[...]).astype(BF16)

    @pl.loop(0, columns // width)
    def _(head):
        base = pl.multiple_of(head * width, width)
        places = [pl.ds(base + i * HEAD_DIM, HEAD_DIM) for i in range(3)]
        queries, keys, values = (turned_ref[place] for place in places)
        part = pl.ds(pl.multiple_of(head * HEAD_DIM, HEAD_DIM), HEAD_DIM)
        grad = grad_att[part]
        prob = prob_ref[head]
        row_dot = jnp.sum(grad.astype(F32) * att_ref[part].astype(F32), axis=0, keepdims=True)
        grad_scores = (prob.astype(F32) * (dot(values.T, grad) - row_dot)).astype(BF16)
        grad_turned[places[0]] = (dot(keys, grad_scores) * root).astype(BF16)
        grad_turned[places[1]] = (dot_last(queries, grad_scores) * root).astype(BF16)
        grad_turned[places[2]] = dot_last(grad, prob).astype(BF16)

    input_grad[...] = before[...] + dot(grad_turned[...].T, weight[:columns])
    token[...] = jnp.zeros_like(token)


def call_attend_backward(deps, columns, grad_low, before, saved, quarter):
    seq, width = before.shape
    inner = columns // 3
    return kernel(
        functools.partial(attend_backward, columns),
        deps,
        ATTEND_MIB,
        in_specs=[VMEM] * 6,
        out_specs=[VMEM] * 2,
        out_shape=[sds((seq, width), F32), sds((8, LANES), F32)],
        scratch_shapes=[pltpu.VMEM((columns, seq), BF16), pltpu.VMEM((inner, seq), BF16)],
        cost_estimate=cost(8),
        name="attend_backward",
    )(grad_low, before, *saved, quarter)


def prepare(meta, down, up, query, key, value, g1, s1, g2, s2, g3, s3, keep, send, lines, shard):
    n_adapters, _, rank = down.shape
    for i in range(n_adapters):
        shard[0, :, i * rank : (i + 1) * rank] = down[i].astype(F32)
        shard[1, :, i * rank : (i + 1) * rank] = up[i].astype(F32)
    for i, ref in enumerate((query, key, value)):
        shard[2 + i] = ref[...].astype(F32)
    half = keep.shape[2]
    mine = pl.multiple_of(meta[CORE] * half, LANES)
    other = pl.multiple_of((1 - meta[CORE]) * half, LANES)
    keep[...] = shard[:, :, pl.ds(mine, half)].astype(BF16)
    send[...] = shard[:, :, pl.ds(other, half)].astype(BF16)
    for i, ref in enumerate((g1, s1, g2, s2, g3, s3)):
        lines[i : i + 1] = ref[...].reshape(1, -1)
    lines[6:8] = jnp.zeros((2, lines.shape[1]), F32)


def call_prepare(meta, down, up, query, key, value, *vectors):
    rows, width = query.shape
    half = sds((5, rows, width // 2), BF16)
    return pl.pallas_call(
        prepare,
        in_specs=[SMEM] + [VMEM] * 11,
        out_specs=[VMEM] * 3,
        out_shape=[half, half, sds((8, width), F32)],
        scratch_shapes=[pltpu.VMEM((5, rows, width), F32)],
        compiler_params=params(16),
        cost_estimate=cost(1),
        name="prepare",
    )(meta, *(in_hbm(a) for a in (down, up, query, key, value, *vectors)))


def prepare_frozen(meta, qkv_turned, attn_out, into, attn, attn_half, in_half):
    columns = qkv_turned.shape[0]
    attn[:columns] = qkv_turned[...]
    attn[columns:] = attn_out[...]
    for entry, whole, half in ((PAIR_Y, attn, attn_half), (PAIR_Z, into, in_half)):
        rows = half.shape[0]
        half[...] = whole[pl.ds(pl.multiple_of(meta[entry] * rows, 16), rows)]


def call_prepare_frozen(meta, qkv_turned, attn_out, into):
    rows, width = qkv_turned.shape[0] + attn_out.shape[0], attn_out.shape[1]
    return kernel(
        prepare_frozen,
        [],
        16,
        in_specs=[SMEM] + [VMEM] * 3,
        out_specs=[VMEM] * 3,
        out_shape=[
            sds((rows, width), BF16),
            sds((rows // 2, width), BF16),
            sds((into.shape[0] // 2, into.shape[1]), BF16),
        ],
        cost_estimate=cost(1),
        name="prepare_frozen",
    )(meta, *(in_hbm(a) for a in (qkv_turned, attn_out, into)))


def chip_tile(meta, keep, got, tile):
    mine, other = keep[...].astype(F32), got[...].astype(F32)
    lower = jnp.where(meta[CORE] == 0, mine, other)
    upper = jnp.where(meta[CORE] == 0, other, mine)
    tile[...] = jnp.concatenate([lower, upper], axis=1).astype(BF16)


def call_chip_tile(meta, keep, got):
    n_mats, rows, half = keep.shape
    return kernel(
        chip_tile,
        [],
        16,
        in_specs=[SMEM] + [VMEM] * 2,
        out_specs=VMEM,
        out_shape=sds((n_mats, 2 * rows, half), BF16),
        cost_estimate=cost(1),
        name="chip_tile",
    )(meta, keep, got)


def add_blocks(*blocks):
    total = functools.reduce(jnp.add, (b.astype(F32) for b in blocks))
    tail = total[-8:-4] + total[-4:]
    return jnp.concatenate([total[:-8], split_lines(tail)], axis=0)


def sum_cores(keep, got, p_keep, p_send, q_keep, q_send):
    half = p_keep.shape[-1]
    for x in range(2):
        for y in range(2):

            @pl.loop(0, 4)
            def _(z, x=x, y=y):
                total = add_blocks(keep[x, y, z], got[x, y, z]).astype(BF16)
                (p_send if x else p_keep)[y, z] = total[:, :half]
                (q_send if y else q_keep)[x, z] = total[:, half:]


def sum_first(p_keep, p_got, q_keep, q_got, p2_keep, p2_send, q2_keep, q2_send):
    @pl.loop(0, 4)
    def _(z):
        for out, index in ((p2_keep, 0), (p2_send, 1)):
            out[z] = add_blocks(p_keep[index, z], p_got[index, z]).astype(BF16)
        for out, index in ((q2_keep, 0), (q2_send, 1)):
            out[z] = add_blocks(q_keep[index, z], q_got[index, z]).astype(BF16)


def sum_second(p_keep, p_got, q_keep, q_got, *outs):
    half = p_keep.shape[-1]
    for z in range(4):
        outs[z][:, :half] = add_blocks(p_keep[z], p_got[z]).astype(BF16)
        outs[z][:, half:] = add_blocks(q_keep[z], q_got[z]).astype(BF16)


def sum_last(n_adapters, keep, got1, got2, got3, query, key, value, gain, bias, mass):
    total = add_blocks(keep[...], got1[...], got2[...], got3[...])
    rows = query.shape[0]
    for i, out in enumerate((query, key, value)):
        out[...] = total[i * rows : (i + 1) * rows]
    lines = total[-8:-4] + total[-4:]
    gain[...] = lines[0]
    bias[...] = lines[1]
    mass[...] = lines[2, :n_adapters] / lines[2:3, n_adapters : n_adapters + 1].reshape(1)


def small_call(body, name, out_shape, dep, *operands):
    return kernel(
        body,
        (dep,),
        16,
        in_specs=[VMEM] * len(operands),
        out_specs=[VMEM] * len(out_shape),
        out_shape=out_shape,
        cost_estimate=cost(1),
        name=name,
    )(*operands)


def sum_gradients(hops, keep, send, n_adapters, works):
    block, width = keep.shape[3:]
    half = width // 2
    pair = [sds((2, 4, block, half), BF16)] * 4
    single = [sds((4, block, half), BF16)] * 4
    got = hops.flip(send, 1)
    dep = works[0](())
    pk, ps, qk, qs = small_call(sum_cores, "sum_cores", pair, dep, keep, got)
    pg, qg = hops.flip(ps, ALONG_X), hops.flip(qs, ALONG_Y)
    dep = works[1]([pk])
    pk, ps, qk, qs = small_call(sum_first, "sum_first", single, dep, pk, pg, qk, qg)
    pg, qg = hops.flip(ps, ALONG_Y), hops.flip(qs, ALONG_X)
    dep = works[2]([pk])
    parts = small_call(
        sum_second, "sum_second", [sds((block, width), BF16)] * 4, dep, pk, pg, qk, qg
    )
    got = [hops.flip(part, z * ALONG_Z) for z, part in enumerate(parts) if z]
    dep = works[3]([parts[0]])
    rows = (block - 8) // 3
    outs = [sds((rows, width), F32)] * 3 + [sds((width,), F32)] * 2 + [sds((n_adapters,), F32)]
    last = functools.partial(sum_last, n_adapters)
    return small_call(last, "sum_last", outs, dep, parts[0], *got)


ALONG_X, ALONG_Y, ALONG_Z = 2, 4, 8


class Hops:
    def __init__(self, mesh):
        self.count = mesh.size
        self.tiled = mesh.shape["dp"] == 8 and mesh.shape["tensor"] == 4

    def flip(self, array, bits):
        return lax.ppermute(array, AXES, [(i, i ^ bits) for i in range(self.count)])


def half_of(block, parity):
    half = block.shape[0] // 2
    return lax.dynamic_slice_in_dim(block, parity * half, half, 0)


def plain_schedule(
    meta, doc_lengths, tokens, out_grad, lines, columns, n_adapters, attn, into, out, shard
):
    attn, into, out = (lax.all_gather(w, "tensor", axis=0) for w in (attn, into, out))
    weights = lax.all_gather(shard, AXES, axis=1, tiled=True)
    pairs = [slice(i, i + 2) for i in range(0, attn.shape[0], 2)]
    before, saved, slopes = tokens, [], []
    for pair in pairs:
        last = pair is pairs[-1]
        results = call_attend_forward(
            [], columns, last, meta, doc_lengths, tokens, before, lines, tuple(attn[pair])
        )
        saved += [results[:3], results[3:6]]
        before = results[6]
    first, normed1, inv_std1 = results[6:]
    sums = first
    for pair in pairs:
        slope, sums = call_ffn_forward([], first, sums, tuple(into[pair]), tuple(out[pair]))
        slopes.append(slope)
    layer_out, *parts, keep, send = call_merging(
        n_adapters, meta, doc_lengths, sums, lines, out_grad, weights
    )
    total, low = call_merging_input([], sums, lines, *parts, weights)
    width = tokens.shape[1]
    blocks = jnp.transpose(jnp.stack([keep, send]), (3, 2, 1, 0, 4, 5)).reshape(32, -1, width)
    squares = blocks[:, :-8].reshape(32, 3, width // 32, width)
    squares = jnp.transpose(squares, (1, 0, 2, 3)).reshape(3, width, width).astype(F32)
    squares = lax.psum_scatter(squares, AXES, scatter_dimension=1, tiled=True)
    tail = blocks[0, -8:].astype(F32)
    totals = lax.psum(tail[:4] + tail[4:], AXES)
    for pair, slope in zip(pairs, slopes):
        for_norm = (normed1, inv_std1, lines) if pair is pairs[-1] else ()
        total, *rest = call_ffn_backward(
            [], low, total, slope, tuple(into[pair]), tuple(out[pair]), *for_norm
        )
    (low,) = rest
    for quarter, kept in zip(attn, saved):
        total, _ = call_attend_backward([], columns, low, total, kept, quarter)
    mass = totals[2, :n_adapters] / totals[2, n_adapters]
    return (layer_out, total, squares[0], squares[1], squares[2], totals[0], totals[1], mass)


def per_device(
    hops,
    tokens,
    doc_lengths,
    qkv_weight,
    attn_out_weight,
    norm1_gain,
    norm1_bias,
    ffn_in_weight,
    ffn_out_weight,
    norm2_gain,
    norm2_bias,
    adapter_down,
    adapter_up,
    merging_query,
    merging_key,
    merging_value,
    merging_gain,
    merging_bias,
    out_grad,
):
    n_adapters, rows, rank = adapter_down.shape
    columns = qkv_weight.shape[1]
    tensor, dp = lax.axis_index("tensor"), lax.axis_index("dp")
    pair_y, pair_z = dp % 2, dp // 2 % 2
    meta = jnp.stack([tensor % 2, tensor // 2, pair_y, pair_z, dp // 2, tensor]).astype(jnp.int32)
    flip = hops.flip
    if not hops.tiled:
        meta = meta * (jnp.arange(meta.shape[0]) == ROW)

    keep, send, lines = call_prepare(
        meta,
        adapter_down,
        jnp.transpose(adapter_up, (0, 2, 1)),
        merging_query,
        merging_key,
        merging_value,
        norm1_gain,
        norm1_bias,
        norm2_gain,
        norm2_bias,
        merging_gain,
        merging_bias,
    )
    attn, attn_half, in_half = call_prepare_frozen(
        meta, qkv_weight.T, attn_out_weight, ffn_in_weight
    )
    if not hops.tiled:
        shard = jnp.concatenate([keep, send], axis=2)
        return plain_schedule(
            meta, doc_lengths, tokens, out_grad, lines, columns, n_adapters, attn, ffn_in_weight, ffn_out_weight, shard
        )
    cut = ffn_out_weight.shape[0] // 3
    out_a, out_b = ffn_out_weight[:cut], ffn_out_weight[cut:]
    attn_core = flip(attn, 1)
    in_core, out_core = flip(ffn_in_weight, 1), flip(ffn_out_weight, 1)
    tile = call_chip_tile(meta, keep, flip(send, 1))
    tile_x = flip(tile, ALONG_X)
    both, attn_half = sync("phase1", meta, [[tile, tile_x]], [attn_half], [attn_core])
    z2, attn_x, y0 = flip(both, 2 * ALONG_Z), flip(attn_half, ALONG_X), flip(both, ALONG_Y)
    saved_near = call_attend_forward(
        [both], columns, False, meta, doc_lengths, tokens, tokens, lines, (attn, attn_core)
    )
    joined, in_half, out_a, attn_x, y0, z2 = sync(
        "phase2", meta, [[both, z2]], [in_half, out_a, attn_x, y0, z2], [saved_near[6]]
    )
    attn_y, z1, in_x = flip(attn_x, ALONG_Y), flip(joined, ALONG_Z), flip(in_half, ALONG_X)
    y2, out_ax = flip(z2, ALONG_Y), flip(out_a, ALONG_X)
    joined_c, y0_c = flip(joined, 1), flip(y0, 1)
    attn_far, in_x, out_ax, out_b, z1, y2 = sync(
        "phase3",
        meta,
        [[PAIR_Y, attn_x, attn_y]],
        [in_x, out_ax, out_b, z1, y2],
        [in_core, out_core, joined_c, y0_c],
    )
    attn_far_c = flip(attn_far, 1)
    y1, out_bx, in_z = flip(z1, ALONG_Y), flip(out_b, ALONG_X), flip(in_x, ALONG_Z)
    z1_c, y2_c, out_ax_c = flip(z1, 1), flip(y2, 1), flip(out_ax, 1)
    *saved_far, first, normed1, inv_std1 = call_attend_forward(
        [], columns, True, meta, doc_lengths, tokens, saved_near[6], lines, (attn_far, attn_far_c)
    )
    slope_near, sums = call_ffn_forward(
        [], first, first, (ffn_in_weight, in_core), (ffn_out_weight, out_core)
    )
    own, other = 0, 1
    weights = assemble(
        "assemble",
        meta,
        None,
        [
            (joined, ((0, 0), (0, 2)), own),
            (joined_c, ((0, 0), (0, 2)), other),
            (z1, ((0, 1), (0, 3)), own),
            (z1_c, ((0, 1), (0, 3)), other),
            (y0, ((1, 0),), own),
            (y0_c, ((1, 0),), other),
            (y2, ((1, 2),), own),
            (y2_c, ((1, 2),), other),
        ],
    )
    in_far, out_bx, y1 = sync(
        "phase4", meta, [[PAIR_Z, in_x, in_z]], [out_bx, y1], [sums, weights, out_ax_c]
    )
    in_far_c, out_bx_c, y1_c = flip(in_far, 1), flip(out_bx, 1), flip(y1, 1)
    out_far = (out_ax, out_bx, out_ax_c, out_bx_c)
    slope_far, sums = call_ffn_forward([], first, sums, (in_far, in_far_c), out_far)
    last_parts = ((1, 1), (1, 3))
    weights = assemble(
        "assemble_last", meta, weights, [(y1, last_parts, own), (y1_c, last_parts, other)]
    )
    layer_out, *parts, grad_keep, grad_send = call_merging(
        n_adapters, meta, doc_lengths, sums, lines, out_grad, weights
    )
    done = {}
    attn_quarters = (attn, attn_core, attn_far, attn_far_c)
    saved = (saved_near[:3], saved_near[3:6], saved_far[:3], saved_far[3:6])

    def attention(deps, *quarters):
        for i in quarters:
            done["sum"], token = call_attend_backward(
                deps, columns, done["low"], done["sum"], saved[i], attn_quarters[i]
            )
        return token

    def first_work(deps):
        grad, low = call_merging_input(deps, sums, lines, *parts, weights)
        done["low"] = low
        (done["sum"],) = call_ffn_backward(
            [], low, grad, slope_near, (ffn_in_weight, in_core), (ffn_out_weight, out_core)
        )
        return done["sum"]

    def second_work(deps):
        done["sum"], done["low"] = call_ffn_backward(
            deps,
            done["low"],
            done["sum"],
            slope_far,
            (in_far, in_far_c),
            out_far,
            normed1,
            inv_std1,
            lines,
        )
        return attention([], 0)

    works = (
        first_work,
        second_work,
        lambda deps: attention(deps, 1),
        lambda deps: attention(deps, 2, 3),
    )
    summed = sum_gradients(hops, grad_keep, grad_send, n_adapters, works)
    return (layer_out, done["sum"], *summed)


def solution(mesh):
    split = P(AXES, None)
    in_specs = (
        split,
        P("dp", None),
        P(None, "tensor"),
        P("tensor", None),
        P(),
        P(),
        P(None, "tensor"),
        P("tensor", None),
        P(),
        P(),
        P(None, AXES, None),
        P(None, None, AXES),
        split,
        split,
        split,
        P(),
        P(),
        split,
    )
    out_specs = (split, split, split, split, split, P(), P(), P())
    return jax.shard_map(
        functools.partial(per_device, Hops(mesh)),
        mesh=mesh,
        in_specs=in_specs,
        out_specs=out_specs,
        check_vma=False,
    )
```

```python
import functools

import jax
import jax.numpy as jnp
from jax import lax
from jax.experimental import pallas as pl
from jax.experimental.pallas import tpu as pltpu
from jax.sharding import PartitionSpec as P

HEAD_DIM = 64
AXES = ("dp", "tensor")
ATTEND_MIB, FFN_MIB, MERGE_MIB = 16, 16, 22
LANES = 128
COST = 0.0
CHUNK = 256
EPS = 1e-12
BIG_NEGATIVE = -1e30
ROOT_HALF = 0.7071067811865476
ROOT_TAU = 0.3989422804014327
F32, BF16 = jnp.float32, jnp.bfloat16

CORE, ACROSS, PAIR_Y, PAIR_Z, DEPTH, ROW = range(6)
GAIN1, SHIFT1, GAIN2, SHIFT2, GAIN3, SHIFT3 = range(6)

SMEM = pl.BlockSpec(memory_space=pltpu.SMEM)
VMEM = pl.BlockSpec(memory_space=pltpu.VMEM)
ANY = pl.BlockSpec(memory_space=pl.ANY)
HBM = pl.BlockSpec(memory_space=pltpu.HBM)


def by_chunks(count, body):
    @pl.loop(0, count // CHUNK)
    def _(i):
        body(pl.ds(pl.multiple_of(i * CHUNK, CHUNK), CHUNK))


def line_of(lines, i):
    return lines[i : i + 1]


def dot(a, b):
    return lax.dot_general(a, b, (((1,), (0,)), ((), ())), preferred_element_type=F32)


def dot_last(a, b):
    return lax.dot_general(a, b, (((1,), (1,)), ((), ())), preferred_element_type=F32)


def dot_first(a, b):
    return lax.dot_general(a, b, (((0,), (0,)), ((), ())), preferred_element_type=F32)


def normalize(u):
    centered = u - jnp.mean(u, axis=-1, keepdims=True)
    inv_std = lax.rsqrt(jnp.mean(centered * centered, axis=-1, keepdims=True) + EPS)
    return centered * inv_std, inv_std


def norm_back(grad, normed, inv_std):
    return inv_std * (
        grad
        - jnp.mean(grad, axis=-1, keepdims=True)
        - normed * jnp.mean(grad * normed, axis=-1, keepdims=True)
    )


def gelu_both(u):
    half = 0.5 * (1.0 + lax.erf(u * ROOT_HALF))
    return u * half, half + u * jnp.exp(-0.5 * u * u) * ROOT_TAU


def segment_bias(meta_ref, lengths_ref, bias_ref):
    seq = bias_ref.shape[0]
    row = meta_ref[ROW]
    by_row = lax.broadcasted_iota(jnp.int32, (seq, 1), 0)
    by_lane = lax.broadcasted_iota(jnp.int32, (1, seq), 1)
    seg_row = jnp.zeros((seq, 1), jnp.int32)
    seg_lane = jnp.zeros((1, seq), jnp.int32)
    end = jnp.int32(0)
    for i in range(lengths_ref.shape[1]):
        end = end + lengths_ref[row, i]
        seg_row = seg_row + jnp.where(by_row >= end, 1, 0)
        seg_lane = seg_lane + jnp.where(by_lane >= end, 1, 0)
    bias_ref[...] = jnp.where(seg_row == seg_lane, 0.0, BIG_NEGATIVE).astype(F32)


def attend_forward(columns, last, meta, lengths, tokens, before, lines, weight0, weight1, *refs):
    saved, first_out, bias = refs[:6], refs[6], refs[-1]
    segment_bias(meta, lengths, bias)
    total = before[...].astype(F32)
    width = 3 * HEAD_DIM
    for quarter, weight in enumerate((weight0, weight1)):
        turned = dot_last(weight[:columns], tokens[...]).astype(BF16)
        turned_out, att_out, prob_out = saved[3 * quarter : 3 * quarter + 3]
        turned_out[...] = turned

        @pl.loop(0, columns // width)
        def _(head, turned_out=turned_out, att_out=att_out, prob_out=prob_out):
            base = pl.multiple_of(head * width, width)
            queries, keys, values = (
                turned_out[pl.ds(base + i * HEAD_DIM, HEAD_DIM)] for i in range(3)
            )
            scores = dot(keys.T, queries * BF16(HEAD_DIM**-0.5)) + bias[...]
            exponent = jnp.exp(scores - jnp.max(scores, axis=0, keepdims=True))
            prob = (exponent * (1.0 / jnp.sum(exponent, axis=0, keepdims=True))).astype(BF16)
            prob_out[head] = prob
            part = pl.ds(pl.multiple_of(head * HEAD_DIM, HEAD_DIM), HEAD_DIM)
            att_out[part] = dot(values, prob).astype(BF16)

        total = total + dot(att_out[...].T, weight[columns:])
    if not last:
        first_out[...] = total
        return
    normed_out, inv_out = refs[7:9]
    normed, inv_std = normalize(total)
    normed_out[...] = normed
    inv_out[...] = inv_std
    first_out[...] = normed * line_of(lines, GAIN1) + line_of(lines, SHIFT1)


def sds(shape, dtype):
    return jax.ShapeDtypeStruct(shape, dtype)


def params(mib):
    return pltpu.CompilerParams(vmem_limit_bytes=mib << 20)


def kernel(body, deps, mib, *, in_specs, **kw):
    n = len(deps)
    call = pl.pallas_call(
        lambda *refs: body(*refs[n:]),
        in_specs=[ANY] * n + in_specs,
        compiler_params=params(mib),
        **kw,
    )
    return functools.partial(call, *deps)


def sync(name, meta, joins, carries, deps):
    sides = [j[0] if isinstance(j[0], int) else None for j in joins]
    parts = [j[1:] if isinstance(j[0], int) else j for j in joins]
    flat = [p for j in parts for p in j]

    def body(meta_ref, *refs):
        refs = refs[len(carries) :]
        sources, outs = list(refs[: len(flat)]), refs[len(flat) : len(flat) + len(parts)]
        for side, join, out in zip(sides, parts, outs):
            row = 0
            for i, part in enumerate(join):
                size = part.shape[0]
                if side is not None:
                    n = len(join) // 2
                    row = pl.multiple_of(((meta_ref[side] ^ (i // n)) * n + i % n) * size, 16)
                out[pl.ds(row, size)] = sources.pop(0)[...]
                row = row + size

    joined = [sds((sum(p.shape[0] for p in j), *j[0].shape[1:]), j[0].dtype) for j in parts]
    n_deps = len(deps)
    out = kernel(
        body,
        deps,
        16,
        in_specs=[SMEM] + [ANY] * len(carries) + [VMEM] * len(flat),
        out_specs=[VMEM] * len(joined) + [ANY] * len(carries),
        out_shape=joined + [sds(c.shape, c.dtype) for c in carries],
        input_output_aliases={n_deps + 1 + i: len(joined) + i for i in range(len(carries))},
        cost_estimate=cost(0),
        name=name,
    )(meta, *carries, *flat)
    return out


def in_hbm(array):
    return pltpu.with_memory_space_constraint(array, pltpu.HBM)


def cost(us):
    return pl.CostEstimate(flops=int(us * 1.1e9 * COST), bytes_accessed=1024, transcendentals=0)


def call_attend_forward(deps, columns, last, meta, lengths, tokens, before, lines, quarters):
    seq, width = tokens.shape
    heads = columns // (3 * HEAD_DIM)
    inner = heads * HEAD_DIM
    square, narrow = sds((seq, width), F32), sds((seq, 1), F32)
    out_shape = [
        pltpu.HBM((columns, seq), BF16),
        pltpu.HBM((inner, seq), BF16),
        pltpu.HBM((heads, seq, seq), BF16),
    ] * 2 + [square] + [square, narrow] * last
    return kernel(
        functools.partial(attend_forward, columns, last),
        deps,
        ATTEND_MIB,
        in_specs=[SMEM, SMEM] + [VMEM] * 5,
        out_specs=[VMEM] * len(out_shape),
        out_shape=out_shape,
        scratch_shapes=[pltpu.VMEM((seq, seq), F32)],
        cost_estimate=cost(8),
        name="attend_forward",
    )(meta, lengths, tokens, before, lines, *quarters)


def ffn_forward(blocks, first, before, *refs):
    slope_out, sum_out = refs[-2:]

    def chunk(rows):
        low = first[rows].astype(BF16)
        total = before[rows]
        outs = list(refs[2:-2])
        for quarter in range(2):
            value, slope = gelu_both(dot(low, refs[quarter][...]))
            slope_out[quarter, rows] = slope.astype(BF16)
            value = value.astype(BF16)
            start = 0
            for _ in range(blocks):
                out = outs.pop(0)
                total = total + dot(value[:, start : start + out.shape[0]], out[...])
                start += out.shape[0]
        sum_out[rows] = total

    by_chunks(first.shape[0], chunk)


def call_ffn_forward(deps, first, before, in_quarters, out_quarters):
    seq, width = first.shape
    hidden = in_quarters[0].shape[1]
    return kernel(
        functools.partial(ffn_forward, len(out_quarters) // 2),
        deps,
        FFN_MIB,
        in_specs=[VMEM] * (4 + len(out_quarters)),
        out_specs=[VMEM] * 2,
        out_shape=[sds((2, seq, hidden), BF16), sds((seq, width), F32)],
        cost_estimate=cost(5),
        name="ffn_forward",
    )(first, before, *in_quarters, *out_quarters)


def assemble(name, meta, weights, tiles):
    n_mats = tiles[0][0].shape[0] // (2 * len(tiles[0][1]))
    rows, half = tiles[0][0].shape[1:]
    count = sum(2 * len(parts) for _, parts, _ in tiles)
    before = [] if weights is None else [weights]

    def body(meta_ref, *refs):
        refs = refs[len(before) :]
        out, sems = refs[-2:]
        copies = []
        for ref, (_, parts, core_rel) in zip(refs, tiles):
            side = pl.multiple_of((meta_ref[CORE] ^ core_rel) * half, LANES)
            for j, (y_rel, z_rel) in enumerate(parts):
                for x_rel in range(2):
                    chip = ((meta_ref[DEPTH] ^ z_rel) * 2 + (meta_ref[PAIR_Y] ^ y_rel)) * 2
                    chip = chip + (meta_ref[ACROSS] ^ x_rel)
                    first = pl.multiple_of(chip * rows, 16)
                    target = out.at[:, pl.ds(first, rows), pl.ds(side, half)]
                    source = ref.at[pl.ds((2 * j + x_rel) * n_mats, n_mats)]
                    copies.append(pltpu.make_async_copy(source, target, sems.at[len(copies)]))
        for copy in copies:
            copy.start()
        for copy in copies:
            copy.wait()

    return kernel(
        body,
        [],
        16,
        in_specs=[SMEM] + [ANY] * len(before) + [VMEM] * len(tiles),
        out_specs=ANY,
        out_shape=sds((n_mats, 2 * half, 2 * half), BF16),
        input_output_aliases={1: 0} if before else {},
        scratch_shapes=[pltpu.SemaphoreType.DMA((count,))],
        cost_estimate=cost(0),
        name=name,
    )(meta, *before, *(tile for tile, _, _ in tiles))


def split_lines(total):
    high = total.astype(BF16).astype(F32)
    return jnp.concatenate([high, total - high], axis=0)


def merging(n_adapters, meta, lengths, sums, lines, out_grad, matrices, *refs):
    layer_out, part_out, fquery_out, middle_out, keep_out, send_out = refs[:6]
    grads, sum_lines, states, probes, blends, values, fqueries = refs[6:]
    seq, width = sums.shape
    scale = width**-0.5
    down, up, query, key, value = (matrices.at[i] for i in range(5))
    gain2, shift2 = line_of(lines, GAIN2), line_of(lines, SHIFT2)
    gain3, shift3 = line_of(lines, GAIN3), line_of(lines, SHIFT3)
    spread = jnp.where(
        lax.broadcasted_iota(jnp.int32, (LANES, width), 0)
        == lax.broadcasted_iota(jnp.int32, (LANES, width), 1) // (width // n_adapters),
        1.0,
        0.0,
    ).astype(BF16)
    lane = lax.broadcasted_iota(jnp.int32, (1, LANES), 1)
    count = jnp.int32(0)
    for i in range(lengths.shape[1]):
        count = count + lengths[meta[ROW], i]
    sum_lines[...] = jnp.zeros_like(sum_lines)

    def by_adapter(terms):
        high = terms.astype(BF16)
        rest = (terms - high.astype(F32)).astype(BF16)
        return dot_last(high, spread) + dot_last(rest, spread)

    def chunk(rows):
        normed2, _ = normalize(sums[rows])
        second = normed2 * gain2 + shift2
        second_low = second.astype(BF16)
        states[rows] = second_low
        act, slope = (v.astype(BF16) for v in gelu_both(dot(second_low, down[...])))
        fquery = dot(second_low, query[...]).astype(BF16)
        fqueries[rows] = fquery
        probe = dot_last(fquery, key[...]).astype(BF16)
        probe_up = dot(probe, up[...])
        logits = scale * (
            jnp.sum(probe.astype(F32) * second, axis=1, keepdims=True)
            + by_adapter(act * probe_up)
        )
        logits = jnp.where(lane < n_adapters, logits, BIG_NEGATIVE)
        exponent = jnp.exp(logits - jnp.max(logits, axis=1, keepdims=True))
        mix = exponent / jnp.sum(exponent, axis=1, keepdims=True)
        mix_low = mix.astype(BF16)
        mix_sum = jnp.sum(mix_low.astype(F32), axis=1, keepdims=True)
        mix_wide = dot(mix_low, spread).astype(BF16)
        blended = second * mix_sum + dot_last((mix_wide * act).astype(BF16), up[...])
        blended = blended.astype(BF16)
        blends[rows] = blended
        normed3, inv_std3 = normalize(second + dot(blended, value[...]))
        layer_out[rows] = normed3 * gain3 + shift3

        token = rows.start + lax.broadcasted_iota(jnp.int32, (CHUNK, 1), 0)
        keep = jnp.where(token < count, 1.0, 0.0)
        cot = out_grad[rows].astype(F32) * keep
        mass = jnp.sum(mix * keep, axis=0, keepdims=True)
        mass = jnp.where(lane == n_adapters, jnp.sum(keep), mass)
        sum_lines[0:1] += jnp.sum(cot * normed3, axis=0, keepdims=True)
        sum_lines[1:2] += jnp.sum(cot, axis=0, keepdims=True)
        sum_lines[2:3, :LANES] += mass

        grad_pre = norm_back(cot * gain3, normed3, inv_std3)
        grad_proj = grad_pre.astype(BF16)
        values[rows] = grad_proj
        grad_blend = dot_last(grad_proj, value[...]).astype(BF16)
        blend_up = dot(grad_blend, up[...])
        grad_mix = jnp.sum(
            grad_blend.astype(F32) * second, axis=1, keepdims=True
        ) + by_adapter(act * blend_up)
        grad_logits = mix * (grad_mix - jnp.sum(grad_mix * mix, axis=1, keepdims=True))
        grad_logits = grad_logits.astype(BF16)
        logit_sum = jnp.sum(grad_logits.astype(F32), axis=1, keepdims=True)
        logit_wide = dot(grad_logits, spread).astype(BF16)
        grad_probe = second * logit_sum + dot_last((logit_wide * act).astype(BF16), up[...])
        grad_probe = (scale * grad_probe).astype(BF16)
        probes[rows] = grad_probe
        fquery_out[rows] = dot(grad_probe, key[...]).astype(BF16)
        grad_act = mix_wide.astype(F32) * blend_up + (scale * logit_wide.astype(F32)) * probe_up
        middle_out[rows] = (grad_act * slope.astype(F32)).astype(BF16)
        part_out[rows] = (
            grad_pre + grad_blend.astype(F32) * mix_sum + probe.astype(F32) * (scale * logit_sum)
        )

    by_chunks(seq, chunk)
    grads[0] = dot_first(states[...], fquery_out[...])
    grads[1] = dot_first(probes[...], fqueries[...])
    grads[2] = dot_first(blends[...], values[...])
    tail = split_lines(sum_lines[0:4])
    rows = width // 32

    @pl.loop(0, 16)
    def _(chip):
        z_rel = (chip // 4) ^ meta[DEPTH]
        y_rel = (chip // 2 % 2) ^ meta[PAIR_Y]
        x_rel = (chip % 2) ^ meta[ACROSS]
        for core_rel, out in ((0, keep_out), (1, send_out)):
            first = pl.multiple_of((chip * 2 + (meta[CORE] ^ core_rel)) * rows, 8)
            block = [grads[i, pl.ds(first, rows)] for i in range(3)] + [tail]
            out[x_rel, y_rel, z_rel] = jnp.concatenate(block, axis=0).astype(BF16)


def call_merging(n_adapters, meta, lengths, sums, lines, out_grad, matrices):
    seq, width = sums.shape
    block = 3 * width // 32 + 8
    return pl.pallas_call(
        functools.partial(merging, n_adapters),
        in_specs=[SMEM, SMEM] + [VMEM] * 4,
        out_specs=[VMEM] * 6,
        out_shape=[sds((seq, width), F32)] * 2
        + [sds((seq, width), BF16)] * 2
        + [sds((2, 2, 4, block, width), BF16)] * 2,
        scratch_shapes=[pltpu.VMEM((3, width, width), F32), pltpu.VMEM((8, width), F32)]
        + [pltpu.VMEM((seq, width), BF16)] * 5,
        compiler_params=params(MERGE_MIB),
        cost_estimate=cost(18),
        name="merging",
    )(meta, lengths, sums, lines, out_grad, matrices)


def merging_input(sums, lines, part, grad_fquery, grad_middle, matrices, grad_out, grad_low_out):
    def chunk(rows):
        normed, inv_std = normalize(sums[rows])
        grad = part[rows] + dot_last(grad_fquery[rows], matrices[2])
        grad = grad + dot_last(grad_middle[rows], matrices[0])
        grad = norm_back(grad * line_of(lines, GAIN2), normed, inv_std)
        grad_out[rows] = grad
        grad_low_out[rows] = grad.astype(BF16)

    by_chunks(part.shape[0], chunk)


def call_merging_input(deps, sums, lines, part, grad_fquery, grad_middle, matrices):
    return kernel(
        merging_input,
        deps,
        FFN_MIB,
        in_specs=[VMEM] * 6,
        out_specs=[VMEM] * 2,
        out_shape=[sds(part.shape, F32), sds(part.shape, BF16)],
        cost_estimate=cost(3),
        name="merging_input",
    )(sums, lines, part, grad_fquery, grad_middle, matrices)


def ffn_backward(last, blocks, grad_low, before, slope, in0, in1, *refs):
    all_outs, refs = refs[: 2 * blocks], refs[2 * blocks :]

    def chunk(rows):
        low = grad_low[rows]
        total = before[rows]
        outs = list(all_outs)
        for quarter, into in enumerate((in0, in1)):
            grad_act = [dot_last(low, outs.pop(0)[...]) for _ in range(blocks)]
            grad_act = grad_act[0] if blocks == 1 else jnp.concatenate(grad_act, axis=1)
            grad_pre = (grad_act * slope[quarter, rows].astype(F32)).astype(BF16)
            total = total + dot_last(grad_pre, into[...])
        if not last:
            refs[0][rows] = total
            return
        normed1, inv_std1, lines, grad_out, grad_low_out = refs
        grad = norm_back(total * line_of(lines, GAIN1), normed1[rows], inv_std1[rows])
        grad_out[rows] = grad
        grad_low_out[rows] = grad.astype(BF16)

    by_chunks(before.shape[0], chunk)


def call_ffn_backward(deps, grad_low, before, slope, in_quarters, out_quarters, *for_norm):
    seq, width = before.shape
    last = bool(for_norm)
    return kernel(
        functools.partial(ffn_backward, last, len(out_quarters) // 2),
        deps,
        FFN_MIB,
        in_specs=[VMEM] * (5 + len(out_quarters) + len(for_norm)),
        out_specs=[VMEM] * (1 + last),
        out_shape=[sds((seq, width), F32)] + [sds((seq, width), BF16)] * last,
        cost_estimate=cost(5),
        name="ffn_backward",
    )(grad_low, before, slope, *in_quarters, *out_quarters, *for_norm)


def attend_backward(
    columns, grad_low, before, turned_ref, att_ref, prob_ref, weight, input_grad, token, grad_turned, grad_att
):
    width = 3 * HEAD_DIM
    root = HEAD_DIM**-0.5
    grad_att[...] = dot_last(weight[columns:], grad_low[...]).astype(BF16)

    @pl.loop(0, columns // width)
    def _(head):
        base = pl.multiple_of(head * width, width)
        places = [pl.ds(base + i * HEAD_DIM, HEAD_DIM) for i in range(3)]
        queries, keys, values = (turned_ref[place] for place in places)
        part = pl.ds(pl.multiple_of(head * HEAD_DIM, HEAD_DIM), HEAD_DIM)
        grad = grad_att[part]
        prob = prob_ref[head]
        row_dot = jnp.sum(grad.astype(F32) * att_ref[part].astype(F32), axis=0, keepdims=True)
        grad_scores = (prob.astype(F32) * (dot(values.T, grad) - row_dot)).astype(BF16)
        grad_turned[places[0]] = (dot(keys, grad_scores) * root).astype(BF16)
        grad_turned[places[1]] = (dot_last(queries, grad_scores) * root).astype(BF16)
        grad_turned[places[2]] = dot_last(grad, prob).astype(BF16)

    input_grad[...] = before[...] + dot(grad_turned[...].T, weight[:columns])
    token[...] = jnp.zeros_like(token)


def call_attend_backward(deps, columns, grad_low, before, saved, quarter):
    seq, width = before.shape
    inner = columns // 3
    return kernel(
        functools.partial(attend_backward, columns),
        deps,
        ATTEND_MIB,
        in_specs=[VMEM] * 6,
        out_specs=[VMEM] * 2,
        out_shape=[sds((seq, width), F32), sds((8, LANES), F32)],
        scratch_shapes=[pltpu.VMEM((columns, seq), BF16), pltpu.VMEM((inner, seq), BF16)],
        cost_estimate=cost(8),
        name="attend_backward",
    )(grad_low, before, *saved, quarter)


def prepare(meta, down, up, query, key, value, g1, s1, g2, s2, g3, s3, keep, send, lines, shard):
    n_adapters, _, rank = down.shape
    for i in range(n_adapters):
        shard[0, :, i * rank : (i + 1) * rank] = down[i].astype(F32)
        shard[1, :, i * rank : (i + 1) * rank] = up[i].astype(F32)
    for i, ref in enumerate((query, key, value)):
        shard[2 + i] = ref[...].astype(F32)
    half = keep.shape[2]
    mine = pl.multiple_of(meta[CORE] * half, LANES)
    other = pl.multiple_of((1 - meta[CORE]) * half, LANES)
    keep[...] = shard[:, :, pl.ds(mine, half)].astype(BF16)
    send[...] = shard[:, :, pl.ds(other, half)].astype(BF16)
    for i, ref in enumerate((g1, s1, g2, s2, g3, s3)):
        lines[i : i + 1] = ref[...].reshape(1, -1)
    lines[6:8] = jnp.zeros((2, lines.shape[1]), F32)


def call_prepare(meta, down, up, query, key, value, *vectors):
    rows, width = query.shape
    half = sds((5, rows, width // 2), BF16)
    return pl.pallas_call(
        prepare,
        in_specs=[SMEM] + [VMEM] * 11,
        out_specs=[VMEM] * 3,
        out_shape=[half, half, sds((8, width), F32)],
        scratch_shapes=[pltpu.VMEM((5, rows, width), F32)],
        compiler_params=params(16),
        cost_estimate=cost(1),
        name="prepare",
    )(meta, *(in_hbm(a) for a in (down, up, query, key, value, *vectors)))


def prepare_frozen(meta, qkv_turned, attn_out, into, attn, attn_half, in_half):
    columns = qkv_turned.shape[0]
    attn[:columns] = qkv_turned[...]
    attn[columns:] = attn_out[...]
    for entry, whole, half in ((PAIR_Y, attn, attn_half), (PAIR_Z, into, in_half)):
        rows = half.shape[0]
        half[...] = whole[pl.ds(pl.multiple_of(meta[entry] * rows, 16), rows)]


def call_prepare_frozen(meta, qkv_turned, attn_out, into):
    rows, width = qkv_turned.shape[0] + attn_out.shape[0], attn_out.shape[1]
    return kernel(
        prepare_frozen,
        [],
        16,
        in_specs=[SMEM] + [VMEM] * 3,
        out_specs=[VMEM] * 3,
        out_shape=[
            sds((rows, width), BF16),
            sds((rows // 2, width), BF16),
            sds((into.shape[0] // 2, into.shape[1]), BF16),
        ],
        cost_estimate=cost(1),
        name="prepare_frozen",
    )(meta, *(in_hbm(a) for a in (qkv_turned, attn_out, into)))


def chip_tile(meta, keep, got, tile):
    mine, other = keep[...].astype(F32), got[...].astype(F32)
    lower = jnp.where(meta[CORE] == 0, mine, other)
    upper = jnp.where(meta[CORE] == 0, other, mine)
    tile[...] = jnp.concatenate([lower, upper], axis=1).astype(BF16)


def call_chip_tile(meta, keep, got):
    n_mats, rows, half = keep.shape
    return kernel(
        chip_tile,
        [],
        16,
        in_specs=[SMEM] + [VMEM] * 2,
        out_specs=VMEM,
        out_shape=sds((n_mats, 2 * rows, half), BF16),
        cost_estimate=cost(1),
        name="chip_tile",
    )(meta, keep, got)


def add_blocks(*blocks):
    total = functools.reduce(jnp.add, (b.astype(F32) for b in blocks))
    tail = total[-8:-4] + total[-4:]
    return jnp.concatenate([total[:-8], split_lines(tail)], axis=0)


def sum_cores(keep, got, p_keep, p_send, q_keep, q_send):
    half = p_keep.shape[-1]
    for x in range(2):
        for y in range(2):

            @pl.loop(0, 4)
            def _(z, x=x, y=y):
                total = add_blocks(keep[x, y, z], got[x, y, z]).astype(BF16)
                (p_send if x else p_keep)[y, z] = total[:, :half]
                (q_send if y else q_keep)[x, z] = total[:, half:]


def sum_first(p_keep, p_got, q_keep, q_got, p2_keep, p2_send, q2_keep, q2_send):
    @pl.loop(0, 4)
    def _(z):
        for out, index in ((p2_keep, 0), (p2_send, 1)):
            out[z] = add_blocks(p_keep[index, z], p_got[index, z]).astype(BF16)
        for out, index in ((q2_keep, 0), (q2_send, 1)):
            out[z] = add_blocks(q_keep[index, z], q_got[index, z]).astype(BF16)


def sum_second(p_keep, p_got, q_keep, q_got, *outs):
    half = p_keep.shape[-1]
    for z in range(4):
        outs[z][:, :half] = add_blocks(p_keep[z], p_got[z]).astype(BF16)
        outs[z][:, half:] = add_blocks(q_keep[z], q_got[z]).astype(BF16)


def sum_last(n_adapters, keep, got1, got2, got3, query, key, value, gain, bias, mass):
    total = add_blocks(keep[...], got1[...], got2[...], got3[...])
    rows = query.shape[0]
    for i, out in enumerate((query, key, value)):
        out[...] = total[i * rows : (i + 1) * rows]
    lines = total[-8:-4] + total[-4:]
    gain[...] = lines[0]
    bias[...] = lines[1]
    mass[...] = lines[2, :n_adapters] / lines[2:3, n_adapters : n_adapters + 1].reshape(1)


def small_call(body, name, out_shape, dep, *operands):
    return kernel(
        body,
        (dep,),
        16,
        in_specs=[VMEM] * len(operands),
        out_specs=[VMEM] * len(out_shape),
        out_shape=out_shape,
        cost_estimate=cost(1),
        name=name,
    )(*operands)


def sum_gradients(hops, keep, send, n_adapters, works):
    block, width = keep.shape[3:]
    half = width // 2
    pair = [sds((2, 4, block, half), BF16)] * 4
    single = [sds((4, block, half), BF16)] * 4
    got = hops.flip(send, 1)
    dep = works[0](())
    pk, ps, qk, qs = small_call(sum_cores, "sum_cores", pair, dep, keep, got)
    pg, qg = hops.flip(ps, ALONG_X), hops.flip(qs, ALONG_Y)
    dep = works[1]([pk])
    pk, ps, qk, qs = small_call(sum_first, "sum_first", single, dep, pk, pg, qk, qg)
    pg, qg = hops.flip(ps, ALONG_Y), hops.flip(qs, ALONG_X)
    dep = works[2]([pk])
    parts = small_call(
        sum_second, "sum_second", [sds((block, width), BF16)] * 4, dep, pk, pg, qk, qg
    )
    got = [hops.flip(part, z * ALONG_Z) for z, part in enumerate(parts) if z]
    dep = works[3]([parts[0]])
    rows = (block - 8) // 3
    outs = [sds((rows, width), F32)] * 3 + [sds((width,), F32)] * 2 + [sds((n_adapters,), F32)]
    last = functools.partial(sum_last, n_adapters)
    return small_call(last, "sum_last", outs, dep, parts[0], *got)


ALONG_X, ALONG_Y, ALONG_Z = 2, 4, 8


class Hops:
    def __init__(self, mesh):
        self.count = mesh.size
        self.tiled = mesh.shape["dp"] == 8 and mesh.shape["tensor"] == 4

    def flip(self, array, bits):
        return lax.ppermute(array, AXES, [(i, i ^ bits) for i in range(self.count)])


def half_of(block, parity):
    half = block.shape[0] // 2
    return lax.dynamic_slice_in_dim(block, parity * half, half, 0)


def plain_schedule(
    meta, doc_lengths, tokens, out_grad, lines, columns, n_adapters, attn, into, out, shard
):
    attn, into, out = (lax.all_gather(w, "tensor", axis=0) for w in (attn, into, out))
    weights = lax.all_gather(shard, AXES, axis=1, tiled=True)
    pairs = [slice(i, i + 2) for i in range(0, attn.shape[0], 2)]
    before, saved, slopes = tokens, [], []
    for pair in pairs:
        last = pair is pairs[-1]
        results = call_attend_forward(
            [], columns, last, meta, doc_lengths, tokens, before, lines, tuple(attn[pair])
        )
        saved += [results[:3], results[3:6]]
        before = results[6]
    first, normed1, inv_std1 = results[6:]
    sums = first
    for pair in pairs:
        slope, sums = call_ffn_forward([], first, sums, tuple(into[pair]), tuple(out[pair]))
        slopes.append(slope)
    layer_out, *parts, keep, send = call_merging(
        n_adapters, meta, doc_lengths, sums, lines, out_grad, weights
    )
    total, low = call_merging_input([], sums, lines, *parts, weights)
    width = tokens.shape[1]
    blocks = jnp.transpose(jnp.stack([keep, send]), (3, 2, 1, 0, 4, 5)).reshape(32, -1, width)
    squares = blocks[:, :-8].reshape(32, 3, width // 32, width)
    squares = jnp.transpose(squares, (1, 0, 2, 3)).reshape(3, width, width).astype(F32)
    squares = lax.psum_scatter(squares, AXES, scatter_dimension=1, tiled=True)
    tail = blocks[0, -8:].astype(F32)
    totals = lax.psum(tail[:4] + tail[4:], AXES)
    for pair, slope in zip(pairs, slopes):
        for_norm = (normed1, inv_std1, lines) if pair is pairs[-1] else ()
        total, *rest = call_ffn_backward(
            [], low, total, slope, tuple(into[pair]), tuple(out[pair]), *for_norm
        )
    (low,) = rest
    for quarter, kept in zip(attn, saved):
        total, _ = call_attend_backward([], columns, low, total, kept, quarter)
    mass = totals[2, :n_adapters] / totals[2, n_adapters]
    return (layer_out, total, squares[0], squares[1], squares[2], totals[0], totals[1], mass)


def per_device(
    hops,
    tokens,
    doc_lengths,
    qkv_weight,
    attn_out_weight,
    norm1_gain,
    norm1_bias,
    ffn_in_weight,
    ffn_out_weight,
    norm2_gain,
    norm2_bias,
    adapter_down,
    adapter_up,
    merging_query,
    merging_key,
    merging_value,
    merging_gain,
    merging_bias,
    out_grad,
):
    n_adapters, rows, rank = adapter_down.shape
    columns = qkv_weight.shape[1]
    tensor, dp = lax.axis_index("tensor"), lax.axis_index("dp")
    pair_y, pair_z = dp % 2, dp // 2 % 2
    meta = jnp.stack([tensor % 2, tensor // 2, pair_y, pair_z, dp // 2, tensor]).astype(jnp.int32)
    flip = hops.flip
    if not hops.tiled:
        meta = meta * (jnp.arange(meta.shape[0]) == ROW)

    keep, send, lines = call_prepare(
        meta,
        adapter_down,
        jnp.transpose(adapter_up, (0, 2, 1)),
        merging_query,
        merging_key,
        merging_value,
        norm1_gain,
        norm1_bias,
        norm2_gain,
        norm2_bias,
        merging_gain,
        merging_bias,
    )
    attn, attn_half, in_half = call_prepare_frozen(
        meta, qkv_weight.T, attn_out_weight, ffn_in_weight
    )
    if not hops.tiled:
        shard = jnp.concatenate([keep, send], axis=2)
        return plain_schedule(
            meta, doc_lengths, tokens, out_grad, lines, columns, n_adapters, attn, ffn_in_weight, ffn_out_weight, shard
        )
    cut = ffn_out_weight.shape[0] // 3
    out_a, out_b = ffn_out_weight[:cut], ffn_out_weight[cut:]
    attn_core = flip(attn, 1)
    in_core, out_core = flip(ffn_in_weight, 1), flip(ffn_out_weight, 1)
    tile = call_chip_tile(meta, keep, flip(send, 1))
    tile_x = flip(tile, ALONG_X)
    both, attn_half = sync("phase1", meta, [[tile, tile_x]], [attn_half], [attn_core])
    z2, attn_x, y0 = flip(both, 2 * ALONG_Z), flip(attn_half, ALONG_X), flip(both, ALONG_Y)
    saved_near = call_attend_forward(
        [both], columns, False, meta, doc_lengths, tokens, tokens, lines, (attn, attn_core)
    )
    joined, in_half, out_a, attn_x, y0, z2 = sync(
        "phase2", meta, [[both, z2]], [in_half, out_a, attn_x, y0, z2], [saved_near[6]]
    )
    attn_y, z1, in_x = flip(attn_x, ALONG_Y), flip(joined, ALONG_Z), flip(in_half, ALONG_X)
    y2, out_ax = flip(z2, ALONG_Y), flip(out_a, ALONG_X)
    joined_c, y0_c = flip(joined, 1), flip(y0, 1)
    attn_far, in_x, out_ax, out_b, z1, y2 = sync(
        "phase3",
        meta,
        [[PAIR_Y, attn_x, attn_y]],
        [in_x, out_ax, out_b, z1, y2],
        [in_core, out_core, joined_c, y0_c],
    )
    attn_far_c = flip(attn_far, 1)
    y1, out_bx, in_z = flip(z1, ALONG_Y), flip(out_b, ALONG_X), flip(in_x, ALONG_Z)
    z1_c, y2_c, out_ax_c = flip(z1, 1), flip(y2, 1), flip(out_ax, 1)
    *saved_far, first, normed1, inv_std1 = call_attend_forward(
        [], columns, True, meta, doc_lengths, tokens, saved_near[6], lines, (attn_far, attn_far_c)
    )
    slope_near, sums = call_ffn_forward(
        [], first, first, (ffn_in_weight, in_core), (ffn_out_weight, out_core)
    )
    own, other = 0, 1
    weights = assemble(
        "assemble",
        meta,
        None,
        [
            (joined, ((0, 0), (0, 2)), own),
            (joined_c, ((0, 0), (0, 2)), other),
            (z1, ((0, 1), (0, 3)), own),
            (z1_c, ((0, 1), (0, 3)), other),
            (y0, ((1, 0),), own),
            (y0_c, ((1, 0),), other),
            (y2, ((1, 2),), own),
            (y2_c, ((1, 2),), other),
        ],
    )
    in_far, out_bx, y1 = sync(
        "phase4", meta, [[PAIR_Z, in_x, in_z]], [out_bx, y1], [sums, weights, out_ax_c]
    )
    in_far_c, out_bx_c, y1_c = flip(in_far, 1), flip(out_bx, 1), flip(y1, 1)
    out_far = (out_ax, out_bx, out_ax_c, out_bx_c)
    slope_far, sums = call_ffn_forward([], first, sums, (in_far, in_far_c), out_far)
    last_parts = ((1, 1), (1, 3))
    weights = assemble(
        "assemble_last", meta, weights, [(y1, last_parts, own), (y1_c, last_parts, other)]
    )
    layer_out, *parts, grad_keep, grad_send = call_merging(
        n_adapters, meta, doc_lengths, sums, lines, out_grad, weights
    )
    done = {}
    attn_quarters = (attn, attn_core, attn_far, attn_far_c)
    saved = (saved_near[:3], saved_near[3:6], saved_far[:3], saved_far[3:6])

    def attention(deps, *quarters):
        for i in quarters:
            done["sum"], token = call_attend_backward(
                deps, columns, done["low"], done["sum"], saved[i], attn_quarters[i]
            )
        return token

    def first_work(deps):
        grad, low = call_merging_input(deps, sums, lines, *parts, weights)
        done["low"] = low
        (done["sum"],) = call_ffn_backward(
            [], low, grad, slope_near, (ffn_in_weight, in_core), (ffn_out_weight, out_core)
        )
        return done["sum"]

    def second_work(deps):
        done["sum"], done["low"] = call_ffn_backward(
            deps,
            done["low"],
            done["sum"],
            slope_far,
            (in_far, in_far_c),
            out_far,
            normed1,
            inv_std1,
            lines,
        )
        return attention([], 0)

    works = (
        first_work,
        second_work,
        lambda deps: attention(deps, 1),
        lambda deps: attention(deps, 2, 3),
    )
    summed = sum_gradients(hops, grad_keep, grad_send, n_adapters, works)
    return (layer_out, done["sum"], *summed)


def solution(mesh):
    split = P(AXES, None)
    in_specs = (
        split,
        P("dp", None),
        P(None, "tensor"),
        P("tensor", None),
        P(),
        P(),
        P(None, "tensor"),
        P("tensor", None),
        P(),
        P(),
        P(None, AXES, None),
        P(None, None, AXES),
        split,
        split,
        split,
        P(),
        P(),
        split,
    )
    out_specs = (split, split, split, split, split, P(), P(), P())
    return jax.shard_map(
        functools.partial(per_device, Hops(mesh)),
        mesh=mesh,
        in_specs=in_specs,
        out_specs=out_specs,
        check_vma=False,
    )
```

```python
import functools

import jax
import jax.numpy as jnp
from jax import lax
from jax.experimental import pallas as pl
from jax.experimental.pallas import tpu as pltpu
from jax.sharding import PartitionSpec as P

HEAD_DIM = 64
AXES = ("dp", "tensor")
ATTEND_MIB, FFN_MIB, MERGE_MIB = 16, 16, 22
LANES = 128
COST = 0.0
CHUNK = 256
EPS = 1e-12
BIG_NEGATIVE = -1e30
ROOT_HALF = 0.7071067811865476
ROOT_TAU = 0.3989422804014327
F32, BF16 = jnp.float32, jnp.bfloat16

CORE, ACROSS, PAIR_Y, PAIR_Z, DEPTH, ROW = range(6)
GAIN1, SHIFT1, GAIN2, SHIFT2, GAIN3, SHIFT3 = range(6)

SMEM = pl.BlockSpec(memory_space=pltpu.SMEM)
VMEM = pl.BlockSpec(memory_space=pltpu.VMEM)
ANY = pl.BlockSpec(memory_space=pl.ANY)
HBM = pl.BlockSpec(memory_space=pltpu.HBM)


def by_chunks(count, body):
    @pl.loop(0, count // CHUNK)
    def _(i):
        body(pl.ds(pl.multiple_of(i * CHUNK, CHUNK), CHUNK))


def line_of(lines, i):
    return lines[i : i + 1]


def dot(a, b):
    return lax.dot_general(a, b, (((1,), (0,)), ((), ())), preferred_element_type=F32)


def dot_last(a, b):
    return lax.dot_general(a, b, (((1,), (1,)), ((), ())), preferred_element_type=F32)


def dot_first(a, b):
    return lax.dot_general(a, b, (((0,), (0,)), ((), ())), preferred_element_type=F32)


def normalize(u):
    centered = u - jnp.mean(u, axis=-1, keepdims=True)
    inv_std = lax.rsqrt(jnp.mean(centered * centered, axis=-1, keepdims=True) + EPS)
    return centered * inv_std, inv_std


def norm_back(grad, normed, inv_std):
    return inv_std * (
        grad
        - jnp.mean(grad, axis=-1, keepdims=True)
        - normed * jnp.mean(grad * normed, axis=-1, keepdims=True)
    )


def gelu_both(u):
    half = 0.5 * (1.0 + lax.erf(u * ROOT_HALF))
    return u * half, half + u * jnp.exp(-0.5 * u * u) * ROOT_TAU


def segment_bias(meta_ref, lengths_ref, bias_ref):
    seq = bias_ref.shape[0]
    row = meta_ref[ROW]
    by_row = lax.broadcasted_iota(jnp.int32, (seq, 1), 0)
    by_lane = lax.broadcasted_iota(jnp.int32, (1, seq), 1)
    seg_row = jnp.zeros((seq, 1), jnp.int32)
    seg_lane = jnp.zeros((1, seq), jnp.int32)
    end = jnp.int32(0)
    for i in range(lengths_ref.shape[1]):
        end = end + lengths_ref[row, i]
        seg_row = seg_row + jnp.where(by_row >= end, 1, 0)
        seg_lane = seg_lane + jnp.where(by_lane >= end, 1, 0)
    bias_ref[...] = jnp.where(seg_row == seg_lane, 0.0, BIG_NEGATIVE).astype(F32)


def attend_forward(columns, last, meta, lengths, tokens, before, lines, weight0, weight1, *refs):
    saved, first_out, bias = refs[:6], refs[6], refs[-1]
    segment_bias(meta, lengths, bias)
    total = before[...].astype(F32)
    width = 3 * HEAD_DIM
    for quarter, weight in enumerate((weight0, weight1)):
        turned = dot_last(weight[:columns], tokens[...]).astype(BF16)
        turned_out, att_out, prob_out = saved[3 * quarter : 3 * quarter + 3]
        turned_out[...] = turned

        @pl.loop(0, columns // width)
        def _(head, turned_out=turned_out, att_out=att_out, prob_out=prob_out):
            base = pl.multiple_of(head * width, width)
            queries, keys, values = (
                turned_out[pl.ds(base + i * HEAD_DIM, HEAD_DIM)] for i in range(3)
            )
            scores = dot(keys.T, queries * BF16(HEAD_DIM**-0.5)) + bias[...]
            exponent = jnp.exp(scores - jnp.max(scores, axis=0, keepdims=True))
            prob = (exponent * (1.0 / jnp.sum(exponent, axis=0, keepdims=True))).astype(BF16)
            prob_out[head] = prob
            part = pl.ds(pl.multiple_of(head * HEAD_DIM, HEAD_DIM), HEAD_DIM)
            att_out[part] = dot(values, prob).astype(BF16)

        total = total + dot(att_out[...].T, weight[columns:])
    if not last:
        first_out[...] = total
        return
    normed_out, inv_out = refs[7:9]
    normed, inv_std = normalize(total)
    normed_out[...] = normed
    inv_out[...] = inv_std
    first_out[...] = normed * line_of(lines, GAIN1) + line_of(lines, SHIFT1)


def sds(shape, dtype):
    return jax.ShapeDtypeStruct(shape, dtype)


def params(mib):
    return pltpu.CompilerParams(vmem_limit_bytes=mib << 20)


def kernel(body, deps, mib, *, in_specs, **kw):
    n = len(deps)
    call = pl.pallas_call(
        lambda *refs: body(*refs[n:]),
        in_specs=[ANY] * n + in_specs,
        compiler_params=params(mib),
        **kw,
    )
    return functools.partial(call, *deps)


def sync(name, meta, joins, carries, deps):
    sides = [j[0] if isinstance(j[0], int) else None for j in joins]
    parts = [j[1:] if isinstance(j[0], int) else j for j in joins]
    parts = [[p if isinstance(p, tuple) else (p, 0, p.shape[0]) for p in j] for j in parts]
    flat = [p[0] for j in parts for p in j]

    def body(meta_ref, *refs):
        refs = refs[len(carries) :]
        sources, outs = list(refs[: len(flat)]), refs[len(flat) : len(flat) + len(parts)]
        for side, join, out in zip(sides, parts, outs):
            row = 0
            for i, (_, start, size) in enumerate(join):
                if side is not None:
                    n = len(join) // 2
                    row = pl.multiple_of(((meta_ref[side] ^ (i // n)) * n + i % n) * size, 16)
                out[pl.ds(row, size)] = sources.pop(0)[start : start + size]
                row = row + size

    joined = [sds((sum(p[2] for p in j), *j[0][0].shape[1:]), j[0][0].dtype) for j in parts]
    n_deps = len(deps)
    out = kernel(
        body,
        deps,
        16,
        in_specs=[SMEM] + [ANY] * len(carries) + [VMEM] * len(flat),
        out_specs=[VMEM] * len(joined) + [ANY] * len(carries),
        out_shape=joined + [sds(c.shape, c.dtype) for c in carries],
        input_output_aliases={n_deps + 1 + i: len(joined) + i for i in range(len(carries))},
        cost_estimate=cost(0),
        name=name,
    )(meta, *carries, *flat)
    return out


def in_hbm(array):
    return pltpu.with_memory_space_constraint(array, pltpu.HBM)


def cost(us):
    return pl.CostEstimate(flops=int(us * 1.1e9 * COST), bytes_accessed=1024, transcendentals=0)


def call_attend_forward(deps, columns, last, meta, lengths, tokens, before, lines, quarters):
    seq, width = tokens.shape
    heads = columns // (3 * HEAD_DIM)
    inner = heads * HEAD_DIM
    square, narrow = sds((seq, width), F32), sds((seq, 1), F32)
    out_shape = [
        pltpu.HBM((columns, seq), BF16),
        pltpu.HBM((inner, seq), BF16),
        pltpu.HBM((heads, seq, seq), BF16),
    ] * 2 + [square] + [square, narrow] * last
    return kernel(
        functools.partial(attend_forward, columns, last),
        deps,
        ATTEND_MIB,
        in_specs=[SMEM, SMEM] + [VMEM] * 5,
        out_specs=[VMEM] * len(out_shape),
        out_shape=out_shape,
        scratch_shapes=[pltpu.VMEM((seq, seq), F32)],
        cost_estimate=cost(8),
        name="attend_forward",
    )(meta, lengths, tokens, before, lines, *quarters)


def ffn_forward(quarters, blocks, first, before, *refs):
    slope_out, sum_out = refs[-2:]

    def chunk(rows):
        low = first[rows].astype(BF16)
        total = before[rows]
        outs = list(refs[quarters:-2])
        for quarter in range(quarters):
            value, slope = gelu_both(dot(low, refs[quarter][...]))
            slope_out[quarter, rows] = slope.astype(BF16)
            value = value.astype(BF16)
            start = 0
            for _ in range(blocks):
                out = outs.pop(0)
                total = total + dot(value[:, start : start + out.shape[0]], out[...])
                start += out.shape[0]
        sum_out[rows] = total

    by_chunks(first.shape[0], chunk)


def call_ffn_forward(deps, first, before, in_quarters, out_quarters):
    seq, width = first.shape
    hidden = in_quarters[0].shape[1]
    quarters = len(in_quarters)
    return kernel(
        functools.partial(ffn_forward, quarters, len(out_quarters) // quarters),
        deps,
        FFN_MIB,
        in_specs=[VMEM] * (2 + quarters + len(out_quarters)),
        out_specs=[VMEM] * 2,
        out_shape=[sds((quarters, seq, hidden), BF16), sds((seq, width), F32)],
        cost_estimate=cost(5),
        name="ffn_forward",
    )(first, before, *in_quarters, *out_quarters)


def assemble(name, deps, meta, weights, tiles):
    n_mats = tiles[0][0].shape[0] // (2 * len(tiles[0][1]))
    rows, half = tiles[0][0].shape[1:]
    count = sum(2 * len(parts) for _, parts, _ in tiles)
    before = [] if weights is None else [weights]

    def body(meta_ref, *refs):
        refs = refs[len(before) :]
        out, sems = refs[-2:]
        copies = []
        for ref, (_, parts, core_rel) in zip(refs, tiles):
            side = pl.multiple_of((meta_ref[CORE] ^ core_rel) * half, LANES)
            for j, (y_rel, z_rel) in enumerate(parts):
                for x_rel in range(2):
                    chip = ((meta_ref[DEPTH] ^ z_rel) * 2 + (meta_ref[PAIR_Y] ^ y_rel)) * 2
                    chip = chip + (meta_ref[ACROSS] ^ x_rel)
                    first = pl.multiple_of(chip * rows, 16)
                    target = out.at[:, pl.ds(first, rows), pl.ds(side, half)]
                    source = ref.at[pl.ds((2 * j + x_rel) * n_mats, n_mats)]
                    copies.append(pltpu.make_async_copy(source, target, sems.at[len(copies)]))
        for copy in copies:
            copy.start()
        for copy in copies:
            copy.wait()

    return kernel(
        body,
        deps,
        16,
        in_specs=[SMEM] + [ANY] * len(before) + [VMEM] * len(tiles),
        out_specs=ANY,
        out_shape=sds((n_mats, 2 * half, 2 * half), BF16),
        input_output_aliases={len(deps) + 1: 0} if before else {},
        scratch_shapes=[pltpu.SemaphoreType.DMA((count,))],
        cost_estimate=cost(0),
        name=name,
    )(meta, *before, *(tile for tile, _, _ in tiles))


def split_lines(total):
    high = total.astype(BF16).astype(F32)
    return jnp.concatenate([high, total - high], axis=0)


def merging(n_adapters, meta, lengths, sums, lines, out_grad, matrices, *refs):
    layer_out, part_out, fquery_out, middle_out, keep_out, send_out = refs[:6]
    grads, sum_lines, states, probes, blends, values, fqueries = refs[6:]
    seq, width = sums.shape
    scale = width**-0.5
    down, up, query, key, value = (matrices.at[i] for i in range(5))
    gain2, shift2 = line_of(lines, GAIN2), line_of(lines, SHIFT2)
    gain3, shift3 = line_of(lines, GAIN3), line_of(lines, SHIFT3)
    spread = jnp.where(
        lax.broadcasted_iota(jnp.int32, (LANES, width), 0)
        == lax.broadcasted_iota(jnp.int32, (LANES, width), 1) // (width // n_adapters),
        1.0,
        0.0,
    ).astype(BF16)
    lane = lax.broadcasted_iota(jnp.int32, (1, LANES), 1)
    count = jnp.int32(0)
    for i in range(lengths.shape[1]):
        count = count + lengths[meta[ROW], i]
    sum_lines[...] = jnp.zeros_like(sum_lines)

    def by_adapter(terms):
        high = terms.astype(BF16)
        rest = (terms - high.astype(F32)).astype(BF16)
        return dot_last(high, spread) + dot_last(rest, spread)

    def chunk(rows):
        normed2, _ = normalize(sums[rows])
        second = normed2 * gain2 + shift2
        second_low = second.astype(BF16)
        states[rows] = second_low
        act, slope = (v.astype(BF16) for v in gelu_both(dot(second_low, down[...])))
        fquery = dot(second_low, query[...]).astype(BF16)
        fqueries[rows] = fquery
        probe = dot_last(fquery, key[...]).astype(BF16)
        probe_up = dot(probe, up[...])
        logits = scale * (
            jnp.sum(probe.astype(F32) * second, axis=1, keepdims=True)
            + by_adapter(act * probe_up)
        )
        logits = jnp.where(lane < n_adapters, logits, BIG_NEGATIVE)
        exponent = jnp.exp(logits - jnp.max(logits, axis=1, keepdims=True))
        mix = exponent / jnp.sum(exponent, axis=1, keepdims=True)
        mix_low = mix.astype(BF16)
        mix_sum = jnp.sum(mix_low.astype(F32), axis=1, keepdims=True)
        mix_wide = dot(mix_low, spread).astype(BF16)
        blended = second * mix_sum + dot_last((mix_wide * act).astype(BF16), up[...])
        blended = blended.astype(BF16)
        blends[rows] = blended
        normed3, inv_std3 = normalize(second + dot(blended, value[...]))
        layer_out[rows] = normed3 * gain3 + shift3

        token = rows.start + lax.broadcasted_iota(jnp.int32, (CHUNK, 1), 0)
        keep = jnp.where(token < count, 1.0, 0.0)
        cot = out_grad[rows].astype(F32) * keep
        mass = jnp.sum(mix * keep, axis=0, keepdims=True)
        mass = jnp.where(lane == n_adapters, jnp.sum(keep), mass)
        sum_lines[0:1] += jnp.sum(cot * normed3, axis=0, keepdims=True)
        sum_lines[1:2] += jnp.sum(cot, axis=0, keepdims=True)
        sum_lines[2:3, :LANES] += mass

        grad_pre = norm_back(cot * gain3, normed3, inv_std3)
        grad_proj = grad_pre.astype(BF16)
        values[rows] = grad_proj
        grad_blend = dot_last(grad_proj, value[...]).astype(BF16)
        blend_up = dot(grad_blend, up[...])
        grad_mix = jnp.sum(
            grad_blend.astype(F32) * second, axis=1, keepdims=True
        ) + by_adapter(act * blend_up)
        grad_logits = mix * (grad_mix - jnp.sum(grad_mix * mix, axis=1, keepdims=True))
        grad_logits = grad_logits.astype(BF16)
        logit_sum = jnp.sum(grad_logits.astype(F32), axis=1, keepdims=True)
        logit_wide = dot(grad_logits, spread).astype(BF16)
        grad_probe = second * logit_sum + dot_last((logit_wide * act).astype(BF16), up[...])
        grad_probe = (scale * grad_probe).astype(BF16)
        probes[rows] = grad_probe
        fquery_out[rows] = dot(grad_probe, key[...]).astype(BF16)
        grad_act = mix_wide.astype(F32) * blend_up + (scale * logit_wide.astype(F32)) * probe_up
        middle_out[rows] = (grad_act * slope.astype(F32)).astype(BF16)
        part_out[rows] = (
            grad_pre + grad_blend.astype(F32) * mix_sum + probe.astype(F32) * (scale * logit_sum)
        )

    by_chunks(seq, chunk)

    @pl.loop(0, width // CHUNK)
    def _(i):
        part = pl.ds(pl.multiple_of(i * CHUNK, CHUNK), CHUNK)
        grads[0, part] = dot_first(states[:, part], fquery_out[...])
        grads[1, part] = dot_first(probes[:, part], fqueries[...])
        grads[2, part] = dot_first(blends[:, part], values[...])

    tail = split_lines(sum_lines[0:4])
    rows = width // 32

    @pl.loop(0, 16)
    def _(chip):
        z_rel = (chip // 4) ^ meta[DEPTH]
        y_rel = (chip // 2 % 2) ^ meta[PAIR_Y]
        x_rel = (chip % 2) ^ meta[ACROSS]
        for core_rel, out in ((0, keep_out), (1, send_out)):
            first = pl.multiple_of((chip * 2 + (meta[CORE] ^ core_rel)) * rows, 8)
            block = [grads[i, pl.ds(first, rows)] for i in range(3)] + [tail]
            out[x_rel, y_rel, z_rel] = jnp.concatenate(block, axis=0).astype(BF16)


def call_merging(n_adapters, meta, lengths, sums, lines, out_grad, matrices):
    seq, width = sums.shape
    block = 3 * width // 32 + 8
    return pl.pallas_call(
        functools.partial(merging, n_adapters),
        in_specs=[SMEM, SMEM] + [VMEM] * 4,
        out_specs=[VMEM] * 6,
        out_shape=[sds((seq, width), F32)] * 2
        + [sds((seq, width), BF16)] * 2
        + [sds((2, 2, 4, block, width), BF16)] * 2,
        scratch_shapes=[pltpu.VMEM((3, width, width), F32), pltpu.VMEM((8, width), F32)]
        + [pltpu.VMEM((seq, width), BF16)] * 5,
        compiler_params=params(MERGE_MIB),
        cost_estimate=cost(18),
        name="merging",
    )(meta, lengths, sums, lines, out_grad, matrices)


def merging_input(sums, lines, part, grad_fquery, grad_middle, matrices, grad_out, grad_low_out):
    def chunk(rows):
        normed, inv_std = normalize(sums[rows])
        grad = part[rows] + dot_last(grad_fquery[rows], matrices[2])
        grad = grad + dot_last(grad_middle[rows], matrices[0])
        grad = norm_back(grad * line_of(lines, GAIN2), normed, inv_std)
        grad_out[rows] = grad
        grad_low_out[rows] = grad.astype(BF16)

    by_chunks(part.shape[0], chunk)


def call_merging_input(deps, sums, lines, part, grad_fquery, grad_middle, matrices):
    return kernel(
        merging_input,
        deps,
        FFN_MIB,
        in_specs=[VMEM] * 6,
        out_specs=[VMEM] * 2,
        out_shape=[sds(part.shape, F32), sds(part.shape, BF16)],
        cost_estimate=cost(3),
        name="merging_input",
    )(sums, lines, part, grad_fquery, grad_middle, matrices)


def ffn_backward(last, blocks, n_slopes, grad_low, before, *refs):
    slopes, (in0, in1), refs = refs[:n_slopes], refs[n_slopes : n_slopes + 2], refs[n_slopes + 2 :]
    slopes = [slope.at[i] for slope in slopes for i in range(slope.shape[0])]
    all_outs, refs = refs[: 2 * blocks], refs[2 * blocks :]

    def chunk(rows):
        low = grad_low[rows]
        total = before[rows]
        outs = list(all_outs)
        for quarter, into in enumerate((in0, in1)):
            grad_act = [dot_last(low, outs.pop(0)[...]) for _ in range(blocks)]
            grad_act = grad_act[0] if blocks == 1 else jnp.concatenate(grad_act, axis=1)
            grad_pre = (grad_act * slopes[quarter][rows].astype(F32)).astype(BF16)
            total = total + dot_last(grad_pre, into[...])
        if not last:
            refs[0][rows] = total
            return
        normed1, inv_std1, lines, grad_out, grad_low_out = refs
        grad = norm_back(total * line_of(lines, GAIN1), normed1[rows], inv_std1[rows])
        grad_out[rows] = grad
        grad_low_out[rows] = grad.astype(BF16)

    by_chunks(before.shape[0], chunk)


def call_ffn_backward(deps, grad_low, before, slopes, in_quarters, out_quarters, *for_norm):
    seq, width = before.shape
    last = bool(for_norm)
    return kernel(
        functools.partial(ffn_backward, last, len(out_quarters) // 2, len(slopes)),
        deps,
        FFN_MIB,
        in_specs=[VMEM] * (4 + len(slopes) + len(out_quarters) + len(for_norm)),
        out_specs=[VMEM] * (1 + last),
        out_shape=[sds((seq, width), F32)] + [sds((seq, width), BF16)] * last,
        cost_estimate=cost(5),
        name="ffn_backward",
    )(grad_low, before, *slopes, *in_quarters, *out_quarters, *for_norm)


def attend_backward(
    columns, grad_low, before, turned_ref, att_ref, prob_ref, weight, input_grad, token, grad_turned, grad_att
):
    width = 3 * HEAD_DIM
    root = HEAD_DIM**-0.5
    grad_att[...] = dot_last(weight[columns:], grad_low[...]).astype(BF16)

    @pl.loop(0, columns // width, unroll=True)
    def _(head):
        base = pl.multiple_of(head * width, width)
        places = [pl.ds(base + i * HEAD_DIM, HEAD_DIM) for i in range(3)]
        queries, keys, values = (turned_ref[place] for place in places)
        part = pl.ds(pl.multiple_of(head * HEAD_DIM, HEAD_DIM), HEAD_DIM)
        grad = grad_att[part]
        prob = prob_ref[head]
        row_dot = jnp.sum(grad.astype(F32) * att_ref[part].astype(F32), axis=0, keepdims=True)
        grad_scores = (prob.astype(F32) * (dot(values.T, grad) - row_dot)).astype(BF16)
        grad_turned[places[0]] = (dot(keys, grad_scores) * root).astype(BF16)
        grad_turned[places[1]] = (dot_last(queries, grad_scores) * root).astype(BF16)
        grad_turned[places[2]] = dot_last(grad, prob).astype(BF16)

    input_grad[...] = before[...] + dot(grad_turned[...].T, weight[:columns])
    token[...] = jnp.zeros_like(token)


def call_attend_backward(deps, columns, grad_low, before, saved, quarter):
    seq, width = before.shape
    inner = columns // 3
    return kernel(
        functools.partial(attend_backward, columns),
        deps,
        ATTEND_MIB,
        in_specs=[VMEM] * 6,
        out_specs=[VMEM] * 2,
        out_shape=[sds((seq, width), F32), sds((8, LANES), F32)],
        scratch_shapes=[pltpu.VMEM((columns, seq), BF16), pltpu.VMEM((inner, seq), BF16)],
        cost_estimate=cost(8),
        name="attend_backward",
    )(grad_low, before, *saved, quarter)


def prepare(meta, down, up, query, key, value, g1, s1, g2, s2, g3, s3, keep, send, lines, shard):
    n_adapters, _, rank = down.shape
    for i in range(n_adapters):
        shard[0, :, i * rank : (i + 1) * rank] = down[i].astype(F32)
        shard[1, :, i * rank : (i + 1) * rank] = up[i].astype(F32)
    for i, ref in enumerate((query, key, value)):
        shard[2 + i] = ref[...].astype(F32)
    half = keep.shape[2]
    mine = pl.multiple_of(meta[CORE] * half, LANES)
    other = pl.multiple_of((1 - meta[CORE]) * half, LANES)
    keep[...] = shard[:, :, pl.ds(mine, half)].astype(BF16)
    send[...] = shard[:, :, pl.ds(other, half)].astype(BF16)
    for i, ref in enumerate((g1, s1, g2, s2, g3, s3)):
        lines[i : i + 1] = ref[...].reshape(1, -1)
    lines[6:8] = jnp.zeros((2, lines.shape[1]), F32)


def call_prepare(meta, down, up, query, key, value, *vectors):
    rows, width = query.shape
    half = sds((5, rows, width // 2), BF16)
    return pl.pallas_call(
        prepare,
        in_specs=[SMEM] + [VMEM] * 11,
        out_specs=[VMEM] * 3,
        out_shape=[half, half, sds((8, width), F32)],
        scratch_shapes=[pltpu.VMEM((5, rows, width), F32)],
        compiler_params=params(16),
        cost_estimate=cost(1),
        name="prepare",
    )(meta, *(in_hbm(a) for a in (down, up, query, key, value, *vectors)))


def prepare_frozen(meta, qkv_turned, attn_out, into, out, attn, with_attn, with_in, out_last, *copies):
    columns = qkv_turned.shape[0]
    attn[:columns] = qkv_turned[...]
    attn[columns:] = attn_out[...]
    row = 0
    for entry, whole, share in ((PAIR_Y, attn, with_attn), (PAIR_Z, into, with_in)):
        half = whole.shape[0] // 2
        cut = share.shape[0] - half
        share[:half] = whole[pl.ds(pl.multiple_of(meta[entry] * half, 16), half)]
        share[half:] = out[row : row + cut]
        row += cut
    out_last[...] = out[row:]
    for source, copy in zip((into, out), copies):
        copy[...] = source[...]


def call_prepare_frozen(deps, meta, qkv_turned, attn_out, into, out):
    rows, width = qkv_turned.shape[0] + attn_out.shape[0], attn_out.shape[1]
    cut = out.shape[0] // 6
    shares = (rows, rows // 2 + cut, into.shape[0] // 2 + cut, out.shape[0] - 2 * cut)
    shares = shares + (into.shape[0], out.shape[0])
    return kernel(
        prepare_frozen,
        deps,
        16,
        in_specs=[SMEM] + [VMEM] * 4,
        out_specs=[VMEM] * 6,
        out_shape=[sds((n, width), BF16) for n in shares],
        cost_estimate=cost(1),
        name="prepare_frozen",
    )(meta, *(in_hbm(a) for a in (qkv_turned, attn_out, into, out)))


def chip_tile(meta, keep, got, tile):
    mine, other = keep[...].astype(F32), got[...].astype(F32)
    lower = jnp.where(meta[CORE] == 0, mine, other)
    upper = jnp.where(meta[CORE] == 0, other, mine)
    tile[...] = jnp.concatenate([lower, upper], axis=1).astype(BF16)


def call_chip_tile(meta, keep, got):
    n_mats, rows, half = keep.shape
    return kernel(
        chip_tile,
        [],
        16,
        in_specs=[SMEM] + [VMEM] * 2,
        out_specs=VMEM,
        out_shape=sds((n_mats, 2 * rows, half), BF16),
        cost_estimate=cost(1),
        name="chip_tile",
    )(meta, keep, got)


def add_blocks(*blocks):
    total = functools.reduce(jnp.add, (b.astype(F32) for b in blocks))
    tail = total[-8:-4] + total[-4:]
    return jnp.concatenate([total[:-8], split_lines(tail)], axis=0)


def sum_cores(keep, got, p_keep, p_send, q_keep, q_send):
    half = p_keep.shape[-1]
    for x in range(2):
        for y in range(2):

            @pl.loop(0, 4)
            def _(z, x=x, y=y):
                total = add_blocks(keep[x, y, z], got[x, y, z]).astype(BF16)
                (p_send if x else p_keep)[y, z] = total[:, :half]
                (q_send if y else q_keep)[x, z] = total[:, half:]


def sum_first(p_keep, p_got, q_keep, q_got, p2_keep, p2_send, q2_keep, q2_send):
    @pl.loop(0, 4)
    def _(z):
        for out, index in ((p2_keep, 0), (p2_send, 1)):
            out[z] = add_blocks(p_keep[index, z], p_got[index, z]).astype(BF16)
        for out, index in ((q2_keep, 0), (q2_send, 1)):
            out[z] = add_blocks(q_keep[index, z], q_got[index, z]).astype(BF16)


def sum_second(p_keep, p_got, q_keep, q_got, *outs):
    half = p_keep.shape[-1]
    for z in range(4):
        outs[z][:, :half] = add_blocks(p_keep[z], p_got[z]).astype(BF16)
        outs[z][:, half:] = add_blocks(q_keep[z], q_got[z]).astype(BF16)


def sum_last(n_adapters, keep, got1, got2, got3, query, key, value, gain, bias, mass):
    total = add_blocks(keep[...], got1[...], got2[...], got3[...])
    rows = query.shape[0]
    for i, out in enumerate((query, key, value)):
        out[...] = total[i * rows : (i + 1) * rows]
    lines = total[-8:-4] + total[-4:]
    gain[...] = lines[0]
    bias[...] = lines[1]
    mass[...] = lines[2, :n_adapters] / lines[2:3, n_adapters : n_adapters + 1].reshape(1)


def small_call(body, name, out_shape, dep, *operands):
    return kernel(
        body,
        (dep,),
        16,
        in_specs=[VMEM] * len(operands),
        out_specs=[VMEM] * len(out_shape),
        out_shape=out_shape,
        cost_estimate=cost(1),
        name=name,
    )(*operands)


def sum_gradients(hops, keep, send, n_adapters, works):
    block, width = keep.shape[3:]
    half = width // 2
    pair = [sds((2, 4, block, half), BF16)] * 4
    single = [sds((4, block, half), BF16)] * 4
    got = hops.flip(send, 1)
    dep = works[0](())
    pk, ps, qk, qs = small_call(sum_cores, "sum_cores", pair, dep, keep, got)
    pg, qg = hops.flip(ps, ALONG_X), hops.flip(qs, ALONG_Y)
    dep = works[1]([pk])
    pk, ps, qk, qs = small_call(sum_first, "sum_first", single, dep, pk, pg, qk, qg)
    pg, qg = hops.flip(ps, ALONG_Y), hops.flip(qs, ALONG_X)
    dep = works[2]([pk])
    parts = small_call(
        sum_second, "sum_second", [sds((block, width), BF16)] * 4, dep, pk, pg, qk, qg
    )
    got = [hops.flip(part, z * ALONG_Z) for z, part in enumerate(parts) if z]
    dep = works[3]([parts[0]])
    rows = (block - 8) // 3
    outs = [sds((rows, width), F32)] * 3 + [sds((width,), F32)] * 2 + [sds((n_adapters,), F32)]
    last = functools.partial(sum_last, n_adapters)
    return small_call(last, "sum_last", outs, dep, parts[0], *got)


ALONG_X, ALONG_Y, ALONG_Z = 2, 4, 8


class Hops:
    def __init__(self, mesh):
        self.count = mesh.size
        self.tiled = mesh.shape["dp"] == 8 and mesh.shape["tensor"] == 4

    def flip(self, array, bits):
        return lax.ppermute(array, AXES, [(i, i ^ bits) for i in range(self.count)])


def half_of(block, parity):
    half = block.shape[0] // 2
    return lax.dynamic_slice_in_dim(block, parity * half, half, 0)


def plain_schedule(
    meta, doc_lengths, tokens, out_grad, lines, columns, n_adapters, attn, into, out, shard
):
    attn, into, out = (lax.all_gather(w, "tensor", axis=0) for w in (attn, into, out))
    weights = lax.all_gather(shard, AXES, axis=1, tiled=True)
    pairs = [slice(i, i + 2) for i in range(0, attn.shape[0], 2)]
    before, saved, slopes = tokens, [], []
    for pair in pairs:
        last = pair is pairs[-1]
        results = call_attend_forward(
            [], columns, last, meta, doc_lengths, tokens, before, lines, tuple(attn[pair])
        )
        saved += [results[:3], results[3:6]]
        before = results[6]
    first, normed1, inv_std1 = results[6:]
    sums = first
    for pair in pairs:
        slope, sums = call_ffn_forward([], first, sums, tuple(into[pair]), tuple(out[pair]))
        slopes.append(slope)
    layer_out, *parts, keep, send = call_merging(
        n_adapters, meta, doc_lengths, sums, lines, out_grad, weights
    )
    total, low = call_merging_input([], sums, lines, *parts, weights)
    width = tokens.shape[1]
    blocks = jnp.transpose(jnp.stack([keep, send]), (3, 2, 1, 0, 4, 5)).reshape(32, -1, width)
    squares = blocks[:, :-8].reshape(32, 3, width // 32, width)
    squares = jnp.transpose(squares, (1, 0, 2, 3)).reshape(3, width, width).astype(F32)
    squares = lax.psum_scatter(squares, AXES, scatter_dimension=1, tiled=True)
    tail = blocks[0, -8:].astype(F32)
    totals = lax.psum(tail[:4] + tail[4:], AXES)
    for pair, slope in zip(pairs, slopes):
        for_norm = (normed1, inv_std1, lines) if pair is pairs[-1] else ()
        total, *rest = call_ffn_backward(
            [], low, total, [slope], tuple(into[pair]), tuple(out[pair]), *for_norm
        )
    (low,) = rest
    for quarter, kept in zip(attn, saved):
        total, _ = call_attend_backward([], columns, low, total, kept, quarter)
    mass = totals[2, :n_adapters] / totals[2, n_adapters]
    return (layer_out, total, squares[0], squares[1], squares[2], totals[0], totals[1], mass)


def per_device(
    hops,
    tokens,
    doc_lengths,
    qkv_weight,
    attn_out_weight,
    norm1_gain,
    norm1_bias,
    ffn_in_weight,
    ffn_out_weight,
    norm2_gain,
    norm2_bias,
    adapter_down,
    adapter_up,
    merging_query,
    merging_key,
    merging_value,
    merging_gain,
    merging_bias,
    out_grad,
):
    n_adapters, rows, rank = adapter_down.shape
    columns = qkv_weight.shape[1]
    tensor, dp = lax.axis_index("tensor"), lax.axis_index("dp")
    pair_y, pair_z = dp % 2, dp // 2 % 2
    meta = jnp.stack([tensor % 2, tensor // 2, pair_y, pair_z, dp // 2, tensor]).astype(jnp.int32)
    flip = hops.flip
    if not hops.tiled:
        meta = meta * (jnp.arange(meta.shape[0]) == ROW)

    keep, send, lines = call_prepare(
        meta,
        adapter_down,
        jnp.transpose(adapter_up, (0, 2, 1)),
        merging_query,
        merging_key,
        merging_value,
        norm1_gain,
        norm1_bias,
        norm2_gain,
        norm2_bias,
        merging_gain,
        merging_bias,
    )
    tile = call_chip_tile(meta, keep, flip(send, 1)) if hops.tiled else keep
    attn, with_attn, with_in, out_2, into, out = call_prepare_frozen(
        [tile], meta, qkv_weight.T, attn_out_weight, ffn_in_weight, ffn_out_weight
    )
    if not hops.tiled:
        shard = jnp.concatenate([keep, send], axis=2)
        return plain_schedule(
            meta, doc_lengths, tokens, out_grad, lines, columns, n_adapters, attn, into, out, shard
        )
    tile_x = flip(tile, ALONG_X)
    attn_core = flip(attn, 1)
    both, with_attn, into, out = sync(
        "phase1", meta, [[tile, tile_x]], [with_attn, into, out], [attn_core]
    )
    z2, y0, with_attn_x = flip(both, 2 * ALONG_Z), flip(both, ALONG_Y), flip(with_attn, ALONG_X)
    in_core, out_core = flip(into, 1), flip(out, 1)
    saved_near = call_attend_forward(
        [both], columns, False, meta, doc_lengths, tokens, tokens, lines, (attn, attn_core)
    )
    half = attn.shape[0] // 2
    joined, attn_x, with_in, y0, z2 = sync(
        "phase2",
        meta,
        [[both, z2], [(with_attn_x, 0, half)]],
        [with_in, y0, z2],
        [saved_near[6], in_core, out_core],
    )
    with_in_x, attn_y, z1 = flip(with_in, ALONG_X), flip(attn_x, ALONG_Y), flip(joined, ALONG_Z)
    y2 = flip(z2, ALONG_Y)
    joined_c, y0_c = flip(joined, 1), flip(y0, 1)
    attn_far, in_x, out_a, out_2, z1, y2 = sync(
        "phase3",
        meta,
        [
            [PAIR_Y, attn_x, attn_y],
            [(with_in_x, 0, half)],
            [(share, half, share.shape[0] - half) for share in (with_attn_x, with_in_x)],
        ],
        [out_2, z1, y2],
        [joined_c, y0_c],
    )
    attn_far_c = flip(attn_far, 1)
    y1, out_b, in_z = flip(z1, ALONG_Y), flip(out_2, ALONG_X), flip(in_x, ALONG_Z)
    z1_c, y2_c, out_a_c = flip(z1, 1), flip(y2, 1), flip(out_a, 1)
    *saved_far, first, normed1, inv_std1 = call_attend_forward(
        [], columns, True, meta, doc_lengths, tokens, saved_near[6], lines, (attn_far, attn_far_c)
    )
    slope_near, sums = call_ffn_forward(
        [], first, first, (ffn_in_weight, in_core), (ffn_out_weight, out_core)
    )
    own, other = 0, 1
    weights = assemble(
        "assemble",
        [],
        meta,
        None,
        [
            (joined, ((0, 0), (0, 2)), own),
            (joined_c, ((0, 0), (0, 2)), other),
            (z1, ((0, 1), (0, 3)), own),
            (z1_c, ((0, 1), (0, 3)), other),
            (y0, ((1, 0),), own),
            (y0_c, ((1, 0),), other),
            (y2, ((1, 2),), own),
            (y2_c, ((1, 2),), other),
        ],
    )
    in_far, out_b, y1 = sync(
        "phase4", meta, [[PAIR_Z, in_x, in_z]], [out_b, y1], [sums, weights, out_a_c]
    )
    in_far_c, out_b_c, y1_c = flip(in_far, 1), flip(out_b, 1), flip(y1, 1)
    out_far = (out_a, out_b, out_a_c, out_b_c)
    slopes_far = []
    for quarter, blocks in ((in_far, out_far[:2]), (in_far_c, out_far[2:])):
        slope, sums = call_ffn_forward([], first, sums, (quarter,), blocks)
        slopes_far.append(slope)
    last_parts = ((1, 1), (1, 3))
    weights = assemble(
        "assemble_last", [sums], meta, weights, [(y1, last_parts, own), (y1_c, last_parts, other)]
    )
    layer_out, *parts, grad_keep, grad_send = call_merging(
        n_adapters, meta, doc_lengths, sums, lines, out_grad, weights
    )
    done = {}
    attn_quarters = (attn, attn_core, attn_far, attn_far_c)
    saved = (saved_near[:3], saved_near[3:6], saved_far[:3], saved_far[3:6])

    def attention(deps, *quarters):
        for i in quarters:
            done["sum"], token = call_attend_backward(
                deps, columns, done["low"], done["sum"], saved[i], attn_quarters[i]
            )
        return token

    def near(deps):
        (done["sum"],) = call_ffn_backward(
            deps,
            done["low"],
            done["sum"],
            [slope_near],
            (ffn_in_weight, in_core),
            (ffn_out_weight, out_core),
        )
        return done["sum"]

    def far(deps):
        done["sum"], done["low"] = call_ffn_backward(
            deps,
            done["low"],
            done["sum"],
            slopes_far,
            (in_far, in_far_c),
            out_far,
            normed1,
            inv_std1,
            lines,
        )

    def first_work(deps):
        done["sum"], done["low"] = call_merging_input(deps, sums, lines, *parts, weights)
        return done["sum"]

    def second_work(deps):
        near(deps)
        far([])
        return attention([], 0)

    works = (
        first_work,
        second_work,
        lambda deps: attention(deps, 1),
        lambda deps: attention(deps, 2, 3),
    )
    summed = sum_gradients(hops, grad_keep, grad_send, n_adapters, works)
    return (layer_out, done["sum"], *summed)


def solution(mesh):
    split = P(AXES, None)
    in_specs = (
        split,
        P("dp", None),
        P(None, "tensor"),
        P("tensor", None),
        P(),
        P(),
        P(None, "tensor"),
        P("tensor", None),
        P(),
        P(),
        P(None, AXES, None),
        P(None, None, AXES),
        split,
        split,
        split,
        P(),
        P(),
        split,
    )
    out_specs = (split, split, split, split, split, P(), P(), P())
    return jax.shard_map(
        functools.partial(per_device, Hops(mesh)),
        mesh=mesh,
        in_specs=in_specs,
        out_specs=out_specs,
        check_vma=False,
    )
```

```python
import functools

import jax
import jax.numpy as jnp
from jax import lax
from jax.experimental import pallas as pl
from jax.experimental.pallas import tpu as pltpu
from jax.sharding import PartitionSpec as P

HEAD_DIM = 64
AXES = ("dp", "tensor")
ATTEND_MIB, FFN_MIB, MERGE_MIB = 16, 16, 24
LANES = 128
COST = 0.0
CHUNK = 256
EPS = 1e-12
BIG_NEGATIVE = -1e30
ROOT_HALF = 0.7071067811865476
ROOT_TAU = 0.3989422804014327
F32, BF16 = jnp.float32, jnp.bfloat16

CORE, ACROSS, PAIR_Y, PAIR_Z, DEPTH, ROW = range(6)
GAIN1, SHIFT1, GAIN2, SHIFT2, GAIN3, SHIFT3 = range(6)

SMEM = pl.BlockSpec(memory_space=pltpu.SMEM)
VMEM = pl.BlockSpec(memory_space=pltpu.VMEM)
ANY = pl.BlockSpec(memory_space=pl.ANY)
HBM = pl.BlockSpec(memory_space=pltpu.HBM)


def by_chunks(count, body, size=CHUNK):
    @pl.loop(0, count // size)
    def _(i):
        body(pl.ds(pl.multiple_of(i * size, size), size))


def line_of(lines, i):
    return lines[i : i + 1]


def dot(a, b):
    return lax.dot_general(a, b, (((1,), (0,)), ((), ())), preferred_element_type=F32)


def dot_last(a, b):
    return lax.dot_general(a, b, (((1,), (1,)), ((), ())), preferred_element_type=F32)


def dot_first(a, b):
    return lax.dot_general(a, b, (((0,), (0,)), ((), ())), preferred_element_type=F32)


def normalize(u):
    centered = u - jnp.mean(u, axis=-1, keepdims=True)
    inv_std = lax.rsqrt(jnp.mean(centered * centered, axis=-1, keepdims=True) + EPS)
    return centered * inv_std, inv_std


def norm_back(grad, normed, inv_std):
    return inv_std * (
        grad
        - jnp.mean(grad, axis=-1, keepdims=True)
        - normed * jnp.mean(grad * normed, axis=-1, keepdims=True)
    )


def gelu_both(u):
    half = 0.5 * (1.0 + lax.erf(u * ROOT_HALF))
    return u * half, half + u * jnp.exp(-0.5 * u * u) * ROOT_TAU


def segment_bias(meta_ref, lengths_ref, bias_ref):
    seq = bias_ref.shape[0]
    row = meta_ref[ROW]
    by_row = lax.broadcasted_iota(jnp.int32, (seq, 1), 0)
    by_lane = lax.broadcasted_iota(jnp.int32, (1, seq), 1)
    seg_row = jnp.zeros((seq, 1), jnp.int32)
    seg_lane = jnp.zeros((1, seq), jnp.int32)
    end = jnp.int32(0)
    for i in range(lengths_ref.shape[1]):
        end = end + lengths_ref[row, i]
        seg_row = seg_row + jnp.where(by_row >= end, 1, 0)
        seg_lane = seg_lane + jnp.where(by_lane >= end, 1, 0)
    bias_ref[...] = jnp.where(seg_row == seg_lane, 0.0, BIG_NEGATIVE).astype(F32)


def attend_forward(columns, last, meta, lengths, tokens, before, lines, weight0, weight1, *refs):
    saved, first_out, bias = refs[:6], refs[6], refs[-1]
    segment_bias(meta, lengths, bias)
    total = before[...].astype(F32)
    width = 3 * HEAD_DIM
    for quarter, weight in enumerate((weight0, weight1)):
        turned = dot_last(weight[:columns], tokens[...]).astype(BF16)
        turned_out, att_out, prob_out = saved[3 * quarter : 3 * quarter + 3]
        turned_out[...] = turned

        @pl.loop(0, columns // width)
        def _(head, turned_out=turned_out, att_out=att_out, prob_out=prob_out):
            base = pl.multiple_of(head * width, width)
            queries, keys, values = (
                turned_out[pl.ds(base + i * HEAD_DIM, HEAD_DIM)] for i in range(3)
            )
            scores = dot(keys.T, queries * BF16(HEAD_DIM**-0.5)) + bias[...]
            exponent = jnp.exp(scores - jnp.max(scores, axis=0, keepdims=True))
            prob = (exponent * (1.0 / jnp.sum(exponent, axis=0, keepdims=True))).astype(BF16)
            prob_out[head] = prob
            part = pl.ds(pl.multiple_of(head * HEAD_DIM, HEAD_DIM), HEAD_DIM)
            att_out[part] = dot(values, prob).astype(BF16)

        total = total + dot(att_out[...].T, weight[columns:])
    if not last:
        first_out[...] = total
        return
    normed_out, inv_out = refs[7:9]
    normed, inv_std = normalize(total)
    normed_out[...] = normed
    inv_out[...] = inv_std
    first_out[...] = normed * line_of(lines, GAIN1) + line_of(lines, SHIFT1)


def sds(shape, dtype):
    return jax.ShapeDtypeStruct(shape, dtype)


def params(mib):
    return pltpu.CompilerParams(vmem_limit_bytes=mib << 20)


def kernel(body, deps, mib, *, in_specs, **kw):
    n = len(deps)
    call = pl.pallas_call(
        lambda *refs: body(*refs[n:]),
        in_specs=[ANY] * n + in_specs,
        compiler_params=params(mib),
        **kw,
    )
    return functools.partial(call, *deps)


def sync(name, meta, joins, carries, deps):
    sides = [j[0] if isinstance(j[0], int) else None for j in joins]
    parts = [j[1:] if isinstance(j[0], int) else j for j in joins]
    parts = [[p if isinstance(p, tuple) else (p, 0, p.shape[0]) for p in j] for j in parts]
    flat = [p[0] for j in parts for p in j]

    def body(meta_ref, *refs):
        refs = refs[len(carries) :]
        sources, outs = list(refs[: len(flat)]), refs[len(flat) : len(flat) + len(parts)]
        for side, join, out in zip(sides, parts, outs):
            row = 0
            for i, (_, start, size) in enumerate(join):
                if side is not None:
                    n = len(join) // 2
                    row = pl.multiple_of(((meta_ref[side] ^ (i // n)) * n + i % n) * size, 16)
                out[pl.ds(row, size)] = sources.pop(0)[start : start + size]
                row = row + size

    joined = [sds((sum(p[2] for p in j), *j[0][0].shape[1:]), j[0][0].dtype) for j in parts]
    n_deps = len(deps)
    out = kernel(
        body,
        deps,
        16,
        in_specs=[SMEM] + [ANY] * len(carries) + [VMEM] * len(flat),
        out_specs=[VMEM] * len(joined) + [ANY] * len(carries),
        out_shape=joined + [sds(c.shape, c.dtype) for c in carries],
        input_output_aliases={n_deps + 1 + i: len(joined) + i for i in range(len(carries))},
        cost_estimate=cost(0),
        name=name,
    )(meta, *carries, *flat)
    return out


def in_hbm(array):
    return pltpu.with_memory_space_constraint(array, pltpu.HBM)


def cost(us):
    return pl.CostEstimate(flops=int(us * 1.1e9 * COST), bytes_accessed=1024, transcendentals=0)


def call_attend_forward(deps, columns, last, meta, lengths, tokens, before, lines, quarters):
    seq, width = tokens.shape
    heads = columns // (3 * HEAD_DIM)
    inner = heads * HEAD_DIM
    square, narrow = sds((seq, width), F32), sds((seq, 1), F32)
    place = pltpu.HBM
    out_shape = [
        place((columns, seq), BF16),
        place((inner, seq), BF16),
        place((heads, seq, seq), BF16),
    ] * 2 + [square] + [square, narrow] * last
    return kernel(
        functools.partial(attend_forward, columns, last),
        deps,
        ATTEND_MIB,
        in_specs=[SMEM, SMEM] + [VMEM] * 5,
        out_specs=[VMEM] * len(out_shape),
        out_shape=out_shape,
        scratch_shapes=[pltpu.VMEM((seq, seq), F32)],
        cost_estimate=cost(8),
        name="attend_forward",
    )(meta, lengths, tokens, before, lines, *quarters)


def ffn_forward(quarters, blocks, first, before, *refs):
    slope_out, sum_out = refs[-2:]

    def chunk(rows):
        low = first[rows].astype(BF16)
        total = before[rows]
        outs = list(refs[quarters:-2])
        for quarter in range(quarters):
            value, slope = gelu_both(dot(low, refs[quarter][...]))
            slope_out[quarter, rows] = slope.astype(BF16)
            value = value.astype(BF16)
            start = 0
            for _ in range(blocks):
                out = outs.pop(0)
                total = total + dot(value[:, start : start + out.shape[0]], out[...])
                start += out.shape[0]
        sum_out[rows] = total

    by_chunks(first.shape[0], chunk)


def call_ffn_forward(deps, first, before, in_quarters, out_quarters):
    seq, width = first.shape
    hidden = in_quarters[0].shape[1]
    quarters = len(in_quarters)
    return kernel(
        functools.partial(ffn_forward, quarters, len(out_quarters) // quarters),
        deps,
        FFN_MIB,
        in_specs=[VMEM] * (2 + quarters + len(out_quarters)),
        out_specs=[VMEM] * 2,
        out_shape=[sds((quarters, seq, hidden), BF16), sds((seq, width), F32)],
        cost_estimate=cost(5),
        name="ffn_forward",
    )(first, before, *in_quarters, *out_quarters)


def assemble(name, deps, meta, weights, tiles):
    n_mats = tiles[0][0].shape[0] // (2 * len(tiles[0][1]))
    rows, half = tiles[0][0].shape[1:]
    count = sum(2 * len(parts) for _, parts, _ in tiles)
    before = [] if weights is None else [weights]

    def body(meta_ref, *refs):
        refs = refs[len(before) :]
        out, sems = refs[-2:]
        copies = []
        for ref, (_, parts, core_rel) in zip(refs, tiles):
            side = pl.multiple_of((meta_ref[CORE] ^ core_rel) * half, LANES)
            for j, (y_rel, z_rel) in enumerate(parts):
                for x_rel in range(2):
                    chip = ((meta_ref[DEPTH] ^ z_rel) * 2 + (meta_ref[PAIR_Y] ^ y_rel)) * 2
                    chip = chip + (meta_ref[ACROSS] ^ x_rel)
                    first = pl.multiple_of(chip * rows, 16)
                    target = out.at[:, pl.ds(first, rows), pl.ds(side, half)]
                    source = ref.at[pl.ds((2 * j + x_rel) * n_mats, n_mats)]
                    copies.append(pltpu.make_async_copy(source, target, sems.at[len(copies)]))
        for copy in copies:
            copy.start()
        for copy in copies:
            copy.wait()

    return kernel(
        body,
        deps,
        16,
        in_specs=[SMEM] + [ANY] * len(before) + [VMEM] * len(tiles),
        out_specs=ANY,
        out_shape=sds((n_mats, 2 * half, 2 * half), BF16),
        input_output_aliases={len(deps) + 1: 0} if before else {},
        scratch_shapes=[pltpu.SemaphoreType.DMA((count,))],
        cost_estimate=cost(0),
        name=name,
    )(meta, *before, *(tile for tile, _, _ in tiles))


def split_lines(total):
    high = total.astype(BF16).astype(F32)
    return jnp.concatenate([high, total - high], axis=0)


def merging(n_adapters, meta, lengths, sums, lines, out_grad, matrices, *refs):
    layer_out, part_out, fquery_out, middle_out, keep_out, send_out = refs[:6]
    grads, sum_lines, states, probes, blends, values, fqueries = refs[6:]
    seq, width = sums.shape
    scale = width**-0.5
    down, up, query, key, value = (matrices.at[i] for i in range(5))
    gain2, shift2 = line_of(lines, GAIN2), line_of(lines, SHIFT2)
    gain3, shift3 = line_of(lines, GAIN3), line_of(lines, SHIFT3)
    spread = jnp.where(
        lax.broadcasted_iota(jnp.int32, (LANES, width), 0)
        == lax.broadcasted_iota(jnp.int32, (LANES, width), 1) // (width // n_adapters),
        1.0,
        0.0,
    ).astype(BF16)
    lane = lax.broadcasted_iota(jnp.int32, (1, LANES), 1)
    count = jnp.int32(0)
    for i in range(lengths.shape[1]):
        count = count + lengths[meta[ROW], i]
    sum_lines[...] = jnp.zeros_like(sum_lines)

    def by_adapter(terms):
        high = terms.astype(BF16)
        rest = (terms - high.astype(F32)).astype(BF16)
        return dot_last(high, spread) + dot_last(rest, spread)

    def chunk(rows):
        normed2, _ = normalize(sums[rows])
        second = normed2 * gain2 + shift2
        second_low = second.astype(BF16)
        states[rows] = second_low
        act, slope = (v.astype(BF16) for v in gelu_both(dot(second_low, down[...])))
        fquery = dot(second_low, query[...]).astype(BF16)
        fqueries[rows] = fquery
        probe = dot_last(fquery, key[...]).astype(BF16)
        probe_up = dot(probe, up[...])
        logits = scale * (
            jnp.sum(probe.astype(F32) * second, axis=1, keepdims=True)
            + by_adapter(act * probe_up)
        )
        logits = jnp.where(lane < n_adapters, logits, BIG_NEGATIVE)
        exponent = jnp.exp(logits - jnp.max(logits, axis=1, keepdims=True))
        mix = exponent / jnp.sum(exponent, axis=1, keepdims=True)
        mix_low = mix.astype(BF16)
        mix_sum = jnp.sum(mix_low.astype(F32), axis=1, keepdims=True)
        mix_wide = dot(mix_low, spread).astype(BF16)
        blended = second * mix_sum + dot_last((mix_wide * act).astype(BF16), up[...])
        blended = blended.astype(BF16)
        blends[rows] = blended
        normed3, inv_std3 = normalize(second + dot(blended, value[...]))
        layer_out[rows] = normed3 * gain3 + shift3

        token = rows.start + lax.broadcasted_iota(jnp.int32, (rows.size, 1), 0)
        keep = jnp.where(token < count, 1.0, 0.0)
        cot = out_grad[rows].astype(F32) * keep
        mass = jnp.sum(mix * keep, axis=0, keepdims=True)
        mass = jnp.where(lane == n_adapters, jnp.sum(keep), mass)
        sum_lines[0:1] += jnp.sum(cot * normed3, axis=0, keepdims=True)
        sum_lines[1:2] += jnp.sum(cot, axis=0, keepdims=True)
        sum_lines[2:3, :LANES] += mass

        grad_pre = norm_back(cot * gain3, normed3, inv_std3)
        grad_proj = grad_pre.astype(BF16)
        values[rows] = grad_proj
        grad_blend = dot_last(grad_proj, value[...]).astype(BF16)
        blend_up = dot(grad_blend, up[...])
        grad_mix = jnp.sum(
            grad_blend.astype(F32) * second, axis=1, keepdims=True
        ) + by_adapter(act * blend_up)
        grad_logits = mix * (grad_mix - jnp.sum(grad_mix * mix, axis=1, keepdims=True))
        grad_logits = grad_logits.astype(BF16)
        logit_sum = jnp.sum(grad_logits.astype(F32), axis=1, keepdims=True)
        logit_wide = dot(grad_logits, spread).astype(BF16)
        grad_probe = second * logit_sum + dot_last((logit_wide * act).astype(BF16), up[...])
        grad_probe = (scale * grad_probe).astype(BF16)
        probes[rows] = grad_probe
        fquery_out[rows] = dot(grad_probe, key[...]).astype(BF16)
        grad_act = mix_wide.astype(F32) * blend_up + (scale * logit_wide.astype(F32)) * probe_up
        middle_out[rows] = (grad_act * slope.astype(F32)).astype(BF16)
        part_out[rows] = (
            grad_pre + grad_blend.astype(F32) * mix_sum + probe.astype(F32) * (scale * logit_sum)
        )

    by_chunks(seq, chunk, seq)

    @pl.loop(0, width // CHUNK)
    def _(i):
        part = pl.ds(pl.multiple_of(i * CHUNK, CHUNK), CHUNK)
        grads[0, part] = dot_first(states[:, part], fquery_out[...])
        grads[1, part] = dot_first(probes[:, part], fqueries[...])
        grads[2, part] = dot_first(blends[:, part], values[...])

    tail = split_lines(sum_lines[0:4])
    rows = width // 32

    @pl.loop(0, 16)
    def _(chip):
        z_rel = (chip // 4) ^ meta[DEPTH]
        y_rel = (chip // 2 % 2) ^ meta[PAIR_Y]
        x_rel = (chip % 2) ^ meta[ACROSS]
        for core_rel, out in ((0, keep_out), (1, send_out)):
            first = pl.multiple_of((chip * 2 + (meta[CORE] ^ core_rel)) * rows, 8)
            block = [grads[i, pl.ds(first, rows)] for i in range(3)] + [tail]
            out[x_rel, y_rel, z_rel] = jnp.concatenate(block, axis=0).astype(BF16)


def call_merging(n_adapters, meta, lengths, sums, lines, out_grad, matrices):
    seq, width = sums.shape
    block = 3 * width // 32 + 8
    return pl.pallas_call(
        functools.partial(merging, n_adapters),
        in_specs=[SMEM, SMEM] + [VMEM] * 4,
        out_specs=[VMEM] * 6,
        out_shape=[sds((seq, width), F32)] * 2
        + [sds((seq, width), BF16)] * 2
        + [sds((2, 2, 4, block, width), BF16)] * 2,
        scratch_shapes=[pltpu.VMEM((3, width, width), F32), pltpu.VMEM((8, width), F32)]
        + [pltpu.VMEM((seq, width), BF16)] * 5,
        compiler_params=params(MERGE_MIB),
        cost_estimate=cost(18),
        name="merging",
    )(meta, lengths, sums, lines, out_grad, matrices)


def merging_input(sums, lines, part, grad_fquery, grad_middle, matrices, grad_out, grad_low_out):
    def chunk(rows):
        normed, inv_std = normalize(sums[rows])
        grad = part[rows] + dot_last(grad_fquery[rows], matrices[2])
        grad = grad + dot_last(grad_middle[rows], matrices[0])
        grad = norm_back(grad * line_of(lines, GAIN2), normed, inv_std)
        grad_out[rows] = grad
        grad_low_out[rows] = grad.astype(BF16)

    by_chunks(part.shape[0], chunk)


def call_merging_input(deps, sums, lines, part, grad_fquery, grad_middle, matrices):
    return kernel(
        merging_input,
        deps,
        FFN_MIB,
        in_specs=[VMEM] * 6,
        out_specs=[VMEM] * 2,
        out_shape=[sds(part.shape, F32), sds(part.shape, BF16)],
        cost_estimate=cost(3),
        name="merging_input",
    )(sums, lines, part, grad_fquery, grad_middle, matrices)


def ffn_backward(last, blocks, n_slopes, grad_low, before, *refs):
    slopes, (in0, in1), refs = refs[:n_slopes], refs[n_slopes : n_slopes + 2], refs[n_slopes + 2 :]
    slopes = [slope.at[i] for slope in slopes for i in range(slope.shape[0])]
    all_outs, refs = refs[: 2 * blocks], refs[2 * blocks :]

    def chunk(rows):
        low = grad_low[rows]
        total = before[rows]
        outs = list(all_outs)
        for quarter, into in enumerate((in0, in1)):
            grad_act = [dot_last(low, outs.pop(0)[...]) for _ in range(blocks)]
            grad_act = grad_act[0] if blocks == 1 else jnp.concatenate(grad_act, axis=1)
            grad_pre = (grad_act * slopes[quarter][rows].astype(F32)).astype(BF16)
            total = total + dot_last(grad_pre, into[...])
        if not last:
            refs[0][rows] = total
            return
        normed1, inv_std1, lines, grad_out, grad_low_out = refs
        grad = norm_back(total * line_of(lines, GAIN1), normed1[rows], inv_std1[rows])
        grad_out[rows] = grad
        grad_low_out[rows] = grad.astype(BF16)

    by_chunks(before.shape[0], chunk)


def call_ffn_backward(deps, grad_low, before, slopes, in_quarters, out_quarters, *for_norm):
    seq, width = before.shape
    last = bool(for_norm)
    return kernel(
        functools.partial(ffn_backward, last, len(out_quarters) // 2, len(slopes)),
        deps,
        FFN_MIB,
        in_specs=[VMEM] * (4 + len(slopes) + len(out_quarters) + len(for_norm)),
        out_specs=[VMEM] * (1 + last),
        out_shape=[sds((seq, width), F32)] + [sds((seq, width), BF16)] * last,
        cost_estimate=cost(5),
        name="ffn_backward",
    )(grad_low, before, *slopes, *in_quarters, *out_quarters, *for_norm)


def attend_backward(
    columns, unroll, grad_low, before, turned_ref, att_ref, prob_ref, weight, input_grad, token, grad_turned, grad_att
):
    width = 3 * HEAD_DIM
    root = HEAD_DIM**-0.5
    grad_att[...] = dot_last(weight[columns:], grad_low[...]).astype(BF16)

    @pl.loop(0, columns // width, unroll=unroll)
    def _(head):
        base = pl.multiple_of(head * width, width)
        places = [pl.ds(base + i * HEAD_DIM, HEAD_DIM) for i in range(3)]
        queries, keys, values = (turned_ref[place] for place in places)
        part = pl.ds(pl.multiple_of(head * HEAD_DIM, HEAD_DIM), HEAD_DIM)
        grad = grad_att[part]
        prob = prob_ref[head]
        row_dot = jnp.sum(grad.astype(F32) * att_ref[part].astype(F32), axis=0, keepdims=True)
        grad_scores = (prob.astype(F32) * (dot(values.T, grad) - row_dot)).astype(BF16)
        grad_turned[places[0]] = (dot(keys, grad_scores) * root).astype(BF16)
        grad_turned[places[1]] = (dot_last(queries, grad_scores) * root).astype(BF16)
        grad_turned[places[2]] = dot_last(grad, prob).astype(BF16)

    input_grad[...] = before[...] + dot(grad_turned[...].T, weight[:columns])
    token[...] = jnp.zeros_like(token)


def call_attend_backward(deps, columns, unroll, grad_low, before, saved, quarter):
    seq, width = before.shape
    inner = columns // 3
    return kernel(
        functools.partial(attend_backward, columns, unroll),
        deps,
        ATTEND_MIB,
        in_specs=[VMEM] * 6,
        out_specs=[VMEM] * 2,
        out_shape=[sds((seq, width), F32), sds((8, LANES), F32)],
        scratch_shapes=[pltpu.VMEM((columns, seq), BF16), pltpu.VMEM((inner, seq), BF16)],
        cost_estimate=cost(8),
        name="attend_backward",
    )(grad_low, before, *saved, quarter)


def prepare(meta, down, up, query, key, value, g1, s1, g2, s2, g3, s3, keep, send, lines, shard):
    n_adapters, _, rank = down.shape
    for i in range(n_adapters):
        shard[0, :, i * rank : (i + 1) * rank] = down[i].astype(F32)
        shard[1, :, i * rank : (i + 1) * rank] = up[i].astype(F32)
    for i, ref in enumerate((query, key, value)):
        shard[2 + i] = ref[...].astype(F32)
    half = keep.shape[2]
    mine = pl.multiple_of(meta[CORE] * half, LANES)
    other = pl.multiple_of((1 - meta[CORE]) * half, LANES)
    keep[...] = shard[:, :, pl.ds(mine, half)].astype(BF16)
    send[...] = shard[:, :, pl.ds(other, half)].astype(BF16)
    for i, ref in enumerate((g1, s1, g2, s2, g3, s3)):
        lines[i : i + 1] = ref[...].reshape(1, -1)
    lines[6:8] = jnp.zeros((2, lines.shape[1]), F32)


def call_prepare(meta, down, up, query, key, value, *vectors):
    rows, width = query.shape
    half = sds((5, rows, width // 2), BF16)
    return pl.pallas_call(
        prepare,
        in_specs=[SMEM] + [VMEM] * 11,
        out_specs=[VMEM] * 3,
        out_shape=[half, half, sds((8, width), F32)],
        scratch_shapes=[pltpu.VMEM((5, rows, width), F32)],
        compiler_params=params(16),
        cost_estimate=cost(1),
        name="prepare",
    )(meta, *(in_hbm(a) for a in (down, up, query, key, value, *vectors)))


def prepare_frozen(meta, qkv_turned, attn_out, into, out, attn, with_attn, with_in, out_last, *copies):
    columns = qkv_turned.shape[0]
    attn[:columns] = qkv_turned[...]
    attn[columns:] = attn_out[...]
    half = attn.shape[0] // 2
    more = half // 3
    mine = pl.multiple_of(meta[PAIR_Y] * half, 16)
    other = pl.multiple_of((1 - meta[PAIR_Y]) * half + 2 * more, 16)
    with_attn[:half] = attn[pl.ds(mine, half)]
    with_attn[half : half + more] = attn[pl.ds(other, more)]
    cut = with_attn.shape[0] - half - more
    with_attn[half + more :] = out[:cut]
    half = into.shape[0] // 2
    with_in[:half] = into[pl.ds(pl.multiple_of(meta[PAIR_Z] * half, 16), half)]
    end = cut + with_in.shape[0] - half
    with_in[half:] = out[cut:end]
    out_last[...] = out[end:]
    for source, copy in zip((into, out), copies):
        copy[...] = source[...]


def call_prepare_frozen(deps, meta, qkv_turned, attn_out, into, out):
    rows, width = qkv_turned.shape[0] + attn_out.shape[0], attn_out.shape[1]
    unit = out.shape[0] // 12
    shares = (rows, rows // 2 + rows // 6 + unit, into.shape[0] // 2 + 3 * unit, 8 * unit)
    shares = shares + (into.shape[0], out.shape[0])
    return kernel(
        prepare_frozen,
        deps,
        16,
        in_specs=[SMEM] + [VMEM] * 4,
        out_specs=[VMEM] * 6,
        out_shape=[sds((n, width), BF16) for n in shares],
        cost_estimate=cost(1),
        name="prepare_frozen",
    )(meta, *(in_hbm(a) for a in (qkv_turned, attn_out, into, out)))


def chip_tile(meta, keep, got, tile):
    mine, other = keep[...].astype(F32), got[...].astype(F32)
    lower = jnp.where(meta[CORE] == 0, mine, other)
    upper = jnp.where(meta[CORE] == 0, other, mine)
    tile[...] = jnp.concatenate([lower, upper], axis=1).astype(BF16)


def call_chip_tile(meta, keep, got):
    n_mats, rows, half = keep.shape
    return kernel(
        chip_tile,
        [],
        16,
        in_specs=[SMEM] + [VMEM] * 2,
        out_specs=VMEM,
        out_shape=sds((n_mats, 2 * rows, half), BF16),
        cost_estimate=cost(1),
        name="chip_tile",
    )(meta, keep, got)


def add_blocks(*blocks):
    total = functools.reduce(jnp.add, (b.astype(F32) for b in blocks))
    tail = total[-8:-4] + total[-4:]
    return jnp.concatenate([total[:-8], split_lines(tail)], axis=0)


def sum_cores(keep, got, p_keep, p_send, q_keep, q_send):
    half = p_keep.shape[-1]
    for x in range(2):
        for y in range(2):

            @pl.loop(0, 4)
            def _(z, x=x, y=y):
                total = add_blocks(keep[x, y, z], got[x, y, z]).astype(BF16)
                (p_send if x else p_keep)[y, z] = total[:, :half]
                (q_send if y else q_keep)[x, z] = total[:, half:]


def sum_first(p_keep, p_got, q_keep, q_got, p2_keep, p2_send, q2_keep, q2_send):
    @pl.loop(0, 4)
    def _(z):
        for out, index in ((p2_keep, 0), (p2_send, 1)):
            out[z] = add_blocks(p_keep[index, z], p_got[index, z]).astype(BF16)
        for out, index in ((q2_keep, 0), (q2_send, 1)):
            out[z] = add_blocks(q_keep[index, z], q_got[index, z]).astype(BF16)


def sum_second(p_keep, p_got, q_keep, q_got, *outs):
    half = p_keep.shape[-1]
    for z in range(4):
        outs[z][:, :half] = add_blocks(p_keep[z], p_got[z]).astype(BF16)
        outs[z][:, half:] = add_blocks(q_keep[z], q_got[z]).astype(BF16)


def sum_last(n_adapters, keep, got1, got2, got3, query, key, value, gain, bias, mass):
    total = add_blocks(keep[...], got1[...], got2[...], got3[...])
    rows = query.shape[0]
    for i, out in enumerate((query, key, value)):
        out[...] = total[i * rows : (i + 1) * rows]
    lines = total[-8:-4] + total[-4:]
    gain[...] = lines[0]
    bias[...] = lines[1]
    mass[...] = lines[2, :n_adapters] / lines[2:3, n_adapters : n_adapters + 1].reshape(1)


def small_call(body, name, out_shape, dep, *operands):
    return kernel(
        body,
        (dep,),
        16,
        in_specs=[VMEM] * len(operands),
        out_specs=[VMEM] * len(out_shape),
        out_shape=out_shape,
        cost_estimate=cost(1),
        name=name,
    )(*operands)


def sum_gradients(hops, keep, send, n_adapters, works):
    block, width = keep.shape[3:]
    half = width // 2
    pair = [sds((2, 4, block, half), BF16)] * 4
    single = [sds((4, block, half), BF16)] * 4
    got = hops.flip(send, 1)
    dep = works[0](())
    pk, ps, qk, qs = small_call(sum_cores, "sum_cores", pair, dep, keep, got)
    pg, qg = hops.flip(ps, ALONG_X), hops.flip(qs, ALONG_Y)
    dep = works[1]([pk])
    pk, ps, qk, qs = small_call(sum_first, "sum_first", single, dep, pk, pg, qk, qg)
    pg, qg = hops.flip(ps, ALONG_Y), hops.flip(qs, ALONG_X)
    dep = works[2]([pk])
    parts = small_call(
        sum_second, "sum_second", [sds((block, width), BF16)] * 4, dep, pk, pg, qk, qg
    )
    got = [hops.flip(part, z * ALONG_Z) for z, part in enumerate(parts) if z]
    dep = works[3]([parts[0]])
    rows = (block - 8) // 3
    outs = [sds((rows, width), F32)] * 3 + [sds((width,), F32)] * 2 + [sds((n_adapters,), F32)]
    last = functools.partial(sum_last, n_adapters)
    return small_call(last, "sum_last", outs, dep, parts[0], *got)


ALONG_X, ALONG_Y, ALONG_Z = 2, 4, 8


class Hops:
    def __init__(self, mesh):
        self.count = mesh.size
        self.tiled = mesh.shape["dp"] == 8 and mesh.shape["tensor"] == 4

    def flip(self, array, bits):
        return lax.ppermute(array, AXES, [(i, i ^ bits) for i in range(self.count)])


def half_of(block, parity):
    half = block.shape[0] // 2
    return lax.dynamic_slice_in_dim(block, parity * half, half, 0)


def plain_schedule(
    meta, doc_lengths, tokens, out_grad, lines, columns, n_adapters, attn, into, out, shard
):
    attn, into, out = (lax.all_gather(w, "tensor", axis=0) for w in (attn, into, out))
    weights = lax.all_gather(shard, AXES, axis=1, tiled=True)
    pairs = [slice(i, i + 2) for i in range(0, attn.shape[0], 2)]
    before, saved, slopes = tokens, [], []
    for pair in pairs:
        last = pair is pairs[-1]
        results = call_attend_forward(
            [], columns, last, meta, doc_lengths, tokens, before, lines, tuple(attn[pair])
        )
        saved += [results[:3], results[3:6]]
        before = results[6]
    first, normed1, inv_std1 = results[6:]
    sums = first
    for pair in pairs:
        slope, sums = call_ffn_forward([], first, sums, tuple(into[pair]), tuple(out[pair]))
        slopes.append(slope)
    layer_out, *parts, keep, send = call_merging(
        n_adapters, meta, doc_lengths, sums, lines, out_grad, weights
    )
    total, low = call_merging_input([], sums, lines, *parts, weights)
    width = tokens.shape[1]
    blocks = jnp.transpose(jnp.stack([keep, send]), (3, 2, 1, 0, 4, 5)).reshape(32, -1, width)
    squares = blocks[:, :-8].reshape(32, 3, width // 32, width)
    squares = jnp.transpose(squares, (1, 0, 2, 3)).reshape(3, width, width).astype(F32)
    squares = lax.psum_scatter(squares, AXES, scatter_dimension=1, tiled=True)
    tail = blocks[0, -8:].astype(F32)
    totals = lax.psum(tail[:4] + tail[4:], AXES)
    for pair, slope in zip(pairs, slopes):
        for_norm = (normed1, inv_std1, lines) if pair is pairs[-1] else ()
        total, *rest = call_ffn_backward(
            [], low, total, [slope], tuple(into[pair]), tuple(out[pair]), *for_norm
        )
    (low,) = rest
    for quarter, kept in zip(attn, saved):
        total, _ = call_attend_backward([], columns, False, low, total, kept, quarter)
    mass = totals[2, :n_adapters] / totals[2, n_adapters]
    return (layer_out, total, squares[0], squares[1], squares[2], totals[0], totals[1], mass)


def per_device(
    hops,
    tokens,
    doc_lengths,
    qkv_weight,
    attn_out_weight,
    norm1_gain,
    norm1_bias,
    ffn_in_weight,
    ffn_out_weight,
    norm2_gain,
    norm2_bias,
    adapter_down,
    adapter_up,
    merging_query,
    merging_key,
    merging_value,
    merging_gain,
    merging_bias,
    out_grad,
):
    n_adapters, rows, rank = adapter_down.shape
    columns = qkv_weight.shape[1]
    tensor, dp = lax.axis_index("tensor"), lax.axis_index("dp")
    pair_y, pair_z = dp % 2, dp // 2 % 2
    meta = jnp.stack([tensor % 2, tensor // 2, pair_y, pair_z, dp // 2, tensor]).astype(jnp.int32)
    flip = hops.flip
    if not hops.tiled:
        meta = meta * (jnp.arange(meta.shape[0]) == ROW)

    keep, send, lines = call_prepare(
        meta,
        adapter_down,
        jnp.transpose(adapter_up, (0, 2, 1)),
        merging_query,
        merging_key,
        merging_value,
        norm1_gain,
        norm1_bias,
        norm2_gain,
        norm2_bias,
        merging_gain,
        merging_bias,
    )
    tile = call_chip_tile(meta, keep, flip(send, 1)) if hops.tiled else keep
    attn, with_attn, with_in, out_2, into, out = call_prepare_frozen(
        [tile], meta, qkv_weight.T, attn_out_weight, ffn_in_weight, ffn_out_weight
    )
    if not hops.tiled:
        shard = jnp.concatenate([keep, send], axis=2)
        return plain_schedule(
            meta, doc_lengths, tokens, out_grad, lines, columns, n_adapters, attn, into, out, shard
        )
    tile_x = flip(tile, ALONG_X)
    attn_core = flip(attn, 1)
    both, with_attn, into, out = sync(
        "phase1", meta, [[tile, tile_x]], [with_attn, into, out], [attn_core]
    )
    z2, y0, with_attn_x = flip(both, 2 * ALONG_Z), flip(both, ALONG_Y), flip(with_attn, ALONG_X)
    in_core, out_core = flip(into, 1), flip(out, 1)
    saved_near = call_attend_forward(
        [both], columns, False, meta, doc_lengths, tokens, tokens, lines, (attn, attn_core)
    )
    half = attn.shape[0] // 2
    third = half // 3
    joined, attn_x, with_in, y0, z2 = sync(
        "phase2",
        meta,
        [[both, z2], [(with_attn_x, 0, 2 * third)]],
        [with_in, y0, z2],
        [saved_near[6], in_core, out_core],
    )
    with_in_x, attn_y, z1 = flip(with_in, ALONG_X), flip(attn_x, ALONG_Y), flip(joined, ALONG_Z)
    y2 = flip(z2, ALONG_Y)
    joined_c, y0_c = flip(joined, 1), flip(y0, 1)
    attn_far, in_x, out_a, out_2, z1, y2 = sync(
        "phase3",
        meta,
        [
            [PAIR_Y]
            + [(with_attn_x, i * third, third) for i in range(3)]
            + [(attn_y, 0, third), (attn_y, third, third), (with_attn_x, half, third)],
            [(with_in_x, 0, half)],
            [
                (share, start, share.shape[0] - start)
                for share, start in ((with_attn_x, half + third), (with_in_x, half))
            ],
        ],
        [out_2, z1, y2],
        [joined_c, y0_c],
    )
    attn_far_c = flip(attn_far, 1)
    y1, out_b, in_z = flip(z1, ALONG_Y), flip(out_2, ALONG_X), flip(in_x, ALONG_Z)
    z1_c, y2_c, out_a_c = flip(z1, 1), flip(y2, 1), flip(out_a, 1)
    *saved_far, first, normed1, inv_std1 = call_attend_forward(
        [], columns, True, meta, doc_lengths, tokens, saved_near[6], lines, (attn_far, attn_far_c)
    )
    slope_near, sums = call_ffn_forward(
        [], first, first, (ffn_in_weight, in_core), (ffn_out_weight, out_core)
    )
    own, other = 0, 1
    weights = assemble(
        "assemble",
        [first],
        meta,
        None,
        [
            (joined, ((0, 0), (0, 2)), own),
            (joined_c, ((0, 0), (0, 2)), other),
            (z1, ((0, 1), (0, 3)), own),
            (z1_c, ((0, 1), (0, 3)), other),
            (y0, ((1, 0),), own),
            (y0_c, ((1, 0),), other),
            (y2, ((1, 2),), own),
            (y2_c, ((1, 2),), other),
        ],
    )
    in_far, out_b, y1 = sync(
        "phase4", meta, [[PAIR_Z, in_x, in_z]], [out_b, y1], [sums, weights, out_a_c]
    )
    in_far_c, out_b_c, y1_c = flip(in_far, 1), flip(out_b, 1), flip(y1, 1)
    out_far = (out_a, out_b, out_a_c, out_b_c)
    slopes_far = []
    for quarter, blocks in ((in_far, out_far[:2]), (in_far_c, out_far[2:])):
        slope, sums = call_ffn_forward([], first, sums, (quarter,), blocks)
        slopes_far.append(slope)
    last_parts = ((1, 1), (1, 3))
    weights = assemble(
        "assemble_last", [sums], meta, weights, [(y1, last_parts, own), (y1_c, last_parts, other)]
    )
    layer_out, *parts, grad_keep, grad_send = call_merging(
        n_adapters, meta, doc_lengths, sums, lines, out_grad, weights
    )
    done = {}
    attn_quarters = (attn, attn_core, attn_far, attn_far_c)
    saved = (saved_near[:3], saved_near[3:6], saved_far[:3], saved_far[3:6])

    def attention(deps, *quarters):
        for i in quarters:
            done["sum"], token = call_attend_backward(
                deps, columns, i > 1, done["low"], done["sum"], saved[i], attn_quarters[i]
            )
        return token

    def near(deps):
        (done["sum"],) = call_ffn_backward(
            deps,
            done["low"],
            done["sum"],
            [slope_near],
            (ffn_in_weight, in_core),
            (ffn_out_weight, out_core),
        )
        return done["sum"]

    def far(deps):
        done["sum"], done["low"] = call_ffn_backward(
            deps,
            done["low"],
            done["sum"],
            slopes_far,
            (in_far, in_far_c),
            out_far,
            normed1,
            inv_std1,
            lines,
        )

    def first_work(deps):
        done["sum"], done["low"] = call_merging_input(deps, sums, lines, *parts, weights)
        return done["sum"]

    def second_work(deps):
        near(deps)
        far([])
        return attention([], 0)

    works = (
        first_work,
        second_work,
        lambda deps: attention(deps, 1),
        lambda deps: attention(deps, 2, 3),
    )
    summed = sum_gradients(hops, grad_keep, grad_send, n_adapters, works)
    return (layer_out, done["sum"], *summed)


def solution(mesh):
    split = P(AXES, None)
    in_specs = (
        split,
        P("dp", None),
        P(None, "tensor"),
        P("tensor", None),
        P(),
        P(),
        P(None, "tensor"),
        P("tensor", None),
        P(),
        P(),
        P(None, AXES, None),
        P(None, None, AXES),
        split,
        split,
        split,
        P(),
        P(),
        split,
    )
    out_specs = (split, split, split, split, split, P(), P(), P())
    return jax.shard_map(
        functools.partial(per_device, Hops(mesh)),
        mesh=mesh,
        in_specs=in_specs,
        out_specs=out_specs,
        check_vma=False,
    )
```

```python
import functools

import jax
import jax.numpy as jnp
from jax import lax
from jax.experimental import pallas as pl
from jax.experimental.pallas import tpu as pltpu
from jax.sharding import PartitionSpec as P

HEAD_DIM = 64
AXES = ("dp", "tensor")
ATTEND_MIB, FFN_MIB, MERGE_MIB = 16, 16, 24
LANES = 128
COST = 0.0
CHUNK = 256
EPS = 1e-12
BIG_NEGATIVE = -1e30
ROOT_HALF = 0.7071067811865476
ROOT_TAU = 0.3989422804014327
F32, BF16 = jnp.float32, jnp.bfloat16

CORE, ACROSS, PAIR_Y, PAIR_Z, DEPTH, ROW = range(6)
GAIN1, SHIFT1, GAIN2, SHIFT2, GAIN3, SHIFT3 = range(6)

SMEM = pl.BlockSpec(memory_space=pltpu.SMEM)
VMEM = pl.BlockSpec(memory_space=pltpu.VMEM)
ANY = pl.BlockSpec(memory_space=pl.ANY)
HBM = pl.BlockSpec(memory_space=pltpu.HBM)


def by_chunks(count, body, size=CHUNK):
    @pl.loop(0, count // size)
    def _(i):
        body(pl.ds(pl.multiple_of(i * size, size), size))


def line_of(lines, i):
    return lines[i : i + 1]


def dot(a, b):
    return lax.dot_general(a, b, (((1,), (0,)), ((), ())), preferred_element_type=F32)


def dot_last(a, b):
    return lax.dot_general(a, b, (((1,), (1,)), ((), ())), preferred_element_type=F32)


def dot_first(a, b):
    return lax.dot_general(a, b, (((0,), (0,)), ((), ())), preferred_element_type=F32)


def normalize(u):
    centered = u - jnp.mean(u, axis=-1, keepdims=True)
    inv_std = lax.rsqrt(jnp.mean(centered * centered, axis=-1, keepdims=True) + EPS)
    return centered * inv_std, inv_std


def norm_back(grad, normed, inv_std):
    return inv_std * (
        grad
        - jnp.mean(grad, axis=-1, keepdims=True)
        - normed * jnp.mean(grad * normed, axis=-1, keepdims=True)
    )


def gelu_both(u):
    half = 0.5 * (1.0 + lax.erf(u * ROOT_HALF))
    return u * half, half + u * jnp.exp(-0.5 * u * u) * ROOT_TAU


def segment_bias(meta_ref, lengths_ref, bias_ref):
    seq = bias_ref.shape[0]
    row = meta_ref[ROW]
    by_row = lax.broadcasted_iota(jnp.int32, (seq, 1), 0)
    by_lane = lax.broadcasted_iota(jnp.int32, (1, seq), 1)
    seg_row = jnp.zeros((seq, 1), jnp.int32)
    seg_lane = jnp.zeros((1, seq), jnp.int32)
    end = jnp.int32(0)
    for i in range(lengths_ref.shape[1]):
        end = end + lengths_ref[row, i]
        seg_row = seg_row + jnp.where(by_row >= end, 1, 0)
        seg_lane = seg_lane + jnp.where(by_lane >= end, 1, 0)
    bias_ref[...] = jnp.where(seg_row == seg_lane, 0.0, BIG_NEGATIVE).astype(F32)


def attend_forward(columns, last, meta, lengths, tokens, before, lines, weight0, weight1, *refs):
    saved, first_out, bias = refs[:6], refs[6], refs[-1]
    segment_bias(meta, lengths, bias)
    total = before[...].astype(F32)
    width = 3 * HEAD_DIM
    for quarter, weight in enumerate((weight0, weight1)):
        turned = dot_last(weight[:columns], tokens[...]).astype(BF16)
        turned_out, att_out, prob_out = saved[3 * quarter : 3 * quarter + 3]
        turned_out[...] = turned

        @pl.loop(0, columns // width)
        def _(head, turned_out=turned_out, att_out=att_out, prob_out=prob_out):
            base = pl.multiple_of(head * width, width)
            queries, keys, values = (
                turned_out[pl.ds(base + i * HEAD_DIM, HEAD_DIM)] for i in range(3)
            )
            scores = dot(keys.T, queries * BF16(HEAD_DIM**-0.5)) + bias[...]
            exponent = jnp.exp(scores - jnp.max(scores, axis=0, keepdims=True))
            prob = (exponent * (1.0 / jnp.sum(exponent, axis=0, keepdims=True))).astype(BF16)
            prob_out[head] = prob
            part = pl.ds(pl.multiple_of(head * HEAD_DIM, HEAD_DIM), HEAD_DIM)
            att_out[part] = dot(values, prob).astype(BF16)

        total = total + dot(att_out[...].T, weight[columns:])
    if not last:
        first_out[...] = total
        return
    normed_out, inv_out = refs[7:9]
    normed, inv_std = normalize(total)
    normed_out[...] = normed
    inv_out[...] = inv_std
    first_out[...] = normed * line_of(lines, GAIN1) + line_of(lines, SHIFT1)


def sds(shape, dtype):
    return jax.ShapeDtypeStruct(shape, dtype)


def params(mib):
    return pltpu.CompilerParams(vmem_limit_bytes=mib << 20)


def kernel(body, deps, mib, *, in_specs, **kw):
    n = len(deps)
    call = pl.pallas_call(
        lambda *refs: body(*refs[n:]),
        in_specs=[ANY] * n + in_specs,
        compiler_params=params(mib),
        **kw,
    )
    return functools.partial(call, *deps)


def sync(name, meta, joins, carries, deps):
    sides = [j[0] if isinstance(j[0], int) else None for j in joins]
    parts = [j[1:] if isinstance(j[0], int) else j for j in joins]
    parts = [[p if isinstance(p, tuple) else (p, 0, p.shape[0]) for p in j] for j in parts]
    flat = [p[0] for j in parts for p in j]

    def body(meta_ref, *refs):
        refs = refs[len(carries) :]
        sources, outs = list(refs[: len(flat)]), refs[len(flat) : len(flat) + len(parts)]
        for side, join, out in zip(sides, parts, outs):
            row = 0
            for i, (_, start, size) in enumerate(join):
                if side is not None:
                    n = len(join) // 2
                    row = pl.multiple_of(((meta_ref[side] ^ (i // n)) * n + i % n) * size, 16)
                out[pl.ds(row, size)] = sources.pop(0)[start : start + size]
                row = row + size

    joined = [sds((sum(p[2] for p in j), *j[0][0].shape[1:]), j[0][0].dtype) for j in parts]
    n_deps = len(deps)
    out = kernel(
        body,
        deps,
        16,
        in_specs=[SMEM] + [ANY] * len(carries) + [VMEM] * len(flat),
        out_specs=[VMEM] * len(joined) + [ANY] * len(carries),
        out_shape=joined + [sds(c.shape, c.dtype) for c in carries],
        input_output_aliases={n_deps + 1 + i: len(joined) + i for i in range(len(carries))},
        cost_estimate=cost(0),
        name=name,
    )(meta, *carries, *flat)
    return out


def in_hbm(array):
    return pltpu.with_memory_space_constraint(array, pltpu.HBM)


def cost(us):
    return pl.CostEstimate(flops=int(us * 1.1e9 * COST), bytes_accessed=1024, transcendentals=0)


def call_attend_forward(deps, columns, last, meta, lengths, tokens, before, lines, quarters):
    seq, width = tokens.shape
    heads = columns // (3 * HEAD_DIM)
    inner = heads * HEAD_DIM
    square, narrow = sds((seq, width), F32), sds((seq, 1), F32)
    place = pltpu.HBM
    out_shape = [
        place((columns, seq), BF16),
        place((inner, seq), BF16),
        place((heads, seq, seq), BF16),
    ] * 2 + [square] + [square, narrow] * last
    return kernel(
        functools.partial(attend_forward, columns, last),
        deps,
        ATTEND_MIB,
        in_specs=[SMEM, SMEM] + [VMEM] * 5,
        out_specs=[VMEM] * len(out_shape),
        out_shape=out_shape,
        scratch_shapes=[pltpu.VMEM((seq, seq), F32)],
        cost_estimate=cost(8),
        name="attend_forward",
    )(meta, lengths, tokens, before, lines, *quarters)


def ffn_forward(quarters, blocks, first, before, *refs):
    slope_out, sum_out = refs[-2:]

    def chunk(rows):
        low = first[rows].astype(BF16)
        total = before[rows]
        outs = list(refs[quarters:-2])
        for quarter in range(quarters):
            value, slope = gelu_both(dot(low, refs[quarter][...]))
            slope_out[quarter, rows] = slope.astype(BF16)
            value = value.astype(BF16)
            start = 0
            for _ in range(blocks):
                out = outs.pop(0)
                total = total + dot(value[:, start : start + out.shape[0]], out[...])
                start += out.shape[0]
        sum_out[rows] = total

    by_chunks(first.shape[0], chunk)


def call_ffn_forward(deps, first, before, in_quarters, out_quarters):
    seq, width = first.shape
    hidden = in_quarters[0].shape[1]
    quarters = len(in_quarters)
    return kernel(
        functools.partial(ffn_forward, quarters, len(out_quarters) // quarters),
        deps,
        FFN_MIB,
        in_specs=[VMEM] * (2 + quarters + len(out_quarters)),
        out_specs=[VMEM] * 2,
        out_shape=[sds((quarters, seq, hidden), BF16), sds((seq, width), F32)],
        cost_estimate=cost(5),
        name="ffn_forward",
    )(first, before, *in_quarters, *out_quarters)


def assemble(name, deps, meta, weights, tiles):
    n_mats = tiles[0][0].shape[0] // (2 * len(tiles[0][1]))
    rows, half = tiles[0][0].shape[1:]
    count = sum(2 * len(parts) for _, parts, _ in tiles)
    before = [] if weights is None else [weights]

    def body(meta_ref, *refs):
        refs = refs[len(before) :]
        out, sems = refs[-2:]
        copies = []
        for ref, (_, parts, core_rel) in zip(refs, tiles):
            side = pl.multiple_of((meta_ref[CORE] ^ core_rel) * half, LANES)
            for j, (y_rel, z_rel) in enumerate(parts):
                for x_rel in range(2):
                    chip = ((meta_ref[DEPTH] ^ z_rel) * 2 + (meta_ref[PAIR_Y] ^ y_rel)) * 2
                    chip = chip + (meta_ref[ACROSS] ^ x_rel)
                    first = pl.multiple_of(chip * rows, 16)
                    target = out.at[:, pl.ds(first, rows), pl.ds(side, half)]
                    source = ref.at[pl.ds((2 * j + x_rel) * n_mats, n_mats)]
                    copies.append(pltpu.make_async_copy(source, target, sems.at[len(copies)]))
        for copy in copies:
            copy.start()
        for copy in copies:
            copy.wait()

    return kernel(
        body,
        deps,
        16,
        in_specs=[SMEM] + [ANY] * len(before) + [VMEM] * len(tiles),
        out_specs=ANY,
        out_shape=sds((n_mats, 2 * half, 2 * half), BF16),
        input_output_aliases={len(deps) + 1: 0} if before else {},
        scratch_shapes=[pltpu.SemaphoreType.DMA((count,))],
        cost_estimate=cost(0),
        name=name,
    )(meta, *before, *(tile for tile, _, _ in tiles))


def split_lines(total):
    high = total.astype(BF16).astype(F32)
    return jnp.concatenate([high, total - high], axis=0)


def merging(n_adapters, meta, lengths, sums, lines, out_grad, matrices, *refs):
    layer_out, part_out, fquery_out, middle_out, keep_out, send_out = refs[:6]
    grads, sum_lines, states, probes, blends, values, fqueries = refs[6:]
    seq, width = sums.shape
    scale = width**-0.5
    down, up, query, key, value = (matrices.at[i] for i in range(5))
    gain2, shift2 = line_of(lines, GAIN2), line_of(lines, SHIFT2)
    gain3, shift3 = line_of(lines, GAIN3), line_of(lines, SHIFT3)
    spread = jnp.where(
        lax.broadcasted_iota(jnp.int32, (LANES, width), 0)
        == lax.broadcasted_iota(jnp.int32, (LANES, width), 1) // (width // n_adapters),
        1.0,
        0.0,
    ).astype(BF16)
    lane = lax.broadcasted_iota(jnp.int32, (1, LANES), 1)
    count = jnp.int32(0)
    for i in range(lengths.shape[1]):
        count = count + lengths[meta[ROW], i]
    sum_lines[...] = jnp.zeros_like(sum_lines)

    def by_adapter(terms):
        high = terms.astype(BF16)
        rest = (terms - high.astype(F32)).astype(BF16)
        return dot_last(high, spread) + dot_last(rest, spread)

    def chunk(rows):
        normed2, _ = normalize(sums[rows])
        second = normed2 * gain2 + shift2
        second_low = second.astype(BF16)
        states[rows] = second_low
        act, slope = (v.astype(BF16) for v in gelu_both(dot(second_low, down[...])))
        fquery = dot(second_low, query[...]).astype(BF16)
        fqueries[rows] = fquery
        probe = dot_last(fquery, key[...]).astype(BF16)
        probe_up = dot(probe, up[...])
        logits = scale * (
            jnp.sum(probe.astype(F32) * second, axis=1, keepdims=True)
            + by_adapter(act * probe_up)
        )
        logits = jnp.where(lane < n_adapters, logits, BIG_NEGATIVE)
        exponent = jnp.exp(logits - jnp.max(logits, axis=1, keepdims=True))
        mix = exponent / jnp.sum(exponent, axis=1, keepdims=True)
        mix_low = mix.astype(BF16)
        mix_sum = jnp.sum(mix_low.astype(F32), axis=1, keepdims=True)
        mix_wide = dot(mix_low, spread).astype(BF16)
        blended = second * mix_sum + dot_last((mix_wide * act).astype(BF16), up[...])
        blended = blended.astype(BF16)
        blends[rows] = blended
        normed3, inv_std3 = normalize(second + dot(blended, value[...]))
        layer_out[rows] = normed3 * gain3 + shift3

        token = rows.start + lax.broadcasted_iota(jnp.int32, (rows.size, 1), 0)
        keep = jnp.where(token < count, 1.0, 0.0)
        cot = out_grad[rows].astype(F32) * keep
        mass = jnp.sum(mix * keep, axis=0, keepdims=True)
        mass = jnp.where(lane == n_adapters, jnp.sum(keep), mass)
        sum_lines[0:1] += jnp.sum(cot * normed3, axis=0, keepdims=True)
        sum_lines[1:2] += jnp.sum(cot, axis=0, keepdims=True)
        sum_lines[2:3, :LANES] += mass

        grad_pre = norm_back(cot * gain3, normed3, inv_std3)
        grad_proj = grad_pre.astype(BF16)
        values[rows] = grad_proj
        grad_blend = dot_last(grad_proj, value[...]).astype(BF16)
        blend_up = dot(grad_blend, up[...])
        grad_mix = jnp.sum(
            grad_blend.astype(F32) * second, axis=1, keepdims=True
        ) + by_adapter(act * blend_up)
        grad_logits = mix * (grad_mix - jnp.sum(grad_mix * mix, axis=1, keepdims=True))
        grad_logits = grad_logits.astype(BF16)
        logit_sum = jnp.sum(grad_logits.astype(F32), axis=1, keepdims=True)
        logit_wide = dot(grad_logits, spread).astype(BF16)
        grad_probe = second * logit_sum + dot_last((logit_wide * act).astype(BF16), up[...])
        grad_probe = (scale * grad_probe).astype(BF16)
        probes[rows] = grad_probe
        fquery_out[rows] = dot(grad_probe, key[...]).astype(BF16)
        grad_act = mix_wide.astype(F32) * blend_up + (scale * logit_wide.astype(F32)) * probe_up
        middle_out[rows] = (grad_act * slope.astype(F32)).astype(BF16)
        part_out[rows] = (
            grad_pre + grad_blend.astype(F32) * mix_sum + probe.astype(F32) * (scale * logit_sum)
        )

    by_chunks(seq, chunk, seq)

    @pl.loop(0, width // CHUNK)
    def _(i):
        part = pl.ds(pl.multiple_of(i * CHUNK, CHUNK), CHUNK)
        grads[0, part] = dot_first(states[:, part], fquery_out[...])
        grads[1, part] = dot_first(probes[:, part], fqueries[...])
        grads[2, part] = dot_first(blends[:, part], values[...])

    tail = split_lines(sum_lines[0:4])
    rows = width // 32

    @pl.loop(0, 16)
    def _(chip):
        z_rel = (chip // 4) ^ meta[DEPTH]
        y_rel = (chip // 2 % 2) ^ meta[PAIR_Y]
        x_rel = (chip % 2) ^ meta[ACROSS]
        for core_rel, out in ((0, keep_out), (1, send_out)):
            first = pl.multiple_of((chip * 2 + (meta[CORE] ^ core_rel)) * rows, 8)
            block = [grads[i, pl.ds(first, rows)] for i in range(3)] + [tail]
            out[x_rel, y_rel, z_rel] = jnp.concatenate(block, axis=0).astype(BF16)


def call_merging(n_adapters, meta, lengths, sums, lines, out_grad, matrices):
    seq, width = sums.shape
    block = 3 * width // 32 + 8
    return pl.pallas_call(
        functools.partial(merging, n_adapters),
        in_specs=[SMEM, SMEM] + [VMEM] * 4,
        out_specs=[VMEM] * 6,
        out_shape=[sds((seq, width), F32)] * 2
        + [sds((seq, width), BF16)] * 2
        + [sds((2, 2, 4, block, width), BF16)] * 2,
        scratch_shapes=[pltpu.VMEM((3, width, width), F32), pltpu.VMEM((8, width), F32)]
        + [pltpu.VMEM((seq, width), BF16)] * 5,
        compiler_params=params(MERGE_MIB),
        cost_estimate=cost(18),
        name="merging",
    )(meta, lengths, sums, lines, out_grad, matrices)


def merging_input(sums, lines, part, grad_fquery, grad_middle, matrices, grad_out, grad_low_out):
    def chunk(rows):
        normed, inv_std = normalize(sums[rows])
        grad = part[rows] + dot_last(grad_fquery[rows], matrices[2])
        grad = grad + dot_last(grad_middle[rows], matrices[0])
        grad = norm_back(grad * line_of(lines, GAIN2), normed, inv_std)
        grad_out[rows] = grad
        grad_low_out[rows] = grad.astype(BF16)

    by_chunks(part.shape[0], chunk)


def call_merging_input(deps, sums, lines, part, grad_fquery, grad_middle, matrices):
    return kernel(
        merging_input,
        deps,
        FFN_MIB,
        in_specs=[VMEM] * 6,
        out_specs=[VMEM] * 2,
        out_shape=[sds(part.shape, F32), sds(part.shape, BF16)],
        cost_estimate=cost(3),
        name="merging_input",
    )(sums, lines, part, grad_fquery, grad_middle, matrices)


def ffn_backward(last, blocks, n_slopes, grad_low, before, *refs):
    slopes, (in0, in1), refs = refs[:n_slopes], refs[n_slopes : n_slopes + 2], refs[n_slopes + 2 :]
    slopes = [slope.at[i] for slope in slopes for i in range(slope.shape[0])]
    all_outs, refs = refs[: 2 * blocks], refs[2 * blocks :]

    def chunk(rows):
        low = grad_low[rows]
        total = before[rows]
        outs = list(all_outs)
        for quarter, into in enumerate((in0, in1)):
            grad_act = [dot_last(low, outs.pop(0)[...]) for _ in range(blocks)]
            grad_act = grad_act[0] if blocks == 1 else jnp.concatenate(grad_act, axis=1)
            grad_pre = (grad_act * slopes[quarter][rows].astype(F32)).astype(BF16)
            total = total + dot_last(grad_pre, into[...])
        if not last:
            refs[0][rows] = total
            return
        normed1, inv_std1, lines, grad_out, grad_low_out = refs
        grad = norm_back(total * line_of(lines, GAIN1), normed1[rows], inv_std1[rows])
        grad_out[rows] = grad
        grad_low_out[rows] = grad.astype(BF16)

    by_chunks(before.shape[0], chunk)


def call_ffn_backward(deps, grad_low, before, slopes, in_quarters, out_quarters, *for_norm):
    seq, width = before.shape
    last = bool(for_norm)
    return kernel(
        functools.partial(ffn_backward, last, len(out_quarters) // 2, len(slopes)),
        deps,
        FFN_MIB,
        in_specs=[VMEM] * (4 + len(slopes) + len(out_quarters) + len(for_norm)),
        out_specs=[VMEM] * (1 + last),
        out_shape=[sds((seq, width), F32)] + [sds((seq, width), BF16)] * last,
        cost_estimate=cost(5),
        name="ffn_backward",
    )(grad_low, before, *slopes, *in_quarters, *out_quarters, *for_norm)


def attend_backward(
    columns, unroll, grad_low, before, turned_ref, att_ref, prob_ref, weight, input_grad, token, grad_turned, grad_att
):
    width = 3 * HEAD_DIM
    root = HEAD_DIM**-0.5
    grad_att[...] = dot_last(weight[columns:], grad_low[...]).astype(BF16)

    @pl.loop(0, columns // width, unroll=unroll)
    def _(head):
        base = pl.multiple_of(head * width, width)
        places = [pl.ds(base + i * HEAD_DIM, HEAD_DIM) for i in range(3)]
        queries, keys, values = (turned_ref[place] for place in places)
        part = pl.ds(pl.multiple_of(head * HEAD_DIM, HEAD_DIM), HEAD_DIM)
        grad = grad_att[part]
        prob = prob_ref[head]
        row_dot = jnp.sum(grad.astype(F32) * att_ref[part].astype(F32), axis=0, keepdims=True)
        grad_scores = (prob.astype(F32) * (dot(values.T, grad) - row_dot)).astype(BF16)
        grad_turned[places[0]] = (dot(keys, grad_scores) * root).astype(BF16)
        grad_turned[places[1]] = (dot_last(queries, grad_scores) * root).astype(BF16)
        grad_turned[places[2]] = dot_last(grad, prob).astype(BF16)

    input_grad[...] = before[...] + dot(grad_turned[...].T, weight[:columns])
    token[...] = jnp.zeros_like(token)


def call_attend_backward(deps, columns, unroll, grad_low, before, saved, quarter):
    seq, width = before.shape
    inner = columns // 3
    return kernel(
        functools.partial(attend_backward, columns, unroll),
        deps,
        ATTEND_MIB,
        in_specs=[VMEM] * 6,
        out_specs=[VMEM] * 2,
        out_shape=[sds((seq, width), F32), sds((8, LANES), F32)],
        scratch_shapes=[pltpu.VMEM((columns, seq), BF16), pltpu.VMEM((inner, seq), BF16)],
        cost_estimate=cost(8),
        name="attend_backward",
    )(grad_low, before, *saved, quarter)


def prepare(meta, down, up, query, key, value, g1, s1, g2, s2, g3, s3, keep, send, lines, shard):
    n_adapters, _, rank = down.shape
    for i in range(n_adapters):
        shard[0, :, i * rank : (i + 1) * rank] = down[i].astype(F32)
        shard[1, :, i * rank : (i + 1) * rank] = up[i].astype(F32)
    for i, ref in enumerate((query, key, value)):
        shard[2 + i] = ref[...].astype(F32)
    half = keep.shape[2]
    mine = pl.multiple_of(meta[CORE] * half, LANES)
    other = pl.multiple_of((1 - meta[CORE]) * half, LANES)
    keep[...] = shard[:, :, pl.ds(mine, half)].astype(BF16)
    send[...] = shard[:, :, pl.ds(other, half)].astype(BF16)
    for i, ref in enumerate((g1, s1, g2, s2, g3, s3)):
        lines[i : i + 1] = ref[...].reshape(1, -1)
    lines[6:8] = jnp.zeros((2, lines.shape[1]), F32)


def call_prepare(meta, down, up, query, key, value, *vectors):
    rows, width = query.shape
    half = sds((5, rows, width // 2), BF16)
    return pl.pallas_call(
        prepare,
        in_specs=[SMEM] + [VMEM] * 11,
        out_specs=[VMEM] * 3,
        out_shape=[half, half, sds((8, width), F32)],
        scratch_shapes=[pltpu.VMEM((5, rows, width), F32)],
        compiler_params=params(16),
        cost_estimate=cost(1),
        name="prepare",
    )(meta, *(in_hbm(a) for a in (down, up, query, key, value, *vectors)))


def join_attention(qkv_turned, attn_out, attn):
    columns = qkv_turned.shape[0]
    attn[:columns] = qkv_turned[...]
    attn[columns:] = attn_out[...]


def call_join_attention(deps, qkv_turned, attn_out):
    rows, width = qkv_turned.shape[0] + attn_out.shape[0], attn_out.shape[1]
    return kernel(
        join_attention,
        deps,
        16,
        in_specs=[VMEM] * 2,
        out_specs=VMEM,
        out_shape=sds((rows, width), BF16),
        cost_estimate=cost(1),
        name="join_attention",
    )(in_hbm(qkv_turned), in_hbm(attn_out))


def prepare_shares(meta, attn, into, out, with_attn, with_in, out_last, *copies):
    half = attn.shape[0] // 2
    more = half // 3
    mine = pl.multiple_of(meta[PAIR_Y] * half, 16)
    other = pl.multiple_of((1 - meta[PAIR_Y]) * half + 2 * more, 16)
    with_attn[:half] = attn[pl.ds(mine, half)]
    with_attn[half : half + more] = attn[pl.ds(other, more)]
    cut = with_attn.shape[0] - half - more
    with_attn[half + more :] = out[:cut]
    half = into.shape[0] // 2
    with_in[:half] = into[pl.ds(pl.multiple_of(meta[PAIR_Z] * half, 16), half)]
    end = cut + with_in.shape[0] - half
    with_in[half:] = out[cut:end]
    out_last[...] = out[end:]
    for source, copy in zip((into, out), copies):
        copy[...] = source[...]


def call_prepare_shares(deps, meta, attn, into, out):
    rows, width = attn.shape
    unit = out.shape[0] // 12
    shares = (rows // 2 + rows // 6 + unit, into.shape[0] // 2 + 3 * unit, 8 * unit)
    shares = shares + (into.shape[0], out.shape[0])
    return kernel(
        prepare_shares,
        deps,
        16,
        in_specs=[SMEM] + [VMEM] * 3,
        out_specs=[VMEM] * 5,
        out_shape=[sds((n, width), BF16) for n in shares],
        cost_estimate=cost(1),
        name="prepare_shares",
    )(meta, attn, in_hbm(into), in_hbm(out))


def chip_tile(meta, keep, got, attn, tile, attn_out):
    mine, other = keep[...].astype(F32), got[...].astype(F32)
    lower = jnp.where(meta[CORE] == 0, mine, other)
    upper = jnp.where(meta[CORE] == 0, other, mine)
    tile[...] = jnp.concatenate([lower, upper], axis=1).astype(BF16)


def call_chip_tile(meta, keep, got, attn):
    n_mats, rows, half = keep.shape
    return kernel(
        chip_tile,
        [],
        16,
        in_specs=[SMEM] + [VMEM] * 2 + [ANY],
        out_specs=[VMEM, ANY],
        out_shape=[sds((n_mats, 2 * rows, half), BF16), sds(attn.shape, attn.dtype)],
        input_output_aliases={3: 1},
        cost_estimate=cost(1),
        name="chip_tile",
    )(meta, keep, got, attn)


def add_blocks(*blocks):
    total = functools.reduce(jnp.add, (b.astype(F32) for b in blocks))
    tail = total[-8:-4] + total[-4:]
    return jnp.concatenate([total[:-8], split_lines(tail)], axis=0)


def sum_cores(keep, got, p_keep, p_send, q_keep, q_send):
    half = p_keep.shape[-1]
    for x in range(2):
        for y in range(2):

            @pl.loop(0, 4)
            def _(z, x=x, y=y):
                total = add_blocks(keep[x, y, z], got[x, y, z]).astype(BF16)
                (p_send if x else p_keep)[y, z] = total[:, :half]
                (q_send if y else q_keep)[x, z] = total[:, half:]


def sum_first(p_keep, p_got, q_keep, q_got, p2_keep, p2_send, q2_keep, q2_send):
    @pl.loop(0, 4)
    def _(z):
        for out, index in ((p2_keep, 0), (p2_send, 1)):
            out[z] = add_blocks(p_keep[index, z], p_got[index, z]).astype(BF16)
        for out, index in ((q2_keep, 0), (q2_send, 1)):
            out[z] = add_blocks(q_keep[index, z], q_got[index, z]).astype(BF16)


def sum_second(p_keep, p_got, q_keep, q_got, *outs):
    half = p_keep.shape[-1]
    for z in range(4):
        outs[z][:, :half] = add_blocks(p_keep[z], p_got[z]).astype(BF16)
        outs[z][:, half:] = add_blocks(q_keep[z], q_got[z]).astype(BF16)


def sum_last(n_adapters, keep, got1, got2, got3, query, key, value, gain, bias, mass):
    total = add_blocks(keep[...], got1[...], got2[...], got3[...])
    rows = query.shape[0]
    for i, out in enumerate((query, key, value)):
        out[...] = total[i * rows : (i + 1) * rows]
    lines = total[-8:-4] + total[-4:]
    gain[...] = lines[0]
    bias[...] = lines[1]
    mass[...] = lines[2, :n_adapters] / lines[2:3, n_adapters : n_adapters + 1].reshape(1)


def small_call(body, name, out_shape, dep, *operands):
    return kernel(
        body,
        (dep,),
        16,
        in_specs=[VMEM] * len(operands),
        out_specs=[VMEM] * len(out_shape),
        out_shape=out_shape,
        cost_estimate=cost(1),
        name=name,
    )(*operands)


def sum_gradients(hops, keep, send, n_adapters, works):
    block, width = keep.shape[3:]
    half = width // 2
    pair = [sds((2, 4, block, half), BF16)] * 4
    single = [sds((4, block, half), BF16)] * 4
    got = hops.flip(send, 1)
    dep = works[0](())
    pk, ps, qk, qs = small_call(sum_cores, "sum_cores", pair, dep, keep, got)
    pg, qg = hops.flip(ps, ALONG_X), hops.flip(qs, ALONG_Y)
    dep = works[1]([pk])
    pk, ps, qk, qs = small_call(sum_first, "sum_first", single, dep, pk, pg, qk, qg)
    pg, qg = hops.flip(ps, ALONG_Y), hops.flip(qs, ALONG_X)
    dep = works[2]([pk])
    parts = small_call(
        sum_second, "sum_second", [sds((block, width), BF16)] * 4, dep, pk, pg, qk, qg
    )
    got = [hops.flip(part, z * ALONG_Z) for z, part in enumerate(parts) if z]
    dep = works[3]([parts[0]])
    rows = (block - 8) // 3
    outs = [sds((rows, width), F32)] * 3 + [sds((width,), F32)] * 2 + [sds((n_adapters,), F32)]
    last = functools.partial(sum_last, n_adapters)
    return small_call(last, "sum_last", outs, dep, parts[0], *got)


ALONG_X, ALONG_Y, ALONG_Z = 2, 4, 8


class Hops:
    def __init__(self, mesh):
        self.count = mesh.size
        self.tiled = mesh.shape["dp"] == 8 and mesh.shape["tensor"] == 4

    def flip(self, array, bits):
        return lax.ppermute(array, AXES, [(i, i ^ bits) for i in range(self.count)])


def half_of(block, parity):
    half = block.shape[0] // 2
    return lax.dynamic_slice_in_dim(block, parity * half, half, 0)


def plain_schedule(
    meta, doc_lengths, tokens, out_grad, lines, columns, n_adapters, attn, into, out, shard
):
    attn, into, out = (lax.all_gather(w, "tensor", axis=0) for w in (attn, into, out))
    weights = lax.all_gather(shard, AXES, axis=1, tiled=True)
    pairs = [slice(i, i + 2) for i in range(0, attn.shape[0], 2)]
    before, saved, slopes = tokens, [], []
    for pair in pairs:
        last = pair is pairs[-1]
        results = call_attend_forward(
            [], columns, last, meta, doc_lengths, tokens, before, lines, tuple(attn[pair])
        )
        saved += [results[:3], results[3:6]]
        before = results[6]
    first, normed1, inv_std1 = results[6:]
    sums = first
    for pair in pairs:
        slope, sums = call_ffn_forward([], first, sums, tuple(into[pair]), tuple(out[pair]))
        slopes.append(slope)
    layer_out, *parts, keep, send = call_merging(
        n_adapters, meta, doc_lengths, sums, lines, out_grad, weights
    )
    total, low = call_merging_input([], sums, lines, *parts, weights)
    width = tokens.shape[1]
    blocks = jnp.transpose(jnp.stack([keep, send]), (3, 2, 1, 0, 4, 5)).reshape(32, -1, width)
    squares = blocks[:, :-8].reshape(32, 3, width // 32, width)
    squares = jnp.transpose(squares, (1, 0, 2, 3)).reshape(3, width, width).astype(F32)
    squares = lax.psum_scatter(squares, AXES, scatter_dimension=1, tiled=True)
    tail = blocks[0, -8:].astype(F32)
    totals = lax.psum(tail[:4] + tail[4:], AXES)
    for pair, slope in zip(pairs, slopes):
        for_norm = (normed1, inv_std1, lines) if pair is pairs[-1] else ()
        total, *rest = call_ffn_backward(
            [], low, total, [slope], tuple(into[pair]), tuple(out[pair]), *for_norm
        )
    (low,) = rest
    for quarter, kept in zip(attn, saved):
        total, _ = call_attend_backward([], columns, False, low, total, kept, quarter)
    mass = totals[2, :n_adapters] / totals[2, n_adapters]
    return (layer_out, total, squares[0], squares[1], squares[2], totals[0], totals[1], mass)


def per_device(
    hops,
    tokens,
    doc_lengths,
    qkv_weight,
    attn_out_weight,
    norm1_gain,
    norm1_bias,
    ffn_in_weight,
    ffn_out_weight,
    norm2_gain,
    norm2_bias,
    adapter_down,
    adapter_up,
    merging_query,
    merging_key,
    merging_value,
    merging_gain,
    merging_bias,
    out_grad,
):
    n_adapters, rows, rank = adapter_down.shape
    columns = qkv_weight.shape[1]
    tensor, dp = lax.axis_index("tensor"), lax.axis_index("dp")
    pair_y, pair_z = dp % 2, dp // 2 % 2
    meta = jnp.stack([tensor % 2, tensor // 2, pair_y, pair_z, dp // 2, tensor]).astype(jnp.int32)
    flip = hops.flip
    if not hops.tiled:
        meta = meta * (jnp.arange(meta.shape[0]) == ROW)

    keep, send, lines = call_prepare(
        meta,
        adapter_down,
        jnp.transpose(adapter_up, (0, 2, 1)),
        merging_query,
        merging_key,
        merging_value,
        norm1_gain,
        norm1_bias,
        norm2_gain,
        norm2_bias,
        merging_gain,
        merging_bias,
    )
    attn = call_join_attention([keep], qkv_weight.T, attn_out_weight)
    if not hops.tiled:
        shard = jnp.concatenate([keep, send], axis=2)
        return plain_schedule(
            meta, doc_lengths, tokens, out_grad, lines, columns, n_adapters, attn, ffn_in_weight, ffn_out_weight, shard
        )
    tile, attn = call_chip_tile(meta, keep, flip(send, 1), attn)
    with_attn, with_in, out_2, into, out = call_prepare_shares(
        [], meta, attn, ffn_in_weight, ffn_out_weight
    )
    tile_x = flip(tile, ALONG_X)
    attn_core = flip(attn, 1)
    both, with_attn, into, out = sync(
        "phase1", meta, [[tile, tile_x]], [with_attn, into, out], [attn_core]
    )
    z2, y0, with_attn_x = flip(both, 2 * ALONG_Z), flip(both, ALONG_Y), flip(with_attn, ALONG_X)
    in_core, out_core = flip(into, 1), flip(out, 1)
    saved_near = call_attend_forward(
        [both], columns, False, meta, doc_lengths, tokens, tokens, lines, (attn, attn_core)
    )
    half = attn.shape[0] // 2
    third = half // 3
    joined, attn_x, with_in, y0, z2 = sync(
        "phase2",
        meta,
        [[both, z2], [(with_attn_x, 0, 2 * third)]],
        [with_in, y0, z2],
        [saved_near[6], in_core, out_core],
    )
    with_in_x, attn_y, z1 = flip(with_in, ALONG_X), flip(attn_x, ALONG_Y), flip(joined, ALONG_Z)
    y2 = flip(z2, ALONG_Y)
    joined_c, y0_c = flip(joined, 1), flip(y0, 1)
    attn_far, in_x, out_a, out_2, z1, y2 = sync(
        "phase3",
        meta,
        [
            [PAIR_Y]
            + [(with_attn_x, i * third, third) for i in range(3)]
            + [(attn_y, 0, third), (attn_y, third, third), (with_attn_x, half, third)],
            [(with_in_x, 0, half)],
            [
                (share, start, share.shape[0] - start)
                for share, start in ((with_attn_x, half + third), (with_in_x, half))
            ],
        ],
        [out_2, z1, y2],
        [joined_c, y0_c],
    )
    attn_far_c = flip(attn_far, 1)
    y1, out_b, in_z = flip(z1, ALONG_Y), flip(out_2, ALONG_X), flip(in_x, ALONG_Z)
    z1_c, y2_c, out_a_c = flip(z1, 1), flip(y2, 1), flip(out_a, 1)
    *saved_far, first, normed1, inv_std1 = call_attend_forward(
        [], columns, True, meta, doc_lengths, tokens, saved_near[6], lines, (attn_far, attn_far_c)
    )
    slope_near, sums = call_ffn_forward(
        [], first, first, (ffn_in_weight, in_core), (ffn_out_weight, out_core)
    )
    own, other = 0, 1
    weights = assemble(
        "assemble",
        [first],
        meta,
        None,
        [
            (joined, ((0, 0), (0, 2)), own),
            (joined_c, ((0, 0), (0, 2)), other),
            (z1, ((0, 1), (0, 3)), own),
            (z1_c, ((0, 1), (0, 3)), other),
            (y0, ((1, 0),), own),
            (y0_c, ((1, 0),), other),
            (y2, ((1, 2),), own),
            (y2_c, ((1, 2),), other),
        ],
    )
    in_far, out_b, y1 = sync(
        "phase4", meta, [[PAIR_Z, in_x, in_z]], [out_b, y1], [sums, weights, out_a_c]
    )
    in_far_c, out_b_c, y1_c = flip(in_far, 1), flip(out_b, 1), flip(y1, 1)
    out_far = (out_a, out_b, out_a_c, out_b_c)
    slopes_far = []
    for quarter, blocks in ((in_far, out_far[:2]), (in_far_c, out_far[2:])):
        slope, sums = call_ffn_forward([], first, sums, (quarter,), blocks)
        slopes_far.append(slope)
    last_parts = ((1, 1), (1, 3))
    weights = assemble(
        "assemble_last", [sums], meta, weights, [(y1, last_parts, own), (y1_c, last_parts, other)]
    )
    layer_out, *parts, grad_keep, grad_send = call_merging(
        n_adapters, meta, doc_lengths, sums, lines, out_grad, weights
    )
    done = {}
    attn_quarters = (attn, attn_core, attn_far, attn_far_c)
    saved = (saved_near[:3], saved_near[3:6], saved_far[:3], saved_far[3:6])

    def attention(deps, *quarters):
        for i in quarters:
            done["sum"], token = call_attend_backward(
                deps, columns, i > 1, done["low"], done["sum"], saved[i], attn_quarters[i]
            )
        return token

    def near(deps):
        (done["sum"],) = call_ffn_backward(
            deps,
            done["low"],
            done["sum"],
            [slope_near],
            (ffn_in_weight, in_core),
            (ffn_out_weight, out_core),
        )
        return done["sum"]

    def far(deps):
        done["sum"], done["low"] = call_ffn_backward(
            deps,
            done["low"],
            done["sum"],
            slopes_far,
            (in_far, in_far_c),
            out_far,
            normed1,
            inv_std1,
            lines,
        )

    def first_work(deps):
        done["sum"], done["low"] = call_merging_input(deps, sums, lines, *parts, weights)
        return done["sum"]

    def second_work(deps):
        near(deps)
        far([])
        return attention([], 0)

    works = (
        first_work,
        second_work,
        lambda deps: attention(deps, 1),
        lambda deps: attention(deps, 2, 3),
    )
    summed = sum_gradients(hops, grad_keep, grad_send, n_adapters, works)
    return (layer_out, done["sum"], *summed)


def solution(mesh):
    split = P(AXES, None)
    in_specs = (
        split,
        P("dp", None),
        P(None, "tensor"),
        P("tensor", None),
        P(),
        P(),
        P(None, "tensor"),
        P("tensor", None),
        P(),
        P(),
        P(None, AXES, None),
        P(None, None, AXES),
        split,
        split,
        split,
        P(),
        P(),
        split,
    )
    out_specs = (split, split, split, split, split, P(), P(), P())
    return jax.shard_map(
        functools.partial(per_device, Hops(mesh)),
        mesh=mesh,
        in_specs=in_specs,
        out_specs=out_specs,
        check_vma=False,
    )
```

```python
import functools

import jax
import jax.numpy as jnp
from jax import lax
from jax.experimental import pallas as pl
from jax.experimental.pallas import tpu as pltpu
from jax.sharding import PartitionSpec as P

HEAD_DIM = 64
AXES = ("dp", "tensor")
ATTEND_MIB, FFN_MIB, MERGE_MIB = 16, 16, 24
LANES = 128
COST = 0.0
CHUNK = 256
EPS = 1e-12
BIG_NEGATIVE = -1e30
ROOT_HALF = 0.7071067811865476
ROOT_TAU = 0.3989422804014327
F32, BF16 = jnp.float32, jnp.bfloat16

CORE, ACROSS, PAIR_Y, PAIR_Z, DEPTH, ROW = range(6)
GAIN1, SHIFT1, GAIN2, SHIFT2, GAIN3, SHIFT3 = range(6)

SMEM = pl.BlockSpec(memory_space=pltpu.SMEM)
VMEM = pl.BlockSpec(memory_space=pltpu.VMEM)
ANY = pl.BlockSpec(memory_space=pl.ANY)
HBM = pl.BlockSpec(memory_space=pltpu.HBM)


def by_chunks(count, body, size=CHUNK):
    @pl.loop(0, count // size)
    def _(i):
        body(pl.ds(pl.multiple_of(i * size, size), size))


def line_of(lines, i):
    return lines[i : i + 1]


def dot(a, b):
    return lax.dot_general(a, b, (((1,), (0,)), ((), ())), preferred_element_type=F32)


def dot_last(a, b):
    return lax.dot_general(a, b, (((1,), (1,)), ((), ())), preferred_element_type=F32)


def dot_first(a, b):
    return lax.dot_general(a, b, (((0,), (0,)), ((), ())), preferred_element_type=F32)


def normalize(u):
    centered = u - jnp.mean(u, axis=-1, keepdims=True)
    inv_std = lax.rsqrt(jnp.mean(centered * centered, axis=-1, keepdims=True) + EPS)
    return centered * inv_std, inv_std


def norm_back(grad, normed, inv_std):
    return inv_std * (
        grad
        - jnp.mean(grad, axis=-1, keepdims=True)
        - normed * jnp.mean(grad * normed, axis=-1, keepdims=True)
    )


def gelu_both(u):
    half = 0.5 * (1.0 + lax.erf(u * ROOT_HALF))
    return u * half, half + u * jnp.exp(-0.5 * u * u) * ROOT_TAU


def segment_bias(meta_ref, lengths_ref, bias_ref):
    seq = bias_ref.shape[0]
    row = meta_ref[ROW]
    by_row = lax.broadcasted_iota(jnp.int32, (seq, 1), 0)
    by_lane = lax.broadcasted_iota(jnp.int32, (1, seq), 1)
    seg_row = jnp.zeros((seq, 1), jnp.int32)
    seg_lane = jnp.zeros((1, seq), jnp.int32)
    end = jnp.int32(0)
    for i in range(lengths_ref.shape[1]):
        end = end + lengths_ref[row, i]
        seg_row = seg_row + jnp.where(by_row >= end, 1, 0)
        seg_lane = seg_lane + jnp.where(by_lane >= end, 1, 0)
    bias_ref[...] = jnp.where(seg_row == seg_lane, 0.0, BIG_NEGATIVE).astype(F32)


def attend_forward(columns, last, meta, lengths, tokens, before, lines, weight0, weight1, *refs):
    saved, first_out, bias = refs[:6], refs[6], refs[-1]
    segment_bias(meta, lengths, bias)
    total = before[...].astype(F32)
    width = 3 * HEAD_DIM
    for quarter, weight in enumerate((weight0, weight1)):
        turned = dot_last(weight[:columns], tokens[...]).astype(BF16)
        turned_out, att_out, prob_out = saved[3 * quarter : 3 * quarter + 3]
        turned_out[...] = turned

        @pl.loop(0, columns // width)
        def _(head, turned_out=turned_out, att_out=att_out, prob_out=prob_out):
            base = pl.multiple_of(head * width, width)
            queries, keys, values = (
                turned_out[pl.ds(base + i * HEAD_DIM, HEAD_DIM)] for i in range(3)
            )
            scores = dot(keys.T, queries * BF16(HEAD_DIM**-0.5)) + bias[...]
            exponent = jnp.exp(scores - jnp.max(scores, axis=0, keepdims=True))
            prob = (exponent * (1.0 / jnp.sum(exponent, axis=0, keepdims=True))).astype(BF16)
            prob_out[head] = prob
            part = pl.ds(pl.multiple_of(head * HEAD_DIM, HEAD_DIM), HEAD_DIM)
            att_out[part] = dot(values, prob).astype(BF16)

        total = total + dot(att_out[...].T, weight[columns:])
    if not last:
        first_out[...] = total
        return
    normed_out, inv_out = refs[7:9]
    normed, inv_std = normalize(total)
    normed_out[...] = normed
    inv_out[...] = inv_std
    first_out[...] = normed * line_of(lines, GAIN1) + line_of(lines, SHIFT1)


def sds(shape, dtype):
    return jax.ShapeDtypeStruct(shape, dtype)


def params(mib):
    return pltpu.CompilerParams(vmem_limit_bytes=mib << 20)


def kernel(body, deps, mib, *, in_specs, **kw):
    n = len(deps)
    call = pl.pallas_call(
        lambda *refs: body(*refs[n:]),
        in_specs=[ANY] * n + in_specs,
        compiler_params=params(mib),
        **kw,
    )
    return functools.partial(call, *deps)


def sync(name, meta, joins, carries, deps):
    sides = [j[0] if isinstance(j[0], int) else None for j in joins]
    parts = [j[1:] if isinstance(j[0], int) else j for j in joins]
    parts = [[p if isinstance(p, tuple) else (p, 0, p.shape[0]) for p in j] for j in parts]
    flat = [p[0] for j in parts for p in j]

    def body(meta_ref, *refs):
        refs = refs[len(carries) :]
        sources, outs = list(refs[: len(flat)]), refs[len(flat) : len(flat) + len(parts)]
        for side, join, out in zip(sides, parts, outs):
            row = 0
            for i, (_, start, size) in enumerate(join):
                if side is not None:
                    n = len(join) // 2
                    row = pl.multiple_of(((meta_ref[side] ^ (i // n)) * n + i % n) * size, 16)
                out[pl.ds(row, size)] = sources.pop(0)[start : start + size]
                row = row + size

    joined = [sds((sum(p[2] for p in j), *j[0][0].shape[1:]), j[0][0].dtype) for j in parts]
    n_deps = len(deps)
    out = kernel(
        body,
        deps,
        16,
        in_specs=[SMEM] + [ANY] * len(carries) + [VMEM] * len(flat),
        out_specs=[VMEM] * len(joined) + [ANY] * len(carries),
        out_shape=joined + [sds(c.shape, c.dtype) for c in carries],
        input_output_aliases={n_deps + 1 + i: len(joined) + i for i in range(len(carries))},
        cost_estimate=cost(0),
        name=name,
    )(meta, *carries, *flat)
    return out


def in_hbm(array):
    return pltpu.with_memory_space_constraint(array, pltpu.HBM)


def cost(us):
    return pl.CostEstimate(flops=int(us * 1.1e9 * COST), bytes_accessed=1024, transcendentals=0)


def call_attend_forward(deps, columns, last, meta, lengths, tokens, before, lines, quarters):
    seq, width = tokens.shape
    heads = columns // (3 * HEAD_DIM)
    inner = heads * HEAD_DIM
    square, narrow = sds((seq, width), F32), sds((seq, 1), F32)
    place = pltpu.HBM
    out_shape = [
        place((columns, seq), BF16),
        place((inner, seq), BF16),
        place((heads, seq, seq), BF16),
    ] * 2 + [square] + [square, narrow] * last
    return kernel(
        functools.partial(attend_forward, columns, last),
        deps,
        ATTEND_MIB,
        in_specs=[SMEM, SMEM] + [VMEM] * 5,
        out_specs=[VMEM] * len(out_shape),
        out_shape=out_shape,
        scratch_shapes=[pltpu.VMEM((seq, seq), F32)],
        cost_estimate=cost(8),
        name="attend_forward",
    )(meta, lengths, tokens, before, lines, *quarters)


def ffn_forward(quarters, blocks, first, before, *refs):
    slope_out, sum_out = refs[-2:]

    def chunk(rows):
        low = first[rows].astype(BF16)
        total = before[rows]
        outs = list(refs[quarters:-2])
        for quarter in range(quarters):
            value, slope = gelu_both(dot(low, refs[quarter][...]))
            slope_out[quarter, rows] = slope.astype(BF16)
            value = value.astype(BF16)
            start = 0
            for _ in range(blocks):
                out = outs.pop(0)
                total = total + dot(value[:, start : start + out.shape[0]], out[...])
                start += out.shape[0]
        sum_out[rows] = total

    by_chunks(first.shape[0], chunk)


def call_ffn_forward(deps, first, before, in_quarters, out_quarters):
    seq, width = first.shape
    hidden = in_quarters[0].shape[1]
    quarters = len(in_quarters)
    return kernel(
        functools.partial(ffn_forward, quarters, len(out_quarters) // quarters),
        deps,
        FFN_MIB,
        in_specs=[VMEM] * (2 + quarters + len(out_quarters)),
        out_specs=[VMEM] * 2,
        out_shape=[sds((quarters, seq, hidden), BF16), sds((seq, width), F32)],
        cost_estimate=cost(5),
        name="ffn_forward",
    )(first, before, *in_quarters, *out_quarters)


def assemble(name, deps, meta, weights, tiles):
    n_mats = tiles[0][0].shape[0] // (2 * len(tiles[0][1]))
    rows, half = tiles[0][0].shape[1:]
    count = sum(2 * len(parts) for _, parts, _ in tiles)
    before = [] if weights is None else [weights]

    def body(meta_ref, *refs):
        refs = refs[len(before) :]
        out, sems = refs[-2:]
        copies = []
        for ref, (_, parts, core_rel) in zip(refs, tiles):
            side = pl.multiple_of((meta_ref[CORE] ^ core_rel) * half, LANES)
            for j, (y_rel, z_rel) in enumerate(parts):
                for x_rel in range(2):
                    chip = ((meta_ref[DEPTH] ^ z_rel) * 2 + (meta_ref[PAIR_Y] ^ y_rel)) * 2
                    chip = chip + (meta_ref[ACROSS] ^ x_rel)
                    first = pl.multiple_of(chip * rows, 16)
                    target = out.at[:, pl.ds(first, rows), pl.ds(side, half)]
                    source = ref.at[pl.ds((2 * j + x_rel) * n_mats, n_mats)]
                    copies.append(pltpu.make_async_copy(source, target, sems.at[len(copies)]))
        for copy in copies:
            copy.start()
        for copy in copies:
            copy.wait()

    return kernel(
        body,
        deps,
        16,
        in_specs=[SMEM] + [ANY] * len(before) + [VMEM] * len(tiles),
        out_specs=ANY,
        out_shape=sds((n_mats, 2 * half, 2 * half), BF16),
        input_output_aliases={len(deps) + 1: 0} if before else {},
        scratch_shapes=[pltpu.SemaphoreType.DMA((count,))],
        cost_estimate=cost(0),
        name=name,
    )(meta, *before, *(tile for tile, _, _ in tiles))


def split_lines(total):
    high = total.astype(BF16).astype(F32)
    return jnp.concatenate([high, total - high], axis=0)


def merging(n_adapters, meta, lengths, sums, lines, out_grad, matrices, *refs):
    layer_out, part_out, fquery_out, middle_out, keep_out, send_out = refs[:6]
    grads, sum_lines, states, probes, blends, values, fqueries, joined, sem = refs[6:]
    leave = pltpu.make_async_copy(joined, layer_out, sem)
    seq, width = sums.shape
    scale = width**-0.5
    down, up, query, key, value = (matrices.at[i] for i in range(5))
    gain2, shift2 = line_of(lines, GAIN2), line_of(lines, SHIFT2)
    gain3, shift3 = line_of(lines, GAIN3), line_of(lines, SHIFT3)
    spread = jnp.where(
        lax.broadcasted_iota(jnp.int32, (LANES, width), 0)
        == lax.broadcasted_iota(jnp.int32, (LANES, width), 1) // (width // n_adapters),
        1.0,
        0.0,
    ).astype(BF16)
    lane = lax.broadcasted_iota(jnp.int32, (1, LANES), 1)
    count = jnp.int32(0)
    for i in range(lengths.shape[1]):
        count = count + lengths[meta[ROW], i]
    sum_lines[...] = jnp.zeros_like(sum_lines)

    def by_adapter(terms):
        high = terms.astype(BF16)
        rest = (terms - high.astype(F32)).astype(BF16)
        return dot_last(high, spread) + dot_last(rest, spread)

    def chunk(rows):
        normed2, _ = normalize(sums[rows])
        second = normed2 * gain2 + shift2
        second_low = second.astype(BF16)
        states[rows] = second_low
        act, slope = (v.astype(BF16) for v in gelu_both(dot(second_low, down[...])))
        fquery = dot(second_low, query[...]).astype(BF16)
        fqueries[rows] = fquery
        probe = dot_last(fquery, key[...]).astype(BF16)
        probe_up = dot(probe, up[...])
        logits = scale * (
            jnp.sum(probe.astype(F32) * second, axis=1, keepdims=True)
            + by_adapter(act * probe_up)
        )
        logits = jnp.where(lane < n_adapters, logits, BIG_NEGATIVE)
        exponent = jnp.exp(logits - jnp.max(logits, axis=1, keepdims=True))
        mix = exponent / jnp.sum(exponent, axis=1, keepdims=True)
        mix_low = mix.astype(BF16)
        mix_sum = jnp.sum(mix_low.astype(F32), axis=1, keepdims=True)
        mix_wide = dot(mix_low, spread).astype(BF16)
        blended = second * mix_sum + dot_last((mix_wide * act).astype(BF16), up[...])
        blended = blended.astype(BF16)
        blends[rows] = blended
        normed3, inv_std3 = normalize(second + dot(blended, value[...]))
        joined[...] = normed3 * gain3 + shift3
        leave.start()

        token = rows.start + lax.broadcasted_iota(jnp.int32, (rows.size, 1), 0)
        keep = jnp.where(token < count, 1.0, 0.0)
        cot = out_grad[rows].astype(F32) * keep
        mass = jnp.sum(mix * keep, axis=0, keepdims=True)
        mass = jnp.where(lane == n_adapters, jnp.sum(keep), mass)
        sum_lines[0:1] += jnp.sum(cot * normed3, axis=0, keepdims=True)
        sum_lines[1:2] += jnp.sum(cot, axis=0, keepdims=True)
        sum_lines[2:3, :LANES] += mass

        grad_pre = norm_back(cot * gain3, normed3, inv_std3)
        grad_proj = grad_pre.astype(BF16)
        values[rows] = grad_proj
        grad_blend = dot_last(grad_proj, value[...]).astype(BF16)
        blend_up = dot(grad_blend, up[...])
        grad_mix = jnp.sum(
            grad_blend.astype(F32) * second, axis=1, keepdims=True
        ) + by_adapter(act * blend_up)
        grad_logits = mix * (grad_mix - jnp.sum(grad_mix * mix, axis=1, keepdims=True))
        grad_logits = grad_logits.astype(BF16)
        logit_sum = jnp.sum(grad_logits.astype(F32), axis=1, keepdims=True)
        logit_wide = dot(grad_logits, spread).astype(BF16)
        grad_probe = second * logit_sum + dot_last((logit_wide * act).astype(BF16), up[...])
        grad_probe = (scale * grad_probe).astype(BF16)
        probes[rows] = grad_probe
        fquery_out[rows] = dot(grad_probe, key[...]).astype(BF16)
        grad_act = mix_wide.astype(F32) * blend_up + (scale * logit_wide.astype(F32)) * probe_up
        middle_out[rows] = (grad_act * slope.astype(F32)).astype(BF16)
        part_out[rows] = (
            grad_pre + grad_blend.astype(F32) * mix_sum + probe.astype(F32) * (scale * logit_sum)
        )

    by_chunks(seq, chunk, seq)

    @pl.loop(0, width // CHUNK)
    def _(i):
        part = pl.ds(pl.multiple_of(i * CHUNK, CHUNK), CHUNK)
        grads[0, part] = dot_first(states[:, part], fquery_out[...])
        grads[1, part] = dot_first(probes[:, part], fqueries[...])
        grads[2, part] = dot_first(blends[:, part], values[...])

    tail = split_lines(sum_lines[0:4])
    rows = width // 32

    @pl.loop(0, 16)
    def _(chip):
        z_rel = (chip // 4) ^ meta[DEPTH]
        y_rel = (chip // 2 % 2) ^ meta[PAIR_Y]
        x_rel = (chip % 2) ^ meta[ACROSS]
        for core_rel, out in ((0, keep_out), (1, send_out)):
            first = pl.multiple_of((chip * 2 + (meta[CORE] ^ core_rel)) * rows, 8)
            block = [grads[i, pl.ds(first, rows)] for i in range(3)] + [tail]
            out[x_rel, y_rel, z_rel] = jnp.concatenate(block, axis=0).astype(BF16)

    leave.wait()


def call_merging(n_adapters, meta, lengths, sums, lines, out_grad, matrices):
    seq, width = sums.shape
    block = 3 * width // 32 + 8
    return pl.pallas_call(
        functools.partial(merging, n_adapters),
        in_specs=[SMEM, SMEM] + [VMEM] * 4,
        out_specs=[ANY] + [VMEM] * 5,
        out_shape=[sds((seq, width), F32)] * 2
        + [sds((seq, width), BF16)] * 2
        + [sds((2, 2, 4, block, width), BF16)] * 2,
        scratch_shapes=[pltpu.VMEM((3, width, width), F32), pltpu.VMEM((8, width), F32)]
        + [pltpu.VMEM((seq, width), BF16)] * 5
        + [pltpu.VMEM((seq, width), F32), pltpu.SemaphoreType.DMA],
        compiler_params=params(MERGE_MIB),
        cost_estimate=cost(18),
        name="merging",
    )(meta, lengths, sums, lines, out_grad, matrices)


def merging_input(sums, lines, part, grad_fquery, grad_middle, matrices, grad_out, grad_low_out):
    def chunk(rows):
        normed, inv_std = normalize(sums[rows])
        grad = part[rows] + dot_last(grad_fquery[rows], matrices[2])
        grad = grad + dot_last(grad_middle[rows], matrices[0])
        grad = norm_back(grad * line_of(lines, GAIN2), normed, inv_std)
        grad_out[rows] = grad
        grad_low_out[rows] = grad.astype(BF16)

    by_chunks(part.shape[0], chunk)


def call_merging_input(deps, sums, lines, part, grad_fquery, grad_middle, matrices):
    return kernel(
        merging_input,
        deps,
        FFN_MIB,
        in_specs=[VMEM] * 6,
        out_specs=[VMEM] * 2,
        out_shape=[sds(part.shape, F32), sds(part.shape, BF16)],
        cost_estimate=cost(3),
        name="merging_input",
    )(sums, lines, part, grad_fquery, grad_middle, matrices)


def ffn_backward(last, blocks, n_slopes, grad_low, before, *refs):
    slopes, (in0, in1), refs = refs[:n_slopes], refs[n_slopes : n_slopes + 2], refs[n_slopes + 2 :]
    slopes = [slope.at[i] for slope in slopes for i in range(slope.shape[0])]
    all_outs, refs = refs[: 2 * blocks], refs[2 * blocks :]

    def chunk(rows):
        low = grad_low[rows]
        total = before[rows]
        outs = list(all_outs)
        for quarter, into in enumerate((in0, in1)):
            grad_act = [dot_last(low, outs.pop(0)[...]) for _ in range(blocks)]
            grad_act = grad_act[0] if blocks == 1 else jnp.concatenate(grad_act, axis=1)
            grad_pre = (grad_act * slopes[quarter][rows].astype(F32)).astype(BF16)
            total = total + dot_last(grad_pre, into[...])
        if not last:
            refs[0][rows] = total
            return
        normed1, inv_std1, lines, grad_out, grad_low_out = refs
        grad = norm_back(total * line_of(lines, GAIN1), normed1[rows], inv_std1[rows])
        grad_out[rows] = grad
        grad_low_out[rows] = grad.astype(BF16)

    by_chunks(before.shape[0], chunk)


def call_ffn_backward(deps, grad_low, before, slopes, in_quarters, out_quarters, *for_norm):
    seq, width = before.shape
    last = bool(for_norm)
    return kernel(
        functools.partial(ffn_backward, last, len(out_quarters) // 2, len(slopes)),
        deps,
        FFN_MIB,
        in_specs=[VMEM] * (4 + len(slopes) + len(out_quarters) + len(for_norm)),
        out_specs=[VMEM] * (1 + last),
        out_shape=[sds((seq, width), F32)] + [sds((seq, width), BF16)] * last,
        cost_estimate=cost(5),
        name="ffn_backward",
    )(grad_low, before, *slopes, *in_quarters, *out_quarters, *for_norm)


def attend_backward(columns, unroll, leaving, grad_low, before, turned_ref, att_ref, prob_ref, weight, *refs):
    input_grad, token, grad_turned, grad_att = refs[:4]
    width = 3 * HEAD_DIM
    root = HEAD_DIM**-0.5
    grad_att[...] = dot_last(weight[columns:], grad_low[...]).astype(BF16)

    @pl.loop(0, columns // width, unroll=unroll)
    def _(head):
        base = pl.multiple_of(head * width, width)
        places = [pl.ds(base + i * HEAD_DIM, HEAD_DIM) for i in range(3)]
        queries, keys, values = (turned_ref[place] for place in places)
        part = pl.ds(pl.multiple_of(head * HEAD_DIM, HEAD_DIM), HEAD_DIM)
        grad = grad_att[part]
        prob = prob_ref[head]
        row_dot = jnp.sum(grad.astype(F32) * att_ref[part].astype(F32), axis=0, keepdims=True)
        grad_scores = (prob.astype(F32) * (dot(values.T, grad) - row_dot)).astype(BF16)
        grad_turned[places[0]] = (dot(keys, grad_scores) * root).astype(BF16)
        grad_turned[places[1]] = (dot_last(queries, grad_scores) * root).astype(BF16)
        grad_turned[places[2]] = dot_last(grad, prob).astype(BF16)

    token[...] = jnp.zeros_like(token)
    grads = grad_turned[...].T
    if not leaving:
        input_grad[...] = before[...] + dot(grads, weight[:columns])
        return
    total, sems = refs[4:]
    parts = [slice(i, i + CHUNK) for i in range(0, before.shape[0], CHUNK)]
    copies = [
        pltpu.make_async_copy(total.at[part], input_grad.at[part], sems.at[i])
        for i, part in enumerate(parts)
    ]
    for part, copy in zip(parts, copies):
        total[part] = before[part] + dot(grads[part], weight[:columns])
        copy.start()
    for copy in copies:
        copy.wait()


def call_attend_backward(deps, columns, unroll, leaving, grad_low, before, saved, quarter):
    seq, width = before.shape
    inner = columns // 3
    return kernel(
        functools.partial(attend_backward, columns, unroll, leaving),
        deps,
        ATTEND_MIB,
        in_specs=[VMEM] * 6,
        out_specs=[ANY if leaving else VMEM, VMEM],
        out_shape=[sds((seq, width), F32), sds((8, LANES), F32)],
        scratch_shapes=[pltpu.VMEM((columns, seq), BF16), pltpu.VMEM((inner, seq), BF16)]
        + [pltpu.VMEM((seq, width), F32), pltpu.SemaphoreType.DMA((seq // CHUNK,))] * leaving,
        cost_estimate=cost(8),
        name="attend_backward",
    )(grad_low, before, *saved, quarter)


def prepare(meta, down, up, query, key, value, g1, s1, g2, s2, g3, s3, keep, send, lines, shard):
    n_adapters, _, rank = down.shape
    for i in range(n_adapters):
        shard[0, :, i * rank : (i + 1) * rank] = down[i].astype(F32)
        shard[1, :, i * rank : (i + 1) * rank] = up[i].astype(F32)
    for i, ref in enumerate((query, key, value)):
        shard[2 + i] = ref[...].astype(F32)
    half = keep.shape[2]
    mine = pl.multiple_of(meta[CORE] * half, LANES)
    other = pl.multiple_of((1 - meta[CORE]) * half, LANES)
    keep[...] = shard[:, :, pl.ds(mine, half)].astype(BF16)
    send[...] = shard[:, :, pl.ds(other, half)].astype(BF16)
    for i, ref in enumerate((g1, s1, g2, s2, g3, s3)):
        lines[i : i + 1] = ref[...].reshape(1, -1)
    lines[6:8] = jnp.zeros((2, lines.shape[1]), F32)


def call_prepare(meta, down, up, query, key, value, *vectors):
    rows, width = query.shape
    half = sds((5, rows, width // 2), BF16)
    return pl.pallas_call(
        prepare,
        in_specs=[SMEM] + [VMEM] * 11,
        out_specs=[VMEM] * 3,
        out_shape=[half, half, sds((8, width), F32)],
        scratch_shapes=[pltpu.VMEM((5, rows, width), F32)],
        compiler_params=params(16),
        cost_estimate=cost(1),
        name="prepare",
    )(meta, *(in_hbm(a) for a in (down, up, query, key, value, *vectors)))


def join_attention(qkv_turned, attn_out, attn):
    columns = qkv_turned.shape[0]
    attn[:columns] = qkv_turned[...]
    attn[columns:] = attn_out[...]


def call_join_attention(deps, qkv_turned, attn_out):
    rows, width = qkv_turned.shape[0] + attn_out.shape[0], attn_out.shape[1]
    return kernel(
        join_attention,
        deps,
        16,
        in_specs=[VMEM] * 2,
        out_specs=VMEM,
        out_shape=sds((rows, width), BF16),
        cost_estimate=cost(1),
        name="join_attention",
    )(in_hbm(qkv_turned), in_hbm(attn_out))


def prepare_shares(meta, attn, into, out, with_attn, with_in, out_last, *copies):
    half = attn.shape[0] // 2
    more = half // 3
    mine = pl.multiple_of(meta[PAIR_Y] * half, 16)
    other = pl.multiple_of((1 - meta[PAIR_Y]) * half + 2 * more, 16)
    with_attn[:half] = attn[pl.ds(mine, half)]
    with_attn[half : half + more] = attn[pl.ds(other, more)]
    cut = with_attn.shape[0] - half - more
    with_attn[half + more :] = out[:cut]
    half = into.shape[0] // 2
    with_in[:half] = into[pl.ds(pl.multiple_of(meta[PAIR_Z] * half, 16), half)]
    end = cut + with_in.shape[0] - half
    with_in[half:] = out[cut:end]
    out_last[...] = out[end:]
    for source, copy in zip((into, out), copies):
        copy[...] = source[...]


def call_prepare_shares(deps, meta, attn, into, out):
    rows, width = attn.shape
    unit = out.shape[0] // 12
    shares = (rows // 2 + rows // 6 + unit, into.shape[0] // 2 + 3 * unit, 8 * unit)
    shares = shares + (into.shape[0], out.shape[0])
    return kernel(
        prepare_shares,
        deps,
        16,
        in_specs=[SMEM] + [VMEM] * 3,
        out_specs=[VMEM] * 5,
        out_shape=[sds((n, width), BF16) for n in shares],
        cost_estimate=cost(1),
        name="prepare_shares",
    )(meta, attn, in_hbm(into), in_hbm(out))


def chip_tile(meta, keep, got, attn, tile, attn_out):
    mine, other = keep[...].astype(F32), got[...].astype(F32)
    lower = jnp.where(meta[CORE] == 0, mine, other)
    upper = jnp.where(meta[CORE] == 0, other, mine)
    tile[...] = jnp.concatenate([lower, upper], axis=1).astype(BF16)


def call_chip_tile(meta, keep, got, attn):
    n_mats, rows, half = keep.shape
    return kernel(
        chip_tile,
        [],
        16,
        in_specs=[SMEM] + [VMEM] * 2 + [ANY],
        out_specs=[VMEM, ANY],
        out_shape=[sds((n_mats, 2 * rows, half), BF16), sds(attn.shape, attn.dtype)],
        input_output_aliases={3: 1},
        cost_estimate=cost(1),
        name="chip_tile",
    )(meta, keep, got, attn)


def add_blocks(*blocks):
    total = functools.reduce(jnp.add, (b.astype(F32) for b in blocks))
    tail = total[-8:-4] + total[-4:]
    return jnp.concatenate([total[:-8], split_lines(tail)], axis=0)


def sum_cores(keep, got, p_keep, p_send, q_keep, q_send):
    half = p_keep.shape[-1]
    for x in range(2):
        for y in range(2):

            @pl.loop(0, 4)
            def _(z, x=x, y=y):
                total = add_blocks(keep[x, y, z], got[x, y, z]).astype(BF16)
                (p_send if x else p_keep)[y, z] = total[:, :half]
                (q_send if y else q_keep)[x, z] = total[:, half:]


def sum_first(p_keep, p_got, q_keep, q_got, p2_keep, p2_send, q2_keep, q2_send):
    @pl.loop(0, 4)
    def _(z):
        for out, index in ((p2_keep, 0), (p2_send, 1)):
            out[z] = add_blocks(p_keep[index, z], p_got[index, z]).astype(BF16)
        for out, index in ((q2_keep, 0), (q2_send, 1)):
            out[z] = add_blocks(q_keep[index, z], q_got[index, z]).astype(BF16)


def sum_second(p_keep, p_got, q_keep, q_got, *outs):
    half = p_keep.shape[-1]
    for z in range(4):
        outs[z][:, :half] = add_blocks(p_keep[z], p_got[z]).astype(BF16)
        outs[z][:, half:] = add_blocks(q_keep[z], q_got[z]).astype(BF16)


def sum_last(n_adapters, keep, got1, got2, got3, query, key, value, gain, bias, mass):
    total = add_blocks(keep[...], got1[...], got2[...], got3[...])
    rows = query.shape[0]
    for i, out in enumerate((query, key, value)):
        out[...] = total[i * rows : (i + 1) * rows]
    lines = total[-8:-4] + total[-4:]
    gain[...] = lines[0]
    bias[...] = lines[1]
    mass[...] = lines[2, :n_adapters] / lines[2:3, n_adapters : n_adapters + 1].reshape(1)


def small_call(body, name, out_shape, dep, *operands):
    return kernel(
        body,
        (dep,),
        16,
        in_specs=[VMEM] * len(operands),
        out_specs=[VMEM] * len(out_shape),
        out_shape=out_shape,
        cost_estimate=cost(1),
        name=name,
    )(*operands)


def sum_gradients(hops, keep, send, n_adapters, works):
    block, width = keep.shape[3:]
    half = width // 2
    pair = [sds((2, 4, block, half), BF16)] * 4
    single = [sds((4, block, half), BF16)] * 4
    got = hops.flip(send, 1)
    dep = works[0](())
    pk, ps, qk, qs = small_call(sum_cores, "sum_cores", pair, dep, keep, got)
    pg, qg = hops.flip(ps, ALONG_X), hops.flip(qs, ALONG_Y)
    dep = works[1]([pk])
    pk, ps, qk, qs = small_call(sum_first, "sum_first", single, dep, pk, pg, qk, qg)
    pg, qg = hops.flip(ps, ALONG_Y), hops.flip(qs, ALONG_X)
    dep = works[2]([pk])
    parts = small_call(
        sum_second, "sum_second", [sds((block, width), BF16)] * 4, dep, pk, pg, qk, qg
    )
    got = [hops.flip(part, z * ALONG_Z) for z, part in enumerate(parts) if z]
    dep = works[3]([parts[0]])
    rows = (block - 8) // 3
    outs = [sds((rows, width), F32)] * 3 + [sds((width,), F32)] * 2 + [sds((n_adapters,), F32)]
    last = functools.partial(sum_last, n_adapters)
    return small_call(last, "sum_last", outs, dep, parts[0], *got)


ALONG_X, ALONG_Y, ALONG_Z = 2, 4, 8


class Hops:
    def __init__(self, mesh):
        self.count = mesh.size
        self.tiled = mesh.shape["dp"] == 8 and mesh.shape["tensor"] == 4

    def flip(self, array, bits):
        return lax.ppermute(array, AXES, [(i, i ^ bits) for i in range(self.count)])


def half_of(block, parity):
    half = block.shape[0] // 2
    return lax.dynamic_slice_in_dim(block, parity * half, half, 0)


def plain_schedule(
    meta, doc_lengths, tokens, out_grad, lines, columns, n_adapters, attn, into, out, shard
):
    attn, into, out = (lax.all_gather(w, "tensor", axis=0) for w in (attn, into, out))
    weights = lax.all_gather(shard, AXES, axis=1, tiled=True)
    pairs = [slice(i, i + 2) for i in range(0, attn.shape[0], 2)]
    before, saved, slopes = tokens, [], []
    for pair in pairs:
        last = pair is pairs[-1]
        results = call_attend_forward(
            [], columns, last, meta, doc_lengths, tokens, before, lines, tuple(attn[pair])
        )
        saved += [results[:3], results[3:6]]
        before = results[6]
    first, normed1, inv_std1 = results[6:]
    sums = first
    for pair in pairs:
        slope, sums = call_ffn_forward([], first, sums, tuple(into[pair]), tuple(out[pair]))
        slopes.append(slope)
    layer_out, *parts, keep, send = call_merging(
        n_adapters, meta, doc_lengths, sums, lines, out_grad, weights
    )
    total, low = call_merging_input([], sums, lines, *parts, weights)
    width = tokens.shape[1]
    blocks = jnp.transpose(jnp.stack([keep, send]), (3, 2, 1, 0, 4, 5)).reshape(32, -1, width)
    squares = blocks[:, :-8].reshape(32, 3, width // 32, width)
    squares = jnp.transpose(squares, (1, 0, 2, 3)).reshape(3, width, width).astype(F32)
    squares = lax.psum_scatter(squares, AXES, scatter_dimension=1, tiled=True)
    tail = blocks[0, -8:].astype(F32)
    totals = lax.psum(tail[:4] + tail[4:], AXES)
    for pair, slope in zip(pairs, slopes):
        for_norm = (normed1, inv_std1, lines) if pair is pairs[-1] else ()
        total, *rest = call_ffn_backward(
            [], low, total, [slope], tuple(into[pair]), tuple(out[pair]), *for_norm
        )
    (low,) = rest
    for quarter, kept in zip(attn, saved):
        total, _ = call_attend_backward([], columns, False, False, low, total, kept, quarter)
    mass = totals[2, :n_adapters] / totals[2, n_adapters]
    return (layer_out, total, squares[0], squares[1], squares[2], totals[0], totals[1], mass)


def per_device(
    hops,
    tokens,
    doc_lengths,
    qkv_weight,
    attn_out_weight,
    norm1_gain,
    norm1_bias,
    ffn_in_weight,
    ffn_out_weight,
    norm2_gain,
    norm2_bias,
    adapter_down,
    adapter_up,
    merging_query,
    merging_key,
    merging_value,
    merging_gain,
    merging_bias,
    out_grad,
):
    n_adapters, rows, rank = adapter_down.shape
    columns = qkv_weight.shape[1]
    tensor, dp = lax.axis_index("tensor"), lax.axis_index("dp")
    pair_y, pair_z = dp % 2, dp // 2 % 2
    meta = jnp.stack([tensor % 2, tensor // 2, pair_y, pair_z, dp // 2, tensor]).astype(jnp.int32)
    flip = hops.flip
    if not hops.tiled:
        meta = meta * (jnp.arange(meta.shape[0]) == ROW)

    keep, send, lines = call_prepare(
        meta,
        adapter_down,
        jnp.transpose(adapter_up, (0, 2, 1)),
        merging_query,
        merging_key,
        merging_value,
        norm1_gain,
        norm1_bias,
        norm2_gain,
        norm2_bias,
        merging_gain,
        merging_bias,
    )
    attn = call_join_attention([keep], qkv_weight.T, attn_out_weight)
    if not hops.tiled:
        shard = jnp.concatenate([keep, send], axis=2)
        return plain_schedule(
            meta, doc_lengths, tokens, out_grad, lines, columns, n_adapters, attn, ffn_in_weight, ffn_out_weight, shard
        )
    tile, attn = call_chip_tile(meta, keep, flip(send, 1), attn)
    with_attn, with_in, out_2, into, out = call_prepare_shares(
        [], meta, attn, ffn_in_weight, ffn_out_weight
    )
    tile_x = flip(tile, ALONG_X)
    attn_core = flip(attn, 1)
    both, with_attn, into, out = sync(
        "phase1", meta, [[tile, tile_x]], [with_attn, into, out], [attn_core]
    )
    z2, y0, with_attn_x = flip(both, 2 * ALONG_Z), flip(both, ALONG_Y), flip(with_attn, ALONG_X)
    in_core, out_core = flip(into, 1), flip(out, 1)
    saved_near = call_attend_forward(
        [both], columns, False, meta, doc_lengths, tokens, tokens, lines, (attn, attn_core)
    )
    half = attn.shape[0] // 2
    third = half // 3
    joined, attn_x, with_in, y0, z2 = sync(
        "phase2",
        meta,
        [[both, z2], [(with_attn_x, 0, 2 * third)]],
        [with_in, y0, z2],
        [saved_near[6], in_core, out_core],
    )
    with_in_x, attn_y, z1 = flip(with_in, ALONG_X), flip(attn_x, ALONG_Y), flip(joined, ALONG_Z)
    y2 = flip(z2, ALONG_Y)
    joined_c, y0_c = flip(joined, 1), flip(y0, 1)
    attn_far, in_x, out_a, out_2, z1, y2 = sync(
        "phase3",
        meta,
        [
            [PAIR_Y]
            + [(with_attn_x, i * third, third) for i in range(3)]
            + [(attn_y, 0, third), (attn_y, third, third), (with_attn_x, half, third)],
            [(with_in_x, 0, half)],
            [
                (share, start, share.shape[0] - start)
                for share, start in ((with_attn_x, half + third), (with_in_x, half))
            ],
        ],
        [out_2, z1, y2],
        [joined_c, y0_c],
    )
    attn_far_c = flip(attn_far, 1)
    y1, out_b, in_z = flip(z1, ALONG_Y), flip(out_2, ALONG_X), flip(in_x, ALONG_Z)
    z1_c, y2_c, out_a_c = flip(z1, 1), flip(y2, 1), flip(out_a, 1)
    *saved_far, first, normed1, inv_std1 = call_attend_forward(
        [], columns, True, meta, doc_lengths, tokens, saved_near[6], lines, (attn_far, attn_far_c)
    )
    slope_near, sums = call_ffn_forward(
        [], first, first, (ffn_in_weight, in_core), (ffn_out_weight, out_core)
    )
    own, other = 0, 1
    weights = assemble(
        "assemble",
        [first],
        meta,
        None,
        [
            (joined, ((0, 0), (0, 2)), own),
            (joined_c, ((0, 0), (0, 2)), other),
            (z1, ((0, 1), (0, 3)), own),
            (z1_c, ((0, 1), (0, 3)), other),
            (y0, ((1, 0),), own),
            (y0_c, ((1, 0),), other),
            (y2, ((1, 2),), own),
            (y2_c, ((1, 2),), other),
        ],
    )
    in_far, out_b, y1 = sync(
        "phase4", meta, [[PAIR_Z, in_x, in_z]], [out_b, y1], [sums, weights, out_a_c]
    )
    in_far_c, out_b_c, y1_c = flip(in_far, 1), flip(out_b, 1), flip(y1, 1)
    out_far = (out_a, out_b, out_a_c, out_b_c)
    slopes_far = []
    for quarter, blocks in ((in_far, out_far[:2]), (in_far_c, out_far[2:])):
        slope, sums = call_ffn_forward([], first, sums, (quarter,), blocks)
        slopes_far.append(slope)
    last_parts = ((1, 1), (1, 3))
    weights = assemble(
        "assemble_last", [sums], meta, weights, [(y1, last_parts, own), (y1_c, last_parts, other)]
    )
    layer_out, *parts, grad_keep, grad_send = call_merging(
        n_adapters, meta, doc_lengths, sums, lines, out_grad, weights
    )
    done = {}
    attn_quarters = (attn, attn_core, attn_far, attn_far_c)
    saved = (saved_near[:3], saved_near[3:6], saved_far[:3], saved_far[3:6])

    def attention(deps, *quarters):
        for i in quarters:
            done["sum"], token = call_attend_backward(
                deps, columns, i > 1, i == 3, done["low"], done["sum"], saved[i], attn_quarters[i]
            )
            deps = [token]
        return token

    def near(deps):
        (done["sum"],) = call_ffn_backward(
            deps,
            done["low"],
            done["sum"],
            [slope_near],
            (ffn_in_weight, in_core),
            (ffn_out_weight, out_core),
        )
        return done["sum"]

    def far(deps):
        done["sum"], done["low"] = call_ffn_backward(
            deps,
            done["low"],
            done["sum"],
            slopes_far,
            (in_far, in_far_c),
            out_far,
            normed1,
            inv_std1,
            lines,
        )

    def first_work(deps):
        done["sum"], done["low"] = call_merging_input(deps, sums, lines, *parts, weights)
        return done["sum"]

    def second_work(deps):
        near(deps)
        far([])
        return attention([], 0)

    works = (
        first_work,
        second_work,
        lambda deps: attention(deps, 1),
        lambda deps: attention(deps, 2, 3),
    )
    summed = sum_gradients(hops, grad_keep, grad_send, n_adapters, works)
    return (layer_out, done["sum"], *summed)


def solution(mesh):
    split = P(AXES, None)
    in_specs = (
        split,
        P("dp", None),
        P(None, "tensor"),
        P("tensor", None),
        P(),
        P(),
        P(None, "tensor"),
        P("tensor", None),
        P(),
        P(),
        P(None, AXES, None),
        P(None, None, AXES),
        split,
        split,
        split,
        P(),
        P(),
        split,
    )
    out_specs = (split, split, split, split, split, P(), P(), P())
    return jax.shard_map(
        functools.partial(per_device, Hops(mesh)),
        mesh=mesh,
        in_specs=in_specs,
        out_specs=out_specs,
        check_vma=False,
    )
```

```python
import functools

import jax
import jax.numpy as jnp
from jax import lax
from jax.experimental import pallas as pl
from jax.experimental.pallas import tpu as pltpu
from jax.sharding import PartitionSpec as P

HEAD_DIM = 64
AXES = ("dp", "tensor")
ATTEND_MIB, FFN_MIB, MERGE_MIB = 16, 16, 24
LANES = 128
COST = 0.0
CHUNK = 256
EPS = 1e-12
BIG_NEGATIVE = -1e30
ROOT_HALF = 0.7071067811865476
ROOT_TAU = 0.3989422804014327
F32, BF16 = jnp.float32, jnp.bfloat16

CORE, ACROSS, PAIR_Y, PAIR_Z, DEPTH, ROW = range(6)
GAIN1, SHIFT1, GAIN2, SHIFT2, GAIN3, SHIFT3 = range(6)

SMEM = pl.BlockSpec(memory_space=pltpu.SMEM)
VMEM = pl.BlockSpec(memory_space=pltpu.VMEM)
ANY = pl.BlockSpec(memory_space=pl.ANY)
HBM = pl.BlockSpec(memory_space=pltpu.HBM)


def by_chunks(count, body, size=CHUNK):
    @pl.loop(0, count // size)
    def _(i):
        body(pl.ds(pl.multiple_of(i * size, size), size))


def line_of(lines, i):
    return lines[i : i + 1]


def dot(a, b):
    return lax.dot_general(a, b, (((1,), (0,)), ((), ())), preferred_element_type=F32)


def dot_last(a, b):
    return lax.dot_general(a, b, (((1,), (1,)), ((), ())), preferred_element_type=F32)


def dot_first(a, b):
    return lax.dot_general(a, b, (((0,), (0,)), ((), ())), preferred_element_type=F32)


def normalize(u):
    centered = u - jnp.mean(u, axis=-1, keepdims=True)
    inv_std = lax.rsqrt(jnp.mean(centered * centered, axis=-1, keepdims=True) + EPS)
    return centered * inv_std, inv_std


def norm_back(grad, normed, inv_std):
    return inv_std * (
        grad
        - jnp.mean(grad, axis=-1, keepdims=True)
        - normed * jnp.mean(grad * normed, axis=-1, keepdims=True)
    )


def gelu_both(u):
    half = 0.5 * (1.0 + lax.erf(u * ROOT_HALF))
    return u * half, half + u * jnp.exp(-0.5 * u * u) * ROOT_TAU


def segment_bias(meta_ref, lengths_ref, bias_ref):
    seq = bias_ref.shape[0]
    row = meta_ref[ROW]
    by_row = lax.broadcasted_iota(jnp.int32, (seq, 1), 0)
    by_lane = lax.broadcasted_iota(jnp.int32, (1, seq), 1)
    seg_row = jnp.zeros((seq, 1), jnp.int32)
    seg_lane = jnp.zeros((1, seq), jnp.int32)
    end = jnp.int32(0)
    for i in range(lengths_ref.shape[1]):
        end = end + lengths_ref[row, i]
        seg_row = seg_row + jnp.where(by_row >= end, 1, 0)
        seg_lane = seg_lane + jnp.where(by_lane >= end, 1, 0)
    bias_ref[...] = jnp.where(seg_row == seg_lane, 0.0, BIG_NEGATIVE).astype(F32)


def attend_forward(columns, last, meta, lengths, tokens, before, lines, weight0, weight1, *refs):
    saved, first_out, bias = refs[:6], refs[6], refs[-1]
    segment_bias(meta, lengths, bias)
    total = before[...].astype(F32)
    width = 3 * HEAD_DIM
    for quarter, weight in enumerate((weight0, weight1)):
        turned = dot_last(weight[:columns], tokens[...]).astype(BF16)
        turned_out, att_out, prob_out = saved[3 * quarter : 3 * quarter + 3]
        turned_out[...] = turned

        @pl.loop(0, columns // width)
        def _(head, turned_out=turned_out, att_out=att_out, prob_out=prob_out):
            base = pl.multiple_of(head * width, width)
            queries, keys, values = (
                turned_out[pl.ds(base + i * HEAD_DIM, HEAD_DIM)] for i in range(3)
            )
            scores = dot(keys.T, queries * BF16(HEAD_DIM**-0.5)) + bias[...]
            exponent = jnp.exp(scores - jnp.max(scores, axis=0, keepdims=True))
            prob = (exponent * (1.0 / jnp.sum(exponent, axis=0, keepdims=True))).astype(BF16)
            prob_out[head] = prob
            part = pl.ds(pl.multiple_of(head * HEAD_DIM, HEAD_DIM), HEAD_DIM)
            att_out[part] = dot(values, prob).astype(BF16)

        total = total + dot(att_out[...].T, weight[columns:])
    if not last:
        first_out[...] = total
        return
    normed_out, inv_out = refs[7:9]
    normed, inv_std = normalize(total)
    normed_out[...] = normed
    inv_out[...] = inv_std
    first_out[...] = normed * line_of(lines, GAIN1) + line_of(lines, SHIFT1)


def sds(shape, dtype):
    return jax.ShapeDtypeStruct(shape, dtype)


def params(mib):
    return pltpu.CompilerParams(vmem_limit_bytes=mib << 20)


def kernel(body, deps, mib, *, in_specs, **kw):
    n = len(deps)
    call = pl.pallas_call(
        lambda *refs: body(*refs[n:]),
        in_specs=[ANY] * n + in_specs,
        compiler_params=params(mib),
        **kw,
    )
    return functools.partial(call, *deps)


def sync(name, meta, joins, carries, deps):
    sides = [j[0] if isinstance(j[0], int) else None for j in joins]
    parts = [j[1:] if isinstance(j[0], int) else j for j in joins]
    parts = [[p if isinstance(p, tuple) else (p, 0, p.shape[0]) for p in j] for j in parts]
    flat = [p[0] for j in parts for p in j]

    def body(meta_ref, *refs):
        refs = refs[len(carries) :]
        sources, outs = list(refs[: len(flat)]), refs[len(flat) : len(flat) + len(parts)]
        for side, join, out in zip(sides, parts, outs):
            row = 0
            for i, (_, start, size) in enumerate(join):
                if side is not None:
                    n = len(join) // 2
                    row = pl.multiple_of(((meta_ref[side] ^ (i // n)) * n + i % n) * size, 16)
                out[pl.ds(row, size)] = sources.pop(0)[start : start + size]
                row = row + size

    joined = [sds((sum(p[2] for p in j), *j[0][0].shape[1:]), j[0][0].dtype) for j in parts]
    n_deps = len(deps)
    out = kernel(
        body,
        deps,
        16,
        in_specs=[SMEM] + [ANY] * len(carries) + [VMEM] * len(flat),
        out_specs=[VMEM] * len(joined) + [ANY] * len(carries),
        out_shape=joined + [sds(c.shape, c.dtype) for c in carries],
        input_output_aliases={n_deps + 1 + i: len(joined) + i for i in range(len(carries))},
        cost_estimate=cost(0),
        name=name,
    )(meta, *carries, *flat)
    return out


def in_hbm(array):
    return pltpu.with_memory_space_constraint(array, pltpu.HBM)


def cost(us):
    return pl.CostEstimate(flops=int(us * 1.1e9 * COST), bytes_accessed=1024, transcendentals=0)


def call_attend_forward(deps, columns, last, meta, lengths, tokens, before, lines, quarters):
    seq, width = tokens.shape
    heads = columns // (3 * HEAD_DIM)
    inner = heads * HEAD_DIM
    square, narrow = sds((seq, width), F32), sds((seq, 1), F32)
    place = pltpu.HBM
    out_shape = [
        place((columns, seq), BF16),
        place((inner, seq), BF16),
        place((heads, seq, seq), BF16),
    ] * 2 + [square] + [square, narrow] * last
    return kernel(
        functools.partial(attend_forward, columns, last),
        deps,
        ATTEND_MIB,
        in_specs=[SMEM, SMEM] + [VMEM] * 5,
        out_specs=[VMEM] * len(out_shape),
        out_shape=out_shape,
        scratch_shapes=[pltpu.VMEM((seq, seq), F32)],
        cost_estimate=cost(8),
        name="attend_forward",
    )(meta, lengths, tokens, before, lines, *quarters)


def ffn_forward(quarters, blocks, first, before, *refs):
    slope_out, sum_out = refs[-2:]

    def chunk(rows):
        low = first[rows].astype(BF16)
        total = before[rows]
        outs = list(refs[quarters:-2])
        for quarter in range(quarters):
            value, slope = gelu_both(dot(low, refs[quarter][...]))
            slope_out[quarter, rows] = slope.astype(BF16)
            value = value.astype(BF16)
            start = 0
            for _ in range(blocks):
                out = outs.pop(0)
                total = total + dot(value[:, start : start + out.shape[0]], out[...])
                start += out.shape[0]
        sum_out[rows] = total

    by_chunks(first.shape[0], chunk)


def call_ffn_forward(deps, first, before, in_quarters, out_quarters):
    seq, width = first.shape
    hidden = in_quarters[0].shape[1]
    quarters = len(in_quarters)
    return kernel(
        functools.partial(ffn_forward, quarters, len(out_quarters) // quarters),
        deps,
        FFN_MIB,
        in_specs=[VMEM] * (2 + quarters + len(out_quarters)),
        out_specs=[VMEM] * 2,
        out_shape=[sds((quarters, seq, hidden), BF16), sds((seq, width), F32)],
        cost_estimate=cost(5),
        name="ffn_forward",
    )(first, before, *in_quarters, *out_quarters)


def assemble(name, deps, meta, weights, tiles):
    n_mats = tiles[0][0].shape[0] // (2 * len(tiles[0][1]))
    rows, half = tiles[0][0].shape[1:]
    count = sum(2 * len(parts) for _, parts, _ in tiles)
    before = [] if weights is None else [weights]

    def body(meta_ref, *refs):
        refs = refs[len(before) :]
        out, sems = refs[-2:]
        copies = []
        for ref, (_, parts, core_rel) in zip(refs, tiles):
            side = pl.multiple_of((meta_ref[CORE] ^ core_rel) * half, LANES)
            for j, (y_rel, z_rel) in enumerate(parts):
                for x_rel in range(2):
                    chip = ((meta_ref[DEPTH] ^ z_rel) * 2 + (meta_ref[PAIR_Y] ^ y_rel)) * 2
                    chip = chip + (meta_ref[ACROSS] ^ x_rel)
                    first = pl.multiple_of(chip * rows, 16)
                    target = out.at[:, pl.ds(first, rows), pl.ds(side, half)]
                    source = ref.at[pl.ds((2 * j + x_rel) * n_mats, n_mats)]
                    copies.append(pltpu.make_async_copy(source, target, sems.at[len(copies)]))
        for copy in copies:
            copy.start()
        for copy in copies:
            copy.wait()

    return kernel(
        body,
        deps,
        16,
        in_specs=[SMEM] + [ANY] * len(before) + [VMEM] * len(tiles),
        out_specs=ANY,
        out_shape=sds((n_mats, 2 * half, 2 * half), BF16),
        input_output_aliases={len(deps) + 1: 0} if before else {},
        scratch_shapes=[pltpu.SemaphoreType.DMA((count,))],
        cost_estimate=cost(0),
        name=name,
    )(meta, *before, *(tile for tile, _, _ in tiles))


def split_lines(total):
    high = total.astype(BF16).astype(F32)
    return jnp.concatenate([high, total - high], axis=0)


def merging(n_adapters, meta, lengths, sums, lines, out_grad, matrices, *refs):
    layer_out, part_out, fquery_out, middle_out, keep_out, send_out = refs[:6]
    grads, sum_lines, states, probes, blends, values, fqueries, joined, sem = refs[6:]
    leave = pltpu.make_async_copy(joined, layer_out, sem)
    seq, width = sums.shape
    scale = width**-0.5
    down, up, query, key, value = (matrices.at[i] for i in range(5))
    gain2, shift2 = line_of(lines, GAIN2), line_of(lines, SHIFT2)
    gain3, shift3 = line_of(lines, GAIN3), line_of(lines, SHIFT3)
    spread = jnp.where(
        lax.broadcasted_iota(jnp.int32, (LANES, width), 0)
        == lax.broadcasted_iota(jnp.int32, (LANES, width), 1) // (width // n_adapters),
        1.0,
        0.0,
    ).astype(BF16)
    lane = lax.broadcasted_iota(jnp.int32, (1, LANES), 1)
    count = jnp.int32(0)
    for i in range(lengths.shape[1]):
        count = count + lengths[meta[ROW], i]
    sum_lines[...] = jnp.zeros_like(sum_lines)

    def by_adapter(terms):
        high = terms.astype(BF16)
        rest = (terms - high.astype(F32)).astype(BF16)
        return dot_last(high, spread) + dot_last(rest, spread)

    def chunk(rows):
        normed2, _ = normalize(sums[rows])
        second = normed2 * gain2 + shift2
        second_low = second.astype(BF16)
        states[rows] = second_low
        act, slope = (v.astype(BF16) for v in gelu_both(dot(second_low, down[...])))
        fquery = dot(second_low, query[...]).astype(BF16)
        fqueries[rows] = fquery
        probe = dot_last(fquery, key[...]).astype(BF16)
        probe_up = dot(probe, up[...])
        logits = scale * (
            jnp.sum(probe.astype(F32) * second, axis=1, keepdims=True)
            + by_adapter(act * probe_up)
        )
        logits = jnp.where(lane < n_adapters, logits, BIG_NEGATIVE)
        exponent = jnp.exp(logits - jnp.max(logits, axis=1, keepdims=True))
        mix = exponent / jnp.sum(exponent, axis=1, keepdims=True)
        mix_low = mix.astype(BF16)
        mix_sum = jnp.sum(mix_low.astype(F32), axis=1, keepdims=True)
        mix_wide = dot(mix_low, spread).astype(BF16)
        blended = second * mix_sum + dot_last((mix_wide * act).astype(BF16), up[...])
        blended = blended.astype(BF16)
        blends[rows] = blended
        normed3, inv_std3 = normalize(second + dot(blended, value[...]))
        joined[...] = normed3 * gain3 + shift3
        leave.start()

        token = rows.start + lax.broadcasted_iota(jnp.int32, (rows.size, 1), 0)
        keep = jnp.where(token < count, 1.0, 0.0)
        cot = out_grad[rows].astype(F32) * keep
        mass = jnp.sum(mix * keep, axis=0, keepdims=True)
        mass = jnp.where(lane == n_adapters, jnp.sum(keep), mass)
        sum_lines[0:1] += jnp.sum(cot * normed3, axis=0, keepdims=True)
        sum_lines[1:2] += jnp.sum(cot, axis=0, keepdims=True)
        sum_lines[2:3, :LANES] += mass

        grad_pre = norm_back(cot * gain3, normed3, inv_std3)
        grad_proj = grad_pre.astype(BF16)
        values[rows] = grad_proj
        grad_blend = dot_last(grad_proj, value[...]).astype(BF16)
        blend_up = dot(grad_blend, up[...])
        grad_mix = jnp.sum(
            grad_blend.astype(F32) * second, axis=1, keepdims=True
        ) + by_adapter(act * blend_up)
        grad_logits = mix * (grad_mix - jnp.sum(grad_mix * mix, axis=1, keepdims=True))
        grad_logits = grad_logits.astype(BF16)
        logit_sum = jnp.sum(grad_logits.astype(F32), axis=1, keepdims=True)
        logit_wide = dot(grad_logits, spread).astype(BF16)
        grad_probe = second * logit_sum + dot_last((logit_wide * act).astype(BF16), up[...])
        grad_probe = (scale * grad_probe).astype(BF16)
        probes[rows] = grad_probe
        fquery_out[rows] = dot(grad_probe, key[...]).astype(BF16)
        grad_act = mix_wide.astype(F32) * blend_up + (scale * logit_wide.astype(F32)) * probe_up
        middle_out[rows] = (grad_act * slope.astype(F32)).astype(BF16)
        part_out[rows] = (
            grad_pre + grad_blend.astype(F32) * mix_sum + probe.astype(F32) * (scale * logit_sum)
        )

    by_chunks(seq, chunk, seq)

    @pl.loop(0, width // CHUNK)
    def _(i):
        part = pl.ds(pl.multiple_of(i * CHUNK, CHUNK), CHUNK)
        grads[0, part] = dot_first(states[:, part], fquery_out[...])
        grads[1, part] = dot_first(probes[:, part], fqueries[...])
        grads[2, part] = dot_first(blends[:, part], values[...])

    tail = split_lines(sum_lines[0:4])
    rows = width // 32

    @pl.loop(0, 16)
    def _(chip):
        z_rel = (chip // 4) ^ meta[DEPTH]
        y_rel = (chip // 2 % 2) ^ meta[PAIR_Y]
        x_rel = (chip % 2) ^ meta[ACROSS]
        for core_rel, out in ((0, keep_out), (1, send_out)):
            first = pl.multiple_of((chip * 2 + (meta[CORE] ^ core_rel)) * rows, 8)
            block = [grads[i, pl.ds(first, rows)] for i in range(3)] + [tail]
            out[x_rel, y_rel, z_rel] = jnp.concatenate(block, axis=0).astype(BF16)

    leave.wait()


def call_merging(n_adapters, meta, lengths, sums, lines, out_grad, matrices):
    seq, width = sums.shape
    block = 3 * width // 32 + 8
    return pl.pallas_call(
        functools.partial(merging, n_adapters),
        in_specs=[SMEM, SMEM] + [VMEM] * 4,
        out_specs=[ANY] + [VMEM] * 5,
        out_shape=[sds((seq, width), F32)] * 2
        + [sds((seq, width), BF16)] * 2
        + [sds((2, 2, 4, block, width), BF16)] * 2,
        scratch_shapes=[pltpu.VMEM((3, width, width), F32), pltpu.VMEM((8, width), F32)]
        + [pltpu.VMEM((seq, width), BF16)] * 5
        + [pltpu.VMEM((seq, width), F32), pltpu.SemaphoreType.DMA],
        compiler_params=params(MERGE_MIB),
        cost_estimate=cost(18),
        name="merging",
    )(meta, lengths, sums, lines, out_grad, matrices)


def merging_input(sums, lines, part, grad_fquery, grad_middle, matrices, grad_out, grad_low_out):
    def chunk(rows):
        normed, inv_std = normalize(sums[rows])
        grad = part[rows] + dot_last(grad_fquery[rows], matrices[2])
        grad = grad + dot_last(grad_middle[rows], matrices[0])
        grad = norm_back(grad * line_of(lines, GAIN2), normed, inv_std)
        grad_out[rows] = grad
        grad_low_out[rows] = grad.astype(BF16)

    by_chunks(part.shape[0], chunk)


def call_merging_input(deps, sums, lines, part, grad_fquery, grad_middle, matrices):
    return kernel(
        merging_input,
        deps,
        FFN_MIB,
        in_specs=[VMEM] * 6,
        out_specs=[VMEM] * 2,
        out_shape=[sds(part.shape, F32), sds(part.shape, BF16)],
        cost_estimate=cost(3),
        name="merging_input",
    )(sums, lines, part, grad_fquery, grad_middle, matrices)


def ffn_backward(last, blocks, n_slopes, grad_low, before, *refs):
    slopes, (in0, in1), refs = refs[:n_slopes], refs[n_slopes : n_slopes + 2], refs[n_slopes + 2 :]
    slopes = [slope.at[i] for slope in slopes for i in range(slope.shape[0])]
    all_outs, refs = refs[: 2 * blocks], refs[2 * blocks :]

    def chunk(rows):
        low = grad_low[rows]
        total = before[rows]
        outs = list(all_outs)
        for quarter, into in enumerate((in0, in1)):
            grad_act = [dot_last(low, outs.pop(0)[...]) for _ in range(blocks)]
            grad_act = grad_act[0] if blocks == 1 else jnp.concatenate(grad_act, axis=1)
            grad_pre = (grad_act * slopes[quarter][rows].astype(F32)).astype(BF16)
            total = total + dot_last(grad_pre, into[...])
        if not last:
            refs[0][rows] = total
            return
        normed1, inv_std1, lines, grad_out, grad_low_out = refs
        grad = norm_back(total * line_of(lines, GAIN1), normed1[rows], inv_std1[rows])
        grad_out[rows] = grad
        grad_low_out[rows] = grad.astype(BF16)

    by_chunks(before.shape[0], chunk)


def call_ffn_backward(deps, grad_low, before, slopes, in_quarters, out_quarters, *for_norm):
    seq, width = before.shape
    last = bool(for_norm)
    return kernel(
        functools.partial(ffn_backward, last, len(out_quarters) // 2, len(slopes)),
        deps,
        FFN_MIB,
        in_specs=[VMEM] * (4 + len(slopes) + len(out_quarters) + len(for_norm)),
        out_specs=[VMEM] * (1 + last),
        out_shape=[sds((seq, width), F32)] + [sds((seq, width), BF16)] * last,
        cost_estimate=cost(5),
        name="ffn_backward",
    )(grad_low, before, *slopes, *in_quarters, *out_quarters, *for_norm)


def attend_backward(columns, unroll, leaving, grad_low, before, turned_ref, att_ref, prob_ref, weight, *refs):
    input_grad, token, grad_turned, grad_att = refs[:4]
    width = 3 * HEAD_DIM
    root = HEAD_DIM**-0.5
    grad_att[...] = dot_last(weight[columns:], grad_low[...]).astype(BF16)

    @pl.loop(0, columns // width, unroll=unroll)
    def _(head):
        base = pl.multiple_of(head * width, width)
        places = [pl.ds(base + i * HEAD_DIM, HEAD_DIM) for i in range(3)]
        queries, keys, values = (turned_ref[place] for place in places)
        part = pl.ds(pl.multiple_of(head * HEAD_DIM, HEAD_DIM), HEAD_DIM)
        grad = grad_att[part]
        prob = prob_ref[head]
        row_dot = jnp.sum(grad.astype(F32) * att_ref[part].astype(F32), axis=0, keepdims=True)
        grad_scores = (prob.astype(F32) * (dot(values.T, grad) - row_dot)).astype(BF16)
        grad_turned[places[0]] = (dot(keys, grad_scores) * root).astype(BF16)
        grad_turned[places[1]] = (dot_last(queries, grad_scores) * root).astype(BF16)
        grad_turned[places[2]] = dot_last(grad, prob).astype(BF16)

    token[...] = jnp.zeros_like(token)
    grads = grad_turned[...].T
    if not leaving:
        input_grad[...] = before[...] + dot(grads, weight[:columns])
        return
    total, sems = refs[4:]
    parts = [slice(i, i + CHUNK) for i in range(0, before.shape[0], CHUNK)]
    copies = [
        pltpu.make_async_copy(total.at[part], input_grad.at[part], sems.at[i])
        for i, part in enumerate(parts)
    ]
    for part, copy in zip(parts, copies):
        total[part] = before[part] + dot(grads[part], weight[:columns])
        copy.start()
    for copy in copies:
        copy.wait()


def call_attend_backward(deps, columns, unroll, leaving, grad_low, before, saved, quarter):
    seq, width = before.shape
    inner = columns // 3
    return kernel(
        functools.partial(attend_backward, columns, unroll, leaving),
        deps,
        ATTEND_MIB,
        in_specs=[VMEM] * 6,
        out_specs=[ANY if leaving else VMEM, VMEM],
        out_shape=[sds((seq, width), F32), sds((8, LANES), F32)],
        scratch_shapes=[pltpu.VMEM((columns, seq), BF16), pltpu.VMEM((inner, seq), BF16)]
        + [pltpu.VMEM((seq, width), F32), pltpu.SemaphoreType.DMA((seq // CHUNK,))] * leaving,
        cost_estimate=cost(8),
        name="attend_backward",
    )(grad_low, before, *saved, quarter)


def prepare(meta, down, up, query, key, value, g1, s1, g2, s2, g3, s3, keep, send, lines, shard):
    n_adapters, _, rank = down.shape
    for i in range(n_adapters):
        shard[0, :, i * rank : (i + 1) * rank] = down[i].astype(F32)
        shard[1, :, i * rank : (i + 1) * rank] = up[i].astype(F32)
    for i, ref in enumerate((query, key, value)):
        shard[2 + i] = ref[...].astype(F32)
    half = keep.shape[2]
    mine = pl.multiple_of(meta[CORE] * half, LANES)
    other = pl.multiple_of((1 - meta[CORE]) * half, LANES)
    keep[...] = shard[:, :, pl.ds(mine, half)].astype(BF16)
    send[...] = shard[:, :, pl.ds(other, half)].astype(BF16)
    for i, ref in enumerate((g1, s1, g2, s2, g3, s3)):
        lines[i : i + 1] = ref[...].reshape(1, -1)
    lines[6:8] = jnp.zeros((2, lines.shape[1]), F32)


def call_prepare(meta, down, up, query, key, value, *vectors):
    rows, width = query.shape
    half = sds((5, rows, width // 2), BF16)
    return pl.pallas_call(
        prepare,
        in_specs=[SMEM] + [VMEM] * 11,
        out_specs=[VMEM] * 3,
        out_shape=[half, half, sds((8, width), F32)],
        scratch_shapes=[pltpu.VMEM((5, rows, width), F32)],
        compiler_params=params(16),
        cost_estimate=cost(1),
        name="prepare",
    )(meta, *(in_hbm(a) for a in (down, up, query, key, value, *vectors)))


def join_attention(qkv_turned, attn_out, attn):
    columns = qkv_turned.shape[0]
    attn[:columns] = qkv_turned[...]
    attn[columns:] = attn_out[...]


def call_join_attention(deps, qkv_turned, attn_out):
    rows, width = qkv_turned.shape[0] + attn_out.shape[0], attn_out.shape[1]
    return kernel(
        join_attention,
        deps,
        16,
        in_specs=[VMEM] * 2,
        out_specs=VMEM,
        out_shape=sds((rows, width), BF16),
        cost_estimate=cost(1),
        name="join_attention",
    )(in_hbm(qkv_turned), in_hbm(attn_out))


def prepare_shares(meta, attn, into, out, with_attn, with_in, out_last, *copies):
    half = attn.shape[0] // 2
    more = half // 3
    mine = pl.multiple_of(meta[PAIR_Y] * half, 16)
    other = pl.multiple_of((1 - meta[PAIR_Y]) * half + 2 * more, 16)
    with_attn[:half] = attn[pl.ds(mine, half)]
    with_attn[half : half + more] = attn[pl.ds(other, more)]
    cut = with_attn.shape[0] - half - more
    with_attn[half + more :] = out[:cut]
    half = into.shape[0] // 2
    with_in[:half] = into[pl.ds(pl.multiple_of(meta[PAIR_Z] * half, 16), half)]
    end = cut + with_in.shape[0] - half
    with_in[half:] = out[cut:end]
    out_last[...] = out[end:]
    for source, copy in zip((into, out), copies):
        copy[...] = source[...]


def call_prepare_shares(deps, meta, attn, into, out):
    rows, width = attn.shape
    unit = out.shape[0] // 12
    shares = (rows // 2 + rows // 6 + unit, into.shape[0] // 2 + 3 * unit, 8 * unit)
    shares = shares + (into.shape[0], out.shape[0])
    return kernel(
        prepare_shares,
        deps,
        16,
        in_specs=[SMEM] + [VMEM] * 3,
        out_specs=[VMEM] * 5,
        out_shape=[sds((n, width), BF16) for n in shares],
        cost_estimate=cost(1),
        name="prepare_shares",
    )(meta, attn, in_hbm(into), in_hbm(out))


def chip_tile(meta, keep, got, attn, tile, attn_out):
    mine, other = keep[...].astype(F32), got[...].astype(F32)
    lower = jnp.where(meta[CORE] == 0, mine, other)
    upper = jnp.where(meta[CORE] == 0, other, mine)
    tile[...] = jnp.concatenate([lower, upper], axis=1).astype(BF16)


def call_chip_tile(meta, keep, got, attn):
    n_mats, rows, half = keep.shape
    return kernel(
        chip_tile,
        [],
        16,
        in_specs=[SMEM] + [VMEM] * 2 + [ANY],
        out_specs=[VMEM, ANY],
        out_shape=[sds((n_mats, 2 * rows, half), BF16), sds(attn.shape, attn.dtype)],
        input_output_aliases={3: 1},
        cost_estimate=cost(1),
        name="chip_tile",
    )(meta, keep, got, attn)


def add_blocks(*blocks):
    total = functools.reduce(jnp.add, (b.astype(F32) for b in blocks))
    tail = total[-8:-4] + total[-4:]
    return jnp.concatenate([total[:-8], split_lines(tail)], axis=0)


def sum_cores(keep, got, p_keep, p_send, q_keep, q_send):
    half = p_keep.shape[-1]
    for x in range(2):
        for y in range(2):

            @pl.loop(0, 4)
            def _(z, x=x, y=y):
                total = add_blocks(keep[x, y, z], got[x, y, z]).astype(BF16)
                (p_send if x else p_keep)[y, z] = total[:, :half]
                (q_send if y else q_keep)[x, z] = total[:, half:]


def sum_first(p_keep, p_got, q_keep, q_got, p2_keep, p2_send, q2_keep, q2_send):
    @pl.loop(0, 4)
    def _(z):
        for out, index in ((p2_keep, 0), (p2_send, 1)):
            out[z] = add_blocks(p_keep[index, z], p_got[index, z]).astype(BF16)
        for out, index in ((q2_keep, 0), (q2_send, 1)):
            out[z] = add_blocks(q_keep[index, z], q_got[index, z]).astype(BF16)


def sum_second(p_keep, p_got, q_keep, q_got, *outs):
    half = p_keep.shape[-1]
    for z in range(4):
        outs[z][:, :half] = add_blocks(p_keep[z], p_got[z]).astype(BF16)
        outs[z][:, half:] = add_blocks(q_keep[z], q_got[z]).astype(BF16)


def sum_last(n_adapters, keep, got1, got2, got3, query, key, value, gain, bias, mass):
    total = add_blocks(keep[...], got1[...], got2[...], got3[...])
    rows = query.shape[0]
    for i, out in enumerate((query, key, value)):
        out[...] = total[i * rows : (i + 1) * rows]
    lines = total[-8:-4] + total[-4:]
    gain[...] = lines[0]
    bias[...] = lines[1]
    mass[...] = lines[2, :n_adapters] / lines[2:3, n_adapters : n_adapters + 1].reshape(1)


def small_call(body, name, out_shape, dep, *operands):
    return kernel(
        body,
        (dep,),
        16,
        in_specs=[VMEM] * len(operands),
        out_specs=[VMEM] * len(out_shape),
        out_shape=out_shape,
        cost_estimate=cost(1),
        name=name,
    )(*operands)


def sum_gradients(hops, keep, send, n_adapters, works):
    block, width = keep.shape[3:]
    half = width // 2
    pair = [sds((2, 4, block, half), BF16)] * 4
    single = [sds((4, block, half), BF16)] * 4
    got = hops.flip(send, 1)
    dep = works[0](())
    pk, ps, qk, qs = small_call(sum_cores, "sum_cores", pair, dep, keep, got)
    pg, qg = hops.flip(ps, ALONG_X), hops.flip(qs, ALONG_Y)
    dep = works[1]([pk])
    pk, ps, qk, qs = small_call(sum_first, "sum_first", single, dep, pk, pg, qk, qg)
    pg, qg = hops.flip(ps, ALONG_Y), hops.flip(qs, ALONG_X)
    dep = works[2]([pk])
    parts = small_call(
        sum_second, "sum_second", [sds((block, width), BF16)] * 4, dep, pk, pg, qk, qg
    )
    got = [hops.flip(parts[z], z * ALONG_Z) for z in (2, 3, 1)]
    dep = works[3]([parts[0]])
    rows = (block - 8) // 3
    outs = [sds((rows, width), F32)] * 3 + [sds((width,), F32)] * 2 + [sds((n_adapters,), F32)]
    last = functools.partial(sum_last, n_adapters)
    return small_call(last, "sum_last", outs, dep, parts[0], *got)


ALONG_X, ALONG_Y, ALONG_Z = 2, 4, 8


class Hops:
    def __init__(self, mesh):
        self.count = mesh.size
        self.tiled = mesh.shape["dp"] == 8 and mesh.shape["tensor"] == 4

    def flip(self, array, bits):
        return lax.ppermute(array, AXES, [(i, i ^ bits) for i in range(self.count)])


def half_of(block, parity):
    half = block.shape[0] // 2
    return lax.dynamic_slice_in_dim(block, parity * half, half, 0)


def plain_schedule(
    meta, doc_lengths, tokens, out_grad, lines, columns, n_adapters, attn, into, out, shard
):
    attn, into, out = (lax.all_gather(w, "tensor", axis=0) for w in (attn, into, out))
    weights = lax.all_gather(shard, AXES, axis=1, tiled=True)
    pairs = [slice(i, i + 2) for i in range(0, attn.shape[0], 2)]
    before, saved, slopes = tokens, [], []
    for pair in pairs:
        last = pair is pairs[-1]
        results = call_attend_forward(
            [], columns, last, meta, doc_lengths, tokens, before, lines, tuple(attn[pair])
        )
        saved += [results[:3], results[3:6]]
        before = results[6]
    first, normed1, inv_std1 = results[6:]
    sums = first
    for pair in pairs:
        slope, sums = call_ffn_forward([], first, sums, tuple(into[pair]), tuple(out[pair]))
        slopes.append(slope)
    layer_out, *parts, keep, send = call_merging(
        n_adapters, meta, doc_lengths, sums, lines, out_grad, weights
    )
    total, low = call_merging_input([], sums, lines, *parts, weights)
    width = tokens.shape[1]
    blocks = jnp.transpose(jnp.stack([keep, send]), (3, 2, 1, 0, 4, 5)).reshape(32, -1, width)
    squares = blocks[:, :-8].reshape(32, 3, width // 32, width)
    squares = jnp.transpose(squares, (1, 0, 2, 3)).reshape(3, width, width).astype(F32)
    squares = lax.psum_scatter(squares, AXES, scatter_dimension=1, tiled=True)
    tail = blocks[0, -8:].astype(F32)
    totals = lax.psum(tail[:4] + tail[4:], AXES)
    for pair, slope in zip(pairs, slopes):
        for_norm = (normed1, inv_std1, lines) if pair is pairs[-1] else ()
        total, *rest = call_ffn_backward(
            [], low, total, [slope], tuple(into[pair]), tuple(out[pair]), *for_norm
        )
    (low,) = rest
    for quarter, kept in zip(attn, saved):
        total, _ = call_attend_backward([], columns, False, False, low, total, kept, quarter)
    mass = totals[2, :n_adapters] / totals[2, n_adapters]
    return (layer_out, total, squares[0], squares[1], squares[2], totals[0], totals[1], mass)


def per_device(
    hops,
    tokens,
    doc_lengths,
    qkv_weight,
    attn_out_weight,
    norm1_gain,
    norm1_bias,
    ffn_in_weight,
    ffn_out_weight,
    norm2_gain,
    norm2_bias,
    adapter_down,
    adapter_up,
    merging_query,
    merging_key,
    merging_value,
    merging_gain,
    merging_bias,
    out_grad,
):
    n_adapters, rows, rank = adapter_down.shape
    columns = qkv_weight.shape[1]
    tensor, dp = lax.axis_index("tensor"), lax.axis_index("dp")
    pair_y, pair_z = dp % 2, dp // 2 % 2
    meta = jnp.stack([tensor % 2, tensor // 2, pair_y, pair_z, dp // 2, tensor]).astype(jnp.int32)
    flip = hops.flip
    if not hops.tiled:
        meta = meta * (jnp.arange(meta.shape[0]) == ROW)

    keep, send, lines = call_prepare(
        meta,
        adapter_down,
        jnp.transpose(adapter_up, (0, 2, 1)),
        merging_query,
        merging_key,
        merging_value,
        norm1_gain,
        norm1_bias,
        norm2_gain,
        norm2_bias,
        merging_gain,
        merging_bias,
    )
    attn = call_join_attention([keep], qkv_weight.T, attn_out_weight)
    if not hops.tiled:
        shard = jnp.concatenate([keep, send], axis=2)
        return plain_schedule(
            meta, doc_lengths, tokens, out_grad, lines, columns, n_adapters, attn, ffn_in_weight, ffn_out_weight, shard
        )
    tile, attn = call_chip_tile(meta, keep, flip(send, 1), attn)
    with_attn, with_in, out_2, into, out = call_prepare_shares(
        [], meta, attn, ffn_in_weight, ffn_out_weight
    )
    tile_x = flip(tile, ALONG_X)
    attn_core = flip(attn, 1)
    both, with_attn, into, out = sync(
        "phase1", meta, [[tile, tile_x]], [with_attn, into, out], [attn_core]
    )
    z2, y0, with_attn_x = flip(both, 2 * ALONG_Z), flip(both, ALONG_Y), flip(with_attn, ALONG_X)
    in_core, out_core = flip(into, 1), flip(out, 1)
    saved_near = call_attend_forward(
        [both], columns, False, meta, doc_lengths, tokens, tokens, lines, (attn, attn_core)
    )
    half = attn.shape[0] // 2
    third = half // 3
    joined, attn_x, with_in, y0, z2 = sync(
        "phase2",
        meta,
        [[both, z2], [(with_attn_x, 0, 2 * third)]],
        [with_in, y0, z2],
        [saved_near[6], in_core, out_core],
    )
    with_in_x, attn_y, z1 = flip(with_in, ALONG_X), flip(attn_x, ALONG_Y), flip(joined, ALONG_Z)
    y2 = flip(z2, ALONG_Y)
    joined_c, y0_c = flip(joined, 1), flip(y0, 1)
    attn_far, in_x, out_a, out_2, z1, y2 = sync(
        "phase3",
        meta,
        [
            [PAIR_Y]
            + [(with_attn_x, i * third, third) for i in range(3)]
            + [(attn_y, 0, third), (attn_y, third, third), (with_attn_x, half, third)],
            [(with_in_x, 0, half)],
            [
                (share, start, share.shape[0] - start)
                for share, start in ((with_attn_x, half + third), (with_in_x, half))
            ],
        ],
        [out_2, z1, y2],
        [joined_c, y0_c],
    )
    attn_far_c = flip(attn_far, 1)
    y1, out_b, in_z = flip(z1, ALONG_Y), flip(out_2, ALONG_X), flip(in_x, ALONG_Z)
    z1_c, y2_c, out_a_c = flip(z1, 1), flip(y2, 1), flip(out_a, 1)
    *saved_far, first, normed1, inv_std1 = call_attend_forward(
        [], columns, True, meta, doc_lengths, tokens, saved_near[6], lines, (attn_far, attn_far_c)
    )
    slope_near, sums = call_ffn_forward(
        [], first, first, (ffn_in_weight, in_core), (ffn_out_weight, out_core)
    )
    own, other = 0, 1
    weights = assemble(
        "assemble",
        [first],
        meta,
        None,
        [
            (joined, ((0, 0), (0, 2)), own),
            (joined_c, ((0, 0), (0, 2)), other),
            (z1, ((0, 1), (0, 3)), own),
            (z1_c, ((0, 1), (0, 3)), other),
            (y0, ((1, 0),), own),
            (y0_c, ((1, 0),), other),
            (y2, ((1, 2),), own),
            (y2_c, ((1, 2),), other),
        ],
    )
    in_far, out_b, y1 = sync(
        "phase4", meta, [[PAIR_Z, in_x, in_z]], [out_b, y1], [sums, weights, out_a_c]
    )
    in_far_c, out_b_c, y1_c = flip(in_far, 1), flip(out_b, 1), flip(y1, 1)
    out_far = (out_a, out_b, out_a_c, out_b_c)
    slopes_far = []
    for quarter, blocks in ((in_far, out_far[:2]), (in_far_c, out_far[2:])):
        slope, sums = call_ffn_forward([], first, sums, (quarter,), blocks)
        slopes_far.append(slope)
    last_parts = ((1, 1), (1, 3))
    weights = assemble(
        "assemble_last", [sums], meta, weights, [(y1, last_parts, own), (y1_c, last_parts, other)]
    )
    layer_out, *parts, grad_keep, grad_send = call_merging(
        n_adapters, meta, doc_lengths, sums, lines, out_grad, weights
    )
    done = {}
    attn_quarters = (attn, attn_core, attn_far, attn_far_c)
    saved = (saved_near[:3], saved_near[3:6], saved_far[:3], saved_far[3:6])

    def attention(deps, *quarters):
        for i in quarters:
            done["sum"], token = call_attend_backward(
                deps, columns, i > 1, i == 3, done["low"], done["sum"], saved[i], attn_quarters[i]
            )
            deps = [token]
        return token

    def near(deps):
        (done["sum"],) = call_ffn_backward(
            deps,
            done["low"],
            done["sum"],
            [slope_near],
            (ffn_in_weight, in_core),
            (ffn_out_weight, out_core),
        )
        return done["sum"]

    def far(deps):
        done["sum"], done["low"] = call_ffn_backward(
            deps,
            done["low"],
            done["sum"],
            slopes_far,
            (in_far, in_far_c),
            out_far,
            normed1,
            inv_std1,
            lines,
        )

    def first_work(deps):
        done["sum"], done["low"] = call_merging_input(deps, sums, lines, *parts, weights)
        return done["sum"]

    def second_work(deps):
        near(deps)
        far([])
        return attention([], 0)

    works = (
        first_work,
        second_work,
        lambda deps: attention(deps, 1),
        lambda deps: attention(deps, 2, 3),
    )
    summed = sum_gradients(hops, grad_keep, grad_send, n_adapters, works)
    return (layer_out, done["sum"], *summed)


def solution(mesh):
    split = P(AXES, None)
    in_specs = (
        split,
        P("dp", None),
        P(None, "tensor"),
        P("tensor", None),
        P(),
        P(),
        P(None, "tensor"),
        P("tensor", None),
        P(),
        P(),
        P(None, AXES, None),
        P(None, None, AXES),
        split,
        split,
        split,
        P(),
        P(),
        split,
    )
    out_specs = (split, split, split, split, split, P(), P(), P())
    return jax.shard_map(
        functools.partial(per_device, Hops(mesh)),
        mesh=mesh,
        in_specs=in_specs,
        out_specs=out_specs,
        check_vma=False,
    )
```

```python
import functools

import jax
import jax.numpy as jnp
from jax import lax
from jax.experimental import pallas as pl
from jax.experimental.pallas import tpu as pltpu
from jax.sharding import PartitionSpec as P

HEAD_DIM = 64
AXES = ("dp", "tensor")
ATTEND_MIB, FFN_MIB, MERGE_MIB = 13, 13, 24
LANES = 128
COST = 0.0
CHUNK = 256
EPS = 1e-12
BIG_NEGATIVE = -1e30
ROOT_HALF = 0.7071067811865476
ROOT_TAU = 0.3989422804014327
F32, BF16 = jnp.float32, jnp.bfloat16

CORE, ACROSS, PAIR_Y, PAIR_Z, DEPTH, ROW = range(6)
GAIN1, SHIFT1, GAIN2, SHIFT2, GAIN3, SHIFT3 = range(6)

SMEM = pl.BlockSpec(memory_space=pltpu.SMEM)
VMEM = pl.BlockSpec(memory_space=pltpu.VMEM)
ANY = pl.BlockSpec(memory_space=pl.ANY)
HBM = pl.BlockSpec(memory_space=pltpu.HBM)


def by_chunks(count, body, size=CHUNK):
    @pl.loop(0, count // size)
    def _(i):
        body(pl.ds(pl.multiple_of(i * size, size), size))


def line_of(lines, i):
    return lines[i : i + 1]


def dot(a, b):
    return lax.dot_general(a, b, (((1,), (0,)), ((), ())), preferred_element_type=F32)


def dot_last(a, b):
    return lax.dot_general(a, b, (((1,), (1,)), ((), ())), preferred_element_type=F32)


def dot_first(a, b):
    return lax.dot_general(a, b, (((0,), (0,)), ((), ())), preferred_element_type=F32)


def normalize(u):
    centered = u - jnp.mean(u, axis=-1, keepdims=True)
    inv_std = lax.rsqrt(jnp.mean(centered * centered, axis=-1, keepdims=True) + EPS)
    return centered * inv_std, inv_std


def norm_back(grad, normed, inv_std):
    return inv_std * (
        grad
        - jnp.mean(grad, axis=-1, keepdims=True)
        - normed * jnp.mean(grad * normed, axis=-1, keepdims=True)
    )


def gelu_both(u):
    half = 0.5 * (1.0 + lax.erf(u * ROOT_HALF))
    return u * half, half + u * jnp.exp(-0.5 * u * u) * ROOT_TAU


def segment_bias(meta_ref, lengths_ref, bias_ref):
    seq = bias_ref.shape[0]
    row = meta_ref[ROW]
    by_row = lax.broadcasted_iota(jnp.int32, (seq, 1), 0)
    by_lane = lax.broadcasted_iota(jnp.int32, (1, seq), 1)
    seg_row = jnp.zeros((seq, 1), jnp.int32)
    seg_lane = jnp.zeros((1, seq), jnp.int32)
    end = jnp.int32(0)
    for i in range(lengths_ref.shape[1]):
        end = end + lengths_ref[row, i]
        seg_row = seg_row + jnp.where(by_row >= end, 1, 0)
        seg_lane = seg_lane + jnp.where(by_lane >= end, 1, 0)
    bias_ref[...] = jnp.where(seg_row == seg_lane, 0.0, BIG_NEGATIVE).astype(F32)


def attend_forward(columns, last, meta, lengths, tokens, before, lines, weight0, weight1, *refs):
    saved, first_out, bias = refs[:6], refs[6], refs[-1]
    segment_bias(meta, lengths, bias)
    total = before[...].astype(F32)
    width = 3 * HEAD_DIM
    for quarter, weight in enumerate((weight0, weight1)):
        turned = dot_last(weight[:columns], tokens[...]).astype(BF16)
        turned_out, att_out, prob_out = saved[3 * quarter : 3 * quarter + 3]
        turned_out[...] = turned

        @pl.loop(0, columns // width)
        def _(head, turned_out=turned_out, att_out=att_out, prob_out=prob_out):
            base = pl.multiple_of(head * width, width)
            queries, keys, values = (
                turned_out[pl.ds(base + i * HEAD_DIM, HEAD_DIM)] for i in range(3)
            )
            scores = dot(keys.T, queries * BF16(HEAD_DIM**-0.5)) + bias[...]
            exponent = jnp.exp(scores - jnp.max(scores, axis=0, keepdims=True))
            prob = (exponent * (1.0 / jnp.sum(exponent, axis=0, keepdims=True))).astype(BF16)
            prob_out[head] = prob
            part = pl.ds(pl.multiple_of(head * HEAD_DIM, HEAD_DIM), HEAD_DIM)
            att_out[part] = dot(values, prob).astype(BF16)

        total = total + dot(att_out[...].T, weight[columns:])
    if not last:
        first_out[...] = total
        return
    normed_out, inv_out = refs[7:9]
    normed, inv_std = normalize(total)
    normed_out[...] = normed
    inv_out[...] = inv_std
    first_out[...] = normed * line_of(lines, GAIN1) + line_of(lines, SHIFT1)


def sds(shape, dtype):
    return jax.ShapeDtypeStruct(shape, dtype)


def params(mib):
    return pltpu.CompilerParams(vmem_limit_bytes=mib << 20)


def kernel(body, deps, mib, *, in_specs, **kw):
    n = len(deps)
    call = pl.pallas_call(
        lambda *refs: body(*refs[n:]),
        in_specs=[ANY] * n + in_specs,
        compiler_params=params(mib),
        **kw,
    )
    return functools.partial(call, *deps)


def sync(name, meta, joins, carries, deps):
    sides = [j[0] if isinstance(j[0], int) else None for j in joins]
    parts = [j[1:] if isinstance(j[0], int) else j for j in joins]
    parts = [[p if isinstance(p, tuple) else (p, 0, p.shape[0]) for p in j] for j in parts]
    flat = [p[0] for j in parts for p in j]

    def body(meta_ref, *refs):
        refs = refs[len(carries) :]
        sources, outs = list(refs[: len(flat)]), refs[len(flat) : len(flat) + len(parts)]
        for side, join, out in zip(sides, parts, outs):
            row = 0
            for i, (_, start, size) in enumerate(join):
                if side is not None:
                    n = len(join) // 2
                    row = pl.multiple_of(((meta_ref[side] ^ (i // n)) * n + i % n) * size, 16)
                out[pl.ds(row, size)] = sources.pop(0)[start : start + size]
                row = row + size

    joined = [sds((sum(p[2] for p in j), *j[0][0].shape[1:]), j[0][0].dtype) for j in parts]
    n_deps = len(deps)
    out = kernel(
        body,
        deps,
        16,
        in_specs=[SMEM] + [ANY] * len(carries) + [VMEM] * len(flat),
        out_specs=[VMEM] * len(joined) + [ANY] * len(carries),
        out_shape=joined + [sds(c.shape, c.dtype) for c in carries],
        input_output_aliases={n_deps + 1 + i: len(joined) + i for i in range(len(carries))},
        cost_estimate=cost(0),
        name=name,
    )(meta, *carries, *flat)
    return out


def in_hbm(array):
    return pltpu.with_memory_space_constraint(array, pltpu.HBM)


def cost(us):
    return pl.CostEstimate(flops=int(us * 1.1e9 * COST), bytes_accessed=1024, transcendentals=0)


def call_attend_forward(deps, columns, last, meta, lengths, tokens, before, lines, quarters):
    seq, width = tokens.shape
    heads = columns // (3 * HEAD_DIM)
    inner = heads * HEAD_DIM
    square, narrow = sds((seq, width), F32), sds((seq, 1), F32)
    place = pltpu.HBM
    out_shape = [
        place((columns, seq), BF16),
        place((inner, seq), BF16),
        place((heads, seq, seq), BF16),
    ] * 2 + [square] + [square, narrow] * last
    return kernel(
        functools.partial(attend_forward, columns, last),
        deps,
        ATTEND_MIB,
        in_specs=[SMEM, SMEM] + [VMEM] * 5,
        out_specs=[VMEM] * len(out_shape),
        out_shape=out_shape,
        scratch_shapes=[pltpu.VMEM((seq, seq), F32)],
        cost_estimate=cost(8),
        name="attend_forward",
    )(meta, lengths, tokens, before, lines, *quarters)


def ffn_forward(quarters, blocks, first, before, *refs):
    slope_out, sum_out = refs[-2:]

    def chunk(rows):
        low = first[rows].astype(BF16)
        total = before[rows]
        outs = list(refs[quarters:-2])
        for quarter in range(quarters):
            value, slope = gelu_both(dot(low, refs[quarter][...]))
            slope_out[quarter, rows] = slope.astype(BF16)
            value = value.astype(BF16)
            start = 0
            for _ in range(blocks):
                out = outs.pop(0)
                total = total + dot(value[:, start : start + out.shape[0]], out[...])
                start += out.shape[0]
        sum_out[rows] = total

    by_chunks(first.shape[0], chunk)


def call_ffn_forward(deps, first, before, in_quarters, out_quarters):
    seq, width = first.shape
    hidden = in_quarters[0].shape[1]
    quarters = len(in_quarters)
    return kernel(
        functools.partial(ffn_forward, quarters, len(out_quarters) // quarters),
        deps,
        FFN_MIB,
        in_specs=[VMEM] * (2 + quarters + len(out_quarters)),
        out_specs=[VMEM] * 2,
        out_shape=[sds((quarters, seq, hidden), BF16), sds((seq, width), F32)],
        cost_estimate=cost(5),
        name="ffn_forward",
    )(first, before, *in_quarters, *out_quarters)


def assemble(name, deps, meta, weights, tiles):
    n_mats = tiles[0][0].shape[0] // (2 * len(tiles[0][1]))
    rows, half = tiles[0][0].shape[1:]
    count = sum(2 * len(parts) for _, parts, _ in tiles)
    before = [] if weights is None else [weights]

    def body(meta_ref, *refs):
        refs = refs[len(before) :]
        out, sems = refs[-2:]
        copies = []
        for ref, (_, parts, core_rel) in zip(refs, tiles):
            side = pl.multiple_of((meta_ref[CORE] ^ core_rel) * half, LANES)
            for j, (y_rel, z_rel) in enumerate(parts):
                for x_rel in range(2):
                    chip = ((meta_ref[DEPTH] ^ z_rel) * 2 + (meta_ref[PAIR_Y] ^ y_rel)) * 2
                    chip = chip + (meta_ref[ACROSS] ^ x_rel)
                    first = pl.multiple_of(chip * rows, 16)
                    target = out.at[:, pl.ds(first, rows), pl.ds(side, half)]
                    source = ref.at[pl.ds((2 * j + x_rel) * n_mats, n_mats)]
                    copies.append(pltpu.make_async_copy(source, target, sems.at[len(copies)]))
        for copy in copies:
            copy.start()
        for copy in copies:
            copy.wait()

    return kernel(
        body,
        deps,
        16,
        in_specs=[SMEM] + [ANY] * len(before) + [VMEM] * len(tiles),
        out_specs=ANY,
        out_shape=sds((n_mats, 2 * half, 2 * half), BF16),
        input_output_aliases={len(deps) + 1: 0} if before else {},
        scratch_shapes=[pltpu.SemaphoreType.DMA((count,))],
        cost_estimate=cost(0),
        name=name,
    )(meta, *before, *(tile for tile, _, _ in tiles))


def split_lines(total):
    high = total.astype(BF16).astype(F32)
    return jnp.concatenate([high, total - high], axis=0)


def merging(n_adapters, meta, lengths, sums, lines, out_grad, matrices, *refs):
    layer_out, part_out, fquery_out, middle_out, keep_out, send_out = refs[:6]
    grads, sum_lines, states, probes, blends, values, fqueries, joined, sem = refs[6:]
    leave = pltpu.make_async_copy(joined, layer_out, sem)
    seq, width = sums.shape
    scale = width**-0.5
    down, up, query, key, value = (matrices.at[i] for i in range(5))
    gain2, shift2 = line_of(lines, GAIN2), line_of(lines, SHIFT2)
    gain3, shift3 = line_of(lines, GAIN3), line_of(lines, SHIFT3)
    spread = jnp.where(
        lax.broadcasted_iota(jnp.int32, (LANES, width), 0)
        == lax.broadcasted_iota(jnp.int32, (LANES, width), 1) // (width // n_adapters),
        1.0,
        0.0,
    ).astype(BF16)
    lane = lax.broadcasted_iota(jnp.int32, (1, LANES), 1)
    count = jnp.int32(0)
    for i in range(lengths.shape[1]):
        count = count + lengths[meta[ROW], i]
    sum_lines[...] = jnp.zeros_like(sum_lines)

    def by_adapter(terms):
        high = terms.astype(BF16)
        rest = (terms - high.astype(F32)).astype(BF16)
        return dot_last(high, spread) + dot_last(rest, spread)

    def chunk(rows):
        normed2, _ = normalize(sums[rows])
        second = normed2 * gain2 + shift2
        second_low = second.astype(BF16)
        states[rows] = second_low
        act, slope = (v.astype(BF16) for v in gelu_both(dot(second_low, down[...])))
        fquery = dot(second_low, query[...]).astype(BF16)
        fqueries[rows] = fquery
        probe = dot_last(fquery, key[...]).astype(BF16)
        probe_up = dot(probe, up[...])
        logits = scale * (
            jnp.sum(probe.astype(F32) * second, axis=1, keepdims=True)
            + by_adapter(act * probe_up)
        )
        logits = jnp.where(lane < n_adapters, logits, BIG_NEGATIVE)
        exponent = jnp.exp(logits - jnp.max(logits, axis=1, keepdims=True))
        mix = exponent / jnp.sum(exponent, axis=1, keepdims=True)
        mix_low = mix.astype(BF16)
        mix_sum = jnp.sum(mix_low.astype(F32), axis=1, keepdims=True)
        mix_wide = dot(mix_low, spread).astype(BF16)
        blended = second * mix_sum + dot_last((mix_wide * act).astype(BF16), up[...])
        blended = blended.astype(BF16)
        blends[rows] = blended
        normed3, inv_std3 = normalize(second + dot(blended, value[...]))
        joined[...] = normed3 * gain3 + shift3
        leave.start()

        token = rows.start + lax.broadcasted_iota(jnp.int32, (rows.size, 1), 0)
        keep = jnp.where(token < count, 1.0, 0.0)
        cot = out_grad[rows].astype(F32) * keep
        mass = jnp.sum(mix * keep, axis=0, keepdims=True)
        mass = jnp.where(lane == n_adapters, jnp.sum(keep), mass)
        sum_lines[0:1] += jnp.sum(cot * normed3, axis=0, keepdims=True)
        sum_lines[1:2] += jnp.sum(cot, axis=0, keepdims=True)
        sum_lines[2:3, :LANES] += mass

        grad_pre = norm_back(cot * gain3, normed3, inv_std3)
        grad_proj = grad_pre.astype(BF16)
        values[rows] = grad_proj
        grad_blend = dot_last(grad_proj, value[...]).astype(BF16)
        blend_up = dot(grad_blend, up[...])
        grad_mix = jnp.sum(
            grad_blend.astype(F32) * second, axis=1, keepdims=True
        ) + by_adapter(act * blend_up)
        grad_logits = mix * (grad_mix - jnp.sum(grad_mix * mix, axis=1, keepdims=True))
        grad_logits = grad_logits.astype(BF16)
        logit_sum = jnp.sum(grad_logits.astype(F32), axis=1, keepdims=True)
        logit_wide = dot(grad_logits, spread).astype(BF16)
        grad_probe = second * logit_sum + dot_last((logit_wide * act).astype(BF16), up[...])
        grad_probe = (scale * grad_probe).astype(BF16)
        probes[rows] = grad_probe
        fquery_out[rows] = dot(grad_probe, key[...]).astype(BF16)
        grad_act = mix_wide.astype(F32) * blend_up + (scale * logit_wide.astype(F32)) * probe_up
        middle_out[rows] = (grad_act * slope.astype(F32)).astype(BF16)
        part_out[rows] = (
            grad_pre + grad_blend.astype(F32) * mix_sum + probe.astype(F32) * (scale * logit_sum)
        )

    by_chunks(seq, chunk, seq)

    @pl.loop(0, width // CHUNK)
    def _(i):
        part = pl.ds(pl.multiple_of(i * CHUNK, CHUNK), CHUNK)
        grads[0, part] = dot_first(states[:, part], fquery_out[...])
        grads[1, part] = dot_first(probes[:, part], fqueries[...])
        grads[2, part] = dot_first(blends[:, part], values[...])

    tail = split_lines(sum_lines[0:4])
    rows = width // 32

    @pl.loop(0, 16)
    def _(chip):
        z_rel = (chip // 4) ^ meta[DEPTH]
        y_rel = (chip // 2 % 2) ^ meta[PAIR_Y]
        x_rel = (chip % 2) ^ meta[ACROSS]
        for core_rel, out in ((0, keep_out), (1, send_out)):
            first = pl.multiple_of((chip * 2 + (meta[CORE] ^ core_rel)) * rows, 8)
            block = [grads[i, pl.ds(first, rows)] for i in range(3)] + [tail]
            out[x_rel, y_rel, z_rel] = jnp.concatenate(block, axis=0).astype(BF16)

    leave.wait()


def call_merging(n_adapters, meta, lengths, sums, lines, out_grad, matrices):
    seq, width = sums.shape
    block = 3 * width // 32 + 8
    return pl.pallas_call(
        functools.partial(merging, n_adapters),
        in_specs=[SMEM, SMEM] + [VMEM] * 4,
        out_specs=[ANY] + [VMEM] * 5,
        out_shape=[sds((seq, width), F32)] * 2
        + [sds((seq, width), BF16)] * 2
        + [sds((2, 2, 4, block, width), BF16)] * 2,
        scratch_shapes=[pltpu.VMEM((3, width, width), F32), pltpu.VMEM((8, width), F32)]
        + [pltpu.VMEM((seq, width), BF16)] * 5
        + [pltpu.VMEM((seq, width), F32), pltpu.SemaphoreType.DMA],
        compiler_params=params(MERGE_MIB),
        cost_estimate=cost(18),
        name="merging",
    )(meta, lengths, sums, lines, out_grad, matrices)


def merging_input(sums, lines, part, grad_fquery, grad_middle, matrices, grad_out, grad_low_out):
    def chunk(rows):
        normed, inv_std = normalize(sums[rows])
        grad = part[rows] + dot_last(grad_fquery[rows], matrices[2])
        grad = grad + dot_last(grad_middle[rows], matrices[0])
        grad = norm_back(grad * line_of(lines, GAIN2), normed, inv_std)
        grad_out[rows] = grad
        grad_low_out[rows] = grad.astype(BF16)

    by_chunks(part.shape[0], chunk)


def call_merging_input(deps, sums, lines, part, grad_fquery, grad_middle, matrices):
    return kernel(
        merging_input,
        deps,
        FFN_MIB,
        in_specs=[VMEM] * 6,
        out_specs=[VMEM] * 2,
        out_shape=[sds(part.shape, F32), sds(part.shape, BF16)],
        cost_estimate=cost(3),
        name="merging_input",
    )(sums, lines, part, grad_fquery, grad_middle, matrices)


def ffn_backward(last, blocks, n_slopes, grad_low, before, *refs):
    slopes, (in0, in1), refs = refs[:n_slopes], refs[n_slopes : n_slopes + 2], refs[n_slopes + 2 :]
    slopes = [slope.at[i] for slope in slopes for i in range(slope.shape[0])]
    all_outs, refs = refs[: 2 * blocks], refs[2 * blocks :]

    def chunk(rows):
        low = grad_low[rows]
        total = before[rows]
        outs = list(all_outs)
        for quarter, into in enumerate((in0, in1)):
            grad_act = [dot_last(low, outs.pop(0)[...]) for _ in range(blocks)]
            grad_act = grad_act[0] if blocks == 1 else jnp.concatenate(grad_act, axis=1)
            grad_pre = (grad_act * slopes[quarter][rows].astype(F32)).astype(BF16)
            total = total + dot_last(grad_pre, into[...])
        if not last:
            refs[0][rows] = total
            return
        normed1, inv_std1, lines, grad_out, grad_low_out = refs
        grad = norm_back(total * line_of(lines, GAIN1), normed1[rows], inv_std1[rows])
        grad_out[rows] = grad
        grad_low_out[rows] = grad.astype(BF16)

    by_chunks(before.shape[0], chunk)


def call_ffn_backward(deps, grad_low, before, slopes, in_quarters, out_quarters, *for_norm):
    seq, width = before.shape
    last = bool(for_norm)
    return kernel(
        functools.partial(ffn_backward, last, len(out_quarters) // 2, len(slopes)),
        deps,
        FFN_MIB,
        in_specs=[VMEM] * (4 + len(slopes) + len(out_quarters) + len(for_norm)),
        out_specs=[VMEM] * (1 + last),
        out_shape=[sds((seq, width), F32)] + [sds((seq, width), BF16)] * last,
        cost_estimate=cost(5),
        name="ffn_backward",
    )(grad_low, before, *slopes, *in_quarters, *out_quarters, *for_norm)


def attend_backward(columns, unroll, leaving, grad_low, before, turned_ref, att_ref, prob_ref, weight, *refs):
    input_grad, token, grad_turned, grad_att = refs[:4]
    width = 3 * HEAD_DIM
    root = HEAD_DIM**-0.5
    grad_att[...] = dot_last(weight[columns:], grad_low[...]).astype(BF16)

    @pl.loop(0, columns // width, unroll=unroll)
    def _(head):
        base = pl.multiple_of(head * width, width)
        places = [pl.ds(base + i * HEAD_DIM, HEAD_DIM) for i in range(3)]
        queries, keys, values = (turned_ref[place] for place in places)
        part = pl.ds(pl.multiple_of(head * HEAD_DIM, HEAD_DIM), HEAD_DIM)
        grad = grad_att[part]
        prob = prob_ref[head]
        row_dot = jnp.sum(grad.astype(F32) * att_ref[part].astype(F32), axis=0, keepdims=True)
        grad_scores = (prob.astype(F32) * (dot(values.T, grad) - row_dot)).astype(BF16)
        grad_turned[places[0]] = (dot(keys, grad_scores) * root).astype(BF16)
        grad_turned[places[1]] = (dot_last(queries, grad_scores) * root).astype(BF16)
        grad_turned[places[2]] = dot_last(grad, prob).astype(BF16)

    token[...] = jnp.zeros_like(token)
    grads = grad_turned[...].T
    if not leaving:
        input_grad[...] = before[...] + dot(grads, weight[:columns])
        return
    total, sems = refs[4:]
    parts = [slice(i, i + CHUNK) for i in range(0, before.shape[0], CHUNK)]
    copies = [
        pltpu.make_async_copy(total.at[part], input_grad.at[part], sems.at[i])
        for i, part in enumerate(parts)
    ]
    for part, copy in zip(parts, copies):
        total[part] = before[part] + dot(grads[part], weight[:columns])
        copy.start()
    for copy in copies:
        copy.wait()


def call_attend_backward(deps, columns, unroll, leaving, grad_low, before, saved, quarter):
    seq, width = before.shape
    inner = columns // 3
    return kernel(
        functools.partial(attend_backward, columns, unroll, leaving),
        deps,
        ATTEND_MIB,
        in_specs=[VMEM] * 6,
        out_specs=[ANY if leaving else VMEM, VMEM],
        out_shape=[sds((seq, width), F32), sds((8, LANES), F32)],
        scratch_shapes=[pltpu.VMEM((columns, seq), BF16), pltpu.VMEM((inner, seq), BF16)]
        + [pltpu.VMEM((seq, width), F32), pltpu.SemaphoreType.DMA((seq // CHUNK,))] * leaving,
        cost_estimate=cost(8),
        name="attend_backward",
    )(grad_low, before, *saved, quarter)


def prepare(meta, down, up, query, key, value, g1, s1, g2, s2, g3, s3, keep, send, lines, shard):
    n_adapters, _, rank = down.shape
    for i in range(n_adapters):
        shard[0, :, i * rank : (i + 1) * rank] = down[i].astype(F32)
        shard[1, :, i * rank : (i + 1) * rank] = up[i].astype(F32)
    for i, ref in enumerate((query, key, value)):
        shard[2 + i] = ref[...].astype(F32)
    half = keep.shape[2]
    mine = pl.multiple_of(meta[CORE] * half, LANES)
    other = pl.multiple_of((1 - meta[CORE]) * half, LANES)
    keep[...] = shard[:, :, pl.ds(mine, half)].astype(BF16)
    send[...] = shard[:, :, pl.ds(other, half)].astype(BF16)
    for i, ref in enumerate((g1, s1, g2, s2, g3, s3)):
        lines[i : i + 1] = ref[...].reshape(1, -1)
    lines[6:8] = jnp.zeros((2, lines.shape[1]), F32)


def call_prepare(meta, down, up, query, key, value, *vectors):
    rows, width = query.shape
    half = sds((5, rows, width // 2), BF16)
    return pl.pallas_call(
        prepare,
        in_specs=[SMEM] + [VMEM] * 11,
        out_specs=[VMEM] * 3,
        out_shape=[half, half, sds((8, width), F32)],
        scratch_shapes=[pltpu.VMEM((5, rows, width), F32)],
        compiler_params=params(16),
        cost_estimate=cost(1),
        name="prepare",
    )(meta, *(in_hbm(a) for a in (down, up, query, key, value, *vectors)))


def join_attention(qkv_turned, attn_out, attn):
    columns = qkv_turned.shape[0]
    attn[:columns] = qkv_turned[...]
    attn[columns:] = attn_out[...]


def call_join_attention(deps, qkv_turned, attn_out):
    rows, width = qkv_turned.shape[0] + attn_out.shape[0], attn_out.shape[1]
    return kernel(
        join_attention,
        deps,
        16,
        in_specs=[VMEM] * 2,
        out_specs=VMEM,
        out_shape=sds((rows, width), BF16),
        cost_estimate=cost(1),
        name="join_attention",
    )(in_hbm(qkv_turned), in_hbm(attn_out))


def prepare_shares(meta, attn, into, out, with_attn, with_in, out_last, *copies):
    half = attn.shape[0] // 2
    more = half // 3
    mine = pl.multiple_of(meta[PAIR_Y] * half, 16)
    other = pl.multiple_of((1 - meta[PAIR_Y]) * half + 2 * more, 16)
    with_attn[:half] = attn[pl.ds(mine, half)]
    with_attn[half : half + more] = attn[pl.ds(other, more)]
    cut = with_attn.shape[0] - half - more
    with_attn[half + more :] = out[:cut]
    half = into.shape[0] // 2
    with_in[:half] = into[pl.ds(pl.multiple_of(meta[PAIR_Z] * half, 16), half)]
    end = cut + with_in.shape[0] - half
    with_in[half:] = out[cut:end]
    out_last[...] = out[end:]
    for source, copy in zip((into, out), copies):
        copy[...] = source[...]


def call_prepare_shares(deps, meta, attn, into, out):
    rows, width = attn.shape
    unit = out.shape[0] // 12
    shares = (rows // 2 + rows // 6 + unit, into.shape[0] // 2 + 3 * unit, 8 * unit)
    shares = shares + (into.shape[0], out.shape[0])
    return kernel(
        prepare_shares,
        deps,
        16,
        in_specs=[SMEM] + [VMEM] * 3,
        out_specs=[VMEM] * 5,
        out_shape=[sds((n, width), BF16) for n in shares],
        cost_estimate=cost(1),
        name="prepare_shares",
    )(meta, attn, in_hbm(into), in_hbm(out))


def chip_tile(meta, keep, got, attn, tile, attn_out):
    mine, other = keep[...].astype(F32), got[...].astype(F32)
    lower = jnp.where(meta[CORE] == 0, mine, other)
    upper = jnp.where(meta[CORE] == 0, other, mine)
    tile[...] = jnp.concatenate([lower, upper], axis=1).astype(BF16)


def call_chip_tile(meta, keep, got, attn):
    n_mats, rows, half = keep.shape
    return kernel(
        chip_tile,
        [],
        16,
        in_specs=[SMEM] + [VMEM] * 2 + [ANY],
        out_specs=[VMEM, ANY],
        out_shape=[sds((n_mats, 2 * rows, half), BF16), sds(attn.shape, attn.dtype)],
        input_output_aliases={3: 1},
        cost_estimate=cost(1),
        name="chip_tile",
    )(meta, keep, got, attn)


def add_blocks(*blocks):
    total = functools.reduce(jnp.add, (b.astype(F32) for b in blocks))
    tail = total[-8:-4] + total[-4:]
    return jnp.concatenate([total[:-8], split_lines(tail)], axis=0)


def sum_cores(keep, got, p_keep, p_send, q_keep, q_send):
    half = p_keep.shape[-1]
    for x in range(2):
        for y in range(2):

            @pl.loop(0, 4)
            def _(z, x=x, y=y):
                total = add_blocks(keep[x, y, z], got[x, y, z]).astype(BF16)
                (p_send if x else p_keep)[y, z] = total[:, :half]
                (q_send if y else q_keep)[x, z] = total[:, half:]


def sum_first(p_keep, p_got, q_keep, q_got, p2_keep, p2_send, q2_keep, q2_send):
    @pl.loop(0, 4)
    def _(z):
        for out, index in ((p2_keep, 0), (p2_send, 1)):
            out[z] = add_blocks(p_keep[index, z], p_got[index, z]).astype(BF16)
        for out, index in ((q2_keep, 0), (q2_send, 1)):
            out[z] = add_blocks(q_keep[index, z], q_got[index, z]).astype(BF16)


def sum_second(p_keep, p_got, q_keep, q_got, *outs):
    half = p_keep.shape[-1]
    for z in range(4):
        outs[z][:, :half] = add_blocks(p_keep[z], p_got[z]).astype(BF16)
        outs[z][:, half:] = add_blocks(q_keep[z], q_got[z]).astype(BF16)


def sum_last(n_adapters, keep, got1, got2, got3, query, key, value, gain, bias, mass):
    total = add_blocks(keep[...], got1[...], got2[...], got3[...])
    rows = query.shape[0]
    for i, out in enumerate((query, key, value)):
        out[...] = total[i * rows : (i + 1) * rows]
    lines = total[-8:-4] + total[-4:]
    gain[...] = lines[0]
    bias[...] = lines[1]
    mass[...] = lines[2, :n_adapters] / lines[2:3, n_adapters : n_adapters + 1].reshape(1)


def small_call(body, name, out_shape, dep, *operands):
    return kernel(
        body,
        (dep,),
        16,
        in_specs=[VMEM] * len(operands),
        out_specs=[VMEM] * len(out_shape),
        out_shape=out_shape,
        cost_estimate=cost(1),
        name=name,
    )(*operands)


def sum_gradients(hops, keep, send, n_adapters, works):
    block, width = keep.shape[3:]
    half = width // 2
    pair = [sds((2, 4, block, half), BF16)] * 4
    single = [sds((4, block, half), BF16)] * 4
    got = hops.flip(send, 1)
    dep = works[0](())
    pk, ps, qk, qs = small_call(sum_cores, "sum_cores", pair, dep, keep, got)
    pg, qg = hops.flip(ps, ALONG_X), hops.flip(qs, ALONG_Y)
    dep = works[1]([pk])
    pk, ps, qk, qs = small_call(sum_first, "sum_first", single, dep, pk, pg, qk, qg)
    pg, qg = hops.flip(ps, ALONG_Y), hops.flip(qs, ALONG_X)
    dep = works[2]([pk])
    parts = small_call(
        sum_second, "sum_second", [sds((block, width), BF16)] * 4, dep, pk, pg, qk, qg
    )
    got = [hops.flip(parts[z], z * ALONG_Z) for z in (2, 3, 1)]
    dep = works[3]([parts[0]])
    rows = (block - 8) // 3
    outs = [sds((rows, width), F32)] * 3 + [sds((width,), F32)] * 2 + [sds((n_adapters,), F32)]
    last = functools.partial(sum_last, n_adapters)
    return small_call(last, "sum_last", outs, dep, parts[0], *got)


ALONG_X, ALONG_Y, ALONG_Z = 2, 4, 8


class Hops:
    def __init__(self, mesh):
        self.count = mesh.size
        self.tiled = mesh.shape["dp"] == 8 and mesh.shape["tensor"] == 4

    def flip(self, array, bits):
        return lax.ppermute(array, AXES, [(i, i ^ bits) for i in range(self.count)])


def half_of(block, parity):
    half = block.shape[0] // 2
    return lax.dynamic_slice_in_dim(block, parity * half, half, 0)


def plain_schedule(
    meta, doc_lengths, tokens, out_grad, lines, columns, n_adapters, attn, into, out, shard
):
    attn, into, out = (lax.all_gather(w, "tensor", axis=0) for w in (attn, into, out))
    weights = lax.all_gather(shard, AXES, axis=1, tiled=True)
    pairs = [slice(i, i + 2) for i in range(0, attn.shape[0], 2)]
    before, saved, slopes = tokens, [], []
    for pair in pairs:
        last = pair is pairs[-1]
        results = call_attend_forward(
            [], columns, last, meta, doc_lengths, tokens, before, lines, tuple(attn[pair])
        )
        saved += [results[:3], results[3:6]]
        before = results[6]
    first, normed1, inv_std1 = results[6:]
    sums = first
    for pair in pairs:
        slope, sums = call_ffn_forward([], first, sums, tuple(into[pair]), tuple(out[pair]))
        slopes.append(slope)
    layer_out, *parts, keep, send = call_merging(
        n_adapters, meta, doc_lengths, sums, lines, out_grad, weights
    )
    total, low = call_merging_input([], sums, lines, *parts, weights)
    width = tokens.shape[1]
    blocks = jnp.transpose(jnp.stack([keep, send]), (3, 2, 1, 0, 4, 5)).reshape(32, -1, width)
    squares = blocks[:, :-8].reshape(32, 3, width // 32, width)
    squares = jnp.transpose(squares, (1, 0, 2, 3)).reshape(3, width, width).astype(F32)
    squares = lax.psum_scatter(squares, AXES, scatter_dimension=1, tiled=True)
    tail = blocks[0, -8:].astype(F32)
    totals = lax.psum(tail[:4] + tail[4:], AXES)
    for pair, slope in zip(pairs, slopes):
        for_norm = (normed1, inv_std1, lines) if pair is pairs[-1] else ()
        total, *rest = call_ffn_backward(
            [], low, total, [slope], tuple(into[pair]), tuple(out[pair]), *for_norm
        )
    (low,) = rest
    for quarter, kept in zip(attn, saved):
        total, _ = call_attend_backward([], columns, False, False, low, total, kept, quarter)
    mass = totals[2, :n_adapters] / totals[2, n_adapters]
    return (layer_out, total, squares[0], squares[1], squares[2], totals[0], totals[1], mass)


def per_device(
    hops,
    tokens,
    doc_lengths,
    qkv_weight,
    attn_out_weight,
    norm1_gain,
    norm1_bias,
    ffn_in_weight,
    ffn_out_weight,
    norm2_gain,
    norm2_bias,
    adapter_down,
    adapter_up,
    merging_query,
    merging_key,
    merging_value,
    merging_gain,
    merging_bias,
    out_grad,
):
    n_adapters, rows, rank = adapter_down.shape
    columns = qkv_weight.shape[1]
    tensor, dp = lax.axis_index("tensor"), lax.axis_index("dp")
    pair_y, pair_z = dp % 2, dp // 2 % 2
    meta = jnp.stack([tensor % 2, tensor // 2, pair_y, pair_z, dp // 2, tensor]).astype(jnp.int32)
    flip = hops.flip
    if not hops.tiled:
        meta = meta * (jnp.arange(meta.shape[0]) == ROW)

    keep, send, lines = call_prepare(
        meta,
        adapter_down,
        jnp.transpose(adapter_up, (0, 2, 1)),
        merging_query,
        merging_key,
        merging_value,
        norm1_gain,
        norm1_bias,
        norm2_gain,
        norm2_bias,
        merging_gain,
        merging_bias,
    )
    attn = call_join_attention([keep], qkv_weight.T, attn_out_weight)
    if not hops.tiled:
        shard = jnp.concatenate([keep, send], axis=2)
        return plain_schedule(
            meta, doc_lengths, tokens, out_grad, lines, columns, n_adapters, attn, ffn_in_weight, ffn_out_weight, shard
        )
    tile, attn = call_chip_tile(meta, keep, flip(send, 1), attn)
    with_attn, with_in, out_2, into, out = call_prepare_shares(
        [], meta, attn, ffn_in_weight, ffn_out_weight
    )
    tile_x = flip(tile, ALONG_X)
    attn_core = flip(attn, 1)
    both, with_attn, into, out = sync(
        "phase1", meta, [[tile, tile_x]], [with_attn, into, out], [attn_core]
    )
    z2, y0, with_attn_x = flip(both, 2 * ALONG_Z), flip(both, ALONG_Y), flip(with_attn, ALONG_X)
    in_core, out_core = flip(into, 1), flip(out, 1)
    saved_near = call_attend_forward(
        [both], columns, False, meta, doc_lengths, tokens, tokens, lines, (attn, attn_core)
    )
    half = attn.shape[0] // 2
    third = half // 3
    joined, attn_x, with_in, y0, z2 = sync(
        "phase2",
        meta,
        [[both, z2], [(with_attn_x, 0, 2 * third)]],
        [with_in, y0, z2],
        [saved_near[6], in_core, out_core],
    )
    with_in_x, attn_y, z1 = flip(with_in, ALONG_X), flip(attn_x, ALONG_Y), flip(joined, ALONG_Z)
    y2 = flip(z2, ALONG_Y)
    joined_c, y0_c = flip(joined, 1), flip(y0, 1)
    attn_far, in_x, out_a, out_2, z1, y2 = sync(
        "phase3",
        meta,
        [
            [PAIR_Y]
            + [(with_attn_x, i * third, third) for i in range(3)]
            + [(attn_y, 0, third), (attn_y, third, third), (with_attn_x, half, third)],
            [(with_in_x, 0, half)],
            [
                (share, start, share.shape[0] - start)
                for share, start in ((with_attn_x, half + third), (with_in_x, half))
            ],
        ],
        [out_2, z1, y2],
        [joined_c, y0_c],
    )
    attn_far_c = flip(attn_far, 1)
    y1, out_b, in_z = flip(z1, ALONG_Y), flip(out_2, ALONG_X), flip(in_x, ALONG_Z)
    z1_c, y2_c, out_a_c = flip(z1, 1), flip(y2, 1), flip(out_a, 1)
    *saved_far, first, normed1, inv_std1 = call_attend_forward(
        [], columns, True, meta, doc_lengths, tokens, saved_near[6], lines, (attn_far, attn_far_c)
    )
    slope_near, sums = call_ffn_forward(
        [], first, first, (ffn_in_weight, in_core), (ffn_out_weight, out_core)
    )
    own, other = 0, 1
    weights = assemble(
        "assemble",
        [first],
        meta,
        None,
        [
            (joined, ((0, 0), (0, 2)), own),
            (joined_c, ((0, 0), (0, 2)), other),
            (z1, ((0, 1), (0, 3)), own),
            (z1_c, ((0, 1), (0, 3)), other),
            (y0, ((1, 0),), own),
            (y0_c, ((1, 0),), other),
            (y2, ((1, 2),), own),
            (y2_c, ((1, 2),), other),
        ],
    )
    in_far, out_b, y1 = sync(
        "phase4", meta, [[PAIR_Z, in_x, in_z]], [out_b, y1], [sums, weights, out_a_c]
    )
    in_far_c, out_b_c, y1_c = flip(in_far, 1), flip(out_b, 1), flip(y1, 1)
    out_far = (out_a, out_b, out_a_c, out_b_c)
    slopes_far = []
    for quarter, blocks in ((in_far, out_far[:2]), (in_far_c, out_far[2:])):
        slope, sums = call_ffn_forward([], first, sums, (quarter,), blocks)
        slopes_far.append(slope)
    last_parts = ((1, 1), (1, 3))
    weights = assemble(
        "assemble_last", [sums], meta, weights, [(y1, last_parts, own), (y1_c, last_parts, other)]
    )
    layer_out, *parts, grad_keep, grad_send = call_merging(
        n_adapters, meta, doc_lengths, sums, lines, out_grad, weights
    )
    done = {}
    attn_quarters = (attn, attn_core, attn_far, attn_far_c)
    saved = (saved_near[:3], saved_near[3:6], saved_far[:3], saved_far[3:6])

    def attention(deps, *quarters):
        for i in quarters:
            done["sum"], token = call_attend_backward(
                deps, columns, i > 1, i == 3, done["low"], done["sum"], saved[i], attn_quarters[i]
            )
            deps = [token]
        return token

    def near(deps):
        (done["sum"],) = call_ffn_backward(
            deps,
            done["low"],
            done["sum"],
            [slope_near],
            (ffn_in_weight, in_core),
            (ffn_out_weight, out_core),
        )
        return done["sum"]

    def far(deps):
        done["sum"], done["low"] = call_ffn_backward(
            deps,
            done["low"],
            done["sum"],
            slopes_far,
            (in_far, in_far_c),
            out_far,
            normed1,
            inv_std1,
            lines,
        )

    def first_work(deps):
        done["sum"], done["low"] = call_merging_input(deps, sums, lines, *parts, weights)
        return done["sum"]

    def second_work(deps):
        near(deps)
        far([])
        return attention([], 0)

    works = (
        first_work,
        second_work,
        lambda deps: attention(deps, 1),
        lambda deps: attention(deps, 2, 3),
    )
    summed = sum_gradients(hops, grad_keep, grad_send, n_adapters, works)
    return (layer_out, done["sum"], *summed)


def solution(mesh):
    split = P(AXES, None)
    in_specs = (
        split,
        P("dp", None),
        P(None, "tensor"),
        P("tensor", None),
        P(),
        P(),
        P(None, "tensor"),
        P("tensor", None),
        P(),
        P(),
        P(None, AXES, None),
        P(None, None, AXES),
        split,
        split,
        split,
        P(),
        P(),
        split,
    )
    out_specs = (split, split, split, split, split, P(), P(), P())
    return jax.shard_map(
        functools.partial(per_device, Hops(mesh)),
        mesh=mesh,
        in_specs=in_specs,
        out_specs=out_specs,
        check_vma=False,
    )
```

```python
import functools

import jax
import jax.numpy as jnp
from jax import lax
from jax.experimental import pallas as pl
from jax.experimental.pallas import tpu as pltpu
from jax.sharding import PartitionSpec as P

HEAD_DIM = 64
AXES = ("dp", "tensor")
ATTEND_MIB, FFN_MIB, MERGE_MIB = 16, 16, 24
LANES = 128
COST = 0.0
CHUNK = 256
EPS = 1e-12
BIG_NEGATIVE = -1e30
ROOT_HALF = 0.7071067811865476
ROOT_TAU = 0.3989422804014327
F32, BF16 = jnp.float32, jnp.bfloat16

CORE, ACROSS, PAIR_Y, PAIR_Z, DEPTH, ROW = range(6)
GAIN1, SHIFT1, GAIN2, SHIFT2, GAIN3, SHIFT3 = range(6)

SMEM = pl.BlockSpec(memory_space=pltpu.SMEM)
VMEM = pl.BlockSpec(memory_space=pltpu.VMEM)
ANY = pl.BlockSpec(memory_space=pl.ANY)
HBM = pl.BlockSpec(memory_space=pltpu.HBM)


def by_chunks(count, body, size=CHUNK):
    @pl.loop(0, count // size)
    def _(i):
        body(pl.ds(pl.multiple_of(i * size, size), size))


def line_of(lines, i):
    return lines[i : i + 1]


def dot(a, b):
    return lax.dot_general(a, b, (((1,), (0,)), ((), ())), preferred_element_type=F32)


def dot_last(a, b):
    return lax.dot_general(a, b, (((1,), (1,)), ((), ())), preferred_element_type=F32)


def dot_first(a, b):
    return lax.dot_general(a, b, (((0,), (0,)), ((), ())), preferred_element_type=F32)


def normalize(u):
    centered = u - jnp.mean(u, axis=-1, keepdims=True)
    inv_std = lax.rsqrt(jnp.mean(centered * centered, axis=-1, keepdims=True) + EPS)
    return centered * inv_std, inv_std


def norm_back(grad, normed, inv_std):
    return inv_std * (
        grad
        - jnp.mean(grad, axis=-1, keepdims=True)
        - normed * jnp.mean(grad * normed, axis=-1, keepdims=True)
    )


def gelu_both(u):
    half = 0.5 * (1.0 + lax.erf(u * ROOT_HALF))
    return u * half, half + u * jnp.exp(-0.5 * u * u) * ROOT_TAU


def segment_bias(meta_ref, lengths_ref, bias_ref):
    seq = bias_ref.shape[0]
    row = meta_ref[ROW]
    by_row = lax.broadcasted_iota(jnp.int32, (seq, 1), 0)
    by_lane = lax.broadcasted_iota(jnp.int32, (1, seq), 1)
    seg_row = jnp.zeros((seq, 1), jnp.int32)
    seg_lane = jnp.zeros((1, seq), jnp.int32)
    end = jnp.int32(0)
    for i in range(lengths_ref.shape[1]):
        end = end + lengths_ref[row, i]
        seg_row = seg_row + jnp.where(by_row >= end, 1, 0)
        seg_lane = seg_lane + jnp.where(by_lane >= end, 1, 0)
    bias_ref[...] = jnp.where(seg_row == seg_lane, 0.0, BIG_NEGATIVE).astype(F32)


def attend_forward(columns, last, meta, lengths, tokens, before, lines, weight0, weight1, *refs):
    saved, first_out, bias = refs[:6], refs[6], refs[-1]
    segment_bias(meta, lengths, bias)
    total = before[...].astype(F32)
    width = 3 * HEAD_DIM
    for quarter, weight in enumerate((weight0, weight1)):
        turned = dot_last(weight[:columns], tokens[...]).astype(BF16)
        turned_out, att_out, prob_out = saved[3 * quarter : 3 * quarter + 3]
        turned_out[...] = turned

        @pl.loop(0, columns // width)
        def _(head, turned_out=turned_out, att_out=att_out, prob_out=prob_out):
            base = pl.multiple_of(head * width, width)
            queries, keys, values = (
                turned_out[pl.ds(base + i * HEAD_DIM, HEAD_DIM)] for i in range(3)
            )
            scores = dot(keys.T, queries * BF16(HEAD_DIM**-0.5)) + bias[...]
            exponent = jnp.exp(scores - jnp.max(scores, axis=0, keepdims=True))
            prob = (exponent * (1.0 / jnp.sum(exponent, axis=0, keepdims=True))).astype(BF16)
            prob_out[head] = prob
            part = pl.ds(pl.multiple_of(head * HEAD_DIM, HEAD_DIM), HEAD_DIM)
            att_out[part] = dot(values, prob).astype(BF16)

        total = total + dot(att_out[...].T, weight[columns:])
    if not last:
        first_out[...] = total
        return
    normed_out, inv_out = refs[7:9]
    normed, inv_std = normalize(total)
    normed_out[...] = normed
    inv_out[...] = inv_std
    first_out[...] = normed * line_of(lines, GAIN1) + line_of(lines, SHIFT1)


def sds(shape, dtype):
    return jax.ShapeDtypeStruct(shape, dtype)


def params(mib):
    return pltpu.CompilerParams(vmem_limit_bytes=mib << 20)


def kernel(body, deps, mib, *, in_specs, **kw):
    n = len(deps)
    call = pl.pallas_call(
        lambda *refs: body(*refs[n:]),
        in_specs=[ANY] * n + in_specs,
        compiler_params=params(mib),
        **kw,
    )
    return functools.partial(call, *deps)


def sync(name, meta, joins, carries, deps):
    sides = [j[0] if isinstance(j[0], int) else None for j in joins]
    parts = [j[1:] if isinstance(j[0], int) else j for j in joins]
    parts = [[p if isinstance(p, tuple) else (p, 0, p.shape[0]) for p in j] for j in parts]
    flat = [p[0] for j in parts for p in j]

    def body(meta_ref, *refs):
        refs = refs[len(carries) :]
        sources, outs = list(refs[: len(flat)]), refs[len(flat) : len(flat) + len(parts)]
        for side, join, out in zip(sides, parts, outs):
            row = 0
            for i, (_, start, size) in enumerate(join):
                if side is not None:
                    n = len(join) // 2
                    row = pl.multiple_of(((meta_ref[side] ^ (i // n)) * n + i % n) * size, 16)
                out[pl.ds(row, size)] = sources.pop(0)[start : start + size]
                row = row + size

    joined = [sds((sum(p[2] for p in j), *j[0][0].shape[1:]), j[0][0].dtype) for j in parts]
    n_deps = len(deps)
    out = kernel(
        body,
        deps,
        16,
        in_specs=[SMEM] + [ANY] * len(carries) + [VMEM] * len(flat),
        out_specs=[VMEM] * len(joined) + [ANY] * len(carries),
        out_shape=joined + [sds(c.shape, c.dtype) for c in carries],
        input_output_aliases={n_deps + 1 + i: len(joined) + i for i in range(len(carries))},
        cost_estimate=cost(0),
        name=name,
    )(meta, *carries, *flat)
    return out


def in_hbm(array):
    return pltpu.with_memory_space_constraint(array, pltpu.HBM)


def cost(us):
    return pl.CostEstimate(flops=int(us * 1.1e9 * COST), bytes_accessed=1024, transcendentals=0)


def call_attend_forward(deps, columns, last, meta, lengths, tokens, before, lines, quarters):
    seq, width = tokens.shape
    heads = columns // (3 * HEAD_DIM)
    inner = heads * HEAD_DIM
    square, narrow = sds((seq, width), F32), sds((seq, 1), F32)
    place = pltpu.HBM
    out_shape = [
        place((columns, seq), BF16),
        place((inner, seq), BF16),
        place((heads, seq, seq), BF16),
    ] * 2 + [square] + [square, narrow] * last
    return kernel(
        functools.partial(attend_forward, columns, last),
        deps,
        ATTEND_MIB,
        in_specs=[SMEM, SMEM] + [VMEM] * 5,
        out_specs=[VMEM] * len(out_shape),
        out_shape=out_shape,
        scratch_shapes=[pltpu.VMEM((seq, seq), F32)],
        cost_estimate=cost(8),
        name="attend_forward",
    )(meta, lengths, tokens, before, lines, *quarters)


def ffn_forward(quarters, blocks, first, before, *refs):
    slope_out, sum_out = refs[-2:]

    def chunk(rows):
        low = first[rows].astype(BF16)
        total = before[rows]
        outs = list(refs[quarters:-2])
        for quarter in range(quarters):
            value, slope = gelu_both(dot(low, refs[quarter][...]))
            slope_out[quarter, rows] = slope.astype(BF16)
            value = value.astype(BF16)
            start = 0
            for _ in range(blocks):
                out = outs.pop(0)
                total = total + dot(value[:, start : start + out.shape[0]], out[...])
                start += out.shape[0]
        sum_out[rows] = total

    by_chunks(first.shape[0], chunk, CHUNK * 2 // quarters)


def call_ffn_forward(deps, first, before, in_quarters, out_quarters):
    seq, width = first.shape
    hidden = in_quarters[0].shape[1]
    quarters = len(in_quarters)
    return kernel(
        functools.partial(ffn_forward, quarters, len(out_quarters) // quarters),
        deps,
        FFN_MIB,
        in_specs=[VMEM] * (2 + quarters + len(out_quarters)),
        out_specs=[VMEM] * 2,
        out_shape=[sds((quarters, seq, hidden), BF16), sds((seq, width), F32)],
        cost_estimate=cost(5),
        name="ffn_forward",
    )(first, before, *in_quarters, *out_quarters)


def assemble(name, deps, meta, weights, tiles):
    n_mats = tiles[0][0].shape[0] // (2 * len(tiles[0][1]))
    rows, half = tiles[0][0].shape[1:]
    count = sum(2 * len(parts) for _, parts, _ in tiles)
    before = [] if weights is None else [weights]

    def body(meta_ref, *refs):
        refs = refs[len(before) :]
        out, sems = refs[-2:]
        copies = []
        for ref, (_, parts, core_rel) in zip(refs, tiles):
            side = pl.multiple_of((meta_ref[CORE] ^ core_rel) * half, LANES)
            for j, (y_rel, z_rel) in enumerate(parts):
                for x_rel in range(2):
                    chip = ((meta_ref[DEPTH] ^ z_rel) * 2 + (meta_ref[PAIR_Y] ^ y_rel)) * 2
                    chip = chip + (meta_ref[ACROSS] ^ x_rel)
                    first = pl.multiple_of(chip * rows, 16)
                    target = out.at[:, pl.ds(first, rows), pl.ds(side, half)]
                    source = ref.at[pl.ds((2 * j + x_rel) * n_mats, n_mats)]
                    copies.append(pltpu.make_async_copy(source, target, sems.at[len(copies)]))
        for copy in copies:
            copy.start()
        for copy in copies:
            copy.wait()

    return kernel(
        body,
        deps,
        16,
        in_specs=[SMEM] + [ANY] * len(before) + [VMEM] * len(tiles),
        out_specs=ANY,
        out_shape=sds((n_mats, 2 * half, 2 * half), BF16),
        input_output_aliases={len(deps) + 1: 0} if before else {},
        scratch_shapes=[pltpu.SemaphoreType.DMA((count,))],
        cost_estimate=cost(0),
        name=name,
    )(meta, *before, *(tile for tile, _, _ in tiles))


def split_lines(total):
    high = total.astype(BF16).astype(F32)
    return jnp.concatenate([high, total - high], axis=0)


def merging(n_adapters, meta, lengths, sums, lines, out_grad, matrices, *refs):
    layer_out, part_out, fquery_out, middle_out, keep_out, send_out = refs[:6]
    grads, sum_lines, states, probes, blends, values, fqueries, joined, sem = refs[6:]
    leave = pltpu.make_async_copy(joined, layer_out, sem)
    seq, width = sums.shape
    scale = width**-0.5
    down, up, query, key, value = (matrices.at[i] for i in range(5))
    gain2, shift2 = line_of(lines, GAIN2), line_of(lines, SHIFT2)
    gain3, shift3 = line_of(lines, GAIN3), line_of(lines, SHIFT3)
    spread = jnp.where(
        lax.broadcasted_iota(jnp.int32, (LANES, width), 0)
        == lax.broadcasted_iota(jnp.int32, (LANES, width), 1) // (width // n_adapters),
        1.0,
        0.0,
    ).astype(BF16)
    lane = lax.broadcasted_iota(jnp.int32, (1, LANES), 1)
    count = jnp.int32(0)
    for i in range(lengths.shape[1]):
        count = count + lengths[meta[ROW], i]
    sum_lines[...] = jnp.zeros_like(sum_lines)

    def by_adapter(terms):
        high = terms.astype(BF16)
        rest = (terms - high.astype(F32)).astype(BF16)
        return dot_last(high, spread) + dot_last(rest, spread)

    def chunk(rows):
        normed2, _ = normalize(sums[rows])
        second = normed2 * gain2 + shift2
        second_low = second.astype(BF16)
        states[rows] = second_low
        act, slope = (v.astype(BF16) for v in gelu_both(dot(second_low, down[...])))
        fquery = dot(second_low, query[...]).astype(BF16)
        fqueries[rows] = fquery
        probe = dot_last(fquery, key[...]).astype(BF16)
        probe_up = dot(probe, up[...])
        logits = scale * (
            jnp.sum(probe.astype(F32) * second, axis=1, keepdims=True)
            + by_adapter(act * probe_up)
        )
        logits = jnp.where(lane < n_adapters, logits, BIG_NEGATIVE)
        exponent = jnp.exp(logits - jnp.max(logits, axis=1, keepdims=True))
        mix = exponent / jnp.sum(exponent, axis=1, keepdims=True)
        mix_low = mix.astype(BF16)
        mix_sum = jnp.sum(mix_low.astype(F32), axis=1, keepdims=True)
        mix_wide = dot(mix_low, spread).astype(BF16)
        blended = second * mix_sum + dot_last((mix_wide * act).astype(BF16), up[...])
        blended = blended.astype(BF16)
        blends[rows] = blended
        normed3, inv_std3 = normalize(second + dot(blended, value[...]))
        joined[...] = normed3 * gain3 + shift3
        leave.start()

        token = rows.start + lax.broadcasted_iota(jnp.int32, (rows.size, 1), 0)
        keep = jnp.where(token < count, 1.0, 0.0)
        cot = out_grad[rows].astype(F32) * keep
        mass = jnp.sum(mix * keep, axis=0, keepdims=True)
        mass = jnp.where(lane == n_adapters, jnp.sum(keep), mass)
        sum_lines[0:1] += jnp.sum(cot * normed3, axis=0, keepdims=True)
        sum_lines[1:2] += jnp.sum(cot, axis=0, keepdims=True)
        sum_lines[2:3, :LANES] += mass

        grad_pre = norm_back(cot * gain3, normed3, inv_std3)
        grad_proj = grad_pre.astype(BF16)
        values[rows] = grad_proj
        grad_blend = dot_last(grad_proj, value[...]).astype(BF16)
        blend_up = dot(grad_blend, up[...])
        grad_mix = jnp.sum(
            grad_blend.astype(F32) * second, axis=1, keepdims=True
        ) + by_adapter(act * blend_up)
        grad_logits = mix * (grad_mix - jnp.sum(grad_mix * mix, axis=1, keepdims=True))
        grad_logits = grad_logits.astype(BF16)
        logit_sum = jnp.sum(grad_logits.astype(F32), axis=1, keepdims=True)
        logit_wide = dot(grad_logits, spread).astype(BF16)
        grad_probe = second * logit_sum + dot_last((logit_wide * act).astype(BF16), up[...])
        grad_probe = (scale * grad_probe).astype(BF16)
        probes[rows] = grad_probe
        fquery_out[rows] = dot(grad_probe, key[...]).astype(BF16)
        grad_act = mix_wide.astype(F32) * blend_up + (scale * logit_wide.astype(F32)) * probe_up
        middle_out[rows] = (grad_act * slope.astype(F32)).astype(BF16)
        part_out[rows] = (
            grad_pre + grad_blend.astype(F32) * mix_sum + probe.astype(F32) * (scale * logit_sum)
        )

    by_chunks(seq, chunk, seq)

    @pl.loop(0, width // CHUNK)
    def _(i):
        part = pl.ds(pl.multiple_of(i * CHUNK, CHUNK), CHUNK)
        grads[0, part] = dot_first(states[:, part], fquery_out[...])
        grads[1, part] = dot_first(probes[:, part], fqueries[...])
        grads[2, part] = dot_first(blends[:, part], values[...])

    tail = split_lines(sum_lines[0:4])
    rows = width // 32

    @pl.loop(0, 16)
    def _(chip):
        z_rel = (chip // 4) ^ meta[DEPTH]
        y_rel = (chip // 2 % 2) ^ meta[PAIR_Y]
        x_rel = (chip % 2) ^ meta[ACROSS]
        for core_rel, out in ((0, keep_out), (1, send_out)):
            first = pl.multiple_of((chip * 2 + (meta[CORE] ^ core_rel)) * rows, 8)
            block = [grads[i, pl.ds(first, rows)] for i in range(3)] + [tail]
            out[x_rel, y_rel, z_rel] = jnp.concatenate(block, axis=0).astype(BF16)

    leave.wait()


def call_merging(n_adapters, meta, lengths, sums, lines, out_grad, matrices):
    seq, width = sums.shape
    block = 3 * width // 32 + 8
    return pl.pallas_call(
        functools.partial(merging, n_adapters),
        in_specs=[SMEM, SMEM] + [VMEM] * 4,
        out_specs=[ANY] + [VMEM] * 5,
        out_shape=[sds((seq, width), F32)] * 2
        + [sds((seq, width), BF16)] * 2
        + [sds((2, 2, 4, block, width), BF16)] * 2,
        scratch_shapes=[pltpu.VMEM((3, width, width), F32), pltpu.VMEM((8, width), F32)]
        + [pltpu.VMEM((seq, width), BF16)] * 5
        + [pltpu.VMEM((seq, width), F32), pltpu.SemaphoreType.DMA],
        compiler_params=params(MERGE_MIB),
        cost_estimate=cost(18),
        name="merging",
    )(meta, lengths, sums, lines, out_grad, matrices)


def merging_input(sums, lines, part, grad_fquery, grad_middle, matrices, grad_out, grad_low_out):
    def chunk(rows):
        normed, inv_std = normalize(sums[rows])
        grad = part[rows] + dot_last(grad_fquery[rows], matrices[2])
        grad = grad + dot_last(grad_middle[rows], matrices[0])
        grad = norm_back(grad * line_of(lines, GAIN2), normed, inv_std)
        grad_out[rows] = grad
        grad_low_out[rows] = grad.astype(BF16)

    by_chunks(part.shape[0], chunk)


def call_merging_input(deps, sums, lines, part, grad_fquery, grad_middle, matrices):
    return kernel(
        merging_input,
        deps,
        FFN_MIB,
        in_specs=[VMEM] * 6,
        out_specs=[VMEM] * 2,
        out_shape=[sds(part.shape, F32), sds(part.shape, BF16)],
        cost_estimate=cost(3),
        name="merging_input",
    )(sums, lines, part, grad_fquery, grad_middle, matrices)


def ffn_backward(last, blocks, n_slopes, grad_low, before, *refs):
    slopes, (in0, in1), refs = refs[:n_slopes], refs[n_slopes : n_slopes + 2], refs[n_slopes + 2 :]
    slopes = [slope.at[i] for slope in slopes for i in range(slope.shape[0])]
    all_outs, refs = refs[: 2 * blocks], refs[2 * blocks :]

    def chunk(rows):
        low = grad_low[rows]
        total = before[rows]
        outs = list(all_outs)
        for quarter, into in enumerate((in0, in1)):
            grad_act = [dot_last(low, outs.pop(0)[...]) for _ in range(blocks)]
            grad_act = grad_act[0] if blocks == 1 else jnp.concatenate(grad_act, axis=1)
            grad_pre = (grad_act * slopes[quarter][rows].astype(F32)).astype(BF16)
            total = total + dot_last(grad_pre, into[...])
        if not last:
            refs[0][rows] = total
            return
        normed1, inv_std1, lines, grad_out, grad_low_out = refs
        grad = norm_back(total * line_of(lines, GAIN1), normed1[rows], inv_std1[rows])
        grad_out[rows] = grad
        grad_low_out[rows] = grad.astype(BF16)

    by_chunks(before.shape[0], chunk)


def call_ffn_backward(deps, grad_low, before, slopes, in_quarters, out_quarters, *for_norm):
    seq, width = before.shape
    last = bool(for_norm)
    return kernel(
        functools.partial(ffn_backward, last, len(out_quarters) // 2, len(slopes)),
        deps,
        FFN_MIB,
        in_specs=[VMEM] * (4 + len(slopes) + len(out_quarters) + len(for_norm)),
        out_specs=[VMEM] * (1 + last),
        out_shape=[sds((seq, width), F32)] + [sds((seq, width), BF16)] * last,
        cost_estimate=cost(5),
        name="ffn_backward",
    )(grad_low, before, *slopes, *in_quarters, *out_quarters, *for_norm)


def attend_backward(columns, unroll, leaving, grad_low, before, turned_ref, att_ref, prob_ref, weight, *refs):
    input_grad, token, grad_turned, grad_att = refs[:4]
    width = 3 * HEAD_DIM
    root = HEAD_DIM**-0.5
    grad_att[...] = dot_last(weight[columns:], grad_low[...]).astype(BF16)

    @pl.loop(0, columns // width, unroll=unroll)
    def _(head):
        base = pl.multiple_of(head * width, width)
        places = [pl.ds(base + i * HEAD_DIM, HEAD_DIM) for i in range(3)]
        queries, keys, values = (turned_ref[place] for place in places)
        part = pl.ds(pl.multiple_of(head * HEAD_DIM, HEAD_DIM), HEAD_DIM)
        grad = grad_att[part]
        prob = prob_ref[head]
        row_dot = jnp.sum(grad.astype(F32) * att_ref[part].astype(F32), axis=0, keepdims=True)
        grad_scores = (prob.astype(F32) * (dot(values.T, grad) - row_dot)).astype(BF16)
        grad_turned[places[0]] = (dot(keys, grad_scores) * root).astype(BF16)
        grad_turned[places[1]] = (dot_last(queries, grad_scores) * root).astype(BF16)
        grad_turned[places[2]] = dot_last(grad, prob).astype(BF16)

    token[...] = jnp.zeros_like(token)
    grads = grad_turned[...].T
    if not leaving:
        input_grad[...] = before[...] + dot(grads, weight[:columns])
        return
    total, sems = refs[4:]
    parts = [slice(i, i + CHUNK) for i in range(0, before.shape[0], CHUNK)]
    copies = [
        pltpu.make_async_copy(total.at[part], input_grad.at[part], sems.at[i])
        for i, part in enumerate(parts)
    ]
    for part, copy in zip(parts, copies):
        total[part] = before[part] + dot(grads[part], weight[:columns])
        copy.start()
    for copy in copies:
        copy.wait()


def call_attend_backward(deps, columns, unroll, leaving, grad_low, before, saved, quarter):
    seq, width = before.shape
    inner = columns // 3
    return kernel(
        functools.partial(attend_backward, columns, unroll, leaving),
        deps,
        ATTEND_MIB,
        in_specs=[VMEM] * 6,
        out_specs=[ANY if leaving else VMEM, VMEM],
        out_shape=[sds((seq, width), F32), sds((8, LANES), F32)],
        scratch_shapes=[pltpu.VMEM((columns, seq), BF16), pltpu.VMEM((inner, seq), BF16)]
        + [pltpu.VMEM((seq, width), F32), pltpu.SemaphoreType.DMA((seq // CHUNK,))] * leaving,
        cost_estimate=cost(8),
        name="attend_backward",
    )(grad_low, before, *saved, quarter)


def prepare(meta, down, up, query, key, value, g1, s1, g2, s2, g3, s3, keep, send, lines, shard):
    n_adapters, _, rank = down.shape
    for i in range(n_adapters):
        shard[0, :, i * rank : (i + 1) * rank] = down[i].astype(F32)
        shard[1, :, i * rank : (i + 1) * rank] = up[i].astype(F32)
    for i, ref in enumerate((query, key, value)):
        shard[2 + i] = ref[...].astype(F32)
    half = keep.shape[2]
    mine = pl.multiple_of(meta[CORE] * half, LANES)
    other = pl.multiple_of((1 - meta[CORE]) * half, LANES)
    keep[...] = shard[:, :, pl.ds(mine, half)].astype(BF16)
    send[...] = shard[:, :, pl.ds(other, half)].astype(BF16)
    for i, ref in enumerate((g1, s1, g2, s2, g3, s3)):
        lines[i : i + 1] = ref[...].reshape(1, -1)
    lines[6:8] = jnp.zeros((2, lines.shape[1]), F32)


def call_prepare(meta, down, up, query, key, value, *vectors):
    rows, width = query.shape
    half = sds((5, rows, width // 2), BF16)
    return pl.pallas_call(
        prepare,
        in_specs=[SMEM] + [VMEM] * 11,
        out_specs=[VMEM] * 3,
        out_shape=[half, half, sds((8, width), F32)],
        scratch_shapes=[pltpu.VMEM((5, rows, width), F32)],
        compiler_params=params(16),
        cost_estimate=cost(1),
        name="prepare",
    )(meta, *(in_hbm(a) for a in (down, up, query, key, value, *vectors)))


def join_attention(qkv_turned, attn_out, attn):
    columns = qkv_turned.shape[0]
    attn[:columns] = qkv_turned[...]
    attn[columns:] = attn_out[...]


def call_join_attention(deps, qkv_turned, attn_out):
    rows, width = qkv_turned.shape[0] + attn_out.shape[0], attn_out.shape[1]
    return kernel(
        join_attention,
        deps,
        16,
        in_specs=[VMEM] * 2,
        out_specs=VMEM,
        out_shape=sds((rows, width), BF16),
        cost_estimate=cost(1),
        name="join_attention",
    )(in_hbm(qkv_turned), in_hbm(attn_out))


def prepare_shares(meta, attn, into, out, with_attn, with_in, out_last, *copies):
    half = attn.shape[0] // 2
    more = half // 3
    mine = pl.multiple_of(meta[PAIR_Y] * half, 16)
    other = pl.multiple_of((1 - meta[PAIR_Y]) * half + 2 * more, 16)
    with_attn[:half] = attn[pl.ds(mine, half)]
    with_attn[half : half + more] = attn[pl.ds(other, more)]
    cut = with_attn.shape[0] - half - more
    with_attn[half + more :] = out[:cut]
    half = into.shape[0] // 2
    with_in[:half] = into[pl.ds(pl.multiple_of(meta[PAIR_Z] * half, 16), half)]
    end = cut + with_in.shape[0] - half
    with_in[half:] = out[cut:end]
    out_last[...] = out[end:]
    for source, copy in zip((into, out), copies):
        copy[...] = source[...]


def call_prepare_shares(deps, meta, attn, into, out):
    rows, width = attn.shape
    unit = out.shape[0] // 12
    shares = (rows // 2 + rows // 6 + unit, into.shape[0] // 2 + 3 * unit, 8 * unit)
    shares = shares + (into.shape[0], out.shape[0])
    return kernel(
        prepare_shares,
        deps,
        16,
        in_specs=[SMEM] + [VMEM] * 3,
        out_specs=[VMEM] * 5,
        out_shape=[sds((n, width), BF16) for n in shares],
        cost_estimate=cost(1),
        name="prepare_shares",
    )(meta, attn, in_hbm(into), in_hbm(out))


def chip_tile(meta, keep, got, attn, tile, attn_out):
    mine, other = keep[...].astype(F32), got[...].astype(F32)
    lower = jnp.where(meta[CORE] == 0, mine, other)
    upper = jnp.where(meta[CORE] == 0, other, mine)
    tile[...] = jnp.concatenate([lower, upper], axis=1).astype(BF16)


def call_chip_tile(meta, keep, got, attn):
    n_mats, rows, half = keep.shape
    return kernel(
        chip_tile,
        [],
        16,
        in_specs=[SMEM] + [VMEM] * 2 + [ANY],
        out_specs=[VMEM, ANY],
        out_shape=[sds((n_mats, 2 * rows, half), BF16), sds(attn.shape, attn.dtype)],
        input_output_aliases={3: 1},
        cost_estimate=cost(1),
        name="chip_tile",
    )(meta, keep, got, attn)


def add_blocks(*blocks):
    total = functools.reduce(jnp.add, (b.astype(F32) for b in blocks))
    tail = total[-8:-4] + total[-4:]
    return jnp.concatenate([total[:-8], split_lines(tail)], axis=0)


def sum_cores(keep, got, p_keep, p_send, q_keep, q_send):
    half = p_keep.shape[-1]
    for x in range(2):
        for y in range(2):

            @pl.loop(0, 4)
            def _(z, x=x, y=y):
                total = add_blocks(keep[x, y, z], got[x, y, z]).astype(BF16)
                (p_send if x else p_keep)[y, z] = total[:, :half]
                (q_send if y else q_keep)[x, z] = total[:, half:]


def sum_first(p_keep, p_got, q_keep, q_got, p2_keep, p2_send, q2_keep, q2_send):
    @pl.loop(0, 4)
    def _(z):
        for out, index in ((p2_keep, 0), (p2_send, 1)):
            out[z] = add_blocks(p_keep[index, z], p_got[index, z]).astype(BF16)
        for out, index in ((q2_keep, 0), (q2_send, 1)):
            out[z] = add_blocks(q_keep[index, z], q_got[index, z]).astype(BF16)


def sum_second(p_keep, p_got, q_keep, q_got, *outs):
    half = p_keep.shape[-1]
    for z in range(4):
        outs[z][:, :half] = add_blocks(p_keep[z], p_got[z]).astype(BF16)
        outs[z][:, half:] = add_blocks(q_keep[z], q_got[z]).astype(BF16)


def sum_last(n_adapters, keep, got1, got2, got3, query, key, value, gain, bias, mass):
    total = add_blocks(keep[...], got1[...], got2[...], got3[...])
    rows = query.shape[0]
    for i, out in enumerate((query, key, value)):
        out[...] = total[i * rows : (i + 1) * rows]
    lines = total[-8:-4] + total[-4:]
    gain[...] = lines[0]
    bias[...] = lines[1]
    mass[...] = lines[2, :n_adapters] / lines[2:3, n_adapters : n_adapters + 1].reshape(1)


def small_call(body, name, out_shape, dep, *operands):
    return kernel(
        body,
        (dep,),
        16,
        in_specs=[VMEM] * len(operands),
        out_specs=[VMEM] * len(out_shape),
        out_shape=out_shape,
        cost_estimate=cost(1),
        name=name,
    )(*operands)


def sum_gradients(hops, keep, send, n_adapters, works):
    block, width = keep.shape[3:]
    half = width // 2
    pair = [sds((2, 4, block, half), BF16)] * 4
    single = [sds((4, block, half), BF16)] * 4
    got = hops.flip(send, 1)
    dep = works[0](())
    pk, ps, qk, qs = small_call(sum_cores, "sum_cores", pair, dep, keep, got)
    pg, qg = hops.flip(ps, ALONG_X), hops.flip(qs, ALONG_Y)
    dep = works[1]([pk])
    pk, ps, qk, qs = small_call(sum_first, "sum_first", single, dep, pk, pg, qk, qg)
    pg, qg = hops.flip(ps, ALONG_Y), hops.flip(qs, ALONG_X)
    dep = works[2]([pk])
    parts = small_call(
        sum_second, "sum_second", [sds((block, width), BF16)] * 4, dep, pk, pg, qk, qg
    )
    got = [hops.flip(parts[z], z * ALONG_Z) for z in (2, 3, 1)]
    dep = works[3]([parts[0]])
    rows = (block - 8) // 3
    outs = [sds((rows, width), F32)] * 3 + [sds((width,), F32)] * 2 + [sds((n_adapters,), F32)]
    last = functools.partial(sum_last, n_adapters)
    return small_call(last, "sum_last", outs, dep, parts[0], *got)


ALONG_X, ALONG_Y, ALONG_Z = 2, 4, 8


class Hops:
    def __init__(self, mesh):
        self.count = mesh.size
        self.tiled = mesh.shape["dp"] == 8 and mesh.shape["tensor"] == 4

    def flip(self, array, bits):
        return lax.ppermute(array, AXES, [(i, i ^ bits) for i in range(self.count)])


def half_of(block, parity):
    half = block.shape[0] // 2
    return lax.dynamic_slice_in_dim(block, parity * half, half, 0)


def plain_schedule(
    meta, doc_lengths, tokens, out_grad, lines, columns, n_adapters, attn, into, out, shard
):
    attn, into, out = (lax.all_gather(w, "tensor", axis=0) for w in (attn, into, out))
    weights = lax.all_gather(shard, AXES, axis=1, tiled=True)
    pairs = [slice(i, i + 2) for i in range(0, attn.shape[0], 2)]
    before, saved, slopes = tokens, [], []
    for pair in pairs:
        last = pair is pairs[-1]
        results = call_attend_forward(
            [], columns, last, meta, doc_lengths, tokens, before, lines, tuple(attn[pair])
        )
        saved += [results[:3], results[3:6]]
        before = results[6]
    first, normed1, inv_std1 = results[6:]
    sums = first
    for pair in pairs:
        slope, sums = call_ffn_forward([], first, sums, tuple(into[pair]), tuple(out[pair]))
        slopes.append(slope)
    layer_out, *parts, keep, send = call_merging(
        n_adapters, meta, doc_lengths, sums, lines, out_grad, weights
    )
    total, low = call_merging_input([], sums, lines, *parts, weights)
    width = tokens.shape[1]
    blocks = jnp.transpose(jnp.stack([keep, send]), (3, 2, 1, 0, 4, 5)).reshape(32, -1, width)
    squares = blocks[:, :-8].reshape(32, 3, width // 32, width)
    squares = jnp.transpose(squares, (1, 0, 2, 3)).reshape(3, width, width).astype(F32)
    squares = lax.psum_scatter(squares, AXES, scatter_dimension=1, tiled=True)
    tail = blocks[0, -8:].astype(F32)
    totals = lax.psum(tail[:4] + tail[4:], AXES)
    for pair, slope in zip(pairs, slopes):
        for_norm = (normed1, inv_std1, lines) if pair is pairs[-1] else ()
        total, *rest = call_ffn_backward(
            [], low, total, [slope], tuple(into[pair]), tuple(out[pair]), *for_norm
        )
    (low,) = rest
    for quarter, kept in zip(attn, saved):
        total, _ = call_attend_backward([], columns, False, False, low, total, kept, quarter)
    mass = totals[2, :n_adapters] / totals[2, n_adapters]
    return (layer_out, total, squares[0], squares[1], squares[2], totals[0], totals[1], mass)


def per_device(
    hops,
    tokens,
    doc_lengths,
    qkv_weight,
    attn_out_weight,
    norm1_gain,
    norm1_bias,
    ffn_in_weight,
    ffn_out_weight,
    norm2_gain,
    norm2_bias,
    adapter_down,
    adapter_up,
    merging_query,
    merging_key,
    merging_value,
    merging_gain,
    merging_bias,
    out_grad,
):
    n_adapters, rows, rank = adapter_down.shape
    columns = qkv_weight.shape[1]
    tensor, dp = lax.axis_index("tensor"), lax.axis_index("dp")
    pair_y, pair_z = dp % 2, dp // 2 % 2
    meta = jnp.stack([tensor % 2, tensor // 2, pair_y, pair_z, dp // 2, tensor]).astype(jnp.int32)
    flip = hops.flip
    if not hops.tiled:
        meta = meta * (jnp.arange(meta.shape[0]) == ROW)

    keep, send, lines = call_prepare(
        meta,
        adapter_down,
        jnp.transpose(adapter_up, (0, 2, 1)),
        merging_query,
        merging_key,
        merging_value,
        norm1_gain,
        norm1_bias,
        norm2_gain,
        norm2_bias,
        merging_gain,
        merging_bias,
    )
    attn = call_join_attention([keep], qkv_weight.T, attn_out_weight)
    if not hops.tiled:
        shard = jnp.concatenate([keep, send], axis=2)
        return plain_schedule(
            meta, doc_lengths, tokens, out_grad, lines, columns, n_adapters, attn, ffn_in_weight, ffn_out_weight, shard
        )
    tile, attn = call_chip_tile(meta, keep, flip(send, 1), attn)
    with_attn, with_in, out_2, into, out = call_prepare_shares(
        [], meta, attn, ffn_in_weight, ffn_out_weight
    )
    tile_x = flip(tile, ALONG_X)
    attn_core = flip(attn, 1)
    both, with_attn, into, out = sync(
        "phase1", meta, [[tile, tile_x]], [with_attn, into, out], [attn_core]
    )
    z2, y0, with_attn_x = flip(both, 2 * ALONG_Z), flip(both, ALONG_Y), flip(with_attn, ALONG_X)
    in_core, out_core = flip(into, 1), flip(out, 1)
    saved_near = call_attend_forward(
        [both], columns, False, meta, doc_lengths, tokens, tokens, lines, (attn, attn_core)
    )
    half = attn.shape[0] // 2
    third = half // 3
    joined, attn_x, with_in, y0, z2 = sync(
        "phase2",
        meta,
        [[both, z2], [(with_attn_x, 0, 2 * third)]],
        [with_in, y0, z2],
        [saved_near[6], in_core, out_core],
    )
    with_in_x, attn_y, z1 = flip(with_in, ALONG_X), flip(attn_x, ALONG_Y), flip(joined, ALONG_Z)
    y2 = flip(z2, ALONG_Y)
    joined_c, y0_c = flip(joined, 1), flip(y0, 1)
    attn_far, in_x, out_a, out_2, z1, y2 = sync(
        "phase3",
        meta,
        [
            [PAIR_Y]
            + [(with_attn_x, i * third, third) for i in range(3)]
            + [(attn_y, 0, third), (attn_y, third, third), (with_attn_x, half, third)],
            [(with_in_x, 0, half)],
            [
                (share, start, share.shape[0] - start)
                for share, start in ((with_attn_x, half + third), (with_in_x, half))
            ],
        ],
        [out_2, z1, y2],
        [joined_c, y0_c],
    )
    attn_far_c = flip(attn_far, 1)
    y1, out_b, in_z = flip(z1, ALONG_Y), flip(out_2, ALONG_X), flip(in_x, ALONG_Z)
    z1_c, y2_c, out_a_c = flip(z1, 1), flip(y2, 1), flip(out_a, 1)
    *saved_far, first, normed1, inv_std1 = call_attend_forward(
        [], columns, True, meta, doc_lengths, tokens, saved_near[6], lines, (attn_far, attn_far_c)
    )
    slope_near, sums = call_ffn_forward(
        [], first, first, (ffn_in_weight, in_core), (ffn_out_weight, out_core)
    )
    own, other = 0, 1
    weights = assemble(
        "assemble",
        [first],
        meta,
        None,
        [
            (joined, ((0, 0), (0, 2)), own),
            (joined_c, ((0, 0), (0, 2)), other),
            (z1, ((0, 1), (0, 3)), own),
            (z1_c, ((0, 1), (0, 3)), other),
            (y0, ((1, 0),), own),
            (y0_c, ((1, 0),), other),
            (y2, ((1, 2),), own),
            (y2_c, ((1, 2),), other),
        ],
    )
    in_far, out_b, y1 = sync(
        "phase4", meta, [[PAIR_Z, in_x, in_z]], [out_b, y1], [sums, weights, out_a_c]
    )
    in_far_c, out_b_c, y1_c = flip(in_far, 1), flip(out_b, 1), flip(y1, 1)
    out_far = (out_a, out_b, out_a_c, out_b_c)
    slopes_far = []
    for quarter, blocks in ((in_far, out_far[:2]), (in_far_c, out_far[2:])):
        slope, sums = call_ffn_forward([], first, sums, (quarter,), blocks)
        slopes_far.append(slope)
    last_parts = ((1, 1), (1, 3))
    weights = assemble(
        "assemble_last", [sums], meta, weights, [(y1, last_parts, own), (y1_c, last_parts, other)]
    )
    layer_out, *parts, grad_keep, grad_send = call_merging(
        n_adapters, meta, doc_lengths, sums, lines, out_grad, weights
    )
    done = {}
    attn_quarters = (attn, attn_core, attn_far, attn_far_c)
    saved = (saved_near[:3], saved_near[3:6], saved_far[:3], saved_far[3:6])

    def attention(deps, *quarters):
        for i in quarters:
            done["sum"], token = call_attend_backward(
                deps, columns, i > 2, i == 3, done["low"], done["sum"], saved[i], attn_quarters[i]
            )
            deps = [token]
        return token

    def near(deps):
        (done["sum"],) = call_ffn_backward(
            deps,
            done["low"],
            done["sum"],
            [slope_near],
            (ffn_in_weight, in_core),
            (ffn_out_weight, out_core),
        )
        return done["sum"]

    def far(deps):
        done["sum"], done["low"] = call_ffn_backward(
            deps,
            done["low"],
            done["sum"],
            slopes_far,
            (in_far, in_far_c),
            out_far,
            normed1,
            inv_std1,
            lines,
        )

    def first_work(deps):
        done["sum"], done["low"] = call_merging_input(deps, sums, lines, *parts, weights)
        return done["sum"]

    def second_work(deps):
        near(deps)
        far([])
        return attention([], 0)

    works = (
        first_work,
        second_work,
        lambda deps: attention(deps, 1),
        lambda deps: attention(deps, 2, 3),
    )
    summed = sum_gradients(hops, grad_keep, grad_send, n_adapters, works)
    return (layer_out, done["sum"], *summed)


def solution(mesh):
    split = P(AXES, None)
    in_specs = (
        split,
        P("dp", None),
        P(None, "tensor"),
        P("tensor", None),
        P(),
        P(),
        P(None, "tensor"),
        P("tensor", None),
        P(),
        P(),
        P(None, AXES, None),
        P(None, None, AXES),
        split,
        split,
        split,
        P(),
        P(),
        split,
    )
    out_specs = (split, split, split, split, split, P(), P(), P())
    return jax.shard_map(
        functools.partial(per_device, Hops(mesh)),
        mesh=mesh,
        in_specs=in_specs,
        out_specs=out_specs,
        check_vma=False,
    )
```
